32 devices in a mesh: img: 8 (over z, x), txt: 4 (over y, core).
Axes of the slice: x: 2, y: 2, z: 4, core: 2. Of those that a mesh axis runs over, the one named last changes fastest.
Arguments:
- image_tokens: bfloat16 [16, 1024, 1024], P('img', 'txt'), may hold values from -6 to 6
- text_states: bfloat16 [8, 128, 1024], P('img', 'txt'), may hold values from -6 to 6
- text_segments: int32 [8, 128], P('img', 'txt'), may hold values from 0 to 1, never falling along the last dimension, each value on 1 to 80 neighbouring positions
- item_segments: int32 [8, 2], P('img'), may hold values from 0 to 1, each once within a row
- norm1_gain: float32 [1024], replicated, may hold values from 0.25 to 1.75
- norm1_bias: float32 [1024], replicated, may hold values from -1.2 to 1.2
- w_qkv: bfloat16 [1024, 3072], replicated, may hold values from -0.1875 to 0.1875
- w_self_out: bfloat16 [1024, 1024], replicated, may hold values from -1.5 to 1.5
- norm2_gain: float32 [1024], replicated, may hold values from 0.25 to 1.75
- norm2_bias: float32 [1024], replicated, may hold values from -1.2 to 1.2
- w_cross_q: bfloat16 [1024, 1024], replicated, may hold values from -0.1875 to 0.1875
- w_cross_kv: bfloat16 [1024, 2048], replicated, may hold values from -0.1875 to 0.1875
- w_cross_out: bfloat16 [1024, 1024], replicated, may hold values from -0.5 to 0.5
- norm3_gain: float32 [1024], replicated, may hold values from 0.25 to 1.75
- norm3_bias: float32 [1024], replicated, may hold values from -1.2 to 1.2
- w_up: bfloat16 [1024, 4096], replicated, may hold values from -0.1875 to 0.1875
- w_down: bfloat16 [4096, 1024], replicated, may hold values from -0.09375 to 0.09375
- cotangent: bfloat16 [16, 1024, 1024], P('img', 'txt'), may hold values from -6 to 6
Outputs:
- block_out: bfloat16 [16, 1024, 1024], P('img', 'txt')
- image_grad: float32 [16, 1024, 1024], P('img', 'txt')
- text_grad: float32 [8, 128, 1024], P('img', 'txt')
- norm1_gain_grad: float32 [1024], P(('img', 'txt'))
- norm1_bias_grad: float32 [1024], P(('img', 'txt'))
- w_qkv_grad: float32 [1024, 3072], P(('img', 'txt'))
- w_self_out_grad: float32 [1024, 1024], P(('img', 'txt'))
- norm2_gain_grad: float32 [1024], P(('img', 'txt'))
- norm2_bias_grad: float32 [1024], P(('img', 'txt'))
- w_cross_q_grad: float32 [1024, 1024], P(('img', 'txt'))
- w_cross_kv_grad: float32 [1024, 2048], P(('img', 'txt'))
- w_cross_out_grad: float32 [1024, 1024], P(('img', 'txt'))
- norm3_gain_grad: float32 [1024], P(('img', 'txt'))
- norm3_bias_grad: float32 [1024], P(('img', 'txt'))
- w_up_grad: float32 [1024, 4096], P(('img', 'txt'))
- w_down_grad: float32 [4096, 1024], P(('img', 'txt'))
The draws below stay inside these ranges and needn't reach their ends.
Inputs may be any that keep to these rules, and one draw needn't show every extreme that they name: `text_segments`: segment numbers never fall along an encoder row, and every number below 2 occurs in each row. `item_segments`: the items of one index of img name each caption of their encoder row exactly once.
All inputs are finite; a program needn't handle non-finite values.
Results may differ from the reference program's by a relative error of at most 0.018.
Values may be sent and summed in bfloat16 or wider, within the bound.
No kernel may reach another device: no remote copies, remote signals or barrier semaphores. Data moves between devices by JAX's collectives and lax.ppermute only.
A program may use at most 320 MiB of HBM per device.

```python
import math
import jax
import jax.numpy as jnp
import numpy as np
from jax import lax

D = 1024
HEADS = 16
HEAD = 64
FF = 4096
ITEM_LEN = 1024
TEXT_LEN = 128
GROUP_ITEMS = 2
ITEMS = 16
N_IMG = 8


def block_levels(rng, shape, pieces, least, top_value):
    level = 1.0
    for position, shards_of in pieces:
        draws = jax.random.uniform(jax.random.fold_in(jax.random.fold_in(rng, 6), position), (shards_of,), jnp.float32, least / len(pieces), top_value / len(pieces))
        level = level * jnp.repeat(jnp.exp(draws), shape[position] // shards_of).reshape((-1,) + (1,) * (len(shape) - 1 - position))
    return level


def length_profile(count, total, limit, lean):
    portions = [(1 << 20) // math.isqrt(standing ** lean) + 1 for standing in range(2, count + 1)]
    rest, holding = total - limit - (count - 1), [1] * (count - 1)
    while rest > 0:
        candidates = [i for i in range(count - 1) if holding[i] < limit]
        whole, budget = sum([portions[i] for i in candidates]), rest
        for i in candidates:
            addition = min(limit - holding[i], max(1, budget * portions[i] // whole), rest)
            holding[i] = holding[i] + addition
            rest = rest - addition
    return np.array([limit] + holding)


def uneven_parts(rng, count, total, limit, slope):
    if count == 2:
        one = jax.random.randint(rng, (), max(1, total - limit), min(limit, total - 1) + 1)
        return jnp.stack([one, total - one])
    lengths = jnp.asarray(length_profile(count, total, limit, slope), jnp.int32)
    twos = (count - 1) // 2
    donor, taker = lengths[1:1 + 2 * twos:2], lengths[2:2 + 2 * twos:2]
    room = jnp.minimum(donor - 1, limit - taker)
    moved = jax.random.randint(jax.random.fold_in(rng, 1), (twos,), 0, 1 << 20) % (room + 1)
    lengths = lengths.at[1:1 + 2 * twos:2].set(donor - moved).at[2:2 + 2 * twos:2].set(taker + moved)
    return lengths[jax.random.permutation(jax.random.fold_in(rng, 2), count)]


def bell_draw(own_key, dims, scale, bound, pieces=(), kind=jnp.bfloat16):
    values = scale * jax.random.normal(own_key, dims, jnp.float32)
    if pieces:
        values = values * block_levels(own_key, dims, pieces, -0.22, 0.18)
    return jnp.clip(values, -bound, bound).astype(kind)


def setup_inputs(seed: int = 0) -> dict:
    key_of = jax.random.split(jax.random.key(seed), 19)
    return {
        "image_tokens": bell_draw(key_of[0], (ITEMS, ITEM_LEN, D), 1.0, 6.0, ((0, 8), (1, 4))),
        "text_states": bell_draw(key_of[1], (N_IMG, TEXT_LEN, D), 1.0, 6.0, ((0, 8), (1, 4))),
        "text_segments": jax.vmap(lambda own: jnp.searchsorted(jnp.cumsum(uneven_parts(own, GROUP_ITEMS, TEXT_LEN, TEXT_LEN * 5 // 8, 1)), jnp.arange(TEXT_LEN), side="right"))(jax.random.split(key_of[2], N_IMG)).reshape((N_IMG, TEXT_LEN)).astype(jnp.int32),
        "item_segments": jax.vmap(lambda own: jax.random.permutation(own, GROUP_ITEMS))(jax.random.split(key_of[3], N_IMG)).reshape((N_IMG, GROUP_ITEMS)).astype(jnp.int32),
        "norm1_gain": jnp.clip(1.0 + 0.15 * jax.random.normal(key_of[4], (D,), jnp.float32), 0.25, 1.75),
        "norm1_bias": bell_draw(key_of[5], (D,), 0.3, 1.2, (), jnp.float32),
        "w_qkv": bell_draw(key_of[6], (D, 3 * D), D ** -0.5, 0.1875),
        "w_self_out": bell_draw(key_of[7], (D, D), (D // 64) ** -0.5, 1.5),
        "norm2_gain": jnp.clip(1.0 + 0.15 * jax.random.normal(key_of[8], (D,), jnp.float32), 0.25, 1.75),
        "norm2_bias": bell_draw(key_of[9], (D,), 0.3, 1.2, (), jnp.float32),
        "w_cross_q": bell_draw(key_of[10], (D, D), D ** -0.5, 0.1875),
        "w_cross_kv": bell_draw(key_of[11], (D, 2 * D), D ** -0.5, 0.1875),
        "w_cross_out": bell_draw(key_of[12], (D, D), (D // 8) ** -0.5, 0.5),
        "norm3_gain": jnp.clip(1.0 + 0.15 * jax.random.normal(key_of[13], (D,), jnp.float32), 0.25, 1.75),
        "norm3_bias": bell_draw(key_of[14], (D,), 0.3, 1.2, (), jnp.float32),
        "w_up": bell_draw(key_of[15], (D, FF), D ** -0.5, 0.1875),
        "w_down": bell_draw(key_of[16], (FF, D), FF ** -0.5, 0.09375),
        "cotangent": bell_draw(key_of[17], (ITEMS, ITEM_LEN, D), 1.0, 6.0, ((0, 8), (1, 4))),
    }


@jax.custom_vjp
def low(v):
    return lax.optimization_barrier(v.astype(jnp.bfloat16)).astype(jnp.float32)

@jax.custom_vjp
def low_back(v):
    return v

def low_keep(v):
    return (low(v), None)

def low_pass(kept, grad):
    return (grad,)

def back_keep(v):
    return (v, None)

def back_low(kept, grad):
    return (low(grad),)
low.defvjp(low_keep, low_pass)
low_back.defvjp(back_keep, back_low)
EPS = 1e-05
MASKED = -1e+30
HIGHEST = lax.Precision.HIGHEST

def layer_norm(values, norm_gain, norm_bias):
    center = values - lax.optimization_barrier(jnp.mean(values, axis=-1, keepdims=True))
    spread = lax.optimization_barrier(jnp.mean(center * center, axis=-1, keepdims=True))
    return center * lax.rsqrt(spread + EPS) * norm_gain + norm_bias

def project(values, weight):
    return jnp.einsum('...d,de->...e', values, weight, precision=HIGHEST)

def group_forward(params, tokens, states, state_ids, item_ids):
    norm1_gain, norm1_bias, w_qkv, w_self_out, norm2_gain, norm2_bias, w_cross_q, w_cross_kv, w_cross_out, norm3_gain, norm3_bias, w_up, w_down = params
    score_scale = HEAD ** (-0.5)
    batch_items = tokens.shape[0]
    normed1 = low(layer_norm(tokens, norm1_gain, norm1_bias))
    joined_qkv = low(low_back(project(normed1, w_qkv))).reshape(batch_items, ITEM_LEN, 3, HEADS, HEAD)
    queries = joined_qkv[:, :, 0]
    key_rows = joined_qkv[:, :, 1]
    value_rows = joined_qkv[:, :, 2]
    places = jnp.arange(ITEM_LEN)
    causal = places[None, :] <= places[:, None]
    scores = low_back(jnp.einsum('ilhe,imhe->ihlm', queries, key_rows, precision=HIGHEST) * score_scale)
    attention = jax.nn.softmax(jnp.where(causal, scores, MASKED), axis=-1)
    attended = jnp.einsum('ihlm,imhe->ilhe', low(attention), value_rows, precision=HIGHEST)
    attended = low(low_back(attended.reshape(batch_items, ITEM_LEN, D)))
    hidden1 = tokens + low_back(project(attended, w_self_out))
    normed2 = low(layer_norm(hidden1, norm2_gain, norm2_bias))
    cross_queries = low(low_back(project(normed2, w_cross_q))).reshape(batch_items, ITEM_LEN, HEADS, HEAD)
    text_kv = low(low_back(project(states, w_cross_kv))).reshape(TEXT_LEN, 2, HEADS, HEAD)
    matches = state_ids[None, :] == item_ids[:, None]
    cross_scores = low_back(jnp.einsum('ilhe,she->ihls', cross_queries, text_kv[:, 0], precision=HIGHEST) * score_scale)
    cross_weights = jax.nn.softmax(jnp.where(matches[:, None, None, :], cross_scores, MASKED), axis=-1)
    cross_mixed = jnp.einsum('ihls,she->ilhe', low(cross_weights), text_kv[:, 1], precision=HIGHEST)
    cross_mixed = low(low_back(cross_mixed.reshape(batch_items, ITEM_LEN, D)))
    hidden2 = hidden1 + low_back(project(cross_mixed, w_cross_out))
    normed3 = low(layer_norm(hidden2, norm3_gain, norm3_bias))
    up_value = low_back(project(normed3, w_up))
    activated = low(jax.nn.gelu(up_value, approximate=False))
    return hidden2 + low_back(project(activated, w_down))

def reference(image_tokens, text_states, text_segments, item_segments, norm1_gain, norm1_bias, w_qkv, w_self_out, norm2_gain, norm2_bias, w_cross_q, w_cross_kv, w_cross_out, norm3_gain, norm3_bias, w_up, w_down, cotangent):
    params = tuple((tensor.astype(jnp.float32) for tensor in (norm1_gain, norm1_bias, w_qkv, w_self_out, norm2_gain, norm2_bias, w_cross_q, w_cross_kv, w_cross_out, norm3_gain, norm3_bias, w_up, w_down)))

    def forward(params, tokens, states):
        grouped = tokens.reshape(N_IMG, ITEMS // N_IMG, ITEM_LEN, D)

        def scan_step(scan_carry, block_in):
            group_tokens, group_states, group_ids, group_items = block_in
            return (scan_carry, jax.checkpoint(group_forward)(params, group_tokens, group_states, group_ids, group_items))
        scan_carry, result = lax.scan(scan_step, jnp.zeros((), jnp.float32), (grouped, states, text_segments, item_segments))
        return result.reshape(ITEMS, ITEM_LEN, D)
    result, pullback = jax.vjp(forward, params, image_tokens.astype(jnp.float32), text_states.astype(jnp.float32))
    param_grads, image_grad, text_grad = pullback(cotangent.astype(jnp.float32))
    return (result.astype(jnp.bfloat16), image_grad, text_grad, param_grads[0], param_grads[1], param_grads[2], param_grads[3], param_grads[4], param_grads[5], param_grads[6], param_grads[7], param_grads[8], param_grads[9], param_grads[10], param_grads[11], param_grads[12])
```

```python
from functools import partial

import jax
import jax.numpy as jnp
import numpy as np
from jax import lax
from jax.experimental import pallas as pl
from jax.experimental.pallas import tpu as pltpu
from jax.sharding import PartitionSpec as P

D = 1024
HEADS = 16
HEAD = 64
EPS = 1e-05
MASKED = -1e30
SCALE = HEAD**-0.5
LOG2E = 1.4426950408889634
BOTH = ("img", "txt")
BF = jnp.bfloat16
F32 = jnp.float32
QUERY_BLOCK = 256
MIB = 1 << 20


def nn(a, b):
    return lax.dot_general(a, b, (((1,), (0,)), ((), ())), preferred_element_type=F32)


def nt(a, b):
    return lax.dot_general(a, b, (((1,), (1,)), ((), ())), preferred_element_type=F32)


def tn(a, b):
    return lax.dot_general(a, b, (((0,), (0,)), ((), ())), preferred_element_type=F32)


def norm_parts(values):
    center = values - jnp.mean(values, axis=-1, keepdims=True)
    rstd = lax.rsqrt(jnp.mean(center * center, axis=-1, keepdims=True) + EPS)
    return center * rstd, rstd


def norm_back(unit, rstd, gain, grad):
    scaled = grad * gain
    return rstd * (
        scaled
        - jnp.mean(scaled, axis=-1, keepdims=True)
        - unit * jnp.mean(scaled * unit, axis=-1, keepdims=True)
    )


def gelu_parts(value):
    inner = jnp.clip(value * (0.5**0.5), -4.0, 4.0)
    square = inner * inner
    top = jnp.full_like(square, -2.72614225801306e-10)
    for term in (
        2.77068142495902e-08,
        -2.10102402082508e-06,
        -5.69250639462346e-05,
        -7.34990630326855e-04,
        -2.95459980854025e-03,
        -1.60960333262415e-02,
    ):
        top = top * square + term
    low = jnp.full_like(square, -1.45660718464996e-05)
    for term in (
        -2.13374055278905e-04,
        -1.68282697438203e-03,
        -7.37332916720468e-03,
        -1.42647390514189e-02,
    ):
        low = low * square + term
    cdf = 0.5 + 0.5 * inner * top / low
    density = jnp.exp2(value * value * (-0.5 * LOG2E)) * (0.5 / np.pi) ** 0.5
    return value * cdf, cdf + value * density


def attend_kernel(q_ref, k_ref, v_ref, out_ref, lse_ref):
    length = q_ref.shape[0]
    block = QUERY_BLOCK
    scale = SCALE * LOG2E
    half = lax.broadcasted_iota(jnp.int32, (block, 2 * HEAD), 1) >= HEAD
    key_row = lax.broadcasted_iota(jnp.int32, (block, block), 0)
    query_col = lax.broadcasted_iota(jnp.int32, (block, block), 1)
    seen = key_row <= query_col
    v_flip = v_ref[...].T
    ones = jnp.ones((16, length), BF)
    v_rows = [jnp.concatenate([v_flip[h * HEAD : (h + 1) * HEAD], ones], 0) for h in range(2)]
    for i in range(length // block):
        lo, hi = i * block, (i + 1) * block
        queries = q_ref[lo:hi, :]
        outs = []
        for h in range(2):
            own = jnp.where(half == (h == 1), queries, jnp.zeros_like(queries))
            diag = jnp.where(seen, nt(k_ref[lo:hi, :], own), MASKED)
            top = jnp.max(diag, axis=0, keepdims=True)
            if i:
                rest = nt(k_ref[:lo, :], own)
                top = jnp.maximum(top, jnp.max(rest, axis=0, keepdims=True))
            base = top * scale
            mixed = nn(v_rows[h][:, lo:hi], jnp.exp2(diag * scale - base).astype(BF))
            if i:
                mixed += nn(v_rows[h][:, :lo], jnp.exp2(rest * scale - base).astype(BF))
            total = mixed[HEAD : HEAD + 1]
            lse_ref[0, h : h + 1, lo:hi] = base + jnp.log2(total)
            outs.append(mixed[:HEAD] / total)
        out_ref[lo:hi, :] = jnp.concatenate(outs, 0).T.astype(BF)


def attend(q, k, v):
    length, width = q.shape
    pairs = width // (2 * HEAD)
    spec = pl.BlockSpec((length, 2 * HEAD), lambda p: (0, p))
    return pl.pallas_call(
        attend_kernel,
        grid=(pairs,),
        in_specs=[spec] * 3,
        out_specs=[spec, pl.BlockSpec((1, 2, length), lambda p: (p, 0, 0))],
        out_shape=[
            jax.ShapeDtypeStruct((length, width), BF),
            jax.ShapeDtypeStruct((pairs, 2, length), F32),
        ],
        compiler_params=pltpu.CompilerParams(vmem_limit_bytes=48 * MIB),
        cost_estimate=pl.CostEstimate(
            flops=4 * length * length * width, bytes_accessed=8 * length * width, transcendentals=0
        ),
        name="self_attention",
    )(q, k, v)


def attend_back_kernel(q_ref, k_ref, v_ref, g_ref, o_ref, lse_ref, dq_ref, dk_ref, dv_ref, dq_sum):
    length = q_ref.shape[0]
    block = QUERY_BLOCK
    scale = SCALE * LOG2E
    half = lax.broadcasted_iota(jnp.int32, (length, 2 * HEAD), 1) >= HEAD
    key_row = lax.broadcasted_iota(jnp.int32, (block, block), 0)
    query_col = lax.broadcasted_iota(jnp.int32, (block, block), 1)
    seen = key_row <= query_col
    k_flip = k_ref[...].T
    zero = jnp.zeros((length, 2 * HEAD), BF)
    queries = [jnp.where(half == (h == 1), q_ref[...], zero) for h in range(2)]
    grads = [jnp.where(half == (h == 1), g_ref[...], zero) for h in range(2)]
    product = (g_ref[...].astype(F32) * o_ref[...].astype(F32)).T
    deltas = [jnp.sum(product[h * HEAD : (h + 1) * HEAD], axis=0, keepdims=True) for h in range(2)]
    for j in range(length // block):
        lo, hi = j * block, (j + 1) * block
        keys, values = k_ref[lo:hi, :], v_ref[lo:hi, :]
        key_grad = value_grad = None
        for h in range(2):
            own_q, own_g = queries[h][lo:], grads[h][lo:]
            scores = nt(keys, own_q) * scale - lse_ref[0, h : h + 1, lo:]
            weights = jnp.exp2(scores)
            first = jnp.where(seen, weights[:, :block], 0.0)
            weights = jnp.concatenate([first, weights[:, block:]], 1) if hi < length else first
            score_grad = (weights * (nt(values, own_g) - deltas[h][:, lo:])).astype(BF)
            weights = weights.astype(BF)
            value_part = nn(weights, own_g)
            key_part = nn(score_grad, own_q)
            value_grad = value_part if h == 0 else value_grad + value_part
            key_grad = key_part if h == 0 else key_grad + key_part
            query_part = nn(k_flip[h * HEAD : (h + 1) * HEAD, lo:hi], score_grad)
            rows = slice(h * HEAD, (h + 1) * HEAD)
            if j == 0:
                dq_sum[rows, :] = query_part
            else:
                dq_sum[rows, lo:] += query_part
        dk_ref[lo:hi, :] = (key_grad * SCALE).astype(BF)
        dv_ref[lo:hi, :] = value_grad.astype(BF)
    dq_ref[...] = (dq_sum[...].T * SCALE).astype(BF)


def attend_back(q, k, v, g, o, lse):
    length, width = q.shape
    pairs = width // (2 * HEAD)
    spec = pl.BlockSpec((length, 2 * HEAD), lambda p: (0, p))
    return pl.pallas_call(
        attend_back_kernel,
        grid=(pairs,),
        in_specs=[spec] * 5 + [pl.BlockSpec((1, 2, length), lambda p: (p, 0, 0))],
        out_specs=[spec] * 3,
        out_shape=[jax.ShapeDtypeStruct((length, width), BF)] * 3,
        scratch_shapes=[pltpu.VMEM((2 * HEAD, length), F32)],
        compiler_params=pltpu.CompilerParams(vmem_limit_bytes=48 * MIB),
        cost_estimate=pl.CostEstimate(
            flops=10 * length * length * width, bytes_accessed=16 * length * width, transcendentals=0
        ),
        name="self_attention_back",
    )(q, k, v, g, o, lse)


def mlp_kernel(
    pieces,
    core_ref,
    rows_from,
    goes_to,
    own_ref,
    other_ref,
    own_g_ref,
    other_g_ref,
    *refs,
):
    ups, downs = refs[:pieces], refs[pieces : 2 * pieces]
    out_ref, norm_ref, sent_ref, keep, send = refs[2 * pieces : 2 * pieces + 5]
    flip_ref, ordered_ref, out_sum, norm_sum, wide_ref, tall_ref, sems = refs[2 * pieces + 5 :]
    step, steps = pl.program_id(0), pl.num_programs(0)
    slot = step % 2
    tokens = own_ref.shape[0]
    half, height = keep.shape[0], keep.shape[1]
    tile = wide_ref.shape[3]
    width = 2 * height
    per_step = tile // width
    units = steps * tile

    @pl.when(step == 0)
    def _():
        flip_ref[:, :tokens] = own_ref[...].T
        flip_ref[:, tokens:] = other_ref[...].T
        for i in range(2 * half):
            at = pl.multiple_of(rows_from[i] * height, height)
            ordered_ref[i * height : (i + 1) * height, :] = flip_ref[pl.ds(at, height), :]
        out_ref[...] = jnp.zeros_like(out_ref)
        norm_ref[...] = jnp.zeros_like(norm_ref)
        out_sum[...] = jnp.zeros_like(out_sum)
        norm_sum[...] = jnp.zeros_like(norm_sum)

    def wide_copy(at, where, side):
        part = wide_ref.at[at, side * half : (side + 1) * half]
        lanes = pl.ds(pl.multiple_of(where * tile, tile), tile)
        return pltpu.make_async_copy(
            part, (keep, send)[side].at[:, :, lanes], sems.at[at, side]
        )

    def tall_copy(at, j, r, target, i):
        rows = slice(j * width + r * height, j * width + (r + 1) * height)
        lanes = slice(units + r * D, units + (r + 1) * D)
        return pltpu.make_async_copy(
            tall_ref.at[at, rows], target.at[i, :, lanes], sems.at[at, 2 + 2 * j + r]
        )

    def wait(at):
        for side in range(2):
            wide_copy(at, 0, side).wait()
        for j in range(per_step):
            for r in range(2):
                tall_copy(at, j, r, keep, 0).wait()

    @pl.when(step >= 2)
    def _():
        wait(slot)

    up_w = jnp.concatenate([r[...] for r in ups], 1) if pieces > 1 else ups[0][...]
    down_w = jnp.concatenate([r[...] for r in downs], 0) if pieces > 1 else downs[0][...]
    chunk = min(256, tokens)
    active, grads = [], []
    for x_ref, g_ref, o_ref, n_ref in (
        (own_ref, own_g_ref, out_ref, norm_ref),
        (other_ref, other_g_ref, out_sum, norm_sum),
    ):
        for at in range(0, tokens, chunk):
            rows = slice(at, at + chunk)
            up_value = nn(x_ref[rows, :], up_w)
            down_grad = nt(g_ref[rows, :], down_w)
            value, slope = gelu_parts(up_value)
            value = value.astype(BF)
            grad = (down_grad * slope).astype(BF)
            o_ref[rows, :] += nn(value, down_w)
            n_ref[rows, :] += nt(grad, up_w)
            active.append(value)
            grads.append(grad)
    grad = jnp.concatenate(grads, 0)
    wide = nn(ordered_ref[...], grad).astype(BF)
    wide_ref[slot] = wide.reshape(wide_ref.shape[1:])
    value = jnp.concatenate(active, 0).T
    tall = nn(value[:, :tokens], own_g_ref[...]) + nn(value[:, tokens:], other_g_ref[...])
    tall_ref[slot] = tall.astype(BF)

    for side in range(2):
        wide_copy(slot, step, side).start()
    for j in range(per_step):
        i = goes_to[step * per_step + j]

        @pl.when(i < half)
        def _(j=j, i=i):
            for r in range(2):
                tall_copy(slot, j, r, keep, i).start()

        @pl.when(i >= half)
        def _(j=j, i=i):
            for r in range(2):
                tall_copy(slot, j, r, send, i - half).start()

    @pl.when(step == steps - 1)
    def _():
        sent_ref[0] = out_sum[...].astype(BF)
        sent_ref[1] = norm_sum[...].astype(BF)
        wait(1 - slot)
        wait(slot)


def mlp(own, other, own_g, other_g, w_up, w_down, core, rows_from, goes_to):
    tokens = own.shape[0]
    chips = rows_from.shape[0]
    tile = 256
    units = w_up.shape[1] // 2
    steps = units // tile
    width = units // chips
    height = D // chips
    if width % 128 == 0:
        pieces, piece = tile // width, width
    else:
        pieces, piece = 1, tile
        w_up = w_up.reshape(D, chips, 2, width)[:, :, core].reshape(D, units)
        w_down = w_down.reshape(chips, 2, width, D)[:, core].reshape(units, D)

    def place(s, c, j):
        return 2 * (s * pieces + j) + c[0] if width % 128 == 0 else s

    whole = pl.BlockSpec((tokens, D), lambda s, *_: (0, 0))
    up_specs = [
        pl.BlockSpec((D, piece), lambda s, c, *_, j=j: (0, place(s, c, j))) for j in range(pieces)
    ]
    down_specs = [
        pl.BlockSpec((piece, D), lambda s, c, *_, j=j: (place(s, c, j), 0)) for j in range(pieces)
    ]
    sums = jax.ShapeDtypeStruct((chips // 2, height, units + 2 * D), BF)
    return pl.pallas_call(
        partial(mlp_kernel, pieces),
        grid_spec=pltpu.PrefetchScalarGridSpec(
            num_scalar_prefetch=3,
            grid=(steps,),
            in_specs=[whole] * 4 + up_specs + down_specs,
            out_specs=[
                whole,
                whole,
                pl.BlockSpec((2, tokens, D), lambda s, *_: (0, 0, 0)),
                pl.BlockSpec(memory_space=pl.ANY),
                pl.BlockSpec(memory_space=pl.ANY),
            ],
            scratch_shapes=[
                pltpu.VMEM((D, 2 * tokens), BF),
                pltpu.VMEM((D, 2 * tokens), BF),
                pltpu.VMEM((tokens, D), F32),
                pltpu.VMEM((tokens, D), F32),
                pltpu.VMEM((2, chips, height, tile), BF),
                pltpu.VMEM((2, tile, D), BF),
                pltpu.SemaphoreType.DMA((2, 2 + 2 * (tile // width))),
            ],
        ),
        out_shape=[
            jax.ShapeDtypeStruct((tokens, D), F32),
            jax.ShapeDtypeStruct((tokens, D), F32),
            jax.ShapeDtypeStruct((2, tokens, D), BF),
            sums,
            sums,
        ],
        compiler_params=pltpu.CompilerParams(vmem_limit_bytes=56 * MIB),
        cost_estimate=pl.CostEstimate(
            flops=24 * tokens * D * units, bytes_accessed=12 * D * units, transcendentals=0
        ),
        name="mlp_both_ways",
    )(
        core.reshape(1),
        rows_from,
        goes_to,
        own,
        other,
        own_g,
        other_g,
        *([w_up] * pieces),
        *([w_down] * pieces),
    )


class Plan:
    def __init__(self, n_img, n_txt):
        self.n_txt = n_txt
        self.n = n_img * n_txt
        self.chips = self.n // 2
        self.ny = n_txt // 2
        self.levels = self.chips.bit_length() - 1
        rest = list(range(2, self.levels))
        self.orders = ([1, 0] + rest, [0, 1] + rest)
        self.me = lax.axis_index("img") * n_txt + lax.axis_index("txt")
        self.core = self.me % 2
        self.chip = self.me // 2
        self.y = lax.axis_index("txt") // 2
        maps = np.zeros((2, self.chips), np.int32)
        for core in range(2):
            for i in range(self.chips):
                for s, bit in enumerate(self.orders[core]):
                    maps[core, i] |= ((i >> (self.levels - 1 - s)) & 1) << bit
        self.blocks = jnp.bitwise_xor(
            self.chip, jnp.where(self.core == 0, jnp.asarray(maps[0]), jnp.asarray(maps[1]))
        ).astype(jnp.int32)
        backs = np.argsort(maps, axis=1).astype(np.int32)
        away = jnp.bitwise_xor(self.chip, jnp.arange(self.chips, dtype=jnp.int32))
        self.goes_to = jnp.take(jnp.asarray(backs)[self.core], away, mode="clip")

    def swap(self, value):
        return lax.ppermute(value, BOTH, [(d, d ^ 1) for d in range(self.n)])

    def shift_y(self, value, by):
        pairs = []
        for d in range(self.n):
            img, txt = divmod(d, self.n_txt)
            y, core = divmod(txt, 2)
            pairs.append((d, img * self.n_txt + ((y + by) % self.ny) * 2 + core))
        return lax.ppermute(value, BOTH, pairs)

    def halve(self, value, step):
        pairs = [(d, d ^ (2 << self.orders[d % 2][step])) for d in range(self.n)]
        return lax.ppermute(value, BOTH, pairs)

    def to_item(self, value):
        parts = [value[self.y]]
        for k in range(1, self.ny):
            parts.append(self.shift_y(value[(self.y + k) % self.ny], k))
        return jnp.stack(parts)

    def from_item(self, value):
        parts = [value[0]]
        for k in range(1, self.ny):
            parts.append(self.shift_y(value[k], -k))
        stacked = jnp.stack(parts)
        order = [(i - self.y) % self.ny for i in range(self.ny)]
        return jnp.stack([stacked[o] for o in order])

    def to_places(self, own, other):
        length = own.shape[0] // self.ny
        both = jnp.concatenate([own, other], 0).reshape(2 * self.ny, length, -1)
        order = [
            ((p % 2) ^ self.core) * self.ny + (self.y - p // 2) % self.ny for p in range(self.n_txt)
        ]
        return jnp.concatenate([both[o] for o in order], 0)

    def from_places(self, value):
        length = value.shape[0] // self.n_txt
        parts = value.reshape(self.n_txt, length, -1)
        own = [parts[((self.y - r) % self.ny) * 2 + self.core] for r in range(self.ny)]
        other = [parts[((self.y - r) % self.ny) * 2 + 1 - self.core] for r in range(self.ny)]
        return jnp.concatenate(own, 0), jnp.concatenate(other, 0)

    def reduce(self, keep, send):
        for s in range(self.levels):
            got = [self.halve(v, s) for v in send]
            total = [a.astype(F32) + b.astype(F32) for a, b in zip(keep, got, strict=True)]
            if s < self.levels - 1:
                half = total[0].shape[0] // 2
                keep = [t[:half].astype(BF) for t in total]
                send = [t[half:].astype(BF) for t in total]
        return [t[0] for t in total]

    def split(self, value):
        ordered = jnp.take(value, self.blocks, axis=0, mode="clip")
        return ordered[: self.chips // 2], ordered[self.chips // 2 :]


def per_device(
    n_img,
    n_txt,
    image_tokens,
    text_states,
    text_segments,
    item_segments,
    norm1_gain,
    norm1_bias,
    w_qkv,
    w_self_out,
    norm2_gain,
    norm2_bias,
    w_cross_q,
    w_cross_kv,
    w_cross_out,
    norm3_gain,
    norm3_bias,
    w_up,
    w_down,
    cotangent,
):
    plan = Plan(n_img, n_txt)
    core, n, chips, ny = plan.core, plan.n, plan.chips, plan.ny
    items, length, _ = image_tokens.shape
    tokens = items * length
    half_d = D // 2
    rows = D // n

    x_own = plan.to_item(image_tokens).reshape(tokens, D)
    g_own = plan.to_item(cotangent).reshape(tokens, D)
    x_other = plan.swap(x_own)
    g_other = plan.swap(g_own)
    x_all = jnp.concatenate([x_own, x_other], 0)

    states = lax.all_gather(text_states[0], "txt", axis=0, tiled=True)
    ids = lax.all_gather(text_segments[0].astype(BF), "txt", axis=0, tiled=True)
    text_kv = nn(states, w_cross_kv).astype(BF)

    unit1_all, rstd1_all = norm_parts(x_all.astype(F32))
    normed1 = (unit1_all * norm1_gain + norm1_bias).astype(BF)
    w_own = [lax.dynamic_slice(w_qkv, (0, s * D + core * half_d), (D, half_d)) for s in range(3)]
    w_own = jnp.concatenate(w_own, 1)
    joined = nn(normed1, w_own).astype(BF)
    placed = plan.to_places(joined[:tokens], joined[tokens:])
    q, k, v = placed[:, :half_d], placed[:, half_d : 2 * half_d], placed[:, 2 * half_d :]
    mixed, lse = attend(q, k, v)
    mixed_own, mixed_other = plan.from_places(mixed)
    mixed_got = plan.swap(mixed_other)
    attended = jnp.where(
        core == 0,
        jnp.concatenate([mixed_own, mixed_got], 1),
        jnp.concatenate([mixed_got, mixed_own], 1),
    )

    hidden1 = x_own.astype(F32) + nn(attended, w_self_out)
    unit2, rstd2 = norm_parts(hidden1)
    normed2 = (unit2 * norm2_gain + norm2_bias).astype(BF)
    cross_q = nn(normed2, w_cross_q).astype(BF)
    cq = cross_q.reshape(tokens, HEADS, HEAD)
    tk = text_kv[:, :D].reshape(-1, HEADS, HEAD)
    tv = text_kv[:, D:].reshape(-1, HEADS, HEAD)
    matches = ids == item_segments[0, plan.y].astype(BF)
    scores = jnp.einsum("lhe,she->hls", cq, tk, preferred_element_type=F32) * SCALE
    scores = jnp.where(matches[None, None, :], scores, MASKED)
    weights = jnp.exp(scores - jnp.max(scores, axis=-1, keepdims=True))
    weights = weights / jnp.sum(weights, axis=-1, keepdims=True)
    weights_low = weights.astype(BF)
    cross_mixed = jnp.einsum("hls,she->lhe", weights_low, tv, preferred_element_type=F32)
    cross_mixed = cross_mixed.reshape(tokens, D).astype(BF)
    hidden2 = hidden1 + nn(cross_mixed, w_cross_out)
    unit3, rstd3 = norm_parts(hidden2)
    normed3 = (unit3 * norm3_gain + norm3_bias).astype(BF)

    normed3_other = plan.swap(normed3)
    per_down = w_down.shape[0] // n
    out, grad3, sent, up_down_keep, up_down_send = mlp(
        normed3, normed3_other, g_own, g_other, w_up, w_down, core, plan.blocks, plan.goes_to
    )
    got = plan.swap(sent).astype(F32)
    block_out = (hidden2 + out + got[0]).astype(BF)
    grad3 = grad3 + got[1]
    (up_down,) = plan.reduce([up_down_keep], [up_down_send])

    block_out = plan.from_item(block_out.reshape(ny, length, D))

    grad_gain3 = jnp.sum(grad3 * unit3, axis=0)
    grad_bias3 = jnp.sum(grad3, axis=0)
    grad_hidden2 = norm_back(unit3, rstd3, norm3_gain, grad3) + g_own.astype(F32)
    branch2 = grad_hidden2.astype(BF)
    cross_out_grad = tn(cross_mixed, branch2)
    grad_mixed = nt(branch2, w_cross_out).astype(BF).reshape(tokens, HEADS, HEAD)
    grad_weights = jnp.einsum("lhe,she->hls", grad_mixed, tv, preferred_element_type=F32)
    grad_tv = jnp.einsum("hls,lhe->she", weights_low, grad_mixed, preferred_element_type=F32)
    grad_scores = weights * (
        grad_weights - jnp.sum(weights * grad_weights, axis=-1, keepdims=True)
    )
    grad_scores = grad_scores.astype(BF)
    grad_cq = jnp.einsum("hls,she->lhe", grad_scores, tk, preferred_element_type=F32) * SCALE
    grad_cq = grad_cq.astype(BF).reshape(tokens, D)
    grad_tk = jnp.einsum("hls,lhe->she", grad_scores, cq, preferred_element_type=F32) * SCALE
    grad_kv = jnp.concatenate([grad_tk.reshape(-1, D), grad_tv.reshape(-1, D)], 1).astype(BF)
    cross_kv_grad = tn(states, grad_kv)
    text_part = nt(grad_kv, w_cross_kv)
    text_grad = lax.psum_scatter(text_part.astype(BF), "txt", scatter_dimension=0, tiled=True)
    cross_q_grad = tn(normed2, grad_cq)
    grad2 = nt(grad_cq, w_cross_q)
    grad_gain2 = jnp.sum(grad2 * unit2, axis=0)
    grad_bias2 = jnp.sum(grad2, axis=0)
    grad_hidden1 = norm_back(unit2, rstd2, norm2_gain, grad2) + grad_hidden2
    branch1 = grad_hidden1.astype(BF)
    self_out_grad = tn(attended, branch1)
    middle = jnp.concatenate([cross_out_grad, cross_q_grad, self_out_grad, cross_kv_grad], 1)
    middle = middle.astype(BF).reshape(chips, 2, rows, -1)
    middle = middle[:, core].astype(F32) + plan.swap(middle[:, 1 - core]).astype(F32)
    mid_keep, mid_send = plan.split(middle.astype(BF))
    (mid_sums,) = plan.reduce([mid_keep], [mid_send])

    grad_attended = nt(branch1, w_self_out).astype(BF).reshape(tokens, 2, half_d)
    grad_got = plan.swap(grad_attended[:, 1 - core])
    grad_placed = plan.to_places(grad_attended[:, core], grad_got)
    dq, dk, dv = attend_back(q, k, v, grad_placed, mixed, lse)
    joined_own, joined_other = plan.from_places(jnp.concatenate([dq, dk, dv], 1))
    joined_grad = jnp.concatenate([joined_own, joined_other], 0)
    part1 = nt(joined_grad, w_own)
    grad1 = part1[:tokens] + plan.swap(part1[tokens:].astype(BF)).astype(F32)
    qkv_grad = tn(normed1, joined_grad)
    unit1, rstd1 = unit1_all[:tokens], rstd1_all[:tokens]
    grad_gain1 = jnp.sum(grad1 * unit1, axis=0)
    grad_bias1 = jnp.sum(grad1, axis=0)
    norms = jnp.stack([grad_gain1, grad_bias1, grad_gain2, grad_bias2, grad_gain3, grad_bias3])
    norms = norms.reshape(6, chips, 2 * rows).transpose(1, 2, 0).astype(BF)
    norms = jnp.pad(norms, ((0, 0), (0, 0), (0, 128 - 6)))
    last = jnp.concatenate([qkv_grad.astype(BF).reshape(chips, 2 * rows, -1), norms], -1)
    last_keep, last_send = plan.split(last)
    (last_sums,) = plan.reduce([last_keep], [last_send])

    image_grad = norm_back(unit1, rstd1, norm1_gain, grad1) + grad_hidden1
    image_grad = plan.from_item(image_grad.astype(BF).reshape(ny, length, D)).astype(F32)

    units = w_up.shape[1] // 2
    down_grad = jnp.concatenate([up_down[:, units : units + D], up_down[:, units + D :]], 0)
    parts = jnp.concatenate([up_down[:, :units], last_sums], 1).reshape(2, rows, -1)
    mine = parts[core]
    theirs = plan.swap(parts[1 - core].astype(BF)).astype(F32)
    by_core = jnp.where(core == 0, jnp.stack([mine, theirs]), jnp.stack([theirs, mine]))
    up_grad = by_core[:, :, :units].reshape(2, rows, chips, per_down)
    up_grad = up_grad.transpose(1, 2, 0, 3).reshape(rows, 2 * units)
    wide = by_core[:, :, units : units + 3 * half_d].reshape(2, rows, 3, half_d)
    wide = wide.transpose(1, 2, 0, 3).reshape(rows, 3 * D)
    norm_sums = mine[:, -128:-122] + theirs[:, -128:-122]
    return (
        block_out,
        image_grad,
        text_grad.astype(F32)[None],
        norm_sums[:, 0],
        norm_sums[:, 1],
        wide,
        mid_sums[:, 2 * D : 3 * D],
        norm_sums[:, 2],
        norm_sums[:, 3],
        mid_sums[:, D : 2 * D],
        mid_sums[:, 3 * D :],
        mid_sums[:, :D],
        norm_sums[:, 4],
        norm_sums[:, 5],
        up_grad,
        down_grad,
    )


def solution(mesh):
    split = P("img", "txt", None)
    rows = P(BOTH)
    wide = P(BOTH, None)
    return jax.shard_map(
        partial(per_device, mesh.shape["img"], mesh.shape["txt"]),
        mesh=mesh,
        in_specs=(split, split, P("img", "txt"), P("img", None)) + (P(),) * 13 + (split,),
        out_specs=(
            (split,) * 3
            + (rows, rows, wide, wide)
            + (rows, rows, wide, wide, wide)
            + (rows, rows, wide, wide)
        ),
        check_vma=False,
    )
```

```python
from functools import partial

import jax
import jax.numpy as jnp
import numpy as np
from jax import lax
from jax.experimental import pallas as pl
from jax.experimental.pallas import tpu as pltpu
from jax.sharding import PartitionSpec as P

D = 1024
HEADS = 16
HEAD = 64
EPS = 1e-05
MASKED = -1e30
SCALE = HEAD**-0.5
LOG2E = 1.4426950408889634
BOTH = ("img", "txt")
BF = jnp.bfloat16
F32 = jnp.float32
QUERY_BLOCK = 256
MIB = 1 << 20


def nn(a, b):
    return lax.dot_general(a, b, (((1,), (0,)), ((), ())), preferred_element_type=F32)


def nt(a, b):
    return lax.dot_general(a, b, (((1,), (1,)), ((), ())), preferred_element_type=F32)


def tn(a, b):
    return lax.dot_general(a, b, (((0,), (0,)), ((), ())), preferred_element_type=F32)


def norm_parts(values):
    center = values - jnp.mean(values, axis=-1, keepdims=True)
    rstd = lax.rsqrt(jnp.mean(center * center, axis=-1, keepdims=True) + EPS)
    return center * rstd, rstd


def norm_back(unit, rstd, gain, grad):
    scaled = grad * gain
    return rstd * (
        scaled
        - jnp.mean(scaled, axis=-1, keepdims=True)
        - unit * jnp.mean(scaled * unit, axis=-1, keepdims=True)
    )


def gelu_parts(value):
    inner = jnp.clip(value * (0.5**0.5), -4.0, 4.0)
    square = inner * inner
    top = jnp.full_like(square, -2.72614225801306e-10)
    for term in (
        2.77068142495902e-08,
        -2.10102402082508e-06,
        -5.69250639462346e-05,
        -7.34990630326855e-04,
        -2.95459980854025e-03,
        -1.60960333262415e-02,
    ):
        top = top * square + term
    low = jnp.full_like(square, -1.45660718464996e-05)
    for term in (
        -2.13374055278905e-04,
        -1.68282697438203e-03,
        -7.37332916720468e-03,
        -1.42647390514189e-02,
    ):
        low = low * square + term
    cdf = 0.5 + 0.5 * inner * top / low
    density = jnp.exp2(value * value * (-0.5 * LOG2E)) * (0.5 / np.pi) ** 0.5
    return value * cdf, cdf + value * density


def project_kernel(
    core_ref, place_ref, own_ref, other_ref, gain_ref, bias_ref, wq_ref, wk_ref, wv_ref, *outs
):
    joined_ref, normed_ref = outs
    block, own_blocks = pl.program_id(0), pl.num_programs(0) // 2
    tokens = jnp.where(block < own_blocks, own_ref[...], other_ref[...]).astype(F32)
    unit, _ = norm_parts(tokens)
    normed = (unit * gain_ref[...] + bias_ref[...]).astype(BF)
    normed_ref[...] = normed
    width = wq_ref.shape[1]
    for s, w_ref in enumerate((wq_ref, wk_ref, wv_ref)):
        joined_ref[:, s * width : (s + 1) * width] = nn(normed, w_ref[...]).astype(BF)


def project_all(own, other, gain, bias, w_qkv, core, places, length):
    blocks = places.shape[0]
    half = blocks // 2
    width = D // 2
    row = pl.BlockSpec((1, D), lambda b, *_: (0, 0))
    weights = [pl.BlockSpec((D, width), lambda b, c, p, s=s: (0, 2 * s + c[0])) for s in range(3)]
    return pl.pallas_call(
        project_kernel,
        grid_spec=pltpu.PrefetchScalarGridSpec(
            num_scalar_prefetch=2,
            grid=(blocks,),
            in_specs=[
                pl.BlockSpec((length, D), lambda b, *_: (jnp.minimum(b, half - 1), 0)),
                pl.BlockSpec((length, D), lambda b, *_: (jnp.maximum(b - half, 0), 0)),
                row,
                row,
            ]
            + weights,
            out_specs=[
                pl.BlockSpec((length, 3 * width), lambda b, c, p: (p[b], 0)),
                pl.BlockSpec((length, D), lambda b, c, p: (p[b], 0)),
            ],
        ),
        out_shape=[
            jax.ShapeDtypeStruct((blocks * length, 3 * width), BF),
            jax.ShapeDtypeStruct((blocks * length, D), BF),
        ],
        compiler_params=pltpu.CompilerParams(vmem_limit_bytes=48 * MIB),
        cost_estimate=pl.CostEstimate(
            flops=6 * blocks * length * D * width,
            bytes_accessed=10 * blocks * length * D,
            transcendentals=0,
        ),
        name="norm_and_project",
    )(
        core.reshape(1),
        places,
        own,
        other,
        gain.reshape(1, D),
        bias.reshape(1, D),
        w_qkv,
        w_qkv,
        w_qkv,
    )


def middle_kernel(
    core_ref,
    x_ref,
    own_ref,
    got_ref,
    keys_ref,
    values_ref,
    seen_ref,
    gain2_ref,
    bias2_ref,
    gain3_ref,
    bias3_ref,
    w_own_ref,
    w_got_ref,
    w_query_ref,
    w_out_ref,
    hidden1_ref,
    hidden2_ref,
    normed3_ref,
    queries_ref,
    mixed_ref,
    lse_ref,
):
    hidden = x_ref[...].astype(F32) + nn(own_ref[...], w_own_ref[...])
    hidden += nn(got_ref[...], w_got_ref[...])
    hidden1_ref[...] = hidden
    unit, _ = norm_parts(hidden)
    normed2 = (unit * gain2_ref[...] + bias2_ref[...]).astype(BF)
    queries = nn(normed2, w_query_ref[...]).astype(BF)
    queries_ref[...] = queries
    rows, states = queries.shape[0], keys_ref.shape[0]
    half = lax.broadcasted_iota(jnp.int32, (rows, 2 * HEAD), 1) >= HEAD
    v_flip = values_ref[...].T
    ones = jnp.ones((16, states), BF)
    zero = jnp.zeros((rows, 2 * HEAD), BF)
    outs, lses = [], []
    for head in range(HEADS):
        at, h = head // 2 * 2 * HEAD, head % 2
        own = jnp.where(half == (h == 1), queries[:, at : at + 2 * HEAD], zero)
        scores = nt(keys_ref[:, at : at + 2 * HEAD], own) * (SCALE * LOG2E) + seen_ref[...]
        top = jnp.max(scores, axis=0, keepdims=True)
        raised = jnp.exp2(scores - top).astype(BF)
        v_rows = jnp.concatenate([v_flip[head * HEAD : (head + 1) * HEAD], ones], 0)
        mixed = nn(v_rows, raised)
        total = mixed[HEAD : HEAD + 1]
        lses.append(top + jnp.log2(total))
        outs.append((mixed[:HEAD] / total).astype(BF))
    lse_ref[...] = jnp.concatenate(lses, 0)
    mixed = jnp.concatenate(outs, 0).T
    mixed_ref[...] = mixed
    hidden += nn(mixed, w_out_ref[...])
    hidden2_ref[...] = hidden
    unit, _ = norm_parts(hidden)
    normed3_ref[...] = (unit * gain3_ref[...] + bias3_ref[...]).astype(BF)


def cross_part(x, own, got, text_kv, seen, norms, w_self_out, w_query, w_out, core):
    tokens, width = own.shape
    states = text_kv.shape[0]
    block = min(256, tokens)
    row = pl.BlockSpec((1, D), lambda b, c: (0, 0))
    wide = pl.BlockSpec((block, D), lambda b, c: (b, 0))
    narrow = pl.BlockSpec((block, width), lambda b, c: (b, 0))
    square = pl.BlockSpec((D, D), lambda b, c: (0, 0))
    return pl.pallas_call(
        middle_kernel,
        grid_spec=pltpu.PrefetchScalarGridSpec(
            num_scalar_prefetch=1,
            grid=(tokens // block,),
            in_specs=[
                wide,
                narrow,
                narrow,
                pl.BlockSpec((states, D), lambda b, c: (0, 0)),
                pl.BlockSpec((states, D), lambda b, c: (0, 1)),
                pl.BlockSpec((states, 1), lambda b, c: (0, 0)),
                row,
                row,
                row,
                row,
                pl.BlockSpec((width, D), lambda b, c: (c[0], 0)),
                pl.BlockSpec((width, D), lambda b, c: (1 - c[0], 0)),
                square,
                square,
            ],
            out_specs=[wide] * 5 + [pl.BlockSpec((HEADS, block), lambda b, c: (0, b))],
        ),
        out_shape=[
            jax.ShapeDtypeStruct((tokens, D), F32),
            jax.ShapeDtypeStruct((tokens, D), F32),
            jax.ShapeDtypeStruct((tokens, D), BF),
            jax.ShapeDtypeStruct((tokens, D), BF),
            jax.ShapeDtypeStruct((tokens, D), BF),
            jax.ShapeDtypeStruct((HEADS, tokens), F32),
        ],
        compiler_params=pltpu.CompilerParams(vmem_limit_bytes=56 * MIB),
        cost_estimate=pl.CostEstimate(
            flops=7 * tokens * D * D, bytes_accessed=6 * D * D + 20 * tokens * D, transcendentals=0
        ),
        name="cross_attention_part",
    )(
        core.reshape(1),
        x,
        own,
        got,
        text_kv,
        text_kv,
        seen,
        *[v.reshape(1, D) for v in norms],
        w_self_out,
        w_self_out,
        w_query,
        w_out,
    )


def attend_kernel(core_ref, row_ref, q_ref, k_ref, v_ref, own_ref, other_ref, lse_ref):
    length = q_ref.shape[0]
    block = QUERY_BLOCK
    scale = SCALE * LOG2E
    half = lax.broadcasted_iota(jnp.int32, (block, 2 * HEAD), 1) >= HEAD
    key_row = lax.broadcasted_iota(jnp.int32, (block, block), 0)
    query_col = lax.broadcasted_iota(jnp.int32, (block, block), 1)
    seen = key_row <= query_col
    v_flip = v_ref[...].T
    ones = jnp.ones((16, length), BF)
    v_rows = [jnp.concatenate([v_flip[h * HEAD : (h + 1) * HEAD], ones], 0) for h in range(2)]
    for i in range(length // block):
        lo, hi = i * block, (i + 1) * block
        queries = q_ref[lo:hi, :]
        outs = []
        for h in range(2):
            own = jnp.where(half == (h == 1), queries, jnp.zeros_like(queries))
            diag = jnp.where(seen, nt(k_ref[lo:hi, :], own), MASKED)
            top = jnp.max(diag, axis=0, keepdims=True)
            if i:
                rest = nt(k_ref[:lo, :], own)
                top = jnp.maximum(top, jnp.max(rest, axis=0, keepdims=True))
            base = top * scale
            mixed = nn(v_rows[h][:, lo:hi], jnp.exp2(diag * scale - base).astype(BF))
            if i:
                mixed += nn(v_rows[h][:, :lo], jnp.exp2(rest * scale - base).astype(BF))
            total = mixed[HEAD : HEAD + 1]
            lse_ref[0, h : h + 1, lo:hi] = base + jnp.log2(total)
            outs.append(mixed[:HEAD] / total)
        result = jnp.concatenate(outs, 0).T.astype(BF)
        part = 2 * own_ref.shape[0] // row_ref.shape[0]
        for at in range(0, block, part):
            place = (lo + at) // part
            row = pl.multiple_of(row_ref[place] * part, part)

            @pl.when(place % 2 == core_ref[0])
            def _(at=at, row=row):
                own_ref[pl.ds(row, part), :] = result[at : at + part]

            @pl.when(place % 2 != core_ref[0])
            def _(at=at, row=row):
                other_ref[pl.ds(row, part), :] = result[at : at + part]


def head_specs(length, pairs):
    return [
        pl.BlockSpec((length, 2 * HEAD), lambda p, *_, s=s: (0, s * pairs + p)) for s in range(3)
    ]


def attend(joined, core, rows):
    length, width = joined.shape[0], joined.shape[1] // 3
    pairs = width // (2 * HEAD)
    half = pl.BlockSpec((length // 2, 2 * HEAD), lambda p, *_: (0, p))
    return pl.pallas_call(
        attend_kernel,
        grid_spec=pltpu.PrefetchScalarGridSpec(
            num_scalar_prefetch=2,
            grid=(pairs,),
            in_specs=head_specs(length, pairs),
            out_specs=[half, half, pl.BlockSpec((1, 2, length), lambda p, *_: (p, 0, 0))],
        ),
        out_shape=[
            jax.ShapeDtypeStruct((length // 2, width), BF),
            jax.ShapeDtypeStruct((length // 2, width), BF),
            jax.ShapeDtypeStruct((pairs, 2, length), F32),
        ],
        compiler_params=pltpu.CompilerParams(vmem_limit_bytes=48 * MIB),
        cost_estimate=pl.CostEstimate(
            flops=4 * length * length * width, bytes_accessed=8 * length * width, transcendentals=0
        ),
        name="self_attention",
    )(core.reshape(1), rows, joined, joined, joined)


def attend_back_kernel(
    core_ref,
    row_ref,
    q_ref,
    k_ref,
    v_ref,
    own_g_ref,
    other_g_ref,
    own_ref,
    other_ref,
    lse_ref,
    dq_ref,
    dk_ref,
    dv_ref,
    dq_sum,
    g_ref,
    o_ref,
):
    length = q_ref.shape[0]
    places = row_ref.shape[0]
    part = length // places
    for place in range(places):
        at = pl.ds(pl.multiple_of(row_ref[place] * part, part), part)
        mine = core_ref[0] == place % 2
        to = slice(place * part, (place + 1) * part)
        g_ref[to, :] = jnp.where(mine, own_g_ref[at, :], other_g_ref[at, :])
        o_ref[to, :] = jnp.where(mine, own_ref[at, :], other_ref[at, :])
    block = QUERY_BLOCK
    scale = SCALE * LOG2E
    half = lax.broadcasted_iota(jnp.int32, (length, 2 * HEAD), 1) >= HEAD
    key_row = lax.broadcasted_iota(jnp.int32, (block, block), 0)
    query_col = lax.broadcasted_iota(jnp.int32, (block, block), 1)
    seen = key_row <= query_col
    k_flip = k_ref[...].T
    zero = jnp.zeros((length, 2 * HEAD), BF)
    queries = [jnp.where(half == (h == 1), q_ref[...], zero) for h in range(2)]
    grads = [jnp.where(half == (h == 1), g_ref[...], zero) for h in range(2)]
    product = (g_ref[...].astype(F32) * o_ref[...].astype(F32)).T
    deltas = [jnp.sum(product[h * HEAD : (h + 1) * HEAD], axis=0, keepdims=True) for h in range(2)]
    for j in range(length // block):
        lo, hi = j * block, (j + 1) * block
        keys, values = k_ref[lo:hi, :], v_ref[lo:hi, :]
        key_grad = value_grad = None
        for h in range(2):
            own_q, own_g = queries[h][lo:], grads[h][lo:]
            scores = nt(keys, own_q) * scale - lse_ref[0, h : h + 1, lo:]
            weights = jnp.exp2(scores)
            first = jnp.where(seen, weights[:, :block], 0.0)
            weights = jnp.concatenate([first, weights[:, block:]], 1) if hi < length else first
            score_grad = (weights * (nt(values, own_g) - deltas[h][:, lo:])).astype(BF)
            weights = weights.astype(BF)
            value_part = nn(weights, own_g)
            key_part = nn(score_grad, own_q)
            value_grad = value_part if h == 0 else value_grad + value_part
            key_grad = key_part if h == 0 else key_grad + key_part
            query_part = nn(k_flip[h * HEAD : (h + 1) * HEAD, lo:hi], score_grad)
            rows = slice(h * HEAD, (h + 1) * HEAD)
            if j == 0:
                dq_sum[rows, :] = query_part
            else:
                dq_sum[rows, lo:] += query_part
        dk_ref[lo:hi, :] = (key_grad * SCALE).astype(BF)
        dv_ref[lo:hi, :] = value_grad.astype(BF)
    dq_ref[...] = (dq_sum[...].T * SCALE).astype(BF)


def attend_back(joined, own_g, other_g, own, other, lse, core, rows):
    length, width = joined.shape[0], joined.shape[1] // 3
    pairs = width // (2 * HEAD)
    spec = pl.BlockSpec((length, 2 * HEAD), lambda p, *_: (0, p))
    half = pl.BlockSpec((length // 2, 2 * HEAD), lambda p, *_: (0, p))
    return pl.pallas_call(
        attend_back_kernel,
        grid_spec=pltpu.PrefetchScalarGridSpec(
            num_scalar_prefetch=2,
            grid=(pairs,),
            in_specs=head_specs(length, pairs)
            + [half] * 4
            + [pl.BlockSpec((1, 2, length), lambda p, *_: (p, 0, 0))],
            out_specs=[spec] * 3,
            scratch_shapes=[
                pltpu.VMEM((2 * HEAD, length), F32),
                pltpu.VMEM((length, 2 * HEAD), BF),
                pltpu.VMEM((length, 2 * HEAD), BF),
            ],
        ),
        out_shape=[jax.ShapeDtypeStruct((length, width), BF)] * 3,
        compiler_params=pltpu.CompilerParams(vmem_limit_bytes=48 * MIB),
        cost_estimate=pl.CostEstimate(
            flops=10 * length * length * width, bytes_accessed=16 * length * width, transcendentals=0
        ),
        name="self_attention_back",
    )(core.reshape(1), rows, joined, joined, joined, own_g, other_g, own, other, lse)


def mlp_grad_kernel(
    pieces,
    core_ref,
    rows_from,
    goes_to,
    own_ref,
    other_ref,
    own_g_ref,
    other_g_ref,
    *refs,
):
    ups, downs = refs[:pieces], refs[pieces : 2 * pieces]
    active_ref, grad_ref, keep, send = refs[2 * pieces : 2 * pieces + 4]
    flip_ref, ordered_ref, wide_ref, tall_ref, sems = refs[2 * pieces + 4 :]
    step, steps = pl.program_id(0), pl.num_programs(0)
    slot = step % 2
    tokens = own_ref.shape[0]
    half, height = keep.shape[0], keep.shape[1]
    tile = wide_ref.shape[3]
    width = 2 * height
    per_step = tile // width
    units = steps * tile

    @pl.when(step == 0)
    def _():
        flip_ref[:, :tokens] = own_ref[...].T
        flip_ref[:, tokens:] = other_ref[...].T
        for i in range(2 * half):
            at = pl.multiple_of(rows_from[i] * height, height)
            ordered_ref[i * height : (i + 1) * height, :] = flip_ref[pl.ds(at, height), :]

    def wide_copy(at, where, side):
        part = wide_ref.at[at, side * half : (side + 1) * half]
        lanes = pl.ds(pl.multiple_of(where * tile, tile), tile)
        return pltpu.make_async_copy(
            part, (keep, send)[side].at[:, :, lanes], sems.at[at, side]
        )

    def tall_copy(at, j, r, target, i):
        rows = slice(j * width + r * height, j * width + (r + 1) * height)
        lanes = slice(units + r * D, units + (r + 1) * D)
        return pltpu.make_async_copy(
            tall_ref.at[at, rows], target.at[i, :, lanes], sems.at[at, 2 + 2 * j + r]
        )

    def wait(at):
        for side in range(2):
            wide_copy(at, 0, side).wait()
        for j in range(per_step):
            for r in range(2):
                tall_copy(at, j, r, keep, 0).wait()

    @pl.when(step >= 2)
    def _():
        wait(slot)

    up_w = jnp.concatenate([r[...] for r in ups], 1) if pieces > 1 else ups[0][...]
    down_w = jnp.concatenate([r[...] for r in downs], 0) if pieces > 1 else downs[0][...]
    chunk = min(512, tokens)
    active, grads = [], []
    for base, x_ref, g_ref in ((0, own_ref, own_g_ref), (tokens, other_ref, other_g_ref)):
        for at in range(0, tokens, chunk):
            rows = slice(at, at + chunk)
            up_value = nn(x_ref[rows, :], up_w)
            down_grad = nt(g_ref[rows, :], down_w)
            value, slope = gelu_parts(up_value)
            value = value.astype(BF)
            grad = (down_grad * slope).astype(BF)
            active_ref[base + at : base + at + chunk, :] = value
            grad_ref[base + at : base + at + chunk, :] = grad
            active.append(value)
            grads.append(grad)
    grad = jnp.concatenate(grads, 0)
    wide = nn(ordered_ref[...], grad).astype(BF)
    wide_ref[slot] = wide.reshape(wide_ref.shape[1:])
    value = jnp.concatenate(active, 0).T
    tall = nn(value[:, :tokens], own_g_ref[...]) + nn(value[:, tokens:], other_g_ref[...])
    tall_ref[slot] = tall.astype(BF)

    for side in range(2):
        wide_copy(slot, step, side).start()
    for j in range(per_step):
        i = goes_to[step * per_step + j]

        @pl.when(i < half)
        def _(j=j, i=i):
            for r in range(2):
                tall_copy(slot, j, r, keep, i).start()

        @pl.when(i >= half)
        def _(j=j, i=i):
            for r in range(2):
                tall_copy(slot, j, r, send, i - half).start()

    @pl.when(step == steps - 1)
    def _():
        wait(1 - slot)
        wait(slot)


def mlp_grads(own, other, own_g, other_g, w_up, w_down, core, rows_from, goes_to):
    tokens = own.shape[0]
    chips = rows_from.shape[0]
    tile = 512
    units = w_up.shape[1] // 2
    steps = units // tile
    width = units // chips
    height = D // chips
    if width % 128 == 0:
        pieces, piece = tile // width, width
    else:
        pieces, piece = 1, tile
        w_up = w_up.reshape(D, chips, 2, width)[:, :, core].reshape(D, units)
        w_down = w_down.reshape(chips, 2, width, D)[:, core].reshape(units, D)

    def place(s, c, j):
        return 2 * (s * pieces + j) + c[0] if width % 128 == 0 else s

    whole = pl.BlockSpec((tokens, D), lambda s, *_: (0, 0))
    hidden = pl.BlockSpec((2 * tokens, tile), lambda s, *_: (0, s))
    up_specs = [
        pl.BlockSpec((D, piece), lambda s, c, *_, j=j: (0, place(s, c, j))) for j in range(pieces)
    ]
    down_specs = [
        pl.BlockSpec((piece, D), lambda s, c, *_, j=j: (place(s, c, j), 0)) for j in range(pieces)
    ]
    sums = jax.ShapeDtypeStruct((chips // 2, height, units + 2 * D), BF)
    return pl.pallas_call(
        partial(mlp_grad_kernel, pieces),
        grid_spec=pltpu.PrefetchScalarGridSpec(
            num_scalar_prefetch=3,
            grid=(steps,),
            in_specs=[whole] * 4 + up_specs + down_specs,
            out_specs=[hidden] * 2 + [pl.BlockSpec(memory_space=pl.ANY)] * 2,
            scratch_shapes=[
                pltpu.VMEM((D, 2 * tokens), BF),
                pltpu.VMEM((D, 2 * tokens), BF),
                pltpu.VMEM((2, chips, height, tile), BF),
                pltpu.VMEM((2, tile, D), BF),
                pltpu.SemaphoreType.DMA((2, 2 + 2 * (tile // width))),
            ],
        ),
        out_shape=[jax.ShapeDtypeStruct((2 * tokens, units), BF)] * 2 + [sums] * 2,
        compiler_params=pltpu.CompilerParams(vmem_limit_bytes=56 * MIB),
        cost_estimate=pl.CostEstimate(
            flops=16 * tokens * D * units, bytes_accessed=20 * D * units, transcendentals=0
        ),
        name="mlp_gradients",
    )(
        core.reshape(1),
        rows_from,
        goes_to,
        own,
        other,
        own_g,
        other_g,
        *([w_up] * pieces),
        *([w_down] * pieces),
    )


def mlp_out_kernel(own_blocks, core_ref, active_ref, grad_ref, down_ref, up_ref, *refs):
    out_ref, norm_ref, sent_ref, up_own, sems = refs
    block = pl.program_id(0)
    chips, _, width, _ = down_ref.shape

    @pl.when(block == 0)
    def _():
        copies = []
        for i in range(chips):
            lanes = pl.ds(pl.multiple_of((2 * i + core_ref[0]) * width, width), width)
            copies.append(
                pltpu.make_async_copy(
                    up_ref.at[:, lanes], up_own.at[:, i * width : (i + 1) * width], sems.at[i]
                )
            )
        for copy in copies:
            copy.start()
        for copy in copies:
            copy.wait()

    out = nn(active_ref[...], down_ref[...].reshape(chips * width, D))
    norm = nt(grad_ref[...], up_own[...])

    @pl.when(block < own_blocks)
    def _():
        sent_ref[0] = out.astype(BF)
        sent_ref[1] = norm.astype(BF)

    @pl.when(block >= own_blocks)
    def _():
        out_ref[...] = out
        norm_ref[...] = norm


def mlp_outputs(active, grad, w_up, w_down, core, chips):
    tokens, units = active.shape[0] // 2, active.shape[1]
    block = min(512, tokens)
    blocks = tokens // block
    width = units // chips
    if width % 128:
        w_up = w_up.reshape(D, chips, 2, width)[:, :, core].reshape(D, units)
        w_up = jnp.concatenate([w_up, w_up], 1)
        width = 128
        w_up = w_up[:, :units].reshape(D, units // width, 1, width)
        w_up = jnp.concatenate([w_up, w_up], 2).reshape(D, 2 * units)
        w_down = w_down.reshape(chips, 2, units // chips, D)[:, core].reshape(units // width, 1, width, D)
        w_down = jnp.concatenate([w_down, w_down], 1)
    else:
        w_down = w_down.reshape(chips, 2, width, D)
    pieces = units // width
    hidden = pl.BlockSpec((block, units), lambda b, c: ((b + blocks) % (2 * blocks), 0))
    kept = pl.BlockSpec((block, D), lambda b, c: (jnp.maximum(b - blocks, 0), 0))
    return pl.pallas_call(
        partial(mlp_out_kernel, blocks),
        grid_spec=pltpu.PrefetchScalarGridSpec(
            num_scalar_prefetch=1,
            grid=(2 * blocks,),
            in_specs=[
                hidden,
                hidden,
                pl.BlockSpec((pieces, 1, width, D), lambda b, c: (0, c[0], 0, 0)),
                pl.BlockSpec(memory_space=pl.ANY),
            ],
            out_specs=[
                kept,
                kept,
                pl.BlockSpec((2, block, D), lambda b, c: (0, jnp.minimum(b, blocks - 1), 0)),
            ],
            scratch_shapes=[pltpu.VMEM((D, units), BF), pltpu.SemaphoreType.DMA((pieces,))],
        ),
        out_shape=[
            jax.ShapeDtypeStruct((tokens, D), F32),
            jax.ShapeDtypeStruct((tokens, D), F32),
            jax.ShapeDtypeStruct((2, tokens, D), BF),
        ],
        compiler_params=pltpu.CompilerParams(vmem_limit_bytes=56 * MIB),
        cost_estimate=pl.CostEstimate(
            flops=8 * tokens * D * units, bytes_accessed=8 * D * units, transcendentals=0
        ),
        name="mlp_outputs",
    )(core.reshape(1), active, grad, w_down, w_up)


def cross_back_kernel(
    scalars,
    order_ref,
    out_ref,
    got_ref,
    grad3_ref,
    hidden2_ref,
    g_ref,
    gain3_ref,
    gain2_ref,
    seen_ref,
    lse_ref,
    mixed_ref,
    w_out_ref,
    keys_ref,
    values_ref,
    queries_ref,
    states_ref,
    w_query_hbm,
    hidden1_hbm,
    own_hbm,
    other_hbm,
    w_self_hbm,
    block_ref,
    hidden_grad_ref,
    own_grad_ref,
    other_grad_ref,
    text_ref,
    norms_ref,
    keep,
    send,
    w_query,
    hidden1,
    own_ref,
    other_ref,
    w_self,
    flip_ref,
    ordered_ref,
    stage_ref,
    sems,
    out_sems,
):
    core = scalars[0]
    loads = [
        pltpu.make_async_copy(a, b, sems.at[i])
        for i, (a, b) in enumerate(
            (
                (w_query_hbm, w_query),
                (hidden1_hbm, hidden1),
                (own_hbm, own_ref),
                (other_hbm, other_ref),
                (w_self_hbm, w_self),
            )
        )
    ]
    for load in loads:
        load.start()
    count = order_ref.shape[0]
    rows = D // count
    half = D // 2
    writes = []

    def weight_part(depth, grads, slot, lane):
        for i in range(count):
            at = pl.multiple_of(order_ref[i] * rows, rows)
            ordered_ref[i * rows : (i + 1) * rows, :depth] = flip_ref[pl.ds(at, rows), :depth]
        width = grads.shape[1]
        product = nn(ordered_ref[:, :depth].astype(BF), grads)
        stage_ref[:, lane : lane + width] = product.astype(BF)
        for i, target in enumerate((send, keep)):
            writes.append(
                pltpu.make_async_copy(
                    stage_ref.at[i * half : (i + 1) * half, lane : lane + width],
                    target.at[:, lane : lane + width],
                    out_sems.at[2 * slot + i],
                )
            )
            writes[-1].start()

    kind = flip_ref.dtype
    tokens = out_ref.shape[0]
    hidden2 = hidden2_ref[...]
    block_ref[...] = (hidden2 + out_ref[...] + got_ref[0].astype(F32)).astype(BF)
    grad3 = grad3_ref[...] + got_ref[1].astype(F32)
    unit, rstd = norm_parts(hidden2)
    norms_ref[4:5, :] = jnp.sum(grad3 * unit, axis=0, keepdims=True)
    norms_ref[5:6, :] = jnp.sum(grad3, axis=0, keepdims=True)
    norms_ref[6:8, :] = jnp.zeros((2, D), F32)
    grad_hidden = norm_back(unit, rstd, gain3_ref[...], grad3) + g_ref[...].astype(F32)
    hidden_grad_ref[...] = grad_hidden
    branch = grad_hidden.astype(BF)
    flip_ref[:, :tokens] = mixed_ref[...].astype(kind).T
    weight_part(tokens, branch, 0, 0)
    grad_mixed = nt(branch, w_out_ref[...]).astype(BF)
    states = keys_ref.shape[0]
    half_lane = lax.broadcasted_iota(jnp.int32, (tokens, 2 * HEAD), 1) >= HEAD
    zero = jnp.zeros((tokens, 2 * HEAD), BF)
    k_flip = keys_ref[...].T
    flips, key_grads, value_grads = [], [], []
    for pair in range(HEADS // 2):
        lanes = slice(pair * 2 * HEAD, (pair + 1) * 2 * HEAD)
        queries, grads = queries_ref[:, lanes], grad_mixed[:, lanes]
        for h in range(2):
            head = 2 * pair + h
            own_q = jnp.where(half_lane == (h == 1), queries, zero)
            own_g = jnp.where(half_lane == (h == 1), grads, zero)
            scores = nt(keys_ref[:, lanes], own_q) * (SCALE * LOG2E) + seen_ref[...]
            weights = jnp.exp2(scores - lse_ref[head : head + 1, :])
            score_grad = nt(values_ref[:, lanes], own_g)
            delta = jnp.sum(weights * score_grad, axis=0, keepdims=True)
            score_grad = (weights * (score_grad - delta)).astype(BF)
            key_part, value_part = nn(score_grad, own_q), nn(weights.astype(BF), own_g)
            if h == 0:
                key_grads.append(key_part)
                value_grads.append(value_part)
            else:
                key_grads[-1] += key_part
                value_grads[-1] += value_part
            part = nn(k_flip[head * HEAD : (head + 1) * HEAD], score_grad)
            flips.append((part * SCALE).astype(BF))
    query_grad = jnp.concatenate(flips, 0).T
    text_grad = jnp.concatenate([p * SCALE for p in key_grads] + value_grads, 1).astype(BF)
    text_ref[...] = text_grad
    flip_ref[:, :states] = states_ref[...].astype(kind).T
    weight_part(states, text_grad, 1, 3 * D)
    for load in loads[:2]:
        load.wait()
    grad2 = nt(query_grad, w_query[...])
    unit, rstd = norm_parts(hidden1[...])
    normed2 = unit * gain2_ref[0:1, :] + gain2_ref[1:2, :]
    flip_ref[:, :tokens] = normed2.astype(BF).astype(kind).T
    weight_part(tokens, query_grad, 2, D)
    norms_ref[2:3, :] = jnp.sum(grad2 * unit, axis=0, keepdims=True)
    norms_ref[3:4, :] = jnp.sum(grad2, axis=0, keepdims=True)
    norms_ref[0:2, :] = jnp.zeros((2, D), F32)
    grad_hidden = norm_back(unit, rstd, gain2_ref[0:1, :], grad2) + hidden_grad_ref[...]
    hidden_grad_ref[...] = grad_hidden
    branch = grad_hidden.astype(BF)
    for load in loads[2:]:
        load.wait()
    own_rows = pl.ds(pl.multiple_of(core * half, half), half)
    other_rows = pl.ds(pl.multiple_of((1 - core) * half, half), half)
    own_grad_ref[...] = nt(branch, w_self[own_rows, :]).astype(BF)
    other_grad_ref[...] = nt(branch, w_self[other_rows, :]).astype(BF)
    flip_ref[own_rows, :tokens] = own_ref[...].astype(kind).T
    flip_ref[other_rows, :tokens] = other_ref[...].astype(kind).T
    weight_part(tokens, branch, 3, 2 * D)
    for write in writes:
        write.wait()


def cross_back(
    out, got, grad3, hidden2, g, norms, seen, lse, mixed, w_out, text_kv, queries, states,
    w_query, hidden1, own, other, w_self, core, order,
):
    tokens, width = own.shape
    count = order.shape[0]
    texts = states.shape[0]
    kind = BF if (D // count) % 16 == 0 else F32

    def full(*shape):
        return pl.BlockSpec(shape, lambda b, *_: (0,) * len(shape))

    wide, late = full(tokens, D), pl.BlockSpec(memory_space=pl.ANY)
    sums = jax.ShapeDtypeStruct((D // 2, 5 * D), BF)
    return pl.pallas_call(
        cross_back_kernel,
        grid_spec=pltpu.PrefetchScalarGridSpec(
            num_scalar_prefetch=2,
            grid=(1,),
            in_specs=[
                wide,
                full(2, tokens, D),
                wide,
                wide,
                wide,
                full(1, D),
                full(2, D),
                full(texts, 1),
                full(HEADS, tokens),
                wide,
                full(D, D),
                full(texts, D),
                pl.BlockSpec((texts, D), lambda b, *_: (0, 1)),
                wide,
                full(texts, D),
                late,
                late,
                late,
                late,
                late,
            ],
            out_specs=[
                wide,
                wide,
                full(tokens, width),
                full(tokens, width),
                full(texts, 2 * D),
                full(8, D),
                late,
                late,
            ],
            scratch_shapes=[
                pltpu.VMEM((D, D), BF),
                pltpu.VMEM((tokens, D), F32),
                pltpu.VMEM((tokens, width), BF),
                pltpu.VMEM((tokens, width), BF),
                pltpu.VMEM((D, D), BF),
                pltpu.VMEM((D, tokens), kind),
                pltpu.VMEM((D, tokens), kind),
                pltpu.VMEM((D, 5 * D), BF),
                pltpu.SemaphoreType.DMA((5,)),
                pltpu.SemaphoreType.DMA((8,)),
            ],
        ),
        out_shape=[
            jax.ShapeDtypeStruct((tokens, D), BF),
            jax.ShapeDtypeStruct((tokens, D), F32),
            jax.ShapeDtypeStruct((tokens, width), BF),
            jax.ShapeDtypeStruct((tokens, width), BF),
            jax.ShapeDtypeStruct((texts, 2 * D), BF),
            jax.ShapeDtypeStruct((8, D), F32),
            sums,
            sums,
        ],
        compiler_params=pltpu.CompilerParams(vmem_limit_bytes=60 * MIB),
        cost_estimate=pl.CostEstimate(
            flops=14 * tokens * D * D, bytes_accessed=36 * tokens * D + 16 * D * D, transcendentals=0
        ),
        name="cross_attention_back",
    )(
        core.reshape(1), order, out, got, grad3, hidden2, g, norms[2].reshape(1, D),
        jnp.stack(norms[:2]), seen, lse, mixed, w_out, text_kv, text_kv, queries, states,
        w_query, hidden1, own, other, w_self,
    )


def behind(value, *others):
    return lax.optimization_barrier((value,) + others)[0]


class Plan:
    def __init__(self, n_img, n_txt):
        self.n_txt = n_txt
        self.n = n_img * n_txt
        self.chips = self.n // 2
        self.ny = n_txt // 2
        self.levels = self.chips.bit_length() - 1
        rest = list(range(2, self.levels))
        self.orders = ([1, 0] + rest, [0, 1] + rest)
        self.me = lax.axis_index("img") * n_txt + lax.axis_index("txt")
        self.core = self.me % 2
        self.chip = self.me // 2
        self.y = lax.axis_index("txt") // 2
        sources = (self.y - jnp.arange(self.ny, dtype=jnp.int32)) % self.ny
        self.places = jnp.concatenate([2 * sources + self.core, 2 * sources + 1 - self.core])
        self.rows = (self.y - jnp.arange(n_txt, dtype=jnp.int32) // 2) % self.ny
        maps = np.zeros((2, self.chips), np.int32)
        for core in range(2):
            for i in range(self.chips):
                for s, bit in enumerate(self.orders[core]):
                    maps[core, i] |= ((i >> (self.levels - 1 - s)) & 1) << bit
        self.blocks = jnp.bitwise_xor(
            self.chip, jnp.where(self.core == 0, jnp.asarray(maps[0]), jnp.asarray(maps[1]))
        ).astype(jnp.int32)
        other_map = jnp.where(self.core == 0, jnp.asarray(maps[1]), jnp.asarray(maps[0]))
        sent = jnp.bitwise_xor(self.chip, other_map).astype(jnp.int32)
        self.devices = jnp.concatenate([2 * sent + 1 - self.core, 2 * self.blocks + self.core])
        backs = np.argsort(maps, axis=1).astype(np.int32)
        away = jnp.bitwise_xor(self.chip, jnp.arange(self.chips, dtype=jnp.int32))
        self.goes_to = jnp.take(jnp.asarray(backs)[self.core], away, mode="clip")

    def swap(self, value):
        return lax.ppermute(value, BOTH, [(d, d ^ 1) for d in range(self.n)])

    def shift_y(self, value, by):
        pairs = []
        for d in range(self.n):
            img, txt = divmod(d, self.n_txt)
            y, core = divmod(txt, 2)
            pairs.append((d, img * self.n_txt + ((y + by) % self.ny) * 2 + core))
        return lax.ppermute(value, BOTH, pairs)

    def halve(self, value, step):
        pairs = [(d, d ^ (2 << self.orders[d % 2][step])) for d in range(self.n)]
        return lax.ppermute(value, BOTH, pairs)

    def send_items(self, value, note=None):
        parts = []
        for k in range(self.ny):
            part = value[(self.y + k) % self.ny]
            if note is not None:
                part = jnp.concatenate([part, note], 0)
            parts.append(self.shift_y(part, k) if k else part)
        return parts

    def join_items(self, parts, length):
        notes = [p[length:] for p in parts] if parts[0].shape[0] > length else []
        return jnp.concatenate([p[:length] for p in parts] + notes, 0)

    def from_item(self, value):
        parts = [value[0]]
        for k in range(1, self.ny):
            parts.append(self.shift_y(value[k], -k))
        stacked = jnp.stack(parts)
        order = [(i - self.y) % self.ny for i in range(self.ny)]
        return jnp.stack([stacked[o] for o in order])

    def to_places(self, own, other):
        length = own.shape[0] // self.ny
        both = jnp.concatenate([own, other], 0).reshape(2 * self.ny, length, -1)
        order = [
            ((p % 2) ^ self.core) * self.ny + (self.y - p // 2) % self.ny for p in range(self.n_txt)
        ]
        return jnp.concatenate([both[o] for o in order], 0)

    def from_places(self, value):
        length = value.shape[0] // self.n_txt
        parts = value.reshape(self.n_txt, length, -1)
        own = [parts[((self.y - r) % self.ny) * 2 + self.core] for r in range(self.ny)]
        other = [parts[((self.y - r) % self.ny) * 2 + 1 - self.core] for r in range(self.ny)]
        return jnp.concatenate(own, 0), jnp.concatenate(other, 0)

    def start(self, keep, send, step=0):
        return keep, self.halve(send, step), step

    def add(self, state):
        keep, got, step = state
        total = keep.astype(F32) + got.astype(F32)
        half = total.shape[0] // 2
        return total if half == 0 else (total[:half].astype(BF), total[half:].astype(BF))

    def advance(self, state, after):
        keep, send = self.add(state)
        keep, send, after = lax.optimization_barrier((keep, send, after))
        return after, self.start(keep, send, state[2] + 1)

    def finish(self, state):
        while state[2] < self.levels - 1:
            keep, send = self.add(state)
            state = self.start(keep, send, state[2] + 1)
        return self.add(state)[0]

    def split(self, value):
        ordered = jnp.take(value, self.blocks, axis=0, mode="clip")
        return ordered[: self.chips // 2], ordered[self.chips // 2 :]


def per_device(
    n_img,
    n_txt,
    image_tokens,
    text_states,
    text_segments,
    item_segments,
    norm1_gain,
    norm1_bias,
    w_qkv,
    w_self_out,
    norm2_gain,
    norm2_bias,
    w_cross_q,
    w_cross_kv,
    w_cross_out,
    norm3_gain,
    norm3_bias,
    w_up,
    w_down,
    cotangent,
):
    plan = Plan(n_img, n_txt)
    core, n, chips, ny = plan.core, plan.n, plan.chips, plan.ny
    items, length, _ = image_tokens.shape
    tokens = items * length
    half_d = D // 2
    rows = D // n

    states = text_states.shape[1]
    ids = jnp.pad(text_segments.astype(BF), ((0, 15), (0, D - states)))
    note = jnp.concatenate([text_states[0], ids], 0)
    x_parts = plan.send_items(image_tokens, note)
    g_parts = plan.send_items(behind(cotangent, x_parts[-1]))
    x_own = plan.join_items(x_parts, length)
    x_other = plan.swap(x_own)

    notes = [v[tokens:].reshape(ny, states + 16, D) for v in (x_own, x_other)]
    notes = jnp.concatenate(notes, 0)
    ids = notes[:, states, :states].reshape(-1)
    states_all = notes[:, :states].reshape(-1, D)
    text_kv = nn(states_all, w_cross_kv).astype(BF)
    matches = ids == item_segments[0, plan.y].astype(BF)
    seen = jnp.where(matches, 0.0, MASKED).astype(F32)[:, None]

    joined, normed1 = project_all(
        x_own, x_other, norm1_gain, norm1_bias, w_qkv, core, plan.places, length
    )
    mixed_own, mixed_other, lse = attend(joined, core, plan.rows)
    mixed_got = plan.swap(mixed_other)
    g_own = plan.join_items([behind(p, mixed_other) for p in g_parts], length)
    g_other = plan.swap(g_own)

    norms = (norm2_gain, norm2_bias, norm3_gain, norm3_bias)
    hidden1, hidden2, normed3, cross_q, cross_mixed, cross_lse = cross_part(
        x_own,
        mixed_own,
        mixed_got,
        text_kv,
        seen,
        norms,
        w_self_out,
        w_cross_q,
        w_cross_out,
        core,
    )

    normed3_other = plan.swap(normed3)
    per_down = w_down.shape[0] // n
    active, grad_up, keep, send = mlp_grads(
        normed3, normed3_other, g_own, g_other, w_up, w_down, core, plan.blocks, plan.goes_to
    )
    mlp_sums = plan.start(keep, send)
    out, grad3, sent = mlp_outputs(active, grad_up, w_up, w_down, core, chips)
    got = plan.swap(sent)

    block_out, grad_hidden1, grad_own, grad_other, grad_kv, norm_sums, keep, send = cross_back(
        out, got, grad3, hidden2, g_own, norms[:3], seen, cross_lse, cross_mixed, w_cross_out,
        text_kv, cross_q, states_all, w_cross_q, hidden1, mixed_own, mixed_got, w_self_out,
        core, plan.devices,
    )
    grad_got = plan.swap(grad_other)
    swapped = plan.swap(send)

    grad_got, mlp_sums = plan.advance(mlp_sums, grad_got)
    dq, dk, dv = attend_back(
        joined, grad_own, grad_got, mixed_own, mixed_other, lse, core, plan.rows
    )
    keep, swapped, _ = lax.optimization_barrier((keep, swapped, dv))
    middle_sums = (keep.astype(F32) + swapped.astype(F32)).astype(BF).reshape(chips, rows, -1)
    middle_keep, middle_send = middle_sums[: chips // 2], middle_sums[chips // 2 :]
    middle_keep, middle_send, dv = lax.optimization_barrier((middle_keep, middle_send, dv))
    middle_sums = plan.start(middle_keep, middle_send)
    dv, mlp_sums = plan.advance(mlp_sums, dv)
    joined_grad = jnp.concatenate([dq, dk, dv], 1)
    w_own = [lax.dynamic_slice(w_qkv, (0, s * D + core * half_d), (D, half_d)) for s in range(3)]
    part_own, part_other = plan.from_places(nt(joined_grad, jnp.concatenate(w_own, 1)))
    grad1 = part_own + plan.swap(part_other.astype(BF)).astype(F32)
    qkv_grad = tn(normed1, joined_grad)
    unit1, rstd1 = norm_parts(x_own[:tokens].astype(F32))
    grad_gain1 = jnp.sum(grad1 * unit1, axis=0)
    grad_bias1 = jnp.sum(grad1, axis=0)
    norms = jnp.concatenate([jnp.stack([grad_gain1, grad_bias1]), norm_sums[2:]], 0)
    norms = norms.reshape(8, chips, 2 * rows).transpose(1, 2, 0).astype(BF)
    norms = jnp.pad(norms, ((0, 0), (0, 0), (0, 128 - 8)))
    last = jnp.concatenate([qkv_grad.astype(BF).reshape(chips, 2 * rows, -1), norms], -1)
    last_keep, last_send = plan.split(last)
    last_keep, mlp_sums = plan.advance(mlp_sums, last_keep)
    last_sums = plan.start(last_keep, last_send)

    grad_kv, block_out, last_send, middle_got = lax.optimization_barrier(
        (grad_kv, block_out, last_send, middle_sums[1])
    )
    middle_sums = (middle_sums[0], middle_got, middle_sums[2])
    text_part = nt(grad_kv, w_cross_kv).astype(BF).reshape(2, ny, states, D)
    text_part = text_part[0].astype(F32) + plan.swap(text_part[1]).astype(F32)
    text_grad = text_part[0]
    for r in range(1, ny):
        text_grad += plan.shift_y(text_part[r].astype(BF), -r).astype(F32)
    block_out = plan.from_item(block_out.reshape(ny, length, D))
    last_sums = plan.finish(last_sums)
    up_down = plan.finish(mlp_sums)
    middle_sums = plan.finish(middle_sums)

    image_grad = norm_back(unit1, rstd1, norm1_gain, grad1) + grad_hidden1
    image_grad = plan.from_item(image_grad.astype(BF).reshape(ny, length, D)).astype(F32)

    units = w_up.shape[1] // 2
    down_grad = jnp.concatenate([up_down[:, units : units + D], up_down[:, units + D :]], 0)
    parts = jnp.concatenate([up_down[:, :units], last_sums], 1).reshape(2, rows, -1)
    mine = parts[core]
    theirs = plan.swap(parts[1 - core].astype(BF)).astype(F32)
    by_core = jnp.where(core == 0, jnp.stack([mine, theirs]), jnp.stack([theirs, mine]))
    up_grad = by_core[:, :, :units].reshape(2, rows, chips, per_down)
    up_grad = up_grad.transpose(1, 2, 0, 3).reshape(rows, 2 * units)
    wide = by_core[:, :, units : units + 3 * half_d].reshape(2, rows, 3, half_d)
    wide = wide.transpose(1, 2, 0, 3).reshape(rows, 3 * D)
    norm_sums = mine[:, -128:-122] + theirs[:, -128:-122]
    return (
        block_out,
        image_grad,
        text_grad[None],
        norm_sums[:, 0],
        norm_sums[:, 1],
        wide,
        middle_sums[:, 2 * D : 3 * D],
        norm_sums[:, 2],
        norm_sums[:, 3],
        middle_sums[:, D : 2 * D],
        middle_sums[:, 3 * D :],
        middle_sums[:, :D],
        norm_sums[:, 4],
        norm_sums[:, 5],
        up_grad,
        down_grad,
    )


def solution(mesh):
    split = P("img", "txt", None)
    rows = P(BOTH)
    wide = P(BOTH, None)
    return jax.shard_map(
        partial(per_device, mesh.shape["img"], mesh.shape["txt"]),
        mesh=mesh,
        in_specs=(split, split, P("img", "txt"), P("img", None)) + (P(),) * 13 + (split,),
        out_specs=(
            (split,) * 3
            + (rows, rows, wide, wide)
            + (rows, rows, wide, wide, wide)
            + (rows, rows, wide, wide)
        ),
        check_vma=False,
    )
```

```python
from functools import partial

import jax
import jax.numpy as jnp
import numpy as np
from jax import lax
from jax.experimental import pallas as pl
from jax.experimental.pallas import tpu as pltpu
from jax.sharding import PartitionSpec as P

D = 1024
HEADS = 16
HEAD = 64
EPS = 1e-05
MASKED = -1e30
SCALE = HEAD**-0.5
LOG2E = 1.4426950408889634
BOTH = ("img", "txt")
BF = jnp.bfloat16
F32 = jnp.float32
QUERY_BLOCK = 256
MIB = 1 << 20
SMALL = pl.CostEstimate(flops=1 << 20, bytes_accessed=1 << 16, transcendentals=0)


def nn(a, b):
    return lax.dot_general(a, b, (((1,), (0,)), ((), ())), preferred_element_type=F32)


def nt(a, b):
    return lax.dot_general(a, b, (((1,), (1,)), ((), ())), preferred_element_type=F32)


def tn(a, b):
    return lax.dot_general(a, b, (((0,), (0,)), ((), ())), preferred_element_type=F32)


def norm_parts(values):
    center = values - jnp.mean(values, axis=-1, keepdims=True)
    rstd = lax.rsqrt(jnp.mean(center * center, axis=-1, keepdims=True) + EPS)
    return center * rstd, rstd


def norm_back(unit, rstd, gain, grad):
    scaled = grad * gain
    return rstd * (
        scaled
        - jnp.mean(scaled, axis=-1, keepdims=True)
        - unit * jnp.mean(scaled * unit, axis=-1, keepdims=True)
    )


def gelu_parts(value):
    inner = jnp.clip(value * (0.5**0.5), -4.0, 4.0)
    square = inner * inner
    top = jnp.full_like(square, -2.72614225801306e-10)
    for term in (
        2.77068142495902e-08,
        -2.10102402082508e-06,
        -5.69250639462346e-05,
        -7.34990630326855e-04,
        -2.95459980854025e-03,
        -1.60960333262415e-02,
    ):
        top = top * square + term
    low = jnp.full_like(square, -1.45660718464996e-05)
    for term in (
        -2.13374055278905e-04,
        -1.68282697438203e-03,
        -7.37332916720468e-03,
        -1.42647390514189e-02,
    ):
        low = low * square + term
    cdf = 0.5 + 0.5 * inner * top / low
    density = jnp.exp2(value * value * (-0.5 * LOG2E)) * (0.5 / np.pi) ** 0.5
    return value * cdf, cdf + value * density


def project_kernel(
    core_ref, place_ref, own_ref, other_ref, gain_ref, bias_ref, wq_ref, wk_ref, wv_ref, *outs
):
    joined_ref, normed_ref = outs
    block, own_blocks = pl.program_id(0), pl.num_programs(0) // 2
    tokens = jnp.where(block < own_blocks, own_ref[...], other_ref[...]).astype(F32)
    unit, _ = norm_parts(tokens)
    normed = (unit * gain_ref[...] + bias_ref[...]).astype(BF)
    normed_ref[...] = normed
    width = wq_ref.shape[1]
    for s, w_ref in enumerate((wq_ref, wk_ref, wv_ref)):
        joined_ref[:, s * width : (s + 1) * width] = nn(normed, w_ref[...]).astype(BF)


def project_all(own, other, gain, bias, w_qkv, core, places, length):
    blocks = places.shape[0]
    half = blocks // 2
    width = D // 2
    row = pl.BlockSpec((1, D), lambda b, *_: (0, 0))
    weights = [pl.BlockSpec((D, width), lambda b, c, p, s=s: (0, 2 * s + c[0])) for s in range(3)]
    return pl.pallas_call(
        project_kernel,
        grid_spec=pltpu.PrefetchScalarGridSpec(
            num_scalar_prefetch=2,
            grid=(blocks,),
            in_specs=[
                pl.BlockSpec((length, D), lambda b, *_: (jnp.minimum(b, half - 1), 0)),
                pl.BlockSpec((length, D), lambda b, *_: (jnp.maximum(b - half, 0), 0)),
                row,
                row,
            ]
            + weights,
            out_specs=[
                pl.BlockSpec((length, 3 * width), lambda b, c, p: (p[b], 0)),
                pl.BlockSpec((length, D), lambda b, c, p: (p[b], 0)),
            ],
        ),
        out_shape=[
            jax.ShapeDtypeStruct((blocks * length, 3 * width), BF),
            jax.ShapeDtypeStruct((blocks * length, D), BF),
        ],
        compiler_params=pltpu.CompilerParams(vmem_limit_bytes=60 * MIB),
        cost_estimate=SMALL,
        name="norm_and_project",
    )(
        core.reshape(1),
        places,
        own,
        other,
        gain.reshape(1, D),
        bias.reshape(1, D),
        w_qkv,
        w_qkv,
        w_qkv,
    )


def middle_kernel(
    core_ref,
    x_ref,
    own_ref,
    got_ref,
    keys_ref,
    values_ref,
    seen_ref,
    gain2_ref,
    bias2_ref,
    gain3_ref,
    bias3_ref,
    w_own_ref,
    w_got_ref,
    w_query_ref,
    w_out_ref,
    hidden1_ref,
    hidden2_ref,
    normed3_ref,
    queries_ref,
    mixed_ref,
    lse_ref,
):
    hidden = x_ref[...].astype(F32) + nn(own_ref[...], w_own_ref[...])
    hidden += nn(got_ref[...], w_got_ref[...])
    hidden1_ref[...] = hidden
    unit, _ = norm_parts(hidden)
    normed2 = (unit * gain2_ref[...] + bias2_ref[...]).astype(BF)
    queries = nn(normed2, w_query_ref[...]).astype(BF)
    queries_ref[...] = queries
    rows, states = queries.shape[0], keys_ref.shape[0]
    half = lax.broadcasted_iota(jnp.int32, (rows, 2 * HEAD), 1) >= HEAD
    v_flip = values_ref[...].T
    ones = jnp.ones((16, states), BF)
    zero = jnp.zeros((rows, 2 * HEAD), BF)
    outs, lses = [], []
    for head in range(HEADS):
        at, h = head // 2 * 2 * HEAD, head % 2
        own = jnp.where(half == (h == 1), queries[:, at : at + 2 * HEAD], zero)
        scores = nt(keys_ref[:, at : at + 2 * HEAD], own) * (SCALE * LOG2E) + seen_ref[...]
        top = jnp.max(scores, axis=0, keepdims=True)
        raised = jnp.exp2(scores - top).astype(BF)
        v_rows = jnp.concatenate([v_flip[head * HEAD : (head + 1) * HEAD], ones], 0)
        mixed = nn(v_rows, raised)
        total = mixed[HEAD : HEAD + 1]
        lses.append(top + jnp.log2(total))
        outs.append((mixed[:HEAD] / total).astype(BF))
    lse_ref[...] = jnp.concatenate(lses, 0)
    mixed = jnp.concatenate(outs, 0).T
    mixed_ref[...] = mixed
    hidden += nn(mixed, w_out_ref[...])
    hidden2_ref[...] = hidden
    unit, _ = norm_parts(hidden)
    normed3_ref[...] = (unit * gain3_ref[...] + bias3_ref[...]).astype(BF)


def cross_part(x, own, got, text_kv, seen, norms, w_self_out, w_query, w_out, core):
    tokens, width = got.shape
    states = text_kv.shape[0]
    block = min(256, tokens)
    row = pl.BlockSpec((1, D), lambda b, c: (0, 0))
    wide = pl.BlockSpec((block, D), lambda b, c: (b, 0))
    narrow = pl.BlockSpec((block, width), lambda b, c: (b, 0))
    square = pl.BlockSpec((D, D), lambda b, c: (0, 0))
    return pl.pallas_call(
        middle_kernel,
        grid_spec=pltpu.PrefetchScalarGridSpec(
            num_scalar_prefetch=1,
            grid=(tokens // block,),
            in_specs=[
                wide,
                narrow,
                narrow,
                pl.BlockSpec((states, D), lambda b, c: (0, 0)),
                pl.BlockSpec((states, D), lambda b, c: (0, 1)),
                pl.BlockSpec((states, 1), lambda b, c: (0, 0)),
                row,
                row,
                row,
                row,
                pl.BlockSpec((width, D), lambda b, c: (c[0], 0)),
                pl.BlockSpec((width, D), lambda b, c: (1 - c[0], 0)),
                square,
                square,
            ],
            out_specs=[wide] * 5 + [pl.BlockSpec((HEADS, block), lambda b, c: (0, b))],
        ),
        out_shape=[
            jax.ShapeDtypeStruct((tokens, D), F32),
            jax.ShapeDtypeStruct((tokens, D), F32),
            jax.ShapeDtypeStruct((tokens, D), BF),
            jax.ShapeDtypeStruct((tokens, D), BF),
            jax.ShapeDtypeStruct((tokens, D), BF),
            jax.ShapeDtypeStruct((HEADS, tokens), F32),
        ],
        compiler_params=pltpu.CompilerParams(vmem_limit_bytes=60 * MIB),
        cost_estimate=SMALL,
        name="cross_attention_part",
    )(
        core.reshape(1),
        x,
        own,
        got,
        text_kv,
        text_kv,
        seen,
        *[v.reshape(1, D) for v in norms],
        w_self_out,
        w_self_out,
        w_query,
        w_out,
    )


def attend_kernel(row_ref, q_ref, k_ref, v_ref, out_ref, lse_ref):
    length = q_ref.shape[0]
    block = QUERY_BLOCK
    scale = SCALE * LOG2E
    half = lax.broadcasted_iota(jnp.int32, (block, 2 * HEAD), 1) >= HEAD
    key_row = lax.broadcasted_iota(jnp.int32, (block, block), 0)
    query_col = lax.broadcasted_iota(jnp.int32, (block, block), 1)
    seen = key_row <= query_col
    v_flip = v_ref[...].T
    ones = jnp.ones((16, length), BF)
    v_rows = [jnp.concatenate([v_flip[h * HEAD : (h + 1) * HEAD], ones], 0) for h in range(2)]
    for i in range(length // block):
        lo, hi = i * block, (i + 1) * block
        queries = q_ref[lo:hi, :]
        outs = []
        for h in range(2):
            own = jnp.where(half == (h == 1), queries, jnp.zeros_like(queries))
            diag = jnp.where(seen, nt(k_ref[lo:hi, :], own), MASKED)
            top = jnp.max(diag, axis=0, keepdims=True)
            if i:
                rest = nt(k_ref[:lo, :], own)
                top = jnp.maximum(top, jnp.max(rest, axis=0, keepdims=True))
            base = top * scale
            mixed = nn(v_rows[h][:, lo:hi], jnp.exp2(diag * scale - base).astype(BF))
            if i:
                mixed += nn(v_rows[h][:, :lo], jnp.exp2(rest * scale - base).astype(BF))
            total = mixed[HEAD : HEAD + 1]
            lse_ref[0, h : h + 1, lo:hi] = base + jnp.log2(total)
            outs.append(mixed[:HEAD] / total)
        result = jnp.concatenate(outs, 0).T.astype(BF)
        part = length // row_ref.shape[0]
        for at in range(0, block, part):
            row = pl.multiple_of(row_ref[(lo + at) // part] * part, part)
            out_ref[pl.ds(row, part), :] = result[at : at + part]


def head_specs(length, pairs):
    return [
        pl.BlockSpec((length, 2 * HEAD), lambda p, *_, s=s: (0, s * pairs + p)) for s in range(3)
    ]


def attend(joined, rows):
    length, width = joined.shape[0], joined.shape[1] // 3
    pairs = width // (2 * HEAD)
    return pl.pallas_call(
        attend_kernel,
        grid_spec=pltpu.PrefetchScalarGridSpec(
            num_scalar_prefetch=1,
            grid=(pairs,),
            in_specs=head_specs(length, pairs),
            out_specs=[pl.BlockSpec((length, 2 * HEAD), lambda p, *_: (0, p)), pl.BlockSpec((1, 2, length), lambda p, *_: (p, 0, 0))],
        ),
        out_shape=[
            jax.ShapeDtypeStruct((length, width), BF),
            jax.ShapeDtypeStruct((pairs, 2, length), F32),
        ],
        compiler_params=pltpu.CompilerParams(vmem_limit_bytes=60 * MIB),
        cost_estimate=SMALL,
        name="self_attention",
    )(rows, joined, joined, joined)


def attend_back_kernel(
    row_ref,
    q_ref,
    k_ref,
    v_ref,
    own_g_ref,
    other_g_ref,
    mixed_ref,
    lse_ref,
    dq_ref,
    dk_ref,
    dv_ref,
    dq_sum,
    g_ref,
    o_ref,
):
    length = q_ref.shape[0]
    places = row_ref.shape[0]
    part = length // places
    for place in range(places):
        row = row_ref[place]
        at = pl.ds(pl.multiple_of(row % (places // 2) * part, part), part)
        to = slice(place * part, (place + 1) * part)
        mine = row < places // 2
        g_ref[to, :] = jnp.where(mine, own_g_ref[at, :], other_g_ref[at, :])
        o_ref[to, :] = mixed_ref[pl.ds(pl.multiple_of(row * part, part), part), :]
    block = QUERY_BLOCK
    scale = SCALE * LOG2E
    half = lax.broadcasted_iota(jnp.int32, (length, 2 * HEAD), 1) >= HEAD
    key_row = lax.broadcasted_iota(jnp.int32, (block, block), 0)
    query_col = lax.broadcasted_iota(jnp.int32, (block, block), 1)
    seen = key_row <= query_col
    k_flip = k_ref[...].T
    zero = jnp.zeros((length, 2 * HEAD), BF)
    queries = [jnp.where(half == (h == 1), q_ref[...], zero) for h in range(2)]
    grads = [jnp.where(half == (h == 1), g_ref[...], zero) for h in range(2)]
    product = (g_ref[...].astype(F32) * o_ref[...].astype(F32)).T
    deltas = [jnp.sum(product[h * HEAD : (h + 1) * HEAD], axis=0, keepdims=True) for h in range(2)]
    for j in range(length // block):
        lo, hi = j * block, (j + 1) * block
        keys, values = k_ref[lo:hi, :], v_ref[lo:hi, :]
        key_grad = value_grad = None
        for h in range(2):
            own_q, own_g = queries[h][lo:], grads[h][lo:]
            scores = nt(keys, own_q) * scale - lse_ref[0, h : h + 1, lo:]
            weights = jnp.exp2(scores)
            first = jnp.where(seen, weights[:, :block], 0.0)
            weights = jnp.concatenate([first, weights[:, block:]], 1) if hi < length else first
            score_grad = (weights * (nt(values, own_g) - deltas[h][:, lo:])).astype(BF)
            weights = weights.astype(BF)
            value_part = nn(weights, own_g)
            key_part = nn(score_grad, own_q)
            value_grad = value_part if h == 0 else value_grad + value_part
            key_grad = key_part if h == 0 else key_grad + key_part
            query_part = nn(k_flip[h * HEAD : (h + 1) * HEAD, lo:hi], score_grad)
            rows = slice(h * HEAD, (h + 1) * HEAD)
            if j == 0:
                dq_sum[rows, :] = query_part
            else:
                dq_sum[rows, lo:] += query_part
        dk_ref[lo:hi, :] = (key_grad * SCALE).astype(BF)
        dv_ref[lo:hi, :] = value_grad.astype(BF)
    dq_ref[...] = (dq_sum[...].T * SCALE).astype(BF)


def attend_back(joined, own_g, other_g, mixed, lse, rows):
    length, width = joined.shape[0], joined.shape[1] // 3
    pairs = width // (2 * HEAD)
    spec = pl.BlockSpec((length, 2 * HEAD), lambda p, *_: (0, p))
    half = pl.BlockSpec((length // 2, 2 * HEAD), lambda p, *_: (0, p))
    return pl.pallas_call(
        attend_back_kernel,
        grid_spec=pltpu.PrefetchScalarGridSpec(
            num_scalar_prefetch=1,
            grid=(pairs,),
            in_specs=head_specs(length, pairs)
            + [half] * 2
            + [spec]
            + [pl.BlockSpec((1, 2, length), lambda p, *_: (p, 0, 0))],
            out_specs=[spec] * 3,
            scratch_shapes=[
                pltpu.VMEM((2 * HEAD, length), F32),
                pltpu.VMEM((length, 2 * HEAD), BF),
                pltpu.VMEM((length, 2 * HEAD), BF),
            ],
        ),
        out_shape=[jax.ShapeDtypeStruct((length, width), BF)] * 3,
        compiler_params=pltpu.CompilerParams(vmem_limit_bytes=60 * MIB),
        cost_estimate=SMALL,
        name="self_attention_back",
    )(rows, joined, joined, joined, own_g, other_g, mixed, lse)


def mlp_kernel(
    pieces,
    steps,
    core_ref,
    rows_from,
    goes_to,
    own_ref,
    other_ref,
    own_g_ref,
    other_g_ref,
    *refs,
):
    ups, downs = refs[:pieces], refs[pieces : 2 * pieces]
    down_ref, up_ref, out_ref, norm_ref, sent_ref, *targets = refs[2 * pieces : 2 * pieces + 9]
    flip_ref, ordered_ref, wide_ref, tall_ref, active_ref, grad_ref, sems = refs[2 * pieces + 9 :]
    step = pl.program_id(0)
    slot = step % 2
    tokens = own_ref.shape[0]
    quarter, height = targets[0].shape[0], targets[0].shape[1]
    tile = wide_ref.shape[3]
    width = 2 * height
    per_step = tile // width
    units = steps * tile

    @pl.when(step == 0)
    def _():
        flip_ref[:, :tokens] = own_ref[...].T
        flip_ref[:, tokens:] = other_ref[...].T
        for i in range(4 * quarter):
            at = pl.multiple_of(rows_from[i] * height, height)
            ordered_ref[i * height : (i + 1) * height, :] = flip_ref[pl.ds(at, height), :]

    def wide_copy(at, where, side):
        part = wide_ref.at[at, side * quarter : (side + 1) * quarter]
        lanes = pl.ds(pl.multiple_of(where * tile, tile), tile)
        return pltpu.make_async_copy(part, targets[side].at[:, :, lanes], sems.at[at, side])

    def tall_copy(at, j, r, target, i):
        rows = slice(j * width + r * height, j * width + (r + 1) * height)
        lanes = slice(units + r * D, units + (r + 1) * D)
        return pltpu.make_async_copy(
            tall_ref.at[at, rows], target.at[i, :, lanes], sems.at[at, 4 + 2 * j + r]
        )

    def wait(at):
        for side in range(4):
            wide_copy(at, 0, side).wait()
        for j in range(per_step):
            for r in range(2):
                tall_copy(at, j, r, targets[0], 0).wait()

    @pl.when((step >= 2) & (step < steps + 2))
    def _():
        wait(slot)

    @pl.when(step < steps)
    def _():
        up_w = jnp.concatenate([r[...] for r in ups], 1) if pieces > 1 else ups[0][...]
        down_w = jnp.concatenate([r[...] for r in downs], 0) if pieces > 1 else downs[0][...]
        chunk = min(512, tokens)
        active, grads = [], []
        for base, x_ref, g_ref in ((0, own_ref, own_g_ref), (tokens, other_ref, other_g_ref)):
            for at in range(0, tokens, chunk):
                rows = slice(at, at + chunk)
                up_value = nn(x_ref[rows, :], up_w)
                down_grad = nt(g_ref[rows, :], down_w)
                value, slope = gelu_parts(up_value)
                value = value.astype(BF)
                grad = (down_grad * slope).astype(BF)
                active_ref[step, base + at : base + at + chunk, :] = value
                grad_ref[step, base + at : base + at + chunk, :] = grad
                active.append(value)
                grads.append(grad)
        grad = jnp.concatenate(grads, 0)
        wide = nn(ordered_ref[...], grad).astype(BF)
        wide_ref[slot] = wide.reshape(wide_ref.shape[1:])
        value = jnp.concatenate(active, 0).T
        tall = nn(value[:, :tokens], own_g_ref[...]) + nn(value[:, tokens:], other_g_ref[...])
        tall_ref[slot] = tall.astype(BF)
        for side in range(4):
            wide_copy(slot, step, side).start()
        for j in range(per_step):
            i = goes_to[step * per_step + j]
            for side, target in enumerate(targets):

                @pl.when(i // quarter == side)
                def _(j=j, i=i, side=side, target=target):
                    for r in range(2):
                        tall_copy(slot, j, r, target, i - side * quarter).start()

    @pl.when(step >= steps)
    def _():
        up = up_ref[...]
        if up.shape[1] > units:
            first = core_ref[0] == 0
            picked = []
            for at in range(0, 2 * units, 2 * width):
                picked.append(
                    jnp.where(first, up[:, at : at + width], up[:, at + width : at + 2 * width])
                )
            up = jnp.concatenate(picked, 1)
        active = jnp.concatenate([active_ref[i] for i in range(steps)], 1)
        out = nn(active, down_ref[...].reshape(units, -1))
        grad = jnp.concatenate([grad_ref[i] for i in range(steps)], 1)
        norm = nt(grad, up)
        out_ref[...] = out[:tokens]
        norm_ref[...] = norm[:tokens]
        sent_ref[0] = out[tokens:].astype(BF)
        sent_ref[1] = norm[tokens:].astype(BF)


def mlp(own, other, own_g, other_g, w_up, w_down, core, rows_from, goes_to):
    tokens = own.shape[0]
    chips = rows_from.shape[0]
    tile, out_tile = 512, 256
    units = w_up.shape[1] // 2
    steps = units // tile
    width = units // chips
    height = D // chips
    fine = width % 128 == 0
    tall = w_down.reshape(chips, 2, width, D)
    if fine:
        pieces, piece = tile // width, width
    else:
        pieces, piece = 1, tile
        w_up = w_up.reshape(D, chips, 2, width)[:, :, core].reshape(D, units)
        w_down = w_down.reshape(chips, 2, width, D)[:, core].reshape(units, D)

    def place(s, c, j):
        s = jnp.minimum(s, steps - 1)
        return 2 * (s * pieces + j) + c[0] if fine else s

    def column(s):
        return jnp.maximum(s - steps, 0)

    whole = pl.BlockSpec((tokens, D), lambda s, *_: (0, 0))
    up_specs = [
        pl.BlockSpec((D, piece), lambda s, c, *_, j=j: (0, place(s, c, j))) for j in range(pieces)
    ]
    down_specs = [
        pl.BlockSpec((piece, D), lambda s, c, *_, j=j: (place(s, c, j), 0)) for j in range(pieces)
    ]
    kept = pl.BlockSpec((tokens, out_tile), lambda s, *_: (0, column(s)))
    sums = jax.ShapeDtypeStruct((chips // 4, height, units + 2 * D), BF)
    return pl.pallas_call(
        partial(mlp_kernel, pieces, steps),
        grid_spec=pltpu.PrefetchScalarGridSpec(
            num_scalar_prefetch=3,
            grid=(steps + D // out_tile,),
            in_specs=[whole] * 4
            + up_specs
            + down_specs
            + [
                pl.BlockSpec((chips, None, width, out_tile), lambda s, c, *_: (0, c[0], 0, column(s))),
                pl.BlockSpec((out_tile, w_up.shape[1]), lambda s, *_: (column(s), 0)),
            ],
            out_specs=[
                kept,
                kept,
                pl.BlockSpec((2, tokens, out_tile), lambda s, *_: (0, 0, column(s))),
            ]
            + [pl.BlockSpec(memory_space=pl.ANY)] * 4,
            scratch_shapes=[
                pltpu.VMEM((D, 2 * tokens), BF),
                pltpu.VMEM((D, 2 * tokens), BF),
                pltpu.VMEM((2, chips, height, tile), BF),
                pltpu.VMEM((2, tile, D), BF),
                pltpu.VMEM((steps, 2 * tokens, tile), BF),
                pltpu.VMEM((steps, 2 * tokens, tile), BF),
                pltpu.SemaphoreType.DMA((2, 4 + 2 * (tile // width))),
            ],
        ),
        out_shape=[
            jax.ShapeDtypeStruct((tokens, D), F32),
            jax.ShapeDtypeStruct((tokens, D), F32),
            jax.ShapeDtypeStruct((2, tokens, D), BF),
            sums,
            sums,
            sums,
            sums,
        ],
        compiler_params=pltpu.CompilerParams(vmem_limit_bytes=60 * MIB),
        cost_estimate=SMALL,
        name="mlp_both_ways",
    )(
        core.reshape(1),
        rows_from,
        goes_to,
        own,
        other,
        own_g,
        other_g,
        *([w_up] * pieces),
        *([w_down] * pieces),
        tall,
        w_up,
    )


def cross_back_kernel(
    scalars,
    order_ref,
    out_ref,
    got_ref,
    grad3_ref,
    hidden2_ref,
    g_ref,
    gain3_ref,
    gain2_ref,
    seen_ref,
    lse_ref,
    mixed_ref,
    w_out_ref,
    keys_ref,
    values_ref,
    queries_ref,
    states_ref,
    w_query_hbm,
    hidden1_hbm,
    own_hbm,
    other_hbm,
    w_self_hbm,
    block_ref,
    hidden_grad_ref,
    own_grad_ref,
    other_grad_ref,
    text_ref,
    norms_ref,
    keep,
    send,
    w_query,
    hidden1,
    own_ref,
    other_ref,
    w_self,
    flip_ref,
    ordered_ref,
    stage_ref,
    sems,
    out_sems,
):
    core = scalars[0]
    tokens = out_ref.shape[0]
    loads = [
        pltpu.make_async_copy(a, b, sems.at[i])
        for i, (a, b) in enumerate(
            (
                (w_query_hbm, w_query),
                (hidden1_hbm, hidden1),
                (own_hbm.at[:tokens], own_ref),
                (other_hbm, other_ref),
                (w_self_hbm, w_self),
            )
        )
    ]
    for load in loads:
        load.start()
    count = order_ref.shape[0]
    rows = D // count
    half = D // 2
    writes = []

    def weight_part(depth, grads, slot, lane):
        for i in range(count):
            at = pl.multiple_of(order_ref[i] * rows, rows)
            ordered_ref[i * rows : (i + 1) * rows, :depth] = flip_ref[pl.ds(at, rows), :depth]
        width = grads.shape[1]
        product = nn(ordered_ref[:, :depth].astype(BF), grads)
        stage_ref[:, lane : lane + width] = product.astype(BF)
        for i, target in enumerate((send, keep)):
            writes.append(
                pltpu.make_async_copy(
                    stage_ref.at[i * half : (i + 1) * half, lane : lane + width],
                    target.at[:, lane : lane + width],
                    out_sems.at[2 * slot + i],
                )
            )
            writes[-1].start()

    kind = flip_ref.dtype
    hidden2 = hidden2_ref[...]
    block_ref[...] = (hidden2 + out_ref[...] + got_ref[0].astype(F32)).astype(BF)
    grad3 = grad3_ref[...] + got_ref[1].astype(F32)
    unit, rstd = norm_parts(hidden2)
    norms_ref[4:5, :] = jnp.sum(grad3 * unit, axis=0, keepdims=True)
    norms_ref[5:6, :] = jnp.sum(grad3, axis=0, keepdims=True)
    norms_ref[6:8, :] = jnp.zeros((2, D), F32)
    grad_hidden = norm_back(unit, rstd, gain3_ref[...], grad3) + g_ref[...].astype(F32)
    hidden_grad_ref[...] = grad_hidden
    branch = grad_hidden.astype(BF)
    flip_ref[:, :tokens] = mixed_ref[...].astype(kind).T
    weight_part(tokens, branch, 0, 0)
    grad_mixed = nt(branch, w_out_ref[...]).astype(BF)
    states = keys_ref.shape[0]
    half_lane = lax.broadcasted_iota(jnp.int32, (tokens, 2 * HEAD), 1) >= HEAD
    zero = jnp.zeros((tokens, 2 * HEAD), BF)
    k_flip = keys_ref[...].T
    flips, key_grads, value_grads = [], [], []
    for pair in range(HEADS // 2):
        lanes = slice(pair * 2 * HEAD, (pair + 1) * 2 * HEAD)
        queries, grads = queries_ref[:, lanes], grad_mixed[:, lanes]
        for h in range(2):
            head = 2 * pair + h
            own_q = jnp.where(half_lane == (h == 1), queries, zero)
            own_g = jnp.where(half_lane == (h == 1), grads, zero)
            scores = nt(keys_ref[:, lanes], own_q) * (SCALE * LOG2E) + seen_ref[...]
            weights = jnp.exp2(scores - lse_ref[head : head + 1, :])
            score_grad = nt(values_ref[:, lanes], own_g)
            delta = jnp.sum(weights * score_grad, axis=0, keepdims=True)
            score_grad = (weights * (score_grad - delta)).astype(BF)
            key_part, value_part = nn(score_grad, own_q), nn(weights.astype(BF), own_g)
            if h == 0:
                key_grads.append(key_part)
                value_grads.append(value_part)
            else:
                key_grads[-1] += key_part
                value_grads[-1] += value_part
            part = nn(k_flip[head * HEAD : (head + 1) * HEAD], score_grad)
            flips.append((part * SCALE).astype(BF))
    query_grad = jnp.concatenate(flips, 0).T
    text_grad = jnp.concatenate([p * SCALE for p in key_grads] + value_grads, 1).astype(BF)
    text_ref[...] = text_grad
    flip_ref[:, :states] = states_ref[...].astype(kind).T
    weight_part(states, text_grad, 1, 3 * D)
    for load in loads[:2]:
        load.wait()
    grad2 = nt(query_grad, w_query[...])
    unit, rstd = norm_parts(hidden1[...])
    normed2 = unit * gain2_ref[0:1, :] + gain2_ref[1:2, :]
    flip_ref[:, :tokens] = normed2.astype(BF).astype(kind).T
    weight_part(tokens, query_grad, 2, D)
    norms_ref[2:3, :] = jnp.sum(grad2 * unit, axis=0, keepdims=True)
    norms_ref[3:4, :] = jnp.sum(grad2, axis=0, keepdims=True)
    norms_ref[0:2, :] = jnp.zeros((2, D), F32)
    grad_hidden = norm_back(unit, rstd, gain2_ref[0:1, :], grad2) + hidden_grad_ref[...]
    hidden_grad_ref[...] = grad_hidden
    branch = grad_hidden.astype(BF)
    for load in loads[2:]:
        load.wait()
    own_rows = pl.ds(pl.multiple_of(core * half, half), half)
    other_rows = pl.ds(pl.multiple_of((1 - core) * half, half), half)
    own_grad_ref[...] = nt(branch, w_self[own_rows, :]).astype(BF)
    other_grad_ref[...] = nt(branch, w_self[other_rows, :]).astype(BF)
    flip_ref[own_rows, :tokens] = own_ref[...].astype(kind).T
    flip_ref[other_rows, :tokens] = other_ref[...].astype(kind).T
    weight_part(tokens, branch, 3, 2 * D)
    for write in writes:
        write.wait()


def cross_back(
    out, got, grad3, hidden2, g, norms, seen, lse, mixed, w_out, text_kv, queries, states,
    w_query, hidden1, own, other, w_self, core, order,
):
    tokens, width = other.shape
    count = order.shape[0]
    texts = states.shape[0]
    kind = BF if (D // count) % 16 == 0 else F32

    def full(*shape):
        return pl.BlockSpec(shape, lambda b, *_: (0,) * len(shape))

    wide, late = full(tokens, D), pl.BlockSpec(memory_space=pl.ANY)
    sums = jax.ShapeDtypeStruct((D // 2, 5 * D), BF)
    return pl.pallas_call(
        cross_back_kernel,
        grid_spec=pltpu.PrefetchScalarGridSpec(
            num_scalar_prefetch=2,
            grid=(1,),
            in_specs=[
                wide,
                full(2, tokens, D),
                wide,
                wide,
                wide,
                full(1, D),
                full(2, D),
                full(texts, 1),
                full(HEADS, tokens),
                wide,
                full(D, D),
                full(texts, D),
                pl.BlockSpec((texts, D), lambda b, *_: (0, 1)),
                wide,
                full(texts, D),
                late,
                late,
                late,
                late,
                late,
            ],
            out_specs=[
                wide,
                wide,
                full(tokens, width),
                full(tokens, width),
                full(texts, 2 * D),
                full(8, D),
                late,
                late,
            ],
            scratch_shapes=[
                pltpu.VMEM((D, D), BF),
                pltpu.VMEM((tokens, D), F32),
                pltpu.VMEM((tokens, width), BF),
                pltpu.VMEM((tokens, width), BF),
                pltpu.VMEM((D, D), BF),
                pltpu.VMEM((D, tokens), kind),
                pltpu.VMEM((D, tokens), kind),
                pltpu.VMEM((D, 5 * D), BF),
                pltpu.SemaphoreType.DMA((5,)),
                pltpu.SemaphoreType.DMA((8,)),
            ],
        ),
        out_shape=[
            jax.ShapeDtypeStruct((tokens, D), BF),
            jax.ShapeDtypeStruct((tokens, D), F32),
            jax.ShapeDtypeStruct((tokens, width), BF),
            jax.ShapeDtypeStruct((tokens, width), BF),
            jax.ShapeDtypeStruct((texts, 2 * D), BF),
            jax.ShapeDtypeStruct((8, D), F32),
            sums,
            sums,
        ],
        compiler_params=pltpu.CompilerParams(vmem_limit_bytes=60 * MIB),
        cost_estimate=SMALL,
        name="cross_attention_back",
    )(
        core.reshape(1), order, out, got, grad3, hidden2, g, norms[2].reshape(1, D),
        jnp.stack(norms[:2]), seen, lse, mixed, w_out, text_kv, text_kv, queries, states,
        w_query, hidden1, own, other, w_self,
    )


def project_back_kernel(place_ref, dq_ref, dk_ref, dv_ref, wq_ref, wk_ref, wv_ref, *refs):
    own_ref, other_ref, sum_ref = refs
    grad = nt(dq_ref[...], wq_ref[...])
    grad += nt(dk_ref[...], wk_ref[...])
    grad += nt(dv_ref[...], wv_ref[...])
    sum_ref[...] = grad
    half = (place_ref.shape[0] - 1) // 2
    part = grad.shape[0] // (2 * half)
    for block in range(2 * half):
        rows = sum_ref[pl.ds(pl.multiple_of(place_ref[block] * part, part), part), :]
        to = slice(block % half * part, (block % half + 1) * part)
        if block < half:
            own_ref[to, :] = rows
        else:
            other_ref[to, :] = rows.astype(BF)


def project_back(dq, dk, dv, w_qkv, core, places):
    length, width = dq.shape
    tile = 256
    grads = pl.BlockSpec((length, width), lambda t, p: (0, 0))
    weights = [
        pl.BlockSpec((tile, width), lambda t, p, s=s: (t, 2 * s + p[p.shape[0] - 1]))
        for s in range(3)
    ]
    out = pl.BlockSpec((length // 2, tile), lambda t, p: (0, t))
    return pl.pallas_call(
        project_back_kernel,
        grid_spec=pltpu.PrefetchScalarGridSpec(
            num_scalar_prefetch=1,
            grid=(D // tile,),
            in_specs=[grads] * 3 + weights,
            out_specs=[out, out],
            scratch_shapes=[pltpu.VMEM((length, tile), F32)],
        ),
        out_shape=[
            jax.ShapeDtypeStruct((length // 2, D), F32),
            jax.ShapeDtypeStruct((length // 2, D), BF),
        ],
        compiler_params=pltpu.CompilerParams(vmem_limit_bytes=60 * MIB),
        cost_estimate=SMALL,
        name="project_back",
    )(jnp.concatenate([places, core.reshape(1)]), dq, dk, dv, w_qkv, w_qkv, w_qkv)


def last_kernel(
    blocks_ref,
    x_ref,
    part_ref,
    got_ref,
    hidden_ref,
    gain_ref,
    norms_ref,
    normed_hbm,
    dq_hbm,
    dk_hbm,
    dv_hbm,
    image_ref,
    keep,
    send,
    normed,
    grads,
    flip_ref,
    ordered_ref,
    norm_flip,
    sems,
):
    loads = [pltpu.make_async_copy(normed_hbm, normed, sems.at[0])]
    for i, source in enumerate((dq_hbm, dk_hbm, dv_hbm)):
        loads.append(pltpu.make_async_copy(source, grads.at[i], sems.at[1 + i]))
    for load in loads:
        load.start()
    count = blocks_ref.shape[0]
    height, half = D // count, D // 2
    grad = part_ref[...] + got_ref[...].astype(F32)
    unit, rstd = norm_parts(x_ref[...].astype(F32))
    sums = [jnp.sum(grad * unit, axis=0, keepdims=True), jnp.sum(grad, axis=0, keepdims=True)]
    image = norm_back(unit, rstd, gain_ref[...], grad) + hidden_ref[...]
    image_ref[...] = image.astype(BF)
    fill = jnp.zeros((norm_flip.shape[1] - 8, D), F32)
    norm_flip[...] = jnp.concatenate(sums + [norms_ref[2:8, :], fill], 0).T
    loads[0].wait()
    flip_ref[...] = normed[...].T
    width = grads.shape[2]
    for i in range(count):
        at = pl.ds(pl.multiple_of(blocks_ref[i] * height, height), height)
        ordered_ref[i * height : (i + 1) * height, :] = flip_ref[at, :]
        to = i * height % half
        target = keep if i < count // 2 else send
        target[to : to + height, 3 * width :] = norm_flip[at, :].astype(BF)
    for s in range(3):
        loads[1 + s].wait()
        product = nn(ordered_ref[...], grads[s]).astype(BF)
        keep[:, s * width : (s + 1) * width] = product[:half]
        send[:, s * width : (s + 1) * width] = product[half:]


def last_part(x, part, got, hidden_grad, gain, norms, normed, dq, dk, dv, blocks):
    tokens = got.shape[0]
    length, width = dq.shape
    lanes = 3 * width + 128

    def full(*shape):
        return pl.BlockSpec(shape, lambda b, *_: (0,) * len(shape))

    wide, late = full(tokens, D), pl.BlockSpec(memory_space=pl.ANY)
    return pl.pallas_call(
        last_kernel,
        grid_spec=pltpu.PrefetchScalarGridSpec(
            num_scalar_prefetch=1,
            grid=(1,),
            in_specs=[wide] * 4 + [full(1, D), full(8, D)] + [late] * 4,
            out_specs=[wide, full(D // 2, lanes), full(D // 2, lanes)],
            scratch_shapes=[
                pltpu.VMEM((length, D), BF),
                pltpu.VMEM((3, length, width), BF),
                pltpu.VMEM((D, length), BF),
                pltpu.VMEM((D, length), BF),
                pltpu.VMEM((D, 128), F32),
                pltpu.SemaphoreType.DMA((4,)),
            ],
        ),
        out_shape=[jax.ShapeDtypeStruct((tokens, D), BF)]
        + [jax.ShapeDtypeStruct((D // 2, lanes), BF)] * 2,
        compiler_params=pltpu.CompilerParams(vmem_limit_bytes=60 * MIB),
        cost_estimate=SMALL,
        name="norm_back_and_qkv_gradient",
    )(blocks, x, part, got, hidden_grad, gain.reshape(1, D), norms, normed, dq, dk, dv)


def add_kernel(a_ref, b_ref, keep_ref, send_ref):
    block, half = pl.program_id(0), pl.num_programs(0) // 2
    total = a_ref[...] + b_ref[...]

    @pl.when(block < half)
    def _():
        send_ref[...] = total

    @pl.when(block >= half)
    def _():
        keep_ref[...] = total


def add_halves(a, b):
    count, height, width = a.shape
    blocks = 4
    half = blocks // 2
    shape = (count // blocks, height, width)
    turned = pl.BlockSpec(shape, lambda i: ((i + half) % blocks, 0, 0))
    return pl.pallas_call(
        add_kernel,
        grid=(blocks,),
        in_specs=[turned] * 2,
        out_specs=[
            pl.BlockSpec(shape, lambda i: (jnp.maximum(i - half, 0), 0, 0)),
            pl.BlockSpec(shape, lambda i: (jnp.minimum(i, half - 1), 0, 0)),
        ],
        out_shape=[jax.ShapeDtypeStruct((count // 2, height, width), BF)] * 2,
        compiler_params=pltpu.CompilerParams(vmem_limit_bytes=60 * MIB),
        cost_estimate=SMALL,
        name="add_halves",
    )(a, b)


def behind(value, *others):
    return lax.optimization_barrier((value,) + others)[0]


class Route:
    def __init__(self, plan, orders):
        self.orders = orders
        count = plan.chips
        maps = np.zeros((2, count), np.int32)
        for core in range(2):
            for i in range(count):
                for s, bit in enumerate(orders[core]):
                    maps[core, i] |= ((i >> (plan.levels - 1 - s)) & 1) << bit
        here, there = jnp.asarray(maps)[plan.core], jnp.asarray(maps)[1 - plan.core]
        self.blocks = jnp.bitwise_xor(plan.chip, here).astype(jnp.int32)
        sent = jnp.bitwise_xor(plan.chip, there).astype(jnp.int32)
        self.devices = jnp.concatenate([2 * sent + 1 - plan.core, 2 * self.blocks + plan.core])
        backs = np.argsort(maps, axis=1).astype(np.int32)
        away = jnp.bitwise_xor(plan.chip, jnp.arange(count, dtype=jnp.int32))
        self.goes_to = jnp.take(jnp.asarray(backs)[plan.core], away, mode="clip")


class Plan:
    def __init__(self, n_img, n_txt):
        self.n_txt = n_txt
        self.n = n_img * n_txt
        self.chips = self.n // 2
        self.ny = n_txt // 2
        self.levels = self.chips.bit_length() - 1
        self.me = lax.axis_index("img") * n_txt + lax.axis_index("txt")
        self.core = self.me % 2
        self.chip = self.me // 2
        self.y = lax.axis_index("txt") // 2
        sources = (self.y - jnp.arange(self.ny, dtype=jnp.int32)) % self.ny
        self.places = jnp.concatenate([2 * sources + self.core, 2 * sources + 1 - self.core])
        at = jnp.arange(n_txt, dtype=jnp.int32)
        self.rows = jnp.bitwise_xor(at % 2, self.core) * self.ny + (self.y - at // 2) % self.ny
        rest = list(range(2, self.levels))
        self.near = Route(self, ([1, 0] + rest, [0, 1] + rest))
        self.mixed = Route(self, ([1, 0] + rest, rest + [0, 1]))
        self.token = None

    def swap(self, value):
        return lax.ppermute(value, BOTH, [(d, d ^ 1) for d in range(self.n)])

    def shift_y(self, value, by):
        pairs = []
        for d in range(self.n):
            img, txt = divmod(d, self.n_txt)
            y, core = divmod(txt, 2)
            pairs.append((d, img * self.n_txt + ((y + by) % self.ny) * 2 + core))
        return lax.ppermute(value, BOTH, pairs)

    def halve(self, value, route, step):
        pairs = [(d, d ^ (2 << route.orders[d % 2][step])) for d in range(self.n)]
        return lax.ppermute(value, BOTH, pairs)

    def send_items(self, value, note=None):
        parts = []
        for k in range(self.ny):
            part = value[(self.y + k) % self.ny]
            if note is not None:
                part = jnp.concatenate([part, note], 0)
            parts.append(self.shift_y(part, k) if k else part)
        return parts

    def join_items(self, parts, length):
        notes = [p[length:] for p in parts] if parts[0].shape[0] > length else []
        return jnp.concatenate([p[:length] for p in parts] + notes, 0)

    def return_items(self, value):
        return [self.shift_y(value[k], -k) if k else value[0] for k in range(self.ny)]

    def order_items(self, parts):
        stacked = jnp.stack(parts)
        return jnp.stack([stacked[(i - self.y) % self.ny] for i in range(self.ny)])

    def start(self, keep, send, route, step=0):
        return keep, self.halve(send, route, step), route, step

    def advance(self, state):
        keep, got, route, step = state
        keep, got, _ = lax.optimization_barrier((keep, got, self.token))
        if keep.shape[0] == 1:
            self.token = keep[0].astype(F32) + got[0].astype(F32)
            return self.token
        if keep.size > 1 << 20:
            keep, send = add_halves(keep, got)
        else:
            total = (keep.astype(F32) + got.astype(F32)).astype(BF)
            keep, send = jnp.split(total, 2)
        keep, send = lax.optimization_barrier((keep, send))
        self.token = send
        return self.start(keep, send, route, step + 1)

    def then(self, *values):
        return lax.optimization_barrier(values + (self.token,))[:-1]


def per_device(
    n_img,
    n_txt,
    image_tokens,
    text_states,
    text_segments,
    item_segments,
    norm1_gain,
    norm1_bias,
    w_qkv,
    w_self_out,
    norm2_gain,
    norm2_bias,
    w_cross_q,
    w_cross_kv,
    w_cross_out,
    norm3_gain,
    norm3_bias,
    w_up,
    w_down,
    cotangent,
):
    plan = Plan(n_img, n_txt)
    core, n, chips, ny = plan.core, plan.n, plan.chips, plan.ny
    items, length, _ = image_tokens.shape
    tokens = items * length
    half_d = D // 2
    rows = D // n

    states = text_states.shape[1]
    ids = jnp.pad(text_segments.astype(BF), ((0, 15), (0, D - states)))
    note = jnp.concatenate([text_states[0], ids], 0)
    x_parts = plan.send_items(image_tokens, note)
    g_parts = plan.send_items(behind(cotangent, x_parts[-1]))
    x_own = plan.join_items(x_parts, length)
    x_other = plan.swap(x_own)

    notes = [v[tokens:].reshape(ny, states + 16, D) for v in (x_own, x_other)]
    notes = jnp.concatenate(notes, 0)
    ids = notes[:, states, :states].reshape(-1)
    states_all = notes[:, :states].reshape(-1, D)
    text_kv = nn(states_all, w_cross_kv).astype(BF)
    matches = ids == item_segments[0, plan.y].astype(BF)
    seen = jnp.where(matches, 0.0, MASKED).astype(F32)[:, None]

    joined, normed1 = project_all(
        x_own, x_other, norm1_gain, norm1_bias, w_qkv, core, plan.places, length
    )
    mixed, lse = attend(joined, plan.rows)
    mixed_got = plan.swap(mixed[tokens:])
    g_own = plan.join_items([behind(p, mixed) for p in g_parts], length)
    g_other = plan.swap(g_own)

    norms = (norm2_gain, norm2_bias, norm3_gain, norm3_bias)
    hidden1, hidden2, normed3, cross_q, cross_mixed, cross_lse = cross_part(
        x_own,
        mixed,
        mixed_got,
        text_kv,
        seen,
        norms,
        w_self_out,
        w_cross_q,
        w_cross_out,
        core,
    )

    normed3_other = plan.swap(normed3)
    per_down = w_down.shape[0] // n
    out, grad3, sent, low_keep, high_keep, low_send, high_send = mlp(
        normed3,
        normed3_other,
        g_own,
        g_other,
        w_up,
        w_down,
        core,
        plan.mixed.blocks,
        plan.mixed.goes_to,
    )
    high_got = plan.halve(high_send, plan.mixed, 0)
    got = plan.swap(sent)

    block_out, grad_hidden1, grad_own, grad_other, grad_kv, norm_sums, keep, send = cross_back(
        out, got, grad3, hidden2, g_own, norms[:3], seen, cross_lse, cross_mixed, w_cross_out,
        text_kv, cross_q, states_all, w_cross_q, hidden1, mixed, mixed_got, w_self_out,
        core, plan.near.devices,
    )
    grad_other, high_got = lax.optimization_barrier((grad_other, high_got))
    grad_got = plan.swap(grad_other)
    swapped = plan.swap(behind(send, grad_got))
    plan.token = grad_other
    high_keep, high_got = plan.then(high_keep, high_got)
    low_got = plan.halve(behind(low_send, high_got), plan.mixed, 0)
    high_sum = (high_keep.astype(F32) + high_got.astype(F32)).astype(BF)
    plan.token = high_sum
    next_got = plan.halve(high_sum, plan.mixed, 1)

    grad_got, grad_own = plan.then(grad_got, grad_own)
    dq, dk, dv = attend_back(joined, grad_own, grad_got, mixed, lse, plan.rows)
    plan.token = dv
    middle_sums = plan.advance(
        (keep.reshape(chips, rows, -1), swapped.reshape(chips, rows, -1), plan.near, -1)
    )
    dq, dk, dv = plan.then(dq, dk, dv)
    part_own, part_other = project_back(dq, dk, dv, w_qkv, core, plan.places)
    plan.token = part_other
    part_got = plan.swap(part_other)
    low_keep, low_got, next_got = plan.then(low_keep, low_got, next_got)
    low_sum = low_keep.astype(F32) + low_got.astype(F32) + next_got.astype(F32)
    plan.token = low_sum = lax.optimization_barrier(low_sum.astype(BF))
    low_keep, low_send = jnp.split(low_sum, 2)
    mlp_sums = plan.start(low_keep, low_send, plan.mixed, 2)
    part_got, part_own = plan.then(part_got, part_own)
    image_grad, keep, send = last_part(
        x_own, part_own, part_got, grad_hidden1, norm1_gain, norm_sums, normed1, dq, dk, dv,
        plan.near.blocks,
    )
    plan.token = send
    last_sums = plan.start(
        keep.reshape(chips // 2, 2 * rows, -1), send.reshape(chips // 2, 2 * rows, -1), plan.near
    )
    (grad_kv,) = plan.then(grad_kv)
    text_part = nt(grad_kv, w_cross_kv).astype(BF)
    plan.token = text_part
    text_part = text_part.reshape(2, ny, states, D)
    text_got = plan.swap(text_part[1])
    middle_sums = plan.advance(middle_sums)
    mlp_sums = plan.advance(mlp_sums)
    last_sums = plan.advance(last_sums)
    middle_sums = plan.advance(middle_sums)
    for _ in range(plan.levels - 3):
        mlp_sums = plan.advance(mlp_sums)
    text_part, text_got = plan.then(text_part, text_got)
    text_part = text_part[0].astype(F32) + text_got.astype(F32)
    plan.token = text_part
    last_sums = plan.advance(last_sums)
    image_grad, block_out, text_part = plan.then(image_grad, block_out, text_part)
    text_parts = [plan.shift_y(text_part[r].astype(BF), -r) for r in range(1, ny)]
    image_parts = plan.return_items(image_grad.reshape(ny, length, D))
    block_parts = plan.return_items(block_out.reshape(ny, length, D))
    for _ in range(plan.levels - 2):
        middle_sums = plan.advance(middle_sums)
        last_sums = plan.advance(last_sums)
    up_down = mlp_sums

    units = w_up.shape[1] // 2
    down_grad = jnp.concatenate([up_down[:, units : units + D], up_down[:, units + D :]], 0)
    parts = jnp.concatenate([up_down[:, :units], last_sums], 1).reshape(2, rows, -1)
    mine = parts[core]
    sent = parts[1 - core].astype(BF)
    plan.token = sent
    text_part, *text_parts = plan.then(text_part, *text_parts)
    text_grad = sum((p.astype(F32) for p in text_parts), text_part[0])
    image_grad = plan.order_items(plan.then(*image_parts)).astype(F32)
    plan.token = image_grad
    block_out = plan.order_items(plan.then(*block_parts))
    theirs = plan.swap(sent).astype(F32)
    by_core = jnp.where(core == 0, jnp.stack([mine, theirs]), jnp.stack([theirs, mine]))
    up_grad = by_core[:, :, :units].reshape(2, rows, chips, per_down)
    up_grad = up_grad.transpose(1, 2, 0, 3).reshape(rows, 2 * units)
    wide = by_core[:, :, units : units + 3 * half_d].reshape(2, rows, 3, half_d)
    wide = wide.transpose(1, 2, 0, 3).reshape(rows, 3 * D)
    norm_sums = mine[:, -128:-122] + theirs[:, -128:-122]
    return (
        block_out,
        image_grad,
        text_grad[None],
        norm_sums[:, 0],
        norm_sums[:, 1],
        wide,
        middle_sums[:, 2 * D : 3 * D],
        norm_sums[:, 2],
        norm_sums[:, 3],
        middle_sums[:, D : 2 * D],
        middle_sums[:, 3 * D :],
        middle_sums[:, :D],
        norm_sums[:, 4],
        norm_sums[:, 5],
        up_grad,
        down_grad,
    )


def solution(mesh):
    split = P("img", "txt", None)
    rows = P(BOTH)
    wide = P(BOTH, None)
    return jax.shard_map(
        partial(per_device, mesh.shape["img"], mesh.shape["txt"]),
        mesh=mesh,
        in_specs=(split, split, P("img", "txt"), P("img", None)) + (P(),) * 13 + (split,),
        out_specs=(
            (split,) * 3
            + (rows, rows, wide, wide)
            + (rows, rows, wide, wide, wide)
            + (rows, rows, wide, wide)
        ),
        check_vma=False,
    )
```

```python
from functools import partial

import jax
import jax.numpy as jnp
import numpy as np
from jax import lax
from jax.experimental import pallas as pl
from jax.experimental.pallas import tpu as pltpu
from jax.sharding import PartitionSpec as P

D = 1024
HEADS = 16
HEAD = 64
EPS = 1e-05
MASKED = -1e30
SCALE = HEAD**-0.5
LOG2E = 1.4426950408889634
BOTH = ("img", "txt")
BF = jnp.bfloat16
F32 = jnp.float32
QUERY_BLOCK = 256
MIB = 1 << 20
SMALL = pl.CostEstimate(flops=1 << 20, bytes_accessed=1 << 16, transcendentals=0)


def nn(a, b):
    return lax.dot_general(a, b, (((1,), (0,)), ((), ())), preferred_element_type=F32)


def nt(a, b):
    return lax.dot_general(a, b, (((1,), (1,)), ((), ())), preferred_element_type=F32)


def tn(a, b):
    return lax.dot_general(a, b, (((0,), (0,)), ((), ())), preferred_element_type=F32)


def norm_parts(values):
    center = values - jnp.mean(values, axis=-1, keepdims=True)
    rstd = lax.rsqrt(jnp.mean(center * center, axis=-1, keepdims=True) + EPS)
    return center * rstd, rstd


def norm_back(unit, rstd, gain, grad):
    scaled = grad * gain
    return rstd * (
        scaled
        - jnp.mean(scaled, axis=-1, keepdims=True)
        - unit * jnp.mean(scaled * unit, axis=-1, keepdims=True)
    )


TAIL = [
    0.5 * c
    for c in (
        -0.22753805372107494,
        0.8866680711331851,
        -0.6354061073102151,
        0.6495639241196378,
        0.09138668583849363,
        0.235325478247137,
    )
]


def gelu_parts(value):
    t = 1.0 / (1.0 + (0.39 * 0.5**0.5) * jnp.abs(value))
    bell = jnp.exp2(value * value * (-0.5 * LOG2E))
    tail = jnp.full_like(t, TAIL[0])
    for term in TAIL[1:]:
        tail = tail * t + term
    tail = tail * t * bell
    cdf = jnp.where(value > 0.0, 1.0 - tail, tail)
    return value * cdf, cdf + value * bell * (0.5 / np.pi) ** 0.5


def project_kernel(
    core_ref, place_ref, own_ref, other_ref, gain_ref, bias_ref, wq_ref, wk_ref, wv_ref, *refs
):
    joined_ref, normed_ref, held_ref = refs
    block, own_blocks = pl.program_id(0), (pl.num_programs(0) - 1) // 2
    slot = block % 2
    width = wq_ref.shape[1]
    before = held_ref[1 - slot]
    normed_ref[...] = before
    for s, w_ref in enumerate((wq_ref, wk_ref, wv_ref)):
        joined_ref[:, s * width : (s + 1) * width] = nn(before, w_ref[...]).astype(BF)
    tokens = jnp.where(block < own_blocks, own_ref[...], other_ref[...]).astype(F32)
    unit, _ = norm_parts(tokens)
    held_ref[slot] = (unit * gain_ref[...] + bias_ref[...]).astype(BF)


def project_all(own, other, gain, bias, w_qkv, core, places, length):
    blocks = places.shape[0]
    half = blocks // 2
    width = D // 2
    row = pl.BlockSpec((1, D), lambda b, *_: (0, 0))
    weights = [pl.BlockSpec((D, width), lambda b, c, p, s=s: (0, 2 * s + c[0])) for s in range(3)]
    return pl.pallas_call(
        project_kernel,
        grid_spec=pltpu.PrefetchScalarGridSpec(
            num_scalar_prefetch=2,
            grid=(blocks + 1,),
            in_specs=[
                pl.BlockSpec((length, D), lambda b, *_: (jnp.minimum(b, half - 1), 0)),
                pl.BlockSpec((length, D), lambda b, *_: (jnp.clip(b - half, 0, half - 1), 0)),
                row,
                row,
            ]
            + weights,
            out_specs=[
                pl.BlockSpec((length, 3 * width), lambda b, c, p: (p[jnp.maximum(b - 1, 0)], 0)),
                pl.BlockSpec((length, D), lambda b, c, p: (p[jnp.maximum(b - 1, 0)], 0)),
            ],
            scratch_shapes=[pltpu.VMEM((2, length, D), BF)],
        ),
        out_shape=[
            jax.ShapeDtypeStruct((blocks * length, 3 * width), BF),
            jax.ShapeDtypeStruct((blocks * length, D), BF),
        ],
        compiler_params=pltpu.CompilerParams(vmem_limit_bytes=60 * MIB),
        cost_estimate=SMALL,
        name="norm_and_project",
    )(
        core.reshape(1),
        places,
        own,
        other,
        gain.reshape(1, D),
        bias.reshape(1, D),
        w_qkv,
        w_qkv,
        w_qkv,
    )


def middle_kernel(
    core_ref,
    x_ref,
    own_ref,
    got_ref,
    keys_ref,
    values_ref,
    seen_ref,
    gain2_ref,
    bias2_ref,
    gain3_ref,
    bias3_ref,
    w_own_ref,
    w_got_ref,
    w_query_ref,
    w_out_ref,
    hidden1_ref,
    hidden2_ref,
    normed3_ref,
    queries_ref,
    mixed_ref,
    lse_ref,
):
    hidden = x_ref[...].astype(F32) + nn(own_ref[...], w_own_ref[...])
    hidden += nn(got_ref[...], w_got_ref[...])
    hidden1_ref[...] = hidden
    unit, _ = norm_parts(hidden)
    normed2 = (unit * gain2_ref[...] + bias2_ref[...]).astype(BF)
    queries = nn(normed2, w_query_ref[...]).astype(BF)
    queries_ref[...] = queries
    rows, states = queries.shape[0], keys_ref.shape[0]
    half = lax.broadcasted_iota(jnp.int32, (rows, 2 * HEAD), 1) >= HEAD
    v_flip = values_ref[...].T
    ones = jnp.ones((16, states), BF)
    zero = jnp.zeros((rows, 2 * HEAD), BF)

    def score(head):
        at, h = head // 2 * 2 * HEAD, head % 2
        own = jnp.where(half == (h == 1), queries[:, at : at + 2 * HEAD], zero)
        return nt(keys_ref[:, at : at + 2 * HEAD], own)

    def soften(scores):
        scores = scores * (SCALE * LOG2E) + seen_ref[...]
        top = jnp.max(scores, axis=0, keepdims=True)
        return jnp.exp2(scores - top).astype(BF), top

    outs, lses, scores, raised = [], [], {}, {}
    for n in range(HEADS + 2):
        if n < HEADS:
            scores[n] = score(n)
        if 0 <= n - 1 < HEADS:
            raised[n - 1] = soften(scores.pop(n - 1))
        if n >= 2:
            weights, top = raised.pop(n - 2)
            v_rows = jnp.concatenate([v_flip[(n - 2) * HEAD : (n - 1) * HEAD], ones], 0)
            mixed = nn(v_rows, weights)
            total = mixed[HEAD : HEAD + 1]
            lses.append(top + jnp.log2(total))
            outs.append((mixed[:HEAD] / total).astype(BF))
    lse_ref[...] = jnp.concatenate(lses, 0)
    mixed = jnp.concatenate(outs, 0).T
    mixed_ref[...] = mixed
    hidden += nn(mixed, w_out_ref[...])
    hidden2_ref[...] = hidden
    unit, _ = norm_parts(hidden)
    normed3_ref[...] = (unit * gain3_ref[...] + bias3_ref[...]).astype(BF)


def cross_part(x, own, got, text_kv, seen, norms, w_self_out, w_query, w_out, core):
    tokens, width = got.shape
    states = text_kv.shape[0]
    block = min(256, tokens)
    row = pl.BlockSpec((1, D), lambda b, c: (0, 0))
    wide = pl.BlockSpec((block, D), lambda b, c: (b, 0))
    narrow = pl.BlockSpec((block, width), lambda b, c: (b, 0))
    square = pl.BlockSpec((D, D), lambda b, c: (0, 0))
    return pl.pallas_call(
        middle_kernel,
        grid_spec=pltpu.PrefetchScalarGridSpec(
            num_scalar_prefetch=1,
            grid=(tokens // block,),
            in_specs=[
                wide,
                narrow,
                narrow,
                pl.BlockSpec((states, D), lambda b, c: (0, 0)),
                pl.BlockSpec((states, D), lambda b, c: (0, 1)),
                pl.BlockSpec((states, 1), lambda b, c: (0, 0)),
                row,
                row,
                row,
                row,
                pl.BlockSpec((width, D), lambda b, c: (c[0], 0)),
                pl.BlockSpec((width, D), lambda b, c: (1 - c[0], 0)),
                square,
                square,
            ],
            out_specs=[wide] * 5 + [pl.BlockSpec((HEADS, block), lambda b, c: (0, b))],
        ),
        out_shape=[
            jax.ShapeDtypeStruct((tokens, D), F32),
            jax.ShapeDtypeStruct((tokens, D), F32),
            jax.ShapeDtypeStruct((tokens, D), BF),
            jax.ShapeDtypeStruct((tokens, D), BF),
            jax.ShapeDtypeStruct((tokens, D), BF),
            jax.ShapeDtypeStruct((HEADS, tokens), F32),
        ],
        compiler_params=pltpu.CompilerParams(vmem_limit_bytes=60 * MIB),
        cost_estimate=SMALL,
        name="cross_attention_part",
    )(
        core.reshape(1),
        x,
        own,
        got,
        text_kv,
        text_kv,
        seen,
        *[v.reshape(1, D) for v in norms],
        w_self_out,
        w_self_out,
        w_query,
        w_out,
    )


def attend_kernel(row_ref, q_ref, k_ref, v_ref, out_ref, lse_ref):
    length = q_ref.shape[0]
    block = QUERY_BLOCK
    scale = SCALE * LOG2E
    half = lax.broadcasted_iota(jnp.int32, (block, 2 * HEAD), 1) >= HEAD
    key_row = lax.broadcasted_iota(jnp.int32, (block, block), 0)
    query_col = lax.broadcasted_iota(jnp.int32, (block, block), 1)
    seen = key_row <= query_col
    v_flip = v_ref[...].T
    ones = jnp.ones((16, length), BF)
    v_rows = [jnp.concatenate([v_flip[h * HEAD : (h + 1) * HEAD], ones], 0) for h in range(2)]

    def score(i, h):
        lo, hi = i * block, (i + 1) * block
        queries = q_ref[lo:hi, :]
        own = jnp.where(half == (h == 1), queries, jnp.zeros_like(queries))
        return nt(k_ref[lo:hi, :], own), nt(k_ref[:lo, :], own) if i else None

    def soften(i, h, diag, rest):
        diag = jnp.where(seen, diag, MASKED)
        top = jnp.max(diag, axis=0, keepdims=True)
        if i:
            top = jnp.maximum(top, jnp.max(rest, axis=0, keepdims=True))
            rest = jnp.exp2(rest * scale - top * scale).astype(BF)
        return jnp.exp2(diag * scale - top * scale).astype(BF), rest, top * scale

    def mix(i, h, diag, rest, base):
        lo, hi = i * block, (i + 1) * block
        mixed = nn(v_rows[h][:, lo:hi], diag)
        if i:
            mixed += nn(v_rows[h][:, :lo], rest)
        total = mixed[HEAD : HEAD + 1]
        lse_ref[0, h : h + 1, lo:hi] = base + jnp.log2(total)
        return mixed[:HEAD] / total

    tasks = [(i, h) for i in range(length // block) for h in range(2)]
    scores, raised, outs = {}, {}, []
    part = length // row_ref.shape[0]
    for n in range(len(tasks) + 2):
        if n < len(tasks):
            scores[n] = score(*tasks[n])
        if 0 <= n - 1 < len(tasks):
            raised[n - 1] = soften(*tasks[n - 1], *scores.pop(n - 1))
        if n >= 2:
            outs.append(mix(*tasks[n - 2], *raised.pop(n - 2)))
        if len(outs) == 2:
            lo = tasks[n - 2][0] * block
            result = jnp.concatenate(outs, 0).T.astype(BF)
            outs = []
            for at in range(0, block, part):
                row = pl.multiple_of(row_ref[(lo + at) // part] * part, part)
                out_ref[pl.ds(row, part), :] = result[at : at + part]


def head_specs(length, pairs):
    return [
        pl.BlockSpec((length, 2 * HEAD), lambda p, *_, s=s: (0, s * pairs + p)) for s in range(3)
    ]


def attend(joined, rows):
    length, width = joined.shape[0], joined.shape[1] // 3
    pairs = width // (2 * HEAD)
    return pl.pallas_call(
        attend_kernel,
        grid_spec=pltpu.PrefetchScalarGridSpec(
            num_scalar_prefetch=1,
            grid=(pairs,),
            in_specs=head_specs(length, pairs),
            out_specs=[pl.BlockSpec((length, 2 * HEAD), lambda p, *_: (0, p)), pl.BlockSpec((1, 2, length), lambda p, *_: (p, 0, 0))],
        ),
        out_shape=[
            jax.ShapeDtypeStruct((length, width), BF),
            jax.ShapeDtypeStruct((pairs, 2, length), F32),
        ],
        compiler_params=pltpu.CompilerParams(vmem_limit_bytes=60 * MIB),
        cost_estimate=SMALL,
        name="self_attention",
    )(rows, joined, joined, joined)


def attend_back_kernel(
    row_ref,
    block_ref,
    q_ref,
    k_ref,
    v_ref,
    own_g_ref,
    other_g_ref,
    mixed_ref,
    lse_ref,
    normed_hbm,
    wq_ref,
    wk_ref,
    wv_ref,
    keep_ref,
    send_ref,
    own_ref,
    other_ref,
    dq_sum,
    g_ref,
    o_ref,
    normed,
    flip_ref,
    ordered_ref,
    sum_ref,
    sem,
):
    pair, pairs = pl.program_id(0), pl.num_programs(0)
    load = pltpu.make_async_copy(normed_hbm, normed, sem)

    @pl.when(pair == 0)
    def _():
        load.start()

    length = q_ref.shape[0]
    places = row_ref.shape[0]
    part = length // places
    for place in range(places):
        row = row_ref[place]
        at = pl.ds(pl.multiple_of(row % (places // 2) * part, part), part)
        to = slice(place * part, (place + 1) * part)
        mine = row < places // 2
        g_ref[to, :] = jnp.where(mine, own_g_ref[at, :], other_g_ref[at, :])
        o_ref[to, :] = mixed_ref[pl.ds(pl.multiple_of(row * part, part), part), :]
    block = QUERY_BLOCK
    scale = SCALE * LOG2E
    half = lax.broadcasted_iota(jnp.int32, (length, 2 * HEAD), 1) >= HEAD
    key_row = lax.broadcasted_iota(jnp.int32, (block, block), 0)
    query_col = lax.broadcasted_iota(jnp.int32, (block, block), 1)
    seen = key_row <= query_col
    k_flip = k_ref[...].T
    zero = jnp.zeros((length, 2 * HEAD), BF)
    queries = [jnp.where(half == (h == 1), q_ref[...], zero) for h in range(2)]
    grads = [jnp.where(half == (h == 1), g_ref[...], zero) for h in range(2)]
    product = (g_ref[...].astype(F32) * o_ref[...].astype(F32)).T
    deltas = [jnp.sum(product[h * HEAD : (h + 1) * HEAD], axis=0, keepdims=True) for h in range(2)]

    def score(j, h):
        lo, hi = j * block, (j + 1) * block
        return nt(k_ref[lo:hi, :], queries[h][lo:]), nt(v_ref[lo:hi, :], grads[h][lo:])

    def soften(j, h, scores, score_grad):
        lo, hi = j * block, (j + 1) * block
        weights = jnp.exp2(scores * scale - lse_ref[0, h : h + 1, lo:])
        first = jnp.where(seen, weights[:, :block], 0.0)
        weights = jnp.concatenate([first, weights[:, block:]], 1) if hi < length else first
        score_grad = (weights * (score_grad - deltas[h][:, lo:])).astype(BF)
        return weights.astype(BF), score_grad

    def mix(j, h, weights, score_grad):
        lo, hi = j * block, (j + 1) * block
        rows = slice(h * HEAD, (h + 1) * HEAD)
        query_part = nn(k_flip[rows, lo:hi], score_grad)
        if j == 0:
            dq_sum[rows, :] = query_part
        else:
            dq_sum[rows, lo:] += query_part
        return nn(score_grad, queries[h][lo:]), nn(weights, grads[h][lo:])

    tasks = [(j, h) for j in range(length // block) for h in range(2)]
    scores, raised, outs, key_grads, value_grads = {}, {}, [], [], []
    for n in range(len(tasks) + 2):
        if n < len(tasks):
            scores[n] = score(*tasks[n])
        if 0 <= n - 1 < len(tasks):
            raised[n - 1] = soften(*tasks[n - 1], *scores.pop(n - 1))
        if n >= 2:
            outs.append(mix(*tasks[n - 2], *raised.pop(n - 2)))
        if len(outs) == 2:
            key_grads.append(((outs[0][0] + outs[1][0]) * SCALE).astype(BF))
            value_grads.append((outs[0][1] + outs[1][1]).astype(BF))
            outs = []
    query_grad = (dq_sum[...].T * SCALE).astype(BF)
    joined = jnp.concatenate(
        [query_grad, jnp.concatenate(key_grads, 0), jnp.concatenate(value_grads, 0)], 1
    )
    weights = jnp.concatenate([wq_ref[...], wk_ref[...], wv_ref[...]], 1)
    grad = nt(joined, weights)

    @pl.when(pair == 0)
    def _():
        sum_ref[...] = grad
        load.wait()
        flip_ref[...] = normed[...].T
        height = D // block_ref.shape[0]
        for i in range(block_ref.shape[0]):
            at = pl.ds(pl.multiple_of(block_ref[i] * height, height), height)
            ordered_ref[i * height : (i + 1) * height, :] = flip_ref[at, :]

    @pl.when(pair > 0)
    def _():
        sum_ref[...] += grad

    wide = nn(ordered_ref[...], joined).astype(BF)
    keep_ref[...] = wide[: D // 2]
    send_ref[...] = wide[D // 2 :]

    @pl.when(pair == pairs - 1)
    def _():
        for place in range(places):
            row = row_ref[place]
            at = pl.ds(pl.multiple_of(row % (places // 2) * part, part), part)
            rows = sum_ref[place * part : (place + 1) * part, :]

            @pl.when(row < places // 2)
            def _(at=at, rows=rows):
                own_ref[at, :] = rows

            @pl.when(row >= places // 2)
            def _(at=at, rows=rows):
                other_ref[at, :] = rows.astype(BF)


def attend_back(joined, own_g, other_g, mixed, lse, normed, w_qkv, core, rows, blocks):
    length, width = joined.shape[0], joined.shape[1] // 3
    pairs = width // (2 * HEAD)
    spec = pl.BlockSpec((length, 2 * HEAD), lambda p, *_: (0, p))
    half = pl.BlockSpec((length // 2, 2 * HEAD), lambda p, *_: (0, p))
    weights = [
        pl.BlockSpec((D, 2 * HEAD), lambda p, r, b, s=s: (0, (2 * s + r[r.shape[0] - 1]) * pairs + p))
        for s in range(3)
    ]
    sums = pl.BlockSpec((D // 2, 6 * HEAD), lambda p, *_: (0, p))
    out = pl.BlockSpec((length // 2, D), lambda p, *_: (0, 0))
    places = rows.shape[0]

    def body(row_ref, *refs):
        attend_back_kernel(Rows(row_ref, places), *refs)

    return pl.pallas_call(
        body,
        grid_spec=pltpu.PrefetchScalarGridSpec(
            num_scalar_prefetch=2,
            grid=(pairs,),
            in_specs=head_specs(length, pairs)
            + [half] * 2
            + [spec]
            + [pl.BlockSpec((1, 2, length), lambda p, *_: (p, 0, 0))]
            + [pl.BlockSpec(memory_space=pl.ANY)]
            + weights,
            out_specs=[sums, sums, out, out],
            scratch_shapes=[
                pltpu.VMEM((2 * HEAD, length), F32),
                pltpu.VMEM((length, 2 * HEAD), BF),
                pltpu.VMEM((length, 2 * HEAD), BF),
                pltpu.VMEM((length, D), BF),
                pltpu.VMEM((D, length), BF),
                pltpu.VMEM((D, length), BF),
                pltpu.VMEM((length, D), F32),
                pltpu.SemaphoreType.DMA,
            ],
        ),
        out_shape=[jax.ShapeDtypeStruct((D // 2, 3 * width), BF)] * 2
        + [
            jax.ShapeDtypeStruct((length // 2, D), F32),
            jax.ShapeDtypeStruct((length // 2, D), BF),
        ],
        compiler_params=pltpu.CompilerParams(vmem_limit_bytes=60 * MIB),
        cost_estimate=SMALL,
        name="self_attention_back",
    )(
        jnp.concatenate([rows, core.reshape(1)]), blocks, joined, joined, joined, own_g, other_g,
        mixed, lse, normed, w_qkv, w_qkv, w_qkv,
    )


class Rows:
    def __init__(self, ref, count):
        self.ref, self.shape = ref, (count,)

    def __getitem__(self, place):
        return self.ref[place]


def mlp_kernel(
    pieces,
    steps,
    core_ref,
    rows_from,
    goes_to,
    own_ref,
    other_ref,
    own_g_ref,
    other_g_ref,
    *refs,
):
    ups, downs = refs[:pieces], refs[pieces : 2 * pieces]
    down_ref, up_ref, out_ref, norm_ref, sent_ref, *targets = refs[2 * pieces : 2 * pieces + 9]
    flip_ref, ordered_ref, wide_ref, tall_ref, active_ref, grad_ref, sems = refs[2 * pieces + 9 :]
    step = pl.program_id(0)
    slot = step % 2
    tokens = own_ref.shape[0]
    quarter, height = targets[0].shape[0], targets[0].shape[1]
    tile = wide_ref.shape[3]
    width = 2 * height
    per_step = tile // width
    units = steps * tile

    @pl.when(step == 0)
    def _():
        flip_ref[:, :tokens] = own_ref[...].T
        flip_ref[:, tokens:] = other_ref[...].T
        for i in range(4 * quarter):
            at = pl.multiple_of(rows_from[i] * height, height)
            ordered_ref[i * height : (i + 1) * height, :] = flip_ref[pl.ds(at, height), :]

    def wide_copy(at, where, side):
        part = wide_ref.at[at, side * quarter : (side + 1) * quarter]
        lanes = pl.ds(pl.multiple_of(where * tile, tile), tile)
        return pltpu.make_async_copy(part, targets[side].at[:, :, lanes], sems.at[at, side])

    def tall_copy(at, j, r, target, i):
        rows = slice(j * width + r * height, j * width + (r + 1) * height)
        lanes = slice(units + r * D, units + (r + 1) * D)
        return pltpu.make_async_copy(
            tall_ref.at[at, rows], target.at[i, :, lanes], sems.at[at, 4 + 2 * j + r]
        )

    def wait(at):
        for side in range(4):
            wide_copy(at, 0, side).wait()
        for j in range(per_step):
            for r in range(2):
                tall_copy(at, j, r, targets[0], 0).wait()

    @pl.when((step >= 2) & (step < steps + 2))
    def _():
        wait(slot)

    @pl.when(step < steps)
    def _():
        up_w = jnp.concatenate([r[...] for r in ups], 1) if pieces > 1 else ups[0][...]
        down_w = jnp.concatenate([r[...] for r in downs], 0) if pieces > 1 else downs[0][...]
        sides = ((0, own_ref, own_g_ref), (tokens, other_ref, other_g_ref))
        cut = 256
        tasks = [(u, side) for u in range(0, tile, cut) for side in sides]
        found, active, grads = {}, {}, {}

        def products(u, side):
            _, x_ref, g_ref = side
            return nn(x_ref[...], up_w[:, u : u + cut]), nt(g_ref[...], down_w[u : u + cut])

        def units_of(n):
            u, (base, _, _) = tasks[n]
            up_value, down_grad = found.pop(n)
            value, slope = gelu_parts(up_value)
            value = value.astype(BF)
            grad = (down_grad * slope).astype(BF)
            active_ref[step, base : base + tokens, u : u + cut] = value
            grad_ref[step, base : base + tokens, u : u + cut] = grad
            active[n], grads[n] = value, grad

        def weights_of(n):
            u = tasks[n][0]
            grad = jnp.concatenate([grads.pop(n - 1), grads.pop(n)], 0)
            wide = nn(ordered_ref[...], grad).astype(BF)
            wide_ref[slot, :, :, u : u + cut] = wide.reshape(wide_ref.shape[1:3] + (cut,))
            tall = nn(active.pop(n - 1).T, own_g_ref[...]) + nn(active.pop(n).T, other_g_ref[...])
            tall_ref[slot, u : u + cut] = tall.astype(BF)

        for n in range(len(tasks) + 2):
            if n < len(tasks):
                found[n] = products(*tasks[n])
            if 0 <= n - 1 < len(tasks):
                units_of(n - 1)
            if n >= 3 and n % 2:
                weights_of(n - 2)
        for side in range(4):
            wide_copy(slot, step, side).start()
        for j in range(per_step):
            i = goes_to[step * per_step + j]
            for side, target in enumerate(targets):

                @pl.when(i // quarter == side)
                def _(j=j, i=i, side=side, target=target):
                    for r in range(2):
                        tall_copy(slot, j, r, target, i - side * quarter).start()

    @pl.when(step >= steps)
    def _():
        up = up_ref[...]
        if up.shape[1] > units:
            first = core_ref[0] == 0
            picked = []
            for at in range(0, 2 * units, 2 * width):
                picked.append(
                    jnp.where(first, up[:, at : at + width], up[:, at + width : at + 2 * width])
                )
            up = jnp.concatenate(picked, 1)
        active = jnp.concatenate([active_ref[i] for i in range(steps)], 1)
        out = nn(active, down_ref[...].reshape(units, -1))
        grad = jnp.concatenate([grad_ref[i] for i in range(steps)], 1)
        norm = nt(grad, up)
        out_ref[...] = out[:tokens]
        norm_ref[...] = norm[:tokens]
        sent_ref[0] = out[tokens:].astype(BF)
        sent_ref[1] = norm[tokens:].astype(BF)


def mlp(own, other, own_g, other_g, w_up, w_down, core, rows_from, goes_to):
    tokens = own.shape[0]
    chips = rows_from.shape[0]
    tile, out_tile = 512, 256
    units = w_up.shape[1] // 2
    steps = units // tile
    width = units // chips
    height = D // chips
    fine = width % 128 == 0
    tall = w_down.reshape(chips, 2, width, D)
    if fine:
        pieces, piece = tile // width, width
    else:
        pieces, piece = 1, tile
        w_up = w_up.reshape(D, chips, 2, width)[:, :, core].reshape(D, units)
        w_down = w_down.reshape(chips, 2, width, D)[:, core].reshape(units, D)

    def place(s, c, j):
        s = jnp.minimum(s, steps - 1)
        return 2 * (s * pieces + j) + c[0] if fine else s

    def column(s):
        return jnp.maximum(s - steps, 0)

    whole = pl.BlockSpec((tokens, D), lambda s, *_: (0, 0))
    up_specs = [
        pl.BlockSpec((D, piece), lambda s, c, *_, j=j: (0, place(s, c, j))) for j in range(pieces)
    ]
    down_specs = [
        pl.BlockSpec((piece, D), lambda s, c, *_, j=j: (place(s, c, j), 0)) for j in range(pieces)
    ]
    kept = pl.BlockSpec((tokens, out_tile), lambda s, *_: (0, column(s)))
    sums = jax.ShapeDtypeStruct((chips // 4, height, units + 2 * D), BF)
    return pl.pallas_call(
        partial(mlp_kernel, pieces, steps),
        grid_spec=pltpu.PrefetchScalarGridSpec(
            num_scalar_prefetch=3,
            grid=(steps + D // out_tile,),
            in_specs=[whole] * 4
            + up_specs
            + down_specs
            + [
                pl.BlockSpec((chips, None, width, out_tile), lambda s, c, *_: (0, c[0], 0, column(s))),
                pl.BlockSpec((out_tile, w_up.shape[1]), lambda s, *_: (column(s), 0)),
            ],
            out_specs=[
                kept,
                kept,
                pl.BlockSpec((2, tokens, out_tile), lambda s, *_: (0, 0, column(s))),
            ]
            + [pl.BlockSpec(memory_space=pl.ANY)] * 4,
            scratch_shapes=[
                pltpu.VMEM((D, 2 * tokens), BF),
                pltpu.VMEM((D, 2 * tokens), BF),
                pltpu.VMEM((2, chips, height, tile), BF),
                pltpu.VMEM((2, tile, D), BF),
                pltpu.VMEM((steps, 2 * tokens, tile), BF),
                pltpu.VMEM((steps, 2 * tokens, tile), BF),
                pltpu.SemaphoreType.DMA((2, 4 + 2 * (tile // width))),
            ],
        ),
        out_shape=[
            jax.ShapeDtypeStruct((tokens, D), F32),
            jax.ShapeDtypeStruct((tokens, D), F32),
            jax.ShapeDtypeStruct((2, tokens, D), BF),
            sums,
            sums,
            sums,
            sums,
        ],
        compiler_params=pltpu.CompilerParams(vmem_limit_bytes=60 * MIB),
        cost_estimate=SMALL,
        name="mlp_both_ways",
    )(
        core.reshape(1),
        rows_from,
        goes_to,
        own,
        other,
        own_g,
        other_g,
        *([w_up] * pieces),
        *([w_down] * pieces),
        tall,
        w_up,
    )


def cross_back_kernel(
    scalars,
    order_ref,
    got_ref,
    grad3_ref,
    hidden2_ref,
    g_ref,
    gain3_ref,
    gain2_ref,
    seen_ref,
    lse_ref,
    keys_ref,
    values_ref,
    states_ref,
    mixed_hbm,
    w_out_hbm,
    queries_hbm,
    w_query_hbm,
    hidden1_hbm,
    own_hbm,
    other_hbm,
    w_self_hbm,
    hidden_grad_ref,
    own_grad_ref,
    other_grad_ref,
    text_ref,
    norms_ref,
    keep,
    send,
    mixed_ref,
    w_out_ref,
    queries_ref,
    w_query,
    hidden1,
    own_ref,
    other_ref,
    w_self,
    flip_ref,
    ordered_ref,
    stage_ref,
    sems,
    out_sems,
):
    core = scalars[0]
    tokens = grad3_ref.shape[0]
    loads = [
        pltpu.make_async_copy(a, b, sems.at[i])
        for i, (a, b) in enumerate(
            (
                (mixed_hbm, mixed_ref),
                (w_out_hbm, w_out_ref),
                (queries_hbm, queries_ref),
                (w_query_hbm, w_query),
                (hidden1_hbm, hidden1),
                (own_hbm.at[:tokens], own_ref),
                (other_hbm, other_ref),
                (w_self_hbm, w_self),
            )
        )
    ]
    for load in loads:
        load.start()
    count = order_ref.shape[0]
    rows = D // count
    half = D // 2
    writes = []

    def order(depth):
        for i in range(count):
            at = pl.multiple_of(order_ref[i] * rows, rows)
            ordered_ref[i * rows : (i + 1) * rows, :depth] = flip_ref[pl.ds(at, rows), :depth]

    def multiply(depth, grads, lane):
        product = nn(ordered_ref[:, :depth].astype(BF), grads)
        stage_ref[:, lane : lane + grads.shape[1]] = product.astype(BF)

    def write(slot, lane, width):
        for i, target in enumerate((send, keep)):
            writes.append(
                pltpu.make_async_copy(
                    stage_ref.at[i * half : (i + 1) * half, lane : lane + width],
                    target.at[:, lane : lane + width],
                    out_sems.at[2 * slot + i],
                )
            )
            writes[-1].start()

    def weight_part(depth, grads, slot, lane):
        order(depth)
        multiply(depth, grads, lane)
        write(slot, lane, grads.shape[1])

    kind = flip_ref.dtype
    loads[0].wait()
    flip_ref[:, :tokens] = mixed_ref[...].astype(kind).T
    hidden2 = hidden2_ref[...]
    grad3 = grad3_ref[...] + got_ref[...].astype(F32)
    unit, rstd = norm_parts(hidden2)
    norms_ref[4:5, :] = jnp.sum(grad3 * unit, axis=0, keepdims=True)
    norms_ref[5:6, :] = jnp.sum(grad3, axis=0, keepdims=True)
    norms_ref[6:8, :] = jnp.zeros((2, D), F32)
    grad_hidden = norm_back(unit, rstd, gain3_ref[...], grad3) + g_ref[...].astype(F32)
    hidden_grad_ref[...] = grad_hidden
    branch = grad_hidden.astype(BF)
    order(tokens)
    loads[1].wait()
    grad_mixed = nt(branch, w_out_ref[...]).astype(BF)
    loads[2].wait()
    states = keys_ref.shape[0]
    half_lane = lax.broadcasted_iota(jnp.int32, (tokens, 2 * HEAD), 1) >= HEAD
    zero = jnp.zeros((tokens, 2 * HEAD), BF)
    k_flip = keys_ref[...].T

    def score(head):
        lanes = slice(head // 2 * 2 * HEAD, (head // 2 + 1) * 2 * HEAD)
        mine = half_lane == (head % 2 == 1)
        own_q = jnp.where(mine, queries_ref[:, lanes], zero)
        own_g = jnp.where(mine, grad_mixed[:, lanes], zero)
        return nt(keys_ref[:, lanes], own_q), nt(values_ref[:, lanes], own_g), own_q, own_g

    def soften(head, scores, score_grad, own_q, own_g):
        scores = scores * (SCALE * LOG2E) + seen_ref[...]
        weights = jnp.exp2(scores - lse_ref[head : head + 1, :])
        delta = jnp.sum(weights * score_grad, axis=0, keepdims=True)
        score_grad = (weights * (score_grad - delta)).astype(BF)
        return weights.astype(BF), score_grad, own_q, own_g

    scores, raised, flips, key_grads, value_grads = {}, {}, [], [], []
    quarter = D // 4
    for n in range(HEADS + 2):
        if n < HEADS:
            scores[n] = score(n)
        if 0 <= n - 1 < HEADS:
            raised[n - 1] = soften(n - 1, *scores.pop(n - 1))
        if n % 4 == 1 and n < HEADS:
            lane = n // 4 * quarter
            multiply(tokens, branch[:, lane : lane + quarter], lane)
        if n >= 2:
            head = n - 2
            weights, score_grad, own_q, own_g = raised.pop(head)
            key_part, value_part = nn(score_grad, own_q), nn(weights, own_g)
            if head % 2 == 0:
                key_grads.append(key_part)
                value_grads.append(value_part)
            else:
                key_grads[-1] += key_part
                value_grads[-1] += value_part
            part = nn(k_flip[head * HEAD : (head + 1) * HEAD], score_grad)
            flips.append((part * SCALE).astype(BF))
    write(0, 0, D)
    query_grad = jnp.concatenate(flips, 0).T
    text_grad = jnp.concatenate([p * SCALE for p in key_grads] + value_grads, 1).astype(BF)
    text_ref[...] = text_grad
    flip_ref[:, :states] = states_ref[...].astype(kind).T
    weight_part(states, text_grad, 1, 3 * D)
    for load in loads[3:5]:
        load.wait()
    grad2 = nt(query_grad, w_query[...])
    unit, rstd = norm_parts(hidden1[...])
    normed2 = unit * gain2_ref[0:1, :] + gain2_ref[1:2, :]
    flip_ref[:, :tokens] = normed2.astype(BF).astype(kind).T
    weight_part(tokens, query_grad, 2, D)
    norms_ref[2:3, :] = jnp.sum(grad2 * unit, axis=0, keepdims=True)
    norms_ref[3:4, :] = jnp.sum(grad2, axis=0, keepdims=True)
    norms_ref[0:2, :] = jnp.zeros((2, D), F32)
    grad_hidden = norm_back(unit, rstd, gain2_ref[0:1, :], grad2) + hidden_grad_ref[...]
    hidden_grad_ref[...] = grad_hidden
    branch = grad_hidden.astype(BF)
    for load in loads[5:]:
        load.wait()
    own_rows = pl.ds(pl.multiple_of(core * half, half), half)
    other_rows = pl.ds(pl.multiple_of((1 - core) * half, half), half)
    own_grad_ref[...] = nt(branch, w_self[own_rows, :]).astype(BF)
    other_grad_ref[...] = nt(branch, w_self[other_rows, :]).astype(BF)
    flip_ref[own_rows, :tokens] = own_ref[...].astype(kind).T
    flip_ref[other_rows, :tokens] = other_ref[...].astype(kind).T
    weight_part(tokens, branch, 3, 2 * D)
    for write in writes:
        write.wait()


def cross_back(
    got, grad3, hidden2, g, norms, seen, lse, mixed, w_out, text_kv, queries, states,
    w_query, hidden1, own, other, w_self, core, order,
):
    tokens, width = other.shape
    count = order.shape[0]
    texts = states.shape[0]
    kind = BF if (D // count) % 16 == 0 else F32

    def full(*shape):
        return pl.BlockSpec(shape, lambda b, *_: (0,) * len(shape))

    wide, late = full(tokens, D), pl.BlockSpec(memory_space=pl.ANY)
    sums = jax.ShapeDtypeStruct((D // 2, 5 * D), BF)
    return pl.pallas_call(
        cross_back_kernel,
        grid_spec=pltpu.PrefetchScalarGridSpec(
            num_scalar_prefetch=2,
            grid=(1,),
            in_specs=[
                pl.BlockSpec((None, tokens, D), lambda b, *_: (1, 0, 0)),
                wide,
                wide,
                wide,
                full(1, D),
                full(2, D),
                full(texts, 1),
                full(HEADS, tokens),
                full(texts, D),
                pl.BlockSpec((texts, D), lambda b, *_: (0, 1)),
                full(texts, D),
            ]
            + [late] * 8,
            out_specs=[
                wide,
                full(tokens, width),
                full(tokens, width),
                full(texts, 2 * D),
                full(8, D),
                late,
                late,
            ],
            scratch_shapes=[
                pltpu.VMEM((tokens, D), BF),
                pltpu.VMEM((D, D), BF),
                pltpu.VMEM((tokens, D), BF),
                pltpu.VMEM((D, D), BF),
                pltpu.VMEM((tokens, D), F32),
                pltpu.VMEM((tokens, width), BF),
                pltpu.VMEM((tokens, width), BF),
                pltpu.VMEM((D, D), BF),
                pltpu.VMEM((D, tokens), kind),
                pltpu.VMEM((D, tokens), kind),
                pltpu.VMEM((D, 5 * D), BF),
                pltpu.SemaphoreType.DMA((8,)),
                pltpu.SemaphoreType.DMA((8,)),
            ],
        ),
        out_shape=[
            jax.ShapeDtypeStruct((tokens, D), F32),
            jax.ShapeDtypeStruct((tokens, width), BF),
            jax.ShapeDtypeStruct((tokens, width), BF),
            jax.ShapeDtypeStruct((texts, 2 * D), BF),
            jax.ShapeDtypeStruct((8, D), F32),
            sums,
            sums,
        ],
        compiler_params=pltpu.CompilerParams(vmem_limit_bytes=60 * MIB),
        cost_estimate=SMALL,
        name="cross_attention_back",
    )(
        core.reshape(1), order, got, grad3, hidden2, g, norms[2].reshape(1, D),
        jnp.stack(norms[:2]), seen, lse, text_kv, text_kv, states, mixed, w_out, queries,
        w_query, hidden1, own, other, w_self,
    )


def last_kernel(
    blocks_ref,
    x_ref,
    part_ref,
    got_ref,
    hidden_ref,
    gain_ref,
    norms_ref,
    image_ref,
    keep,
    send,
    norm_flip,
):
    count = blocks_ref.shape[0]
    height, half = D // count, D // 2
    grad = part_ref[...] + got_ref[...].astype(F32)
    unit, rstd = norm_parts(x_ref[...].astype(F32))
    sums = [jnp.sum(grad * unit, axis=0, keepdims=True), jnp.sum(grad, axis=0, keepdims=True)]
    image = norm_back(unit, rstd, gain_ref[...], grad) + hidden_ref[...]
    image_ref[...] = image.astype(BF)
    fill = jnp.zeros((norm_flip.shape[1] - 8, D), F32)
    norm_flip[...] = jnp.concatenate(sums + [norms_ref[2:8, :], fill], 0).T
    for i in range(count):
        at = pl.ds(pl.multiple_of(blocks_ref[i] * height, height), height)
        to = i * height % half
        target = keep if i < count // 2 else send
        target[to : to + height, :] = norm_flip[at, :].astype(BF)


def last_part(x, part, got, hidden_grad, gain, norms, blocks):
    tokens = got.shape[0]

    def full(*shape):
        return pl.BlockSpec(shape, lambda b, *_: (0,) * len(shape))

    wide = full(tokens, D)
    return pl.pallas_call(
        last_kernel,
        grid_spec=pltpu.PrefetchScalarGridSpec(
            num_scalar_prefetch=1,
            grid=(1,),
            in_specs=[wide] * 4 + [full(1, D), full(8, D)],
            out_specs=[wide, full(D // 2, 128), full(D // 2, 128)],
            scratch_shapes=[pltpu.VMEM((D, 128), F32)],
        ),
        out_shape=[jax.ShapeDtypeStruct((tokens, D), BF)]
        + [jax.ShapeDtypeStruct((D // 2, 128), BF)] * 2,
        compiler_params=pltpu.CompilerParams(vmem_limit_bytes=60 * MIB),
        cost_estimate=SMALL,
        name="norm_back",
    )(blocks, x, part, got, hidden_grad, gain.reshape(1, D), norms)


def add_kernel(a_ref, b_ref, keep_ref, send_ref):
    block, half = pl.program_id(0), pl.num_programs(0) // 2
    total = a_ref[...] + b_ref[...]

    @pl.when(block < half)
    def _():
        send_ref[...] = total

    @pl.when(block >= half)
    def _():
        keep_ref[...] = total


def add_halves(a, b):
    count, height, width = a.shape
    blocks = 4
    half = blocks // 2
    shape = (count // blocks, height, width)
    turned = pl.BlockSpec(shape, lambda i: ((i + half) % blocks, 0, 0))
    return pl.pallas_call(
        add_kernel,
        grid=(blocks,),
        in_specs=[turned] * 2,
        out_specs=[
            pl.BlockSpec(shape, lambda i: (jnp.maximum(i - half, 0), 0, 0)),
            pl.BlockSpec(shape, lambda i: (jnp.minimum(i, half - 1), 0, 0)),
        ],
        out_shape=[jax.ShapeDtypeStruct((count // 2, height, width), BF)] * 2,
        compiler_params=pltpu.CompilerParams(vmem_limit_bytes=60 * MIB),
        cost_estimate=SMALL,
        name="add_halves",
    )(a, b)


def behind(value, *others):
    return lax.optimization_barrier((value,) + others)[0]


class Route:
    def __init__(self, plan, orders):
        self.orders = orders
        count = plan.chips
        maps = np.zeros((2, count), np.int32)
        for core in range(2):
            for i in range(count):
                for s, bit in enumerate(orders[core]):
                    maps[core, i] |= ((i >> (plan.levels - 1 - s)) & 1) << bit
        here, there = jnp.asarray(maps)[plan.core], jnp.asarray(maps)[1 - plan.core]
        self.blocks = jnp.bitwise_xor(plan.chip, here).astype(jnp.int32)
        sent = jnp.bitwise_xor(plan.chip, there).astype(jnp.int32)
        self.devices = jnp.concatenate([2 * sent + 1 - plan.core, 2 * self.blocks + plan.core])
        backs = np.argsort(maps, axis=1).astype(np.int32)
        away = jnp.bitwise_xor(plan.chip, jnp.arange(count, dtype=jnp.int32))
        self.goes_to = jnp.take(jnp.asarray(backs)[plan.core], away, mode="clip")


class Plan:
    def __init__(self, n_img, n_txt):
        self.n_txt = n_txt
        self.n = n_img * n_txt
        self.chips = self.n // 2
        self.ny = n_txt // 2
        self.levels = self.chips.bit_length() - 1
        self.me = lax.axis_index("img") * n_txt + lax.axis_index("txt")
        self.core = self.me % 2
        self.chip = self.me // 2
        self.y = lax.axis_index("txt") // 2
        sources = (self.y - jnp.arange(self.ny, dtype=jnp.int32)) % self.ny
        self.places = jnp.concatenate([2 * sources + self.core, 2 * sources + 1 - self.core])
        at = jnp.arange(n_txt, dtype=jnp.int32)
        self.rows = jnp.bitwise_xor(at % 2, self.core) * self.ny + (self.y - at // 2) % self.ny
        rest = list(range(2, self.levels))
        self.near = Route(self, ([1, 0] + rest, [0, 1] + rest))
        self.small = Route(self, ([0] + rest + [1], [0] + rest + [1]))
        self.mixed = Route(self, ([1, 0] + rest, rest + [0, 1]))
        self.token = None

    def swap(self, value):
        return lax.ppermute(value, BOTH, [(d, d ^ 1) for d in range(self.n)])

    def shift_y(self, value, by):
        pairs = []
        for d in range(self.n):
            img, txt = divmod(d, self.n_txt)
            y, core = divmod(txt, 2)
            pairs.append((d, img * self.n_txt + ((y + by) % self.ny) * 2 + core))
        return lax.ppermute(value, BOTH, pairs)

    def halve(self, value, route, step):
        pairs = [(d, d ^ (2 << route.orders[d % 2][step])) for d in range(self.n)]
        return lax.ppermute(value, BOTH, pairs)

    def send_items(self, value, note=None):
        parts = []
        for k in range(self.ny):
            part = value[(self.y + k) % self.ny]
            if note is not None:
                part = jnp.concatenate([part, note], 0)
            parts.append(self.shift_y(part, k) if k else part)
        return parts

    def join_items(self, parts, length):
        notes = [p[length:] for p in parts] if parts[0].shape[0] > length else []
        return jnp.concatenate([p[:length] for p in parts] + notes, 0)

    def return_items(self, value):
        return [self.shift_y(value[k], -k) if k else value[0] for k in range(self.ny)]

    def order_items(self, parts):
        stacked = jnp.stack(parts)
        return jnp.stack([stacked[(i - self.y) % self.ny] for i in range(self.ny)])

    def start(self, keep, send, route, step=0):
        return keep, self.halve(send, route, step), route, step

    def advance(self, state):
        keep, got, route, step = state
        keep, got, _ = lax.optimization_barrier((keep, got, self.token))
        if keep.shape[0] == 1:
            self.token = keep[0].astype(F32) + got[0].astype(F32)
            return self.token
        if keep.size > 1 << 20:
            keep, send = add_halves(keep, got)
        else:
            total = (keep.astype(F32) + got.astype(F32)).astype(BF)
            keep, send = jnp.split(total, 2)
        keep, send = lax.optimization_barrier((keep, send))
        self.token = send
        return self.start(keep, send, route, step + 1)

    def then(self, *values):
        return lax.optimization_barrier(values + (self.token,))[:-1]


def per_device(
    n_img,
    n_txt,
    image_tokens,
    text_states,
    text_segments,
    item_segments,
    norm1_gain,
    norm1_bias,
    w_qkv,
    w_self_out,
    norm2_gain,
    norm2_bias,
    w_cross_q,
    w_cross_kv,
    w_cross_out,
    norm3_gain,
    norm3_bias,
    w_up,
    w_down,
    cotangent,
):
    plan = Plan(n_img, n_txt)
    core, n, chips, ny = plan.core, plan.n, plan.chips, plan.ny
    items, length, _ = image_tokens.shape
    tokens = items * length
    half_d = D // 2
    rows = D // n

    states = text_states.shape[1]
    ids = jnp.pad(text_segments.astype(BF), ((0, 15), (0, D - states)))
    note = jnp.concatenate([text_states[0], ids], 0)
    x_parts = plan.send_items(image_tokens, note)
    g_parts = plan.send_items(behind(cotangent, x_parts[-1]))
    x_own = plan.join_items(x_parts, length)
    x_other = plan.swap(x_own)

    notes = [v[tokens:].reshape(ny, states + 16, D) for v in (x_own, x_other)]
    notes = jnp.concatenate(notes, 0)
    ids = notes[:, states, :states].reshape(-1)
    states_all = notes[:, :states].reshape(-1, D)
    text_kv = nn(states_all, w_cross_kv).astype(BF)
    matches = ids == item_segments[0, plan.y].astype(BF)
    seen = jnp.where(matches, 0.0, MASKED).astype(F32)[:, None]

    joined, normed1 = project_all(
        x_own, x_other, norm1_gain, norm1_bias, w_qkv, core, plan.places, length
    )
    mixed, lse = attend(joined, plan.rows)
    mixed_got = plan.swap(mixed[tokens:])
    g_own = plan.join_items([behind(p, mixed) for p in g_parts], length)
    g_other = plan.swap(g_own)

    norms = (norm2_gain, norm2_bias, norm3_gain, norm3_bias)
    hidden1, hidden2, normed3, cross_q, cross_mixed, cross_lse = cross_part(
        x_own,
        mixed,
        mixed_got,
        text_kv,
        seen,
        norms,
        w_self_out,
        w_cross_q,
        w_cross_out,
        core,
    )

    normed3_other = plan.swap(normed3)
    per_down = w_down.shape[0] // n
    out, grad3, sent, low_keep, high_keep, low_send, high_send = mlp(
        normed3,
        normed3_other,
        g_own,
        g_other,
        w_up,
        w_down,
        core,
        plan.mixed.blocks,
        plan.mixed.goes_to,
    )
    high_got = plan.halve(high_send, plan.mixed, 0)
    got = plan.swap(sent)

    block_out = (hidden2 + out + got[0].astype(F32)).astype(BF)
    block_parts = plan.return_items(block_out.reshape(ny, length, D))

    grad_hidden1, grad_own, grad_other, grad_kv, norm_sums, keep, send = cross_back(
        got, grad3, hidden2, g_own, norms[:3], seen, cross_lse, cross_mixed, w_cross_out,
        text_kv, cross_q, states_all, w_cross_q, hidden1, mixed, mixed_got, w_self_out,
        core, plan.mixed.devices,
    )
    grad_other, high_got, *block_parts = lax.optimization_barrier(
        (grad_other, high_got, *block_parts)
    )
    grad_got = plan.swap(grad_other)
    swapped = plan.swap(behind(send, grad_got))
    plan.token = grad_other
    high_keep, high_got = plan.then(high_keep, high_got)
    low_got = plan.halve(behind(low_send, high_got), plan.mixed, 0)
    high_sum = (high_keep.astype(F32) + high_got.astype(F32)).astype(BF)
    plan.token = high_sum
    next_got = plan.halve(high_sum, plan.mixed, 1)

    grad_got, grad_own = plan.then(grad_got, grad_own)
    last_keep, last_send, part_own, part_other = attend_back(
        joined, grad_own, grad_got, mixed, lse, normed1, w_qkv, core, plan.rows, plan.near.blocks
    )
    plan.token = part_other
    last_sums = plan.start(
        last_keep.reshape(chips // 2, 2 * rows, -1),
        last_send.reshape(chips // 2, 2 * rows, -1),
        plan.near,
    )
    part_got = plan.swap(part_other)
    middle_sums = plan.advance(
        (keep.reshape(chips, rows, -1), swapped.reshape(chips, rows, -1), plan.mixed, -1)
    )
    part_got, part_own = plan.then(part_got, part_own)
    image_grad, norm_keep, norm_send = last_part(
        x_own, part_own, part_got, grad_hidden1, norm1_gain, norm_sums, plan.small.blocks
    )
    plan.token = norm_send
    norm_group = plan.start(
        norm_keep.reshape(chips // 2, 2 * rows, -1),
        norm_send.reshape(chips // 2, 2 * rows, -1),
        plan.small,
    )
    low_keep, low_got, next_got = plan.then(low_keep, low_got, next_got)
    low_sum = low_keep.astype(F32) + low_got.astype(F32) + next_got.astype(F32)
    plan.token = low_sum = lax.optimization_barrier(low_sum.astype(BF))
    low_keep, low_send = jnp.split(low_sum, 2)
    mlp_sums = plan.start(low_keep, low_send, plan.mixed, 2)
    last_sums = plan.advance(last_sums)
    mlp_sums = plan.advance(mlp_sums)
    norm_group = plan.advance(norm_group)
    (grad_kv,) = plan.then(grad_kv)
    text_part = nt(grad_kv, w_cross_kv).astype(BF)
    plan.token = text_part
    text_part = text_part.reshape(2, ny, states, D)
    text_got = plan.swap(text_part[1])
    middle_sums = plan.advance(middle_sums)
    last_sums = plan.advance(last_sums)
    norm_group = plan.advance(norm_group)
    text_part, text_got, image_grad = plan.then(text_part, text_got, image_grad)
    text_part = text_part[0].astype(F32) + text_got.astype(F32)
    plan.token = text_part
    image_parts = plan.return_items(image_grad.reshape(ny, length, D))
    text_parts = [plan.shift_y(text_part[r].astype(BF), -r) for r in range(1, ny)]
    for _ in range(plan.levels - 3):
        mlp_sums = plan.advance(mlp_sums)
    for _ in range(plan.levels - 3):
        last_sums = plan.advance(last_sums)
        norm_group = plan.advance(norm_group)
        middle_sums = plan.advance(middle_sums)
    last_sums = plan.advance(last_sums)
    norm_group = plan.advance(norm_group)
    last_sums = jnp.concatenate([last_sums, norm_group], 1)
    for _ in range(2):
        middle_sums = plan.advance(middle_sums)
    up_down = mlp_sums

    units = w_up.shape[1] // 2
    down_grad = jnp.concatenate([up_down[:, units : units + D], up_down[:, units + D :]], 0)
    parts = jnp.concatenate([up_down[:, :units], last_sums], 1).reshape(2, rows, -1)
    mine = parts[core]
    sent = parts[1 - core].astype(BF)
    plan.token = sent
    text_part, *text_parts = plan.then(text_part, *text_parts)
    text_grad = sum((p.astype(F32) for p in text_parts), text_part[0])
    image_grad = plan.order_items(plan.then(*image_parts)).astype(F32)
    plan.token = image_grad
    block_out = plan.order_items(plan.then(*block_parts))
    theirs = plan.swap(sent).astype(F32)
    by_core = jnp.where(core == 0, jnp.stack([mine, theirs]), jnp.stack([theirs, mine]))
    up_grad = by_core[:, :, :units].reshape(2, rows, chips, per_down)
    up_grad = up_grad.transpose(1, 2, 0, 3).reshape(rows, 2 * units)
    wide = by_core[:, :, units : units + 3 * half_d].reshape(2, rows, -1, 3, 2 * HEAD)
    wide = wide.transpose(1, 3, 0, 2, 4).reshape(rows, 3 * D)
    norm_sums = mine[:, -128:-122] + theirs[:, -128:-122]
    return (
        block_out,
        image_grad,
        text_grad[None],
        norm_sums[:, 0],
        norm_sums[:, 1],
        wide,
        middle_sums[:, 2 * D : 3 * D],
        norm_sums[:, 2],
        norm_sums[:, 3],
        middle_sums[:, D : 2 * D],
        middle_sums[:, 3 * D :],
        middle_sums[:, :D],
        norm_sums[:, 4],
        norm_sums[:, 5],
        up_grad,
        down_grad,
    )


def solution(mesh):
    split = P("img", "txt", None)
    rows = P(BOTH)
    wide = P(BOTH, None)
    return jax.shard_map(
        partial(per_device, mesh.shape["img"], mesh.shape["txt"]),
        mesh=mesh,
        in_specs=(split, split, P("img", "txt"), P("img", None)) + (P(),) * 13 + (split,),
        out_specs=(
            (split,) * 3
            + (rows, rows, wide, wide)
            + (rows, rows, wide, wide, wide)
            + (rows, rows, wide, wide)
        ),
        check_vma=False,
    )
```

```python
from functools import partial

import jax
import jax.numpy as jnp
import numpy as np
from jax import lax
from jax.experimental import pallas as pl
from jax.experimental.pallas import tpu as pltpu
from jax.sharding import PartitionSpec as P

D = 1024
HEADS = 16
HEAD = 64
EPS = 1e-05
MASKED = -1e30
SCALE = HEAD**-0.5
LOG2E = 1.4426950408889634
BOTH = ("img", "txt")
BF = jnp.bfloat16
F32 = jnp.float32
QUERY_BLOCK = 256
MIB = 1 << 20
SMALL = pl.CostEstimate(flops=1 << 20, bytes_accessed=1 << 16, transcendentals=0)
LARGE = pl.CostEstimate(flops=1 << 38, bytes_accessed=1 << 30, transcendentals=0)


def nn(a, b):
    return lax.dot_general(a, b, (((1,), (0,)), ((), ())), preferred_element_type=F32)


def nt(a, b):
    return lax.dot_general(a, b, (((1,), (1,)), ((), ())), preferred_element_type=F32)


def tn(a, b):
    return lax.dot_general(a, b, (((0,), (0,)), ((), ())), preferred_element_type=F32)


def norm_parts(values):
    center = values - jnp.mean(values, axis=-1, keepdims=True)
    rstd = lax.rsqrt(jnp.mean(center * center, axis=-1, keepdims=True) + EPS)
    return center * rstd, rstd


def norm_back(unit, rstd, gain, grad):
    scaled = grad * gain
    return rstd * (
        scaled
        - jnp.mean(scaled, axis=-1, keepdims=True)
        - unit * jnp.mean(scaled * unit, axis=-1, keepdims=True)
    )


TAIL = [
    0.5 * c
    for c in (
        -0.22753805372107494,
        0.8866680711331851,
        -0.6354061073102151,
        0.6495639241196378,
        0.09138668583849363,
        0.235325478247137,
    )
]


def gelu_parts(value):
    t = 1.0 / (1.0 + (0.39 * 0.5**0.5) * jnp.abs(value))
    bell = jnp.exp2(value * value * (-0.5 * LOG2E))
    tail = jnp.full_like(t, TAIL[0])
    for term in TAIL[1:]:
        tail = tail * t + term
    tail = tail * t * bell
    cdf = jnp.where(value > 0.0, 1.0 - tail, tail)
    return value * cdf, cdf + value * bell * (0.5 / np.pi) ** 0.5


def project_kernel(
    core_ref, place_ref, own_ref, other_ref, gain_ref, bias_ref, wq_ref, wk_ref, wv_ref, *refs
):
    joined_ref, normed_ref, held_ref = refs
    block, own_blocks = pl.program_id(0), (pl.num_programs(0) - 1) // 2
    slot = block % 2
    width = wq_ref.shape[1]
    before = held_ref[1 - slot]
    normed_ref[...] = before
    for s, w_ref in enumerate((wq_ref, wk_ref, wv_ref)):
        joined_ref[:, s * width : (s + 1) * width] = nn(before, w_ref[...]).astype(BF)
    tokens = jnp.where(block < own_blocks, own_ref[...], other_ref[...]).astype(F32)
    unit, _ = norm_parts(tokens)
    held_ref[slot] = (unit * gain_ref[...] + bias_ref[...]).astype(BF)


def project_all(own, other, gain, bias, w_qkv, core, places, length):
    blocks = places.shape[0]
    half = blocks // 2
    width = D // 2
    row = pl.BlockSpec((1, D), lambda b, *_: (0, 0))
    weights = [pl.BlockSpec((D, width), lambda b, c, p, s=s: (0, 2 * s + c[0])) for s in range(3)]
    return pl.pallas_call(
        project_kernel,
        grid_spec=pltpu.PrefetchScalarGridSpec(
            num_scalar_prefetch=2,
            grid=(blocks + 1,),
            in_specs=[
                pl.BlockSpec((length, D), lambda b, *_: (jnp.minimum(b, half - 1), 0)),
                pl.BlockSpec((length, D), lambda b, *_: (jnp.clip(b - half, 0, half - 1), 0)),
                row,
                row,
            ]
            + weights,
            out_specs=[
                pl.BlockSpec((length, 3 * width), lambda b, c, p: (p[jnp.maximum(b - 1, 0)], 0)),
                pl.BlockSpec((length, D), lambda b, c, p: (p[jnp.maximum(b - 1, 0)], 0)),
            ],
            scratch_shapes=[pltpu.VMEM((2, length, D), BF)],
        ),
        out_shape=[
            jax.ShapeDtypeStruct((blocks * length, 3 * width), BF),
            jax.ShapeDtypeStruct((blocks * length, D), BF),
        ],
        compiler_params=pltpu.CompilerParams(vmem_limit_bytes=60 * MIB),
        cost_estimate=SMALL,
        name="norm_and_project",
    )(
        core.reshape(1),
        places,
        own,
        other,
        gain.reshape(1, D),
        bias.reshape(1, D),
        w_qkv,
        w_qkv,
        w_qkv,
    )


def middle_kernel(
    core_ref,
    x_ref,
    own_ref,
    got_ref,
    keys_ref,
    values_ref,
    seen_ref,
    gain2_ref,
    bias2_ref,
    gain3_ref,
    bias3_ref,
    w_own_ref,
    w_got_ref,
    w_query_ref,
    w_out_ref,
    hidden1_ref,
    hidden2_ref,
    normed3_ref,
    queries_ref,
    mixed_ref,
    lse_ref,
):
    hidden = x_ref[...].astype(F32) + nn(own_ref[...], w_own_ref[...])
    hidden += nn(got_ref[...], w_got_ref[...])
    hidden1_ref[...] = hidden
    unit, _ = norm_parts(hidden)
    normed2 = (unit * gain2_ref[...] + bias2_ref[...]).astype(BF)
    queries = nn(normed2, w_query_ref[...]).astype(BF)
    queries_ref[...] = queries
    rows, states = queries.shape[0], keys_ref.shape[0]
    half = lax.broadcasted_iota(jnp.int32, (rows, 2 * HEAD), 1) >= HEAD
    v_flip = values_ref[...].T
    ones = jnp.ones((16, states), BF)
    zero = jnp.zeros((rows, 2 * HEAD), BF)

    def score(head):
        at, h = head // 2 * 2 * HEAD, head % 2
        own = jnp.where(half == (h == 1), queries[:, at : at + 2 * HEAD], zero)
        return nt(keys_ref[:, at : at + 2 * HEAD], own)

    def soften(scores):
        scores = scores * (SCALE * LOG2E) + seen_ref[...]
        top = jnp.max(scores, axis=0, keepdims=True)
        return jnp.exp2(scores - top).astype(BF), top

    outs, lses, scores, raised = [], [], {}, {}
    for n in range(HEADS + 2):
        if n < HEADS:
            scores[n] = score(n)
        if 0 <= n - 1 < HEADS:
            raised[n - 1] = soften(scores.pop(n - 1))
        if n >= 2:
            weights, top = raised.pop(n - 2)
            v_rows = jnp.concatenate([v_flip[(n - 2) * HEAD : (n - 1) * HEAD], ones], 0)
            mixed = nn(v_rows, weights)
            total = mixed[HEAD : HEAD + 1]
            lses.append(top + jnp.log2(total))
            outs.append((mixed[:HEAD] / total).astype(BF))
    lse_ref[...] = jnp.concatenate(lses, 0)
    mixed = jnp.concatenate(outs, 0).T
    mixed_ref[...] = mixed
    hidden += nn(mixed, w_out_ref[...])
    hidden2_ref[...] = hidden
    unit, _ = norm_parts(hidden)
    normed3_ref[...] = (unit * gain3_ref[...] + bias3_ref[...]).astype(BF)


def cross_part(x, own, got, text_kv, seen, norms, w_self_out, w_query, w_out, core):
    tokens, width = got.shape
    states = text_kv.shape[0]
    block = min(256, tokens)
    row = pl.BlockSpec((1, D), lambda b, c: (0, 0))
    wide = pl.BlockSpec((block, D), lambda b, c: (b, 0))
    narrow = pl.BlockSpec((block, width), lambda b, c: (b, 0))
    square = pl.BlockSpec((D, D), lambda b, c: (0, 0))
    return pl.pallas_call(
        middle_kernel,
        grid_spec=pltpu.PrefetchScalarGridSpec(
            num_scalar_prefetch=1,
            grid=(tokens // block,),
            in_specs=[
                wide,
                narrow,
                narrow,
                pl.BlockSpec((states, D), lambda b, c: (0, 0)),
                pl.BlockSpec((states, D), lambda b, c: (0, 1)),
                pl.BlockSpec((states, 1), lambda b, c: (0, 0)),
                row,
                row,
                row,
                row,
                pl.BlockSpec((width, D), lambda b, c: (c[0], 0)),
                pl.BlockSpec((width, D), lambda b, c: (1 - c[0], 0)),
                square,
                square,
            ],
            out_specs=[wide] * 5 + [pl.BlockSpec((HEADS, block), lambda b, c: (0, b))],
        ),
        out_shape=[
            jax.ShapeDtypeStruct((tokens, D), F32),
            jax.ShapeDtypeStruct((tokens, D), F32),
            jax.ShapeDtypeStruct((tokens, D), BF),
            jax.ShapeDtypeStruct((tokens, D), BF),
            jax.ShapeDtypeStruct((tokens, D), BF),
            jax.ShapeDtypeStruct((HEADS, tokens), F32),
        ],
        compiler_params=pltpu.CompilerParams(vmem_limit_bytes=60 * MIB),
        cost_estimate=SMALL,
        name="cross_attention_part",
    )(
        core.reshape(1),
        x,
        own,
        got,
        text_kv,
        text_kv,
        seen,
        *[v.reshape(1, D) for v in norms],
        w_self_out,
        w_self_out,
        w_query,
        w_out,
    )


def attend_kernel(row_ref, q_ref, k_ref, v_ref, all_ref, other_ref, lse_ref, out_ref):
    length = q_ref.shape[0]
    block = QUERY_BLOCK
    scale = SCALE * LOG2E
    half = lax.broadcasted_iota(jnp.int32, (block, 2 * HEAD), 1) >= HEAD
    key_row = lax.broadcasted_iota(jnp.int32, (block, block), 0)
    query_col = lax.broadcasted_iota(jnp.int32, (block, block), 1)
    seen = key_row <= query_col
    v_flip = v_ref[...].T
    ones = jnp.ones((16, length), BF)
    v_rows = [jnp.concatenate([v_flip[h * HEAD : (h + 1) * HEAD], ones], 0) for h in range(2)]

    def score(i, h):
        lo, hi = i * block, (i + 1) * block
        queries = q_ref[lo:hi, :]
        own = jnp.where(half == (h == 1), queries, jnp.zeros_like(queries))
        return nt(k_ref[lo:hi, :], own), nt(k_ref[:lo, :], own) if i else None

    def soften(i, h, diag, rest):
        diag = jnp.where(seen, diag, MASKED)
        top = jnp.max(diag, axis=0, keepdims=True)
        if i:
            top = jnp.maximum(top, jnp.max(rest, axis=0, keepdims=True))
            rest = jnp.exp2(rest * scale - top * scale).astype(BF)
        return jnp.exp2(diag * scale - top * scale).astype(BF), rest, top * scale

    def mix(i, h, diag, rest, base):
        lo, hi = i * block, (i + 1) * block
        mixed = nn(v_rows[h][:, lo:hi], diag)
        if i:
            mixed += nn(v_rows[h][:, :lo], rest)
        total = mixed[HEAD : HEAD + 1]
        lse_ref[0, h : h + 1, lo:hi] = base + jnp.log2(total)
        return mixed[:HEAD] / total

    tasks = [(i, h) for i in range(length // block) for h in range(2)]
    scores, raised, outs = {}, {}, []
    part = length // row_ref.shape[0]
    for n in range(len(tasks) + 2):
        if n < len(tasks):
            scores[n] = score(*tasks[n])
        if 0 <= n - 1 < len(tasks):
            raised[n - 1] = soften(*tasks[n - 1], *scores.pop(n - 1))
        if n >= 2:
            outs.append(mix(*tasks[n - 2], *raised.pop(n - 2)))
        if len(outs) == 2:
            lo = tasks[n - 2][0] * block
            result = jnp.concatenate(outs, 0).T.astype(BF)
            outs = []
            for at in range(0, block, part):
                row = pl.multiple_of(row_ref[(lo + at) // part] * part, part)
                out_ref[pl.ds(row, part), :] = result[at : at + part]
    all_ref[...] = out_ref[...]
    other_ref[...] = out_ref[length // 2 :, :]


def head_specs(length, pairs):
    return [
        pl.BlockSpec((length, 2 * HEAD), lambda p, *_, s=s: (0, s * pairs + p)) for s in range(3)
    ]


def attend(joined, rows):
    length, width = joined.shape[0], joined.shape[1] // 3
    pairs = width // (2 * HEAD)
    return pl.pallas_call(
        attend_kernel,
        grid_spec=pltpu.PrefetchScalarGridSpec(
            num_scalar_prefetch=1,
            grid=(pairs,),
            in_specs=head_specs(length, pairs),
            out_specs=[
                pl.BlockSpec((length, 2 * HEAD), lambda p, *_: (0, p)),
                pl.BlockSpec((length // 2, 2 * HEAD), lambda p, *_: (0, p)),
                pl.BlockSpec((1, 2, length), lambda p, *_: (p, 0, 0)),
            ],
            scratch_shapes=[pltpu.VMEM((length, 2 * HEAD), BF)],
        ),
        out_shape=[
            jax.ShapeDtypeStruct((length, width), BF),
            jax.ShapeDtypeStruct((length // 2, width), BF),
            jax.ShapeDtypeStruct((pairs, 2, length), F32),
        ],
        compiler_params=pltpu.CompilerParams(vmem_limit_bytes=60 * MIB),
        cost_estimate=SMALL,
        name="self_attention",
    )(rows, joined, joined, joined)


def attend_back_kernel(
    row_ref,
    q_ref,
    k_ref,
    v_ref,
    own_g_ref,
    other_g_ref,
    mixed_ref,
    lse_ref,
    ordered_hbm,
    wq_ref,
    wk_ref,
    wv_ref,
    keep_ref,
    send_ref,
    own_ref,
    other_ref,
    dq_sum,
    g_ref,
    o_ref,
    ordered_ref,
    sum_ref,
    sem,
):
    pair, pairs = pl.program_id(0), pl.num_programs(0)
    load = pltpu.make_async_copy(ordered_hbm, ordered_ref, sem)

    @pl.when(pair == 0)
    def _():
        load.start()

    length = q_ref.shape[0]
    places = row_ref.shape[0]
    part = length // places
    for place in range(places):
        row = row_ref[place]
        at = pl.ds(pl.multiple_of(row % (places // 2) * part, part), part)
        to = slice(place * part, (place + 1) * part)
        mine = row < places // 2
        g_ref[to, :] = jnp.where(mine, own_g_ref[at, :], other_g_ref[at, :])
        o_ref[to, :] = mixed_ref[pl.ds(pl.multiple_of(row * part, part), part), :]
    block = QUERY_BLOCK
    scale = SCALE * LOG2E
    half = lax.broadcasted_iota(jnp.int32, (length, 2 * HEAD), 1) >= HEAD
    key_row = lax.broadcasted_iota(jnp.int32, (block, block), 0)
    query_col = lax.broadcasted_iota(jnp.int32, (block, block), 1)
    seen = key_row <= query_col
    k_flip = k_ref[...].T
    zero = jnp.zeros((length, 2 * HEAD), BF)
    queries = [jnp.where(half == (h == 1), q_ref[...], zero) for h in range(2)]
    grads = [jnp.where(half == (h == 1), g_ref[...], zero) for h in range(2)]
    product = (g_ref[...].astype(F32) * o_ref[...].astype(F32)).T
    deltas = [jnp.sum(product[h * HEAD : (h + 1) * HEAD], axis=0, keepdims=True) for h in range(2)]

    def score(j, h):
        lo, hi = j * block, (j + 1) * block
        return nt(k_ref[lo:hi, :], queries[h][lo:]), nt(v_ref[lo:hi, :], grads[h][lo:])

    def soften(j, h, scores, score_grad):
        lo, hi = j * block, (j + 1) * block
        weights = jnp.exp2(scores * scale - lse_ref[0, h : h + 1, lo:])
        first = jnp.where(seen, weights[:, :block], 0.0)
        weights = jnp.concatenate([first, weights[:, block:]], 1) if hi < length else first
        score_grad = (weights * (score_grad - deltas[h][:, lo:])).astype(BF)
        return weights.astype(BF), score_grad

    def mix(j, h, weights, score_grad):
        lo, hi = j * block, (j + 1) * block
        rows = slice(h * HEAD, (h + 1) * HEAD)
        query_part = nn(k_flip[rows, lo:hi], score_grad)
        if j == 0:
            dq_sum[rows, :] = query_part
        else:
            dq_sum[rows, lo:] += query_part
        return nn(score_grad, queries[h][lo:]), nn(weights, grads[h][lo:])

    tasks = [(j, h) for j in range(length // block) for h in range(2)]
    scores, raised, outs, key_grads, value_grads = {}, {}, [], [], []
    for n in range(len(tasks) + 2):
        if n < len(tasks):
            scores[n] = score(*tasks[n])
        if 0 <= n - 1 < len(tasks):
            raised[n - 1] = soften(*tasks[n - 1], *scores.pop(n - 1))
        if n >= 2:
            outs.append(mix(*tasks[n - 2], *raised.pop(n - 2)))
        if len(outs) == 2:
            key_grads.append(((outs[0][0] + outs[1][0]) * SCALE).astype(BF))
            value_grads.append((outs[0][1] + outs[1][1]).astype(BF))
            outs = []
    query_grad = (dq_sum[...].T * SCALE).astype(BF)
    joined = jnp.concatenate(
        [query_grad, jnp.concatenate(key_grads, 0), jnp.concatenate(value_grads, 0)], 1
    )
    weights = jnp.concatenate([wq_ref[...], wk_ref[...], wv_ref[...]], 1)
    grad = nt(joined, weights)

    @pl.when(pair == 0)
    def _():
        sum_ref[...] = grad
        load.wait()

    @pl.when(pair > 0)
    def _():
        sum_ref[...] += grad

    wide = nn(ordered_ref[...], joined).astype(BF)
    keep_ref[...] = wide[: D // 2]
    send_ref[...] = wide[D // 2 :]

    @pl.when(pair == pairs - 1)
    def _():
        for place in range(places):
            row = row_ref[place]
            at = pl.ds(pl.multiple_of(row % (places // 2) * part, part), part)
            rows = sum_ref[place * part : (place + 1) * part, :]

            @pl.when(row < places // 2)
            def _(at=at, rows=rows):
                own_ref[at, :] = rows

            @pl.when(row >= places // 2)
            def _(at=at, rows=rows):
                other_ref[at, :] = rows.astype(BF)


def attend_back(joined, own_g, other_g, mixed, lse, ordered, w_qkv, core, rows):
    length, width = joined.shape[0], joined.shape[1] // 3
    pairs = width // (2 * HEAD)
    spec = pl.BlockSpec((length, 2 * HEAD), lambda p, *_: (0, p))
    half = pl.BlockSpec((length // 2, 2 * HEAD), lambda p, *_: (0, p))
    weights = [
        pl.BlockSpec((D, 2 * HEAD), lambda p, r, s=s: (0, (2 * s + r[r.shape[0] - 1]) * pairs + p))
        for s in range(3)
    ]
    sums = pl.BlockSpec((D // 2, 6 * HEAD), lambda p, *_: (0, p))
    out = pl.BlockSpec((length // 2, D), lambda p, *_: (0, 0))
    places = rows.shape[0]

    def body(row_ref, *refs):
        attend_back_kernel(Rows(row_ref, places), *refs)

    return pl.pallas_call(
        body,
        grid_spec=pltpu.PrefetchScalarGridSpec(
            num_scalar_prefetch=1,
            grid=(pairs,),
            in_specs=head_specs(length, pairs)
            + [half] * 2
            + [spec]
            + [pl.BlockSpec((1, 2, length), lambda p, *_: (p, 0, 0))]
            + [pl.BlockSpec(memory_space=pl.ANY)]
            + weights,
            out_specs=[sums, sums, out, out],
            scratch_shapes=[
                pltpu.VMEM((2 * HEAD, length), F32),
                pltpu.VMEM((length, 2 * HEAD), BF),
                pltpu.VMEM((length, 2 * HEAD), BF),
                pltpu.VMEM((D, length), BF),
                pltpu.VMEM((length, D), F32),
                pltpu.SemaphoreType.DMA,
            ],
        ),
        out_shape=[jax.ShapeDtypeStruct((D // 2, 3 * width), BF)] * 2
        + [
            jax.ShapeDtypeStruct((length // 2, D), F32),
            jax.ShapeDtypeStruct((length // 2, D), BF),
        ],
        compiler_params=pltpu.CompilerParams(vmem_limit_bytes=60 * MIB),
        cost_estimate=SMALL,
        name="self_attention_back",
    )(
        jnp.concatenate([rows, core.reshape(1)]), joined, joined, joined, own_g, other_g,
        mixed, lse, ordered, w_qkv, w_qkv, w_qkv,
    )


def flip_kernel(block_ref, value_ref, out_ref, flip_ref):
    flip_ref[...] = value_ref[...].T
    height = D // block_ref.shape[0]
    for i in range(block_ref.shape[0]):
        at = pl.ds(pl.multiple_of(block_ref[i] * height, height), height)
        out_ref[i * height : (i + 1) * height, :] = flip_ref[at, :]


def flip_ordered(value, blocks):
    tokens = value.shape[0]
    part = 256
    return pl.pallas_call(
        flip_kernel,
        grid_spec=pltpu.PrefetchScalarGridSpec(
            num_scalar_prefetch=1,
            grid=(tokens // part,),
            in_specs=[pl.BlockSpec((part, D), lambda t, b: (t, 0))],
            out_specs=pl.BlockSpec((D, part), lambda t, b: (0, t)),
            scratch_shapes=[pltpu.VMEM((D, part), BF)],
        ),
        out_shape=jax.ShapeDtypeStruct((D, tokens), BF),
        compiler_params=pltpu.CompilerParams(vmem_limit_bytes=60 * MIB),
        cost_estimate=LARGE,
        name="flip_ordered",
    )(blocks, value)


class Rows:
    def __init__(self, ref, count):
        self.ref, self.shape = ref, (count,)

    def __getitem__(self, place):
        return self.ref[place]


def mlp_kernel(
    pieces,
    steps,
    core_ref,
    rows_from,
    goes_to,
    own_ref,
    other_ref,
    own_g_ref,
    other_g_ref,
    *refs,
):
    ups, downs = refs[:pieces], refs[pieces : 2 * pieces]
    down_ref, up_ref, out_ref, norm_ref, sent_ref, *targets = refs[2 * pieces : 2 * pieces + 9]
    flip_ref, ordered_ref, wide_ref, tall_ref, active_ref, grad_ref, sems = refs[2 * pieces + 9 :]
    step = pl.program_id(0)
    slot = step % 2
    tokens = own_ref.shape[0]
    quarter, height = targets[0].shape[0], targets[0].shape[1]
    tile = wide_ref.shape[3]
    width = 2 * height
    per_step = tile // width
    units = steps * tile

    @pl.when(step == 0)
    def _():
        flip_ref[:, :tokens] = own_ref[...].T
        flip_ref[:, tokens:] = other_ref[...].T
        for i in range(4 * quarter):
            at = pl.multiple_of(rows_from[i] * height, height)
            ordered_ref[i * height : (i + 1) * height, :] = flip_ref[pl.ds(at, height), :]

    def wide_copy(at, where, side):
        part = wide_ref.at[at, side * quarter : (side + 1) * quarter]
        lanes = pl.ds(pl.multiple_of(where * tile, tile), tile)
        return pltpu.make_async_copy(part, targets[side].at[:, :, lanes], sems.at[at, side])

    def tall_copy(at, j, r, target, i):
        rows = slice(j * width + r * height, j * width + (r + 1) * height)
        lanes = slice(units + r * D, units + (r + 1) * D)
        return pltpu.make_async_copy(
            tall_ref.at[at, rows], target.at[i, :, lanes], sems.at[at, 4 + 2 * j + r]
        )

    def wait(at):
        for side in range(4):
            wide_copy(at, 0, side).wait()
        for j in range(per_step):
            for r in range(2):
                tall_copy(at, j, r, targets[0], 0).wait()

    @pl.when((step >= 2) & (step < steps + 2))
    def _():
        wait(slot)

    @pl.when(step < steps)
    def _():
        up_w = jnp.concatenate([r[...] for r in ups], 1) if pieces > 1 else ups[0][...]
        down_w = jnp.concatenate([r[...] for r in downs], 0) if pieces > 1 else downs[0][...]
        sides = ((0, own_ref, own_g_ref), (tokens, other_ref, other_g_ref))
        cut = 256
        tasks = [(u, side) for u in range(0, tile, cut) for side in sides]
        found, active, grads = {}, {}, {}

        def products(u, side):
            _, x_ref, g_ref = side
            return nn(x_ref[...], up_w[:, u : u + cut]), nt(g_ref[...], down_w[u : u + cut])

        def units_of(n):
            u, (base, _, _) = tasks[n]
            up_value, down_grad = found.pop(n)
            value, slope = gelu_parts(up_value)
            value = value.astype(BF)
            grad = (down_grad * slope).astype(BF)
            active_ref[step, base : base + tokens, u : u + cut] = value
            grad_ref[step, base : base + tokens, u : u + cut] = grad
            active[n], grads[n] = value, grad

        def weights_of(n):
            u = tasks[n][0]
            grad = jnp.concatenate([grads.pop(n - 1), grads.pop(n)], 0)
            wide = nn(ordered_ref[...], grad).astype(BF)
            wide_ref[slot, :, :, u : u + cut] = wide.reshape(wide_ref.shape[1:3] + (cut,))
            tall = nn(active.pop(n - 1).T, own_g_ref[...]) + nn(active.pop(n).T, other_g_ref[...])
            tall_ref[slot, u : u + cut] = tall.astype(BF)

        for n in range(len(tasks) + 2):
            if n < len(tasks):
                found[n] = products(*tasks[n])
            if 0 <= n - 1 < len(tasks):
                units_of(n - 1)
            if n >= 3 and n % 2:
                weights_of(n - 2)
        for side in range(4):
            wide_copy(slot, step, side).start()
        for j in range(per_step):
            i = goes_to[step * per_step + j]
            for side, target in enumerate(targets):

                @pl.when(i // quarter == side)
                def _(j=j, i=i, side=side, target=target):
                    for r in range(2):
                        tall_copy(slot, j, r, target, i - side * quarter).start()

    @pl.when(step >= steps)
    def _():
        up = up_ref[...]
        if up.shape[1] > units:
            first = core_ref[0] == 0
            picked = []
            for at in range(0, 2 * units, 2 * width):
                picked.append(
                    jnp.where(first, up[:, at : at + width], up[:, at + width : at + 2 * width])
                )
            up = jnp.concatenate(picked, 1)
        active = jnp.concatenate([active_ref[i] for i in range(steps)], 1)
        out = nn(active, down_ref[...].reshape(units, -1))
        grad = jnp.concatenate([grad_ref[i] for i in range(steps)], 1)
        norm = nt(grad, up)
        out_ref[...] = out[:tokens]
        norm_ref[...] = norm[:tokens]
        sent_ref[0] = out[tokens:].astype(BF)
        sent_ref[1] = norm[tokens:].astype(BF)


def mlp(own, other, own_g, other_g, w_up, w_down, core, rows_from, goes_to):
    tokens = own.shape[0]
    chips = rows_from.shape[0]
    tile, out_tile = 512, 256
    units = w_up.shape[1] // 2
    steps = units // tile
    width = units // chips
    height = D // chips
    fine = width % 128 == 0
    tall = w_down.reshape(chips, 2, width, D)
    if fine:
        pieces, piece = tile // width, width
    else:
        pieces, piece = 1, tile
        w_up = w_up.reshape(D, chips, 2, width)[:, :, core].reshape(D, units)
        w_down = w_down.reshape(chips, 2, width, D)[:, core].reshape(units, D)

    def place(s, c, j):
        s = jnp.minimum(s, steps - 1)
        return 2 * (s * pieces + j) + c[0] if fine else s

    def column(s):
        return jnp.maximum(s - steps, 0)

    whole = pl.BlockSpec((tokens, D), lambda s, *_: (0, 0))
    up_specs = [
        pl.BlockSpec((D, piece), lambda s, c, *_, j=j: (0, place(s, c, j))) for j in range(pieces)
    ]
    down_specs = [
        pl.BlockSpec((piece, D), lambda s, c, *_, j=j: (place(s, c, j), 0)) for j in range(pieces)
    ]
    kept = pl.BlockSpec((tokens, out_tile), lambda s, *_: (0, column(s)))
    sums = jax.ShapeDtypeStruct((chips // 4, height, units + 2 * D), BF)
    return pl.pallas_call(
        partial(mlp_kernel, pieces, steps),
        grid_spec=pltpu.PrefetchScalarGridSpec(
            num_scalar_prefetch=3,
            grid=(steps + D // out_tile,),
            in_specs=[whole] * 4
            + up_specs
            + down_specs
            + [
                pl.BlockSpec((chips, None, width, out_tile), lambda s, c, *_: (0, c[0], 0, column(s))),
                pl.BlockSpec((out_tile, w_up.shape[1]), lambda s, *_: (column(s), 0)),
            ],
            out_specs=[
                kept,
                kept,
                pl.BlockSpec((2, tokens, out_tile), lambda s, *_: (0, 0, column(s))),
            ]
            + [pl.BlockSpec(memory_space=pl.ANY)] * 4,
            scratch_shapes=[
                pltpu.VMEM((D, 2 * tokens), BF),
                pltpu.VMEM((D, 2 * tokens), BF),
                pltpu.VMEM((2, chips, height, tile), BF),
                pltpu.VMEM((2, tile, D), BF),
                pltpu.VMEM((steps, 2 * tokens, tile), BF),
                pltpu.VMEM((steps, 2 * tokens, tile), BF),
                pltpu.SemaphoreType.DMA((2, 4 + 2 * (tile // width))),
            ],
        ),
        out_shape=[
            jax.ShapeDtypeStruct((tokens, D), F32),
            jax.ShapeDtypeStruct((tokens, D), F32),
            jax.ShapeDtypeStruct((2, tokens, D), BF),
            sums,
            sums,
            sums,
            sums,
        ],
        compiler_params=pltpu.CompilerParams(vmem_limit_bytes=60 * MIB),
        cost_estimate=SMALL,
        name="mlp_both_ways",
    )(
        core.reshape(1),
        rows_from,
        goes_to,
        own,
        other,
        own_g,
        other_g,
        *([w_up] * pieces),
        *([w_down] * pieces),
        tall,
        w_up,
    )


def cross_back_kernel(
    scalars,
    order_ref,
    got_ref,
    grad3_ref,
    hidden2_ref,
    g_ref,
    gain3_ref,
    gain2_ref,
    seen_ref,
    lse_ref,
    keys_ref,
    values_ref,
    states_ref,
    mixed_hbm,
    w_out_hbm,
    queries_hbm,
    w_query_hbm,
    hidden1_hbm,
    own_hbm,
    other_hbm,
    w_self_hbm,
    out_hbm,
    got_hbm,
    block_ref,
    hidden_grad_ref,
    own_grad_ref,
    other_grad_ref,
    text_ref,
    norms_ref,
    states_flip_ref,
    keep,
    send,
    mixed_ref,
    w_out_ref,
    queries_ref,
    w_query,
    hidden1,
    own_ref,
    other_ref,
    w_self,
    out_ref,
    out_got_ref,
    flip_ref,
    ordered_ref,
    keep_stage,
    send_stage,
    sems,
    out_sems,
):
    core = scalars[0]
    tokens = grad3_ref.shape[0]
    loads = [
        pltpu.make_async_copy(a, b, sems.at[i])
        for i, (a, b) in enumerate(
            (
                (mixed_hbm, mixed_ref),
                (w_out_hbm, w_out_ref),
                (queries_hbm, queries_ref),
                (w_query_hbm, w_query),
                (hidden1_hbm, hidden1),
                (own_hbm.at[:tokens], own_ref),
                (other_hbm, other_ref),
                (w_self_hbm, w_self),
                (out_hbm, out_ref),
                (got_hbm.at[0], out_got_ref),
            )
        )
    ]
    for load in loads:
        load.start()
    count = order_ref.shape[0]
    rows = D // count
    half = D // 2
    writes = []

    def order(depth):
        for i in range(count):
            at = pl.multiple_of(order_ref[i] * rows, rows)
            ordered_ref[i * rows : (i + 1) * rows, :depth] = flip_ref[pl.ds(at, rows), :depth]

    def write(slot, grads):
        keep_stage[slot] = ordered_ref[half:, :tokens].astype(BF)
        lane = slot * (tokens + D)
        lanes = slice(lane, lane + tokens + D)
        send_stage[:, lane : lane + tokens] = ordered_ref[:half, :tokens].astype(BF)
        send_stage[:, lane + tokens : lane + tokens + D] = grads
        writes.append(
            pltpu.make_async_copy(send_stage.at[:, lanes], send.at[:, lanes], out_sems.at[slot])
        )
        writes.append(
            pltpu.make_async_copy(keep_stage.at[slot], keep.at[slot], out_sems.at[4 + slot])
        )
        for copy in writes[-2:]:
            copy.start()

    kind = flip_ref.dtype
    loads[0].wait()
    flip_ref[:, :tokens] = mixed_ref[...].astype(kind).T
    hidden2 = hidden2_ref[...]
    grad3 = grad3_ref[...] + got_ref[...].astype(F32)
    unit, rstd = norm_parts(hidden2)
    norms_ref[4:5, :] = jnp.sum(grad3 * unit, axis=0, keepdims=True)
    norms_ref[5:6, :] = jnp.sum(grad3, axis=0, keepdims=True)
    norms_ref[6:8, :] = jnp.zeros((2, D), F32)
    grad_hidden = norm_back(unit, rstd, gain3_ref[...], grad3) + g_ref[...].astype(F32)
    hidden_grad_ref[...] = grad_hidden
    branch = grad_hidden.astype(BF)
    order(tokens)
    write(0, branch)
    loads[1].wait()
    grad_mixed = nt(branch, w_out_ref[...]).astype(BF)
    loads[2].wait()
    states = keys_ref.shape[0]
    half_lane = lax.broadcasted_iota(jnp.int32, (tokens, 2 * HEAD), 1) >= HEAD
    zero = jnp.zeros((tokens, 2 * HEAD), BF)
    k_flip = keys_ref[...].T

    def score(head):
        lanes = slice(head // 2 * 2 * HEAD, (head // 2 + 1) * 2 * HEAD)
        mine = half_lane == (head % 2 == 1)
        own_q = jnp.where(mine, queries_ref[:, lanes], zero)
        own_g = jnp.where(mine, grad_mixed[:, lanes], zero)
        return nt(keys_ref[:, lanes], own_q), nt(values_ref[:, lanes], own_g), own_q, own_g

    def soften(head, scores, score_grad, own_q, own_g):
        scores = scores * (SCALE * LOG2E) + seen_ref[...]
        weights = jnp.exp2(scores - lse_ref[head : head + 1, :])
        delta = jnp.sum(weights * score_grad, axis=0, keepdims=True)
        score_grad = (weights * (score_grad - delta)).astype(BF)
        return weights.astype(BF), score_grad, own_q, own_g

    scores, raised, flips, key_grads, value_grads = {}, {}, [], [], []
    for n in range(HEADS + 2):
        if n < HEADS:
            scores[n] = score(n)
        if 0 <= n - 1 < HEADS:
            raised[n - 1] = soften(n - 1, *scores.pop(n - 1))
        if n >= 2:
            head = n - 2
            weights, score_grad, own_q, own_g = raised.pop(head)
            key_part, value_part = nn(score_grad, own_q), nn(weights, own_g)
            if head % 2 == 0:
                key_grads.append(key_part)
                value_grads.append(value_part)
            else:
                key_grads[-1] += key_part
                value_grads[-1] += value_part
            part = nn(k_flip[head * HEAD : (head + 1) * HEAD], score_grad)
            flips.append((part * SCALE).astype(BF))
    query_grad = jnp.concatenate(flips, 0).T
    text_grad = jnp.concatenate([p * SCALE for p in key_grads] + value_grads, 1).astype(BF)
    text_ref[...] = text_grad
    flip_ref[:, :states] = states_ref[...].astype(kind).T
    order(states)
    states_flip_ref[...] = ordered_ref[half:, :states].astype(BF)
    part = states * 2 * D // half
    for i in range(half // states):
        send_stage[i * states : (i + 1) * states, 3 * (tokens + D) :] = text_grad[
            :, i * part : (i + 1) * part
        ]
    lanes = slice(3 * (tokens + D), 3 * (tokens + D) + part)
    writes.append(
        pltpu.make_async_copy(send_stage.at[:, lanes], send.at[:, lanes], out_sems.at[3])
    )
    writes[-1].start()
    for load in loads[3:5]:
        load.wait()
    grad2 = nt(query_grad, w_query[...])
    unit, rstd = norm_parts(hidden1[...])
    normed2 = unit * gain2_ref[0:1, :] + gain2_ref[1:2, :]
    flip_ref[:, :tokens] = normed2.astype(BF).astype(kind).T
    order(tokens)
    write(1, query_grad)
    norms_ref[2:3, :] = jnp.sum(grad2 * unit, axis=0, keepdims=True)
    norms_ref[3:4, :] = jnp.sum(grad2, axis=0, keepdims=True)
    norms_ref[0:2, :] = jnp.zeros((2, D), F32)
    grad_hidden = norm_back(unit, rstd, gain2_ref[0:1, :], grad2) + hidden_grad_ref[...]
    hidden_grad_ref[...] = grad_hidden
    branch = grad_hidden.astype(BF)
    for load in loads[5:8]:
        load.wait()
    own_rows = pl.ds(pl.multiple_of(core * half, half), half)
    other_rows = pl.ds(pl.multiple_of((1 - core) * half, half), half)
    own_grad_ref[...] = nt(branch, w_self[own_rows, :]).astype(BF)
    other_grad_ref[...] = nt(branch, w_self[other_rows, :]).astype(BF)
    flip_ref[own_rows, :tokens] = own_ref[...].astype(kind).T
    flip_ref[other_rows, :tokens] = other_ref[...].astype(kind).T
    order(tokens)
    write(2, branch)
    for load in loads[8:]:
        load.wait()
    block_ref[...] = (hidden2_ref[...] + out_ref[...] + out_got_ref[...].astype(F32)).astype(BF)
    for copy in writes:
        copy.wait()


def cross_back(
    out, got, grad3, hidden2, g, norms, seen, lse, mixed, w_out, text_kv, queries, states,
    w_query, hidden1, own, other, w_self, core, order,
):
    tokens, width = other.shape
    count = order.shape[0]
    texts = states.shape[0]
    kind = BF if (D // count) % 16 == 0 else F32

    def full(*shape):
        return pl.BlockSpec(shape, lambda b, *_: (0,) * len(shape))

    wide, late = full(tokens, D), pl.BlockSpec(memory_space=pl.ANY)
    return pl.pallas_call(
        cross_back_kernel,
        grid_spec=pltpu.PrefetchScalarGridSpec(
            num_scalar_prefetch=2,
            grid=(1,),
            in_specs=[
                pl.BlockSpec((None, tokens, D), lambda b, *_: (1, 0, 0)),
                wide,
                wide,
                wide,
                full(1, D),
                full(2, D),
                full(texts, 1),
                full(HEADS, tokens),
                full(texts, D),
                pl.BlockSpec((texts, D), lambda b, *_: (0, 1)),
                full(texts, D),
            ]
            + [late] * 10,
            out_specs=[
                wide,
                wide,
                full(tokens, width),
                full(tokens, width),
                full(texts, 2 * D),
                full(8, D),
                full(D // 2, texts),
                late,
                late,
            ],
            scratch_shapes=[
                pltpu.VMEM((tokens, D), BF),
                pltpu.VMEM((D, D), BF),
                pltpu.VMEM((tokens, D), BF),
                pltpu.VMEM((D, D), BF),
                pltpu.VMEM((tokens, D), F32),
                pltpu.VMEM((tokens, width), BF),
                pltpu.VMEM((tokens, width), BF),
                pltpu.VMEM((D, D), BF),
                pltpu.VMEM((tokens, D), F32),
                pltpu.VMEM((tokens, D), BF),
                pltpu.VMEM((D, tokens), kind),
                pltpu.VMEM((D, tokens), kind),
                pltpu.VMEM((3, D // 2, tokens), BF),
                pltpu.VMEM((D // 2, 3 * (tokens + D) + 4 * texts), BF),
                pltpu.SemaphoreType.DMA((10,)),
                pltpu.SemaphoreType.DMA((7,)),
            ],
        ),
        out_shape=[
            jax.ShapeDtypeStruct((tokens, D), BF),
            jax.ShapeDtypeStruct((tokens, D), F32),
            jax.ShapeDtypeStruct((tokens, width), BF),
            jax.ShapeDtypeStruct((tokens, width), BF),
            jax.ShapeDtypeStruct((texts, 2 * D), BF),
            jax.ShapeDtypeStruct((8, D), F32),
            jax.ShapeDtypeStruct((D // 2, texts), BF),
            jax.ShapeDtypeStruct((3, D // 2, tokens), BF),
            jax.ShapeDtypeStruct((D // 2, 3 * (tokens + D) + 4 * texts), BF),
        ],
        compiler_params=pltpu.CompilerParams(vmem_limit_bytes=60 * MIB),
        cost_estimate=SMALL,
        name="cross_attention_back",
    )(
        core.reshape(1), order, got, grad3, hidden2, g, norms[2].reshape(1, D),
        jnp.stack(norms[:2]), seen, lse, text_kv, text_kv, states, mixed, w_out, queries,
        w_query, hidden1, own, other, w_self, out, got,
    )


def pair_kernel(keep_ref, own_ref, got_ref, states_ref, grad_ref, grad_got_ref, *outs):
    first_ref, second_ref, text_ref = outs
    step = pl.program_id(0)
    half, tokens = keep_ref.shape
    texts = grad_ref.shape[0]

    def put(product):
        first_ref[...] = product[: half // 2].astype(BF)
        second_ref[...] = product[half // 2 :].astype(BF)

    @pl.when(step < 3)
    def _():
        product = nn(keep_ref[...], own_ref[:, tokens:])
        put(product + nn(got_ref[:, :tokens], got_ref[:, tokens:]))

    @pl.when(step >= 3)
    def _():
        got = grad_got_ref[...].astype(F32)
        got = jnp.concatenate([got[:texts], got[texts:]], 1)
        got = jnp.concatenate([got[texts // 2 :], got[: texts // 2]], 0)
        grad = (grad_ref[...].astype(F32) + got).astype(BF)
        text_ref[...] = grad[: texts // 2]
        put(nn(states_ref[...], grad))


def pair_gradients(keep, own, got, states, grad):
    _, half, tokens = keep.shape
    texts = grad.shape[0]

    def third(s):
        return jnp.minimum(s, 2)

    def later(s):
        return jnp.maximum(s - 3, 0)

    wide = pl.BlockSpec((half, tokens + D), lambda s: (0, third(s)))
    lane = 3 * (tokens + D) // (4 * texts)
    grads = pl.BlockSpec((texts, D), lambda s: (0, later(s)))
    out = pl.BlockSpec((half // 2, D), lambda s: (0, s))
    return pl.pallas_call(
        pair_kernel,
        grid=(5,),
        in_specs=[
            pl.BlockSpec((None, half, tokens), lambda s: (third(s), 0, 0)),
            wide,
            wide,
            pl.BlockSpec((half, texts), lambda s: (0, 0)),
            grads,
            pl.BlockSpec((2 * texts, 4 * texts), lambda s: (later(s), lane)),
        ],
        out_specs=[out, out, pl.BlockSpec((texts // 2, D), lambda s: (0, later(s)))],
        out_shape=[jax.ShapeDtypeStruct((half // 2, 5 * D), BF)] * 2
        + [jax.ShapeDtypeStruct((texts // 2, 2 * D), BF)],
        compiler_params=pltpu.CompilerParams(vmem_limit_bytes=60 * MIB),
        cost_estimate=SMALL,
        name="pair_gradients",
    )(keep, own, got, states, grad, got)


def last_kernel(
    blocks_ref,
    x_ref,
    part_ref,
    got_ref,
    hidden_ref,
    gain_ref,
    norms_ref,
    image_ref,
    keep,
    send,
    norm_flip,
):
    count = blocks_ref.shape[0]
    height, half = D // count, D // 2
    grad = part_ref[...] + got_ref[...].astype(F32)
    unit, rstd = norm_parts(x_ref[...].astype(F32))
    sums = [jnp.sum(grad * unit, axis=0, keepdims=True), jnp.sum(grad, axis=0, keepdims=True)]
    image = norm_back(unit, rstd, gain_ref[...], grad) + hidden_ref[...]
    image_ref[...] = image.astype(BF)
    fill = jnp.zeros((norm_flip.shape[1] - 8, D), F32)
    norm_flip[...] = jnp.concatenate(sums + [norms_ref[2:8, :], fill], 0).T
    for i in range(count):
        at = pl.ds(pl.multiple_of(blocks_ref[i] * height, height), height)
        to = i * height % half
        target = keep if i < count // 2 else send
        target[to : to + height, :] = norm_flip[at, :].astype(BF)


def last_part(x, part, got, hidden_grad, gain, norms, blocks):
    tokens = got.shape[0]

    def full(*shape):
        return pl.BlockSpec(shape, lambda b, *_: (0,) * len(shape))

    wide = full(tokens, D)
    return pl.pallas_call(
        last_kernel,
        grid_spec=pltpu.PrefetchScalarGridSpec(
            num_scalar_prefetch=1,
            grid=(1,),
            in_specs=[wide] * 4 + [full(1, D), full(8, D)],
            out_specs=[wide, full(D // 2, 128), full(D // 2, 128)],
            scratch_shapes=[pltpu.VMEM((D, 128), F32)],
        ),
        out_shape=[jax.ShapeDtypeStruct((tokens, D), BF)]
        + [jax.ShapeDtypeStruct((D // 2, 128), BF)] * 2,
        compiler_params=pltpu.CompilerParams(vmem_limit_bytes=60 * MIB),
        cost_estimate=SMALL,
        name="norm_back",
    )(blocks, x, part, got, hidden_grad, gain.reshape(1, D), norms)


def add_kernel(a_ref, b_ref, keep_ref, send_ref):
    block, half = pl.program_id(0), pl.num_programs(0) // 2
    total = a_ref[...] + b_ref[...]

    @pl.when(block < half)
    def _():
        send_ref[...] = total

    @pl.when(block >= half)
    def _():
        keep_ref[...] = total


def add_halves(a, b):
    count, height, width = a.shape
    blocks = 4
    half = blocks // 2
    shape = (count // blocks, height, width)
    turned = pl.BlockSpec(shape, lambda i: ((i + half) % blocks, 0, 0))
    return pl.pallas_call(
        add_kernel,
        grid=(blocks,),
        in_specs=[turned] * 2,
        out_specs=[
            pl.BlockSpec(shape, lambda i: (jnp.maximum(i - half, 0), 0, 0)),
            pl.BlockSpec(shape, lambda i: (jnp.minimum(i, half - 1), 0, 0)),
        ],
        out_shape=[jax.ShapeDtypeStruct((count // 2, height, width), BF)] * 2,
        compiler_params=pltpu.CompilerParams(vmem_limit_bytes=60 * MIB),
        cost_estimate=SMALL,
        name="add_halves",
    )(a, b)


def sum_kernel(a_ref, b_ref, sum_ref):
    sum_ref[...] = a_ref[...] + b_ref[...]


def add_rounded(a, b):
    spec = pl.BlockSpec((a.shape[0] // 4,) + a.shape[1:], lambda i: (i, 0, 0))
    return pl.pallas_call(
        sum_kernel,
        grid=(4,),
        in_specs=[spec] * 2,
        out_specs=spec,
        out_shape=jax.ShapeDtypeStruct(a.shape, BF),
        compiler_params=pltpu.CompilerParams(vmem_limit_bytes=60 * MIB),
        cost_estimate=SMALL,
        name="add_rounded",
    )(a, b)


def behind(value, *others):
    return lax.optimization_barrier((value,) + others)[0]


class Route:
    def __init__(self, plan, orders):
        self.orders = orders
        count = plan.chips
        maps = np.zeros((2, count), np.int32)
        for core in range(2):
            for i in range(count):
                for s, bit in enumerate(orders[core]):
                    maps[core, i] |= ((i >> (plan.levels - 1 - s)) & 1) << bit
        here, there = jnp.asarray(maps)[plan.core], jnp.asarray(maps)[1 - plan.core]
        self.blocks = jnp.bitwise_xor(plan.chip, here).astype(jnp.int32)
        sent = jnp.bitwise_xor(plan.chip, there).astype(jnp.int32)
        self.devices = jnp.concatenate([2 * sent + 1 - plan.core, 2 * self.blocks + plan.core])
        backs = np.argsort(maps, axis=1).astype(np.int32)
        away = jnp.bitwise_xor(plan.chip, jnp.arange(count, dtype=jnp.int32))
        self.goes_to = jnp.take(jnp.asarray(backs)[plan.core], away, mode="clip")


class Plan:
    def __init__(self, n_img, n_txt):
        self.n_txt = n_txt
        self.n = n_img * n_txt
        self.chips = self.n // 2
        self.ny = n_txt // 2
        self.levels = self.chips.bit_length() - 1
        self.me = lax.axis_index("img") * n_txt + lax.axis_index("txt")
        self.core = self.me % 2
        self.chip = self.me // 2
        self.y = lax.axis_index("txt") // 2
        sources = (self.y - jnp.arange(self.ny, dtype=jnp.int32)) % self.ny
        self.places = jnp.concatenate([2 * sources + self.core, 2 * sources + 1 - self.core])
        at = jnp.arange(n_txt, dtype=jnp.int32)
        self.rows = jnp.bitwise_xor(at % 2, self.core) * self.ny + (self.y - at // 2) % self.ny
        rest = list(range(2, self.levels))
        self.near = Route(self, ([1, 0] + rest, [0, 1] + rest))
        self.small = Route(self, ([0] + rest + [1], [0] + rest + [1]))
        self.mixed = Route(self, ([1, 0] + rest, rest + [0, 1]))
        self.token = None

    def swap(self, value):
        return lax.ppermute(value, BOTH, [(d, d ^ 1) for d in range(self.n)])

    def shift_y(self, value, by):
        pairs = []
        for d in range(self.n):
            img, txt = divmod(d, self.n_txt)
            y, core = divmod(txt, 2)
            pairs.append((d, img * self.n_txt + ((y + by) % self.ny) * 2 + core))
        return lax.ppermute(value, BOTH, pairs)

    def halve(self, value, route, step):
        pairs = [(d, d ^ (2 << route.orders[d % 2][step])) for d in range(self.n)]
        return lax.ppermute(value, BOTH, pairs)

    def send_items(self, value, note=None):
        parts = []
        for k in range(self.ny):
            part = value[(self.y + k) % self.ny]
            if note is not None:
                part = jnp.concatenate([part, note], 0)
            parts.append(self.shift_y(part, k) if k else part)
        return parts

    def join_items(self, parts, length):
        notes = [p[length:] for p in parts] if parts[0].shape[0] > length else []
        return jnp.concatenate([p[:length] for p in parts] + notes, 0)

    def return_items(self, value):
        return [self.shift_y(value[k], -k) if k else value[0] for k in range(self.ny)]

    def order_items(self, parts):
        stacked = jnp.stack(parts)
        return jnp.stack([stacked[(i - self.y) % self.ny] for i in range(self.ny)])

    def start(self, keep, send, route, step=0):
        return keep, self.halve(send, route, step), route, step

    def advance(self, state):
        keep, got, route, step = state
        keep, got, _ = lax.optimization_barrier((keep, got, self.token))
        if keep.shape[0] == 1:
            self.token = keep[0].astype(F32) + got[0].astype(F32)
            return self.token
        if keep.size > 1 << 20:
            keep, send = add_halves(keep, got)
        else:
            total = (keep.astype(F32) + got.astype(F32)).astype(BF)
            keep, send = jnp.split(total, 2)
        keep, send = lax.optimization_barrier((keep, send))
        self.token = send
        return self.start(keep, send, route, step + 1)

    def then(self, *values):
        return lax.optimization_barrier(values + (self.token,))[:-1]


def per_device(
    n_img,
    n_txt,
    image_tokens,
    text_states,
    text_segments,
    item_segments,
    norm1_gain,
    norm1_bias,
    w_qkv,
    w_self_out,
    norm2_gain,
    norm2_bias,
    w_cross_q,
    w_cross_kv,
    w_cross_out,
    norm3_gain,
    norm3_bias,
    w_up,
    w_down,
    cotangent,
):
    plan = Plan(n_img, n_txt)
    core, n, chips, ny = plan.core, plan.n, plan.chips, plan.ny
    items, length, _ = image_tokens.shape
    tokens = items * length
    half_d = D // 2
    rows = D // n

    states = text_states.shape[1]
    ids = jnp.pad(text_segments.astype(BF), ((0, 15), (0, D - states)))
    note = jnp.concatenate([text_states[0], ids], 0)
    x_parts = plan.send_items(image_tokens, note)
    g_parts = plan.send_items(behind(cotangent, x_parts[-1]))
    x_own = plan.join_items(x_parts, length)
    x_other = plan.swap(x_own)

    notes = [v[tokens:].reshape(ny, states + 16, D) for v in (x_own, x_other)]
    notes = jnp.concatenate(notes, 0)
    ids = notes[:, states, :states].reshape(-1)
    states_all = notes[:, :states].reshape(-1, D)
    text_kv = nn(states_all, w_cross_kv).astype(BF)
    matches = ids == item_segments[0, plan.y].astype(BF)
    seen = jnp.where(matches, 0.0, MASKED).astype(F32)[:, None]

    joined, normed1 = project_all(
        x_own, x_other, norm1_gain, norm1_bias, w_qkv, core, plan.places, length
    )
    mixed, mixed_other, lse = attend(joined, plan.rows)
    mixed_got = plan.swap(mixed_other)
    g_own = plan.join_items([behind(p, mixed_got) for p in g_parts], length)
    g_other = plan.swap(g_own)

    norms = (norm2_gain, norm2_bias, norm3_gain, norm3_bias)
    hidden1, hidden2, normed3, cross_q, cross_mixed, cross_lse = cross_part(
        x_own,
        mixed,
        mixed_got,
        text_kv,
        seen,
        norms,
        w_self_out,
        w_cross_q,
        w_cross_out,
        core,
    )

    normed3_other = plan.swap(normed3)
    per_down = w_down.shape[0] // n
    out, grad3, sent, low_keep, high_keep, low_send, high_send = mlp(
        normed3,
        normed3_other,
        g_own,
        g_other,
        w_up,
        w_down,
        core,
        plan.mixed.blocks,
        plan.mixed.goes_to,
    )
    high_got = plan.halve(high_send, plan.mixed, 0)
    got = plan.swap(sent)


    block_out, grad_hidden1, grad_own, grad_other, grad_kv, norm_sums, states_flip, keep, send = (
        cross_back(
            out, got, grad3, hidden2, g_own, norms[:3], seen, cross_lse, cross_mixed, w_cross_out,
            text_kv, cross_q, states_all, w_cross_q, hidden1, mixed, mixed_got, w_self_out,
            core, plan.near.devices,
        )
    )
    grad_other, high_got = lax.optimization_barrier((grad_other, high_got))
    grad_got = plan.swap(grad_other)
    pair_got = plan.swap(behind(send, grad_got))
    plan.token = grad_other
    high_keep, high_got = plan.then(high_keep, high_got)
    low_got = plan.halve(behind(low_send, high_got), plan.mixed, 0)
    high_sum = add_rounded(high_keep, high_got)
    plan.token = high_sum
    next_got = plan.halve(high_sum, plan.mixed, 1)
    (normed1,) = plan.then(normed1)
    plan.token = ordered1 = flip_ordered(normed1, plan.near.blocks)
    send, pair_got = plan.then(send, pair_got)
    middle_keep, middle_send, text_sum = pair_gradients(
        keep, send, pair_got, states_flip, grad_kv
    )
    plan.token = middle_send
    middle_sums = plan.start(
        middle_keep.reshape(chips // 2, rows, -1),
        middle_send.reshape(chips // 2, rows, -1),
        plan.near,
    )

    grad_got, grad_own = plan.then(grad_got, grad_own)
    last_keep, last_send, part_own, part_other = attend_back(
        joined, grad_own, grad_got, mixed, lse, ordered1, w_qkv, core, plan.rows
    )
    plan.token = part_other
    last_sums = plan.start(
        last_keep.reshape(chips // 2, 2 * rows, -1),
        last_send.reshape(chips // 2, 2 * rows, -1),
        plan.near,
    )
    part_got = plan.swap(part_other)
    low_keep, low_got, next_got = plan.then(low_keep, low_got, next_got)
    low_sum = low_keep.astype(F32) + low_got.astype(F32) + next_got.astype(F32)
    plan.token = low_sum = lax.optimization_barrier(low_sum.astype(BF))
    low_keep, low_send = jnp.split(low_sum, 2)
    mlp_sums = plan.start(low_keep, low_send, plan.mixed, 2)
    middle_sums = plan.advance(middle_sums)
    part_got, part_own = plan.then(part_got, part_own)
    image_grad, norm_keep, norm_send = last_part(
        x_own, part_own, part_got, grad_hidden1, norm1_gain, norm_sums, plan.small.blocks
    )
    plan.token = norm_send
    norm_group = plan.start(
        norm_keep.reshape(chips // 2, 2 * rows, -1),
        norm_send.reshape(chips // 2, 2 * rows, -1),
        plan.small,
    )
    last_sums = plan.advance(last_sums)
    middle_sums = plan.advance(middle_sums)
    last_sums = plan.advance(last_sums)
    mlp_sums = plan.advance(mlp_sums)
    norm_group = plan.advance(norm_group)
    text_sum, image_grad, block_out = plan.then(text_sum, image_grad, block_out)
    text_part = nt(text_sum, w_cross_kv)
    plan.token = text_part
    text_part = text_part.reshape(ny, states, D)
    text_parts = [plan.shift_y(text_part[r].astype(BF), -r) for r in range(1, ny)]
    image_parts = plan.return_items(image_grad.reshape(ny, length, D))
    block_parts = plan.return_items(block_out.reshape(ny, length, D))
    for _ in range(plan.levels - 3):
        last_sums = plan.advance(last_sums)
    norm_group = plan.advance(norm_group)
    for _ in range(plan.levels - 3):
        mlp_sums = plan.advance(mlp_sums)
    for _ in range(plan.levels - 3):
        middle_sums = plan.advance(middle_sums)
        norm_group = plan.advance(norm_group)
    middle_sums = plan.advance(middle_sums)
    norm_group = plan.advance(norm_group)
    last_sums = plan.advance(last_sums)
    last_sums = jnp.concatenate([last_sums, norm_group], 1)
    up_down = mlp_sums

    units = w_up.shape[1] // 2
    down_grad = jnp.concatenate([up_down[:, units : units + D], up_down[:, units + D :]], 0)
    parts = jnp.concatenate([up_down[:, :units], last_sums], 1).reshape(2, rows, -1)
    mine = parts[core]
    sent = parts[1 - core].astype(BF)
    theirs = plan.swap(sent).astype(F32)
    (theirs,) = plan.then(theirs)
    text_part, *text_parts = plan.then(text_part, *text_parts)
    text_grad = sum((p.astype(F32) for p in text_parts), text_part[0])
    image_grad = plan.order_items(plan.then(*image_parts)).astype(F32)
    plan.token = image_grad
    block_out = plan.order_items(plan.then(*block_parts))
    by_core = jnp.where(core == 0, jnp.stack([mine, theirs]), jnp.stack([theirs, mine]))
    up_grad = by_core[:, :, :units].reshape(2, rows, chips, per_down)
    up_grad = up_grad.transpose(1, 2, 0, 3).reshape(rows, 2 * units)
    wide = by_core[:, :, units : units + 3 * half_d].reshape(2, rows, -1, 3, 2 * HEAD)
    wide = wide.transpose(1, 3, 0, 2, 4).reshape(rows, 3 * D)
    norm_sums = mine[:, -128:-122] + theirs[:, -128:-122]
    return (
        block_out,
        image_grad,
        text_grad[None],
        norm_sums[:, 0],
        norm_sums[:, 1],
        wide,
        middle_sums[:, 2 * D : 3 * D],
        norm_sums[:, 2],
        norm_sums[:, 3],
        middle_sums[:, D : 2 * D],
        middle_sums[:, 3 * D :],
        middle_sums[:, :D],
        norm_sums[:, 4],
        norm_sums[:, 5],
        up_grad,
        down_grad,
    )


def solution(mesh):
    split = P("img", "txt", None)
    rows = P(BOTH)
    wide = P(BOTH, None)
    return jax.shard_map(
        partial(per_device, mesh.shape["img"], mesh.shape["txt"]),
        mesh=mesh,
        in_specs=(split, split, P("img", "txt"), P("img", None)) + (P(),) * 13 + (split,),
        out_specs=(
            (split,) * 3
            + (rows, rows, wide, wide)
            + (rows, rows, wide, wide, wide)
            + (rows, rows, wide, wide)
        ),
        check_vma=False,
    )
```

```python
from functools import partial

import jax
import jax.numpy as jnp
import numpy as np
from jax import lax
from jax.experimental import pallas as pl
from jax.experimental.pallas import tpu as pltpu
from jax.sharding import PartitionSpec as P

D = 1024
HEADS = 16
HEAD = 64
EPS = 1e-05
MASKED = -1e30
SCALE = HEAD**-0.5
LOG2E = 1.4426950408889634
BOTH = ("img", "txt")
BF = jnp.bfloat16
F32 = jnp.float32
QUERY_BLOCK = 256
MIB = 1 << 20
SMALL = pl.CostEstimate(flops=1 << 20, bytes_accessed=1 << 16, transcendentals=0)
LARGE = pl.CostEstimate(flops=1 << 38, bytes_accessed=1 << 30, transcendentals=0)


def nn(a, b):
    return lax.dot_general(a, b, (((1,), (0,)), ((), ())), preferred_element_type=F32)


def nt(a, b):
    return lax.dot_general(a, b, (((1,), (1,)), ((), ())), preferred_element_type=F32)


def tn(a, b):
    return lax.dot_general(a, b, (((0,), (0,)), ((), ())), preferred_element_type=F32)


def norm_parts(values):
    center = values - jnp.mean(values, axis=-1, keepdims=True)
    rstd = lax.rsqrt(jnp.mean(center * center, axis=-1, keepdims=True) + EPS)
    return center * rstd, rstd


def norm_back(unit, rstd, gain, grad):
    scaled = grad * gain
    return rstd * (
        scaled
        - jnp.mean(scaled, axis=-1, keepdims=True)
        - unit * jnp.mean(scaled * unit, axis=-1, keepdims=True)
    )


TAIL = [
    0.5 * c
    for c in (
        -0.22753805372107494,
        0.8866680711331851,
        -0.6354061073102151,
        0.6495639241196378,
        0.09138668583849363,
        0.235325478247137,
    )
]


def gelu_parts(value):
    t = 1.0 / (1.0 + (0.39 * 0.5**0.5) * jnp.abs(value))
    bell = jnp.exp2(value * value * (-0.5 * LOG2E))
    tail = jnp.full_like(t, TAIL[0])
    for term in TAIL[1:]:
        tail = tail * t + term
    tail = tail * t * bell
    cdf = jnp.where(value > 0.0, 1.0 - tail, tail)
    return value * cdf, cdf + value * bell * (0.5 / np.pi) ** 0.5


def project_kernel(
    core_ref, place_ref, own_ref, other_ref, gain_ref, bias_ref, wq_ref, wk_ref, wv_ref, *refs
):
    joined_ref, normed_ref, held_ref = refs
    block, own_blocks = pl.program_id(0), (pl.num_programs(0) - 1) // 2
    slot = block % 2
    width = wq_ref.shape[1]
    before = held_ref[1 - slot]
    normed_ref[...] = before
    for s, w_ref in enumerate((wq_ref, wk_ref, wv_ref)):
        joined_ref[:, s * width : (s + 1) * width] = nn(before, w_ref[...]).astype(BF)
    tokens = jnp.where(block < own_blocks, own_ref[...], other_ref[...]).astype(F32)
    unit, _ = norm_parts(tokens)
    held_ref[slot] = (unit * gain_ref[...] + bias_ref[...]).astype(BF)


def project_all(own, other, gain, bias, w_qkv, core, places, length):
    blocks = places.shape[0]
    half = blocks // 2
    width = D // 2
    row = pl.BlockSpec((1, D), lambda b, *_: (0, 0))
    weights = [pl.BlockSpec((D, width), lambda b, c, p, s=s: (0, 2 * s + c[0])) for s in range(3)]
    return pl.pallas_call(
        project_kernel,
        grid_spec=pltpu.PrefetchScalarGridSpec(
            num_scalar_prefetch=2,
            grid=(blocks + 1,),
            in_specs=[
                pl.BlockSpec((length, D), lambda b, *_: (jnp.minimum(b, half - 1), 0)),
                pl.BlockSpec((length, D), lambda b, *_: (jnp.clip(b - half, 0, half - 1), 0)),
                row,
                row,
            ]
            + weights,
            out_specs=[
                pl.BlockSpec((length, 3 * width), lambda b, c, p: (p[jnp.maximum(b - 1, 0)], 0)),
                pl.BlockSpec((length, D), lambda b, c, p: (p[jnp.maximum(b - 1, 0)], 0)),
            ],
            scratch_shapes=[pltpu.VMEM((2, length, D), BF)],
        ),
        out_shape=[
            jax.ShapeDtypeStruct((blocks * length, 3 * width), BF),
            jax.ShapeDtypeStruct((blocks * length, D), BF),
        ],
        compiler_params=pltpu.CompilerParams(vmem_limit_bytes=60 * MIB),
        cost_estimate=SMALL,
        name="norm_and_project",
    )(
        core.reshape(1),
        places,
        own,
        other,
        gain.reshape(1, D),
        bias.reshape(1, D),
        w_qkv,
        w_qkv,
        w_qkv,
    )


def middle_kernel(
    core_ref,
    x_ref,
    own_ref,
    got_ref,
    keys_ref,
    values_ref,
    seen_ref,
    gain2_ref,
    bias2_ref,
    gain3_ref,
    bias3_ref,
    w_own_ref,
    w_got_ref,
    w_query_ref,
    w_out_ref,
    hidden1_ref,
    hidden2_ref,
    normed3_ref,
    queries_ref,
    mixed_ref,
    lse_ref,
):
    hidden = x_ref[...].astype(F32) + nn(own_ref[...], w_own_ref[...])
    hidden += nn(got_ref[...], w_got_ref[...])
    hidden1_ref[...] = hidden
    unit, _ = norm_parts(hidden)
    normed2 = (unit * gain2_ref[...] + bias2_ref[...]).astype(BF)
    queries = nn(normed2, w_query_ref[...]).astype(BF)
    queries_ref[...] = queries
    rows, states = queries.shape[0], keys_ref.shape[0]
    half = lax.broadcasted_iota(jnp.int32, (rows, 2 * HEAD), 1) >= HEAD
    v_flip = values_ref[...].T
    ones = jnp.ones((16, states), BF)
    zero = jnp.zeros((rows, 2 * HEAD), BF)

    def score(head):
        at, h = head // 2 * 2 * HEAD, head % 2
        own = jnp.where(half == (h == 1), queries[:, at : at + 2 * HEAD], zero)
        return nt(keys_ref[:, at : at + 2 * HEAD], own)

    def soften(scores):
        scores = scores * (SCALE * LOG2E) + seen_ref[...]
        top = jnp.max(scores, axis=0, keepdims=True)
        return jnp.exp2(scores - top).astype(BF), top

    outs, lses, scores, raised = [], [], {}, {}
    for n in range(HEADS + 2):
        if n < HEADS:
            scores[n] = score(n)
        if 0 <= n - 1 < HEADS:
            raised[n - 1] = soften(scores.pop(n - 1))
        if n >= 2:
            weights, top = raised.pop(n - 2)
            v_rows = jnp.concatenate([v_flip[(n - 2) * HEAD : (n - 1) * HEAD], ones], 0)
            mixed = nn(v_rows, weights)
            total = mixed[HEAD : HEAD + 1]
            lses.append(top + jnp.log2(total))
            outs.append((mixed[:HEAD] / total).astype(BF))
    lse_ref[...] = jnp.concatenate(lses, 0)
    mixed = jnp.concatenate(outs, 0).T
    mixed_ref[...] = mixed
    hidden += nn(mixed, w_out_ref[...])
    hidden2_ref[...] = hidden
    unit, _ = norm_parts(hidden)
    normed3_ref[...] = (unit * gain3_ref[...] + bias3_ref[...]).astype(BF)


def cross_part(x, own, got, text_kv, seen, norms, w_self_out, w_query, w_out, core):
    tokens, width = got.shape
    states = text_kv.shape[0]
    block = min(256, tokens)
    row = pl.BlockSpec((1, D), lambda b, c: (0, 0))
    wide = pl.BlockSpec((block, D), lambda b, c: (b, 0))
    narrow = pl.BlockSpec((block, width), lambda b, c: (b, 0))
    square = pl.BlockSpec((D, D), lambda b, c: (0, 0))
    return pl.pallas_call(
        middle_kernel,
        grid_spec=pltpu.PrefetchScalarGridSpec(
            num_scalar_prefetch=1,
            grid=(tokens // block,),
            in_specs=[
                wide,
                narrow,
                narrow,
                pl.BlockSpec((states, D), lambda b, c: (0, 0)),
                pl.BlockSpec((states, D), lambda b, c: (0, 1)),
                pl.BlockSpec((states, 1), lambda b, c: (0, 0)),
                row,
                row,
                row,
                row,
                pl.BlockSpec((width, D), lambda b, c: (c[0], 0)),
                pl.BlockSpec((width, D), lambda b, c: (1 - c[0], 0)),
                square,
                square,
            ],
            out_specs=[wide] * 5 + [pl.BlockSpec((HEADS, block), lambda b, c: (0, b))],
        ),
        out_shape=[
            jax.ShapeDtypeStruct((tokens, D), F32),
            jax.ShapeDtypeStruct((tokens, D), F32),
            jax.ShapeDtypeStruct((tokens, D), BF),
            jax.ShapeDtypeStruct((tokens, D), BF),
            jax.ShapeDtypeStruct((tokens, D), BF),
            jax.ShapeDtypeStruct((HEADS, tokens), F32),
        ],
        compiler_params=pltpu.CompilerParams(vmem_limit_bytes=60 * MIB),
        cost_estimate=SMALL,
        name="cross_attention_part",
    )(
        core.reshape(1),
        x,
        own,
        got,
        text_kv,
        text_kv,
        seen,
        *[v.reshape(1, D) for v in norms],
        w_self_out,
        w_self_out,
        w_query,
        w_out,
    )


def attend_kernel(row_ref, q_ref, k_ref, v_ref, all_ref, other_ref, lse_ref, out_ref):
    length = q_ref.shape[0]
    block = QUERY_BLOCK
    scale = SCALE * LOG2E
    half = lax.broadcasted_iota(jnp.int32, (block, 2 * HEAD), 1) >= HEAD
    key_row = lax.broadcasted_iota(jnp.int32, (block, block), 0)
    query_col = lax.broadcasted_iota(jnp.int32, (block, block), 1)
    seen = key_row <= query_col
    v_flip = v_ref[...].T
    ones = jnp.ones((16, length), BF)
    v_rows = [jnp.concatenate([v_flip[h * HEAD : (h + 1) * HEAD], ones], 0) for h in range(2)]

    def score(i, h):
        lo, hi = i * block, (i + 1) * block
        queries = q_ref[lo:hi, :]
        own = jnp.where(half == (h == 1), queries, jnp.zeros_like(queries))
        return nt(k_ref[lo:hi, :], own), nt(k_ref[:lo, :], own) if i else None

    def soften(i, h, diag, rest):
        diag = jnp.where(seen, diag, MASKED)
        top = jnp.max(diag, axis=0, keepdims=True)
        if i:
            top = jnp.maximum(top, jnp.max(rest, axis=0, keepdims=True))
            rest = jnp.exp2(rest * scale - top * scale).astype(BF)
        return jnp.exp2(diag * scale - top * scale).astype(BF), rest, top * scale

    def mix(i, h, diag, rest, base):
        lo, hi = i * block, (i + 1) * block
        mixed = nn(v_rows[h][:, lo:hi], diag)
        if i:
            mixed += nn(v_rows[h][:, :lo], rest)
        total = mixed[HEAD : HEAD + 1]
        lse_ref[0, h : h + 1, lo:hi] = base + jnp.log2(total)
        return mixed[:HEAD] / total

    tasks = [(i, h) for i in range(length // block) for h in range(2)]
    scores, raised, outs = {}, {}, []
    part = length // row_ref.shape[0]
    for n in range(len(tasks) + 2):
        if n < len(tasks):
            scores[n] = score(*tasks[n])
        if 0 <= n - 1 < len(tasks):
            raised[n - 1] = soften(*tasks[n - 1], *scores.pop(n - 1))
        if n >= 2:
            outs.append(mix(*tasks[n - 2], *raised.pop(n - 2)))
        if len(outs) == 2:
            lo = tasks[n - 2][0] * block
            result = jnp.concatenate(outs, 0).T.astype(BF)
            outs = []
            for at in range(0, block, part):
                row = pl.multiple_of(row_ref[(lo + at) // part] * part, part)
                out_ref[pl.ds(row, part), :] = result[at : at + part]
    all_ref[...] = out_ref[...]
    other_ref[...] = out_ref[length // 2 :, :]


def head_specs(length, pairs):
    return [
        pl.BlockSpec((length, 2 * HEAD), lambda p, *_, s=s: (0, s * pairs + p)) for s in range(3)
    ]


def attend(joined, rows):
    length, width = joined.shape[0], joined.shape[1] // 3
    pairs = width // (2 * HEAD)
    return pl.pallas_call(
        attend_kernel,
        grid_spec=pltpu.PrefetchScalarGridSpec(
            num_scalar_prefetch=1,
            grid=(pairs,),
            in_specs=head_specs(length, pairs),
            out_specs=[
                pl.BlockSpec((length, 2 * HEAD), lambda p, *_: (0, p)),
                pl.BlockSpec((length // 2, 2 * HEAD), lambda p, *_: (0, p)),
                pl.BlockSpec((1, 2, length), lambda p, *_: (p, 0, 0)),
            ],
            scratch_shapes=[pltpu.VMEM((length, 2 * HEAD), BF)],
        ),
        out_shape=[
            jax.ShapeDtypeStruct((length, width), BF),
            jax.ShapeDtypeStruct((length // 2, width), BF),
            jax.ShapeDtypeStruct((pairs, 2, length), F32),
        ],
        compiler_params=pltpu.CompilerParams(vmem_limit_bytes=60 * MIB),
        cost_estimate=SMALL,
        name="self_attention",
    )(rows, joined, joined, joined)


def attend_back_kernel(
    row_ref,
    q_ref,
    k_ref,
    v_ref,
    own_g_ref,
    other_g_ref,
    mixed_ref,
    lse_ref,
    ordered_hbm,
    wq_ref,
    wk_ref,
    wv_ref,
    keep_ref,
    send_ref,
    own_ref,
    other_ref,
    dq_sum,
    g_ref,
    o_ref,
    ordered_ref,
    sum_ref,
    sem,
):
    pair, pairs = pl.program_id(0), pl.num_programs(0)
    load = pltpu.make_async_copy(ordered_hbm, ordered_ref, sem)

    @pl.when(pair == 0)
    def _():
        load.start()

    length = q_ref.shape[0]
    places = row_ref.shape[0]
    part = length // places
    for place in range(places):
        row = row_ref[place]
        at = pl.ds(pl.multiple_of(row % (places // 2) * part, part), part)
        to = slice(place * part, (place + 1) * part)
        mine = row < places // 2
        g_ref[to, :] = jnp.where(mine, own_g_ref[at, :], other_g_ref[at, :])
        o_ref[to, :] = mixed_ref[pl.ds(pl.multiple_of(row * part, part), part), :]
    block = QUERY_BLOCK
    scale = SCALE * LOG2E
    half = lax.broadcasted_iota(jnp.int32, (length, 2 * HEAD), 1) >= HEAD
    key_row = lax.broadcasted_iota(jnp.int32, (block, block), 0)
    query_col = lax.broadcasted_iota(jnp.int32, (block, block), 1)
    seen = key_row <= query_col
    k_flip = k_ref[...].T
    zero = jnp.zeros((length, 2 * HEAD), BF)
    queries = [jnp.where(half == (h == 1), q_ref[...], zero) for h in range(2)]
    grads = [jnp.where(half == (h == 1), g_ref[...], zero) for h in range(2)]
    product = (g_ref[...].astype(F32) * o_ref[...].astype(F32)).T
    deltas = [jnp.sum(product[h * HEAD : (h + 1) * HEAD], axis=0, keepdims=True) for h in range(2)]

    def score(j, h):
        lo, hi = j * block, (j + 1) * block
        return nt(k_ref[lo:hi, :], queries[h][lo:]), nt(v_ref[lo:hi, :], grads[h][lo:])

    def soften(j, h, scores, score_grad):
        lo, hi = j * block, (j + 1) * block
        weights = jnp.exp2(scores * scale - lse_ref[0, h : h + 1, lo:])
        first = jnp.where(seen, weights[:, :block], 0.0)
        weights = jnp.concatenate([first, weights[:, block:]], 1) if hi < length else first
        score_grad = (weights * (score_grad - deltas[h][:, lo:])).astype(BF)
        return weights.astype(BF), score_grad

    def mix(j, h, weights, score_grad):
        lo, hi = j * block, (j + 1) * block
        rows = slice(h * HEAD, (h + 1) * HEAD)
        query_part = nn(k_flip[rows, lo:hi], score_grad)
        if j == 0:
            dq_sum[rows, :] = query_part
        else:
            dq_sum[rows, lo:] += query_part
        return nn(score_grad, queries[h][lo:]), nn(weights, grads[h][lo:])

    tasks = [(j, h) for j in range(length // block) for h in range(2)]
    scores, raised, outs, key_grads, value_grads = {}, {}, [], [], []
    for n in range(len(tasks) + 2):
        if n < len(tasks):
            scores[n] = score(*tasks[n])
        if 0 <= n - 1 < len(tasks):
            raised[n - 1] = soften(*tasks[n - 1], *scores.pop(n - 1))
        if n >= 2:
            outs.append(mix(*tasks[n - 2], *raised.pop(n - 2)))
        if len(outs) == 2:
            key_grads.append(((outs[0][0] + outs[1][0]) * SCALE).astype(BF))
            value_grads.append((outs[0][1] + outs[1][1]).astype(BF))
            outs = []
    query_grad = (dq_sum[...].T * SCALE).astype(BF)
    joined = jnp.concatenate(
        [query_grad, jnp.concatenate(key_grads, 0), jnp.concatenate(value_grads, 0)], 1
    )
    weights = jnp.concatenate([wq_ref[...], wk_ref[...], wv_ref[...]], 1)
    grad = nt(joined, weights)

    @pl.when(pair == 0)
    def _():
        sum_ref[...] = grad
        load.wait()

    @pl.when(pair > 0)
    def _():
        sum_ref[...] += grad

    wide = nn(ordered_ref[...], joined).astype(BF)
    keep_ref[...] = wide[: D // 2]
    send_ref[...] = wide[D // 2 :]

    @pl.when(pair == pairs - 1)
    def _():
        for place in range(places):
            row = row_ref[place]
            at = pl.ds(pl.multiple_of(row % (places // 2) * part, part), part)
            rows = sum_ref[place * part : (place + 1) * part, :]

            @pl.when(row < places // 2)
            def _(at=at, rows=rows):
                own_ref[at, :] = rows

            @pl.when(row >= places // 2)
            def _(at=at, rows=rows):
                other_ref[at, :] = rows.astype(BF)


def attend_back(joined, own_g, other_g, mixed, lse, ordered, w_qkv, core, rows):
    length, width = joined.shape[0], joined.shape[1] // 3
    pairs = width // (2 * HEAD)
    spec = pl.BlockSpec((length, 2 * HEAD), lambda p, *_: (0, p))
    half = pl.BlockSpec((length // 2, 2 * HEAD), lambda p, *_: (0, p))
    weights = [
        pl.BlockSpec((D, 2 * HEAD), lambda p, r, s=s: (0, (2 * s + r[r.shape[0] - 1]) * pairs + p))
        for s in range(3)
    ]
    sums = pl.BlockSpec((D // 2, 6 * HEAD), lambda p, *_: (0, p))
    out = pl.BlockSpec((length // 2, D), lambda p, *_: (0, 0))
    places = rows.shape[0]

    def body(row_ref, *refs):
        attend_back_kernel(Rows(row_ref, places), *refs)

    return pl.pallas_call(
        body,
        grid_spec=pltpu.PrefetchScalarGridSpec(
            num_scalar_prefetch=1,
            grid=(pairs,),
            in_specs=head_specs(length, pairs)
            + [half] * 2
            + [spec]
            + [pl.BlockSpec((1, 2, length), lambda p, *_: (p, 0, 0))]
            + [pl.BlockSpec(memory_space=pl.ANY)]
            + weights,
            out_specs=[sums, sums, out, out],
            scratch_shapes=[
                pltpu.VMEM((2 * HEAD, length), F32),
                pltpu.VMEM((length, 2 * HEAD), BF),
                pltpu.VMEM((length, 2 * HEAD), BF),
                pltpu.VMEM((D, length), BF),
                pltpu.VMEM((length, D), F32),
                pltpu.SemaphoreType.DMA,
            ],
        ),
        out_shape=[jax.ShapeDtypeStruct((D // 2, 3 * width), BF)] * 2
        + [
            jax.ShapeDtypeStruct((length // 2, D), F32),
            jax.ShapeDtypeStruct((length // 2, D), BF),
        ],
        compiler_params=pltpu.CompilerParams(vmem_limit_bytes=60 * MIB),
        cost_estimate=SMALL,
        name="self_attention_back",
    )(
        jnp.concatenate([rows, core.reshape(1)]), joined, joined, joined, own_g, other_g,
        mixed, lse, ordered, w_qkv, w_qkv, w_qkv,
    )


def flip_kernel(block_ref, value_ref, out_ref, flip_ref):
    flip_ref[...] = value_ref[...].T
    height = D // block_ref.shape[0]
    for i in range(block_ref.shape[0]):
        at = pl.ds(pl.multiple_of(block_ref[i] * height, height), height)
        out_ref[i * height : (i + 1) * height, :] = flip_ref[at, :]


def flip_ordered(value, blocks):
    tokens = value.shape[0]
    part = 256
    return pl.pallas_call(
        flip_kernel,
        grid_spec=pltpu.PrefetchScalarGridSpec(
            num_scalar_prefetch=1,
            grid=(tokens // part,),
            in_specs=[pl.BlockSpec((part, D), lambda t, b: (t, 0))],
            out_specs=pl.BlockSpec((D, part), lambda t, b: (0, t)),
            scratch_shapes=[pltpu.VMEM((D, part), BF)],
        ),
        out_shape=jax.ShapeDtypeStruct((D, tokens), BF),
        compiler_params=pltpu.CompilerParams(vmem_limit_bytes=60 * MIB),
        cost_estimate=LARGE,
        name="flip_ordered",
    )(blocks, value)


class Rows:
    def __init__(self, ref, count):
        self.ref, self.shape = ref, (count,)

    def __getitem__(self, place):
        return self.ref[place]


def mlp_kernel(
    pieces,
    steps,
    core_ref,
    rows_from,
    goes_to,
    own_ref,
    other_ref,
    own_g_ref,
    other_g_ref,
    *refs,
):
    ups, downs = refs[:pieces], refs[pieces : 2 * pieces]
    down_ref, up_ref, out_ref, norm_ref, sent_ref, *targets = refs[2 * pieces : 2 * pieces + 9]
    flip_ref, ordered_ref, wide_ref, tall_ref, active_ref, grad_ref, sems = refs[2 * pieces + 9 :]
    step = pl.program_id(0)
    slot = step % 2
    tokens = own_ref.shape[0]
    quarter, height = targets[0].shape[0], targets[0].shape[1]
    tile = wide_ref.shape[3]
    width = 2 * height
    per_step = tile // width
    units = steps * tile

    @pl.when(step == 0)
    def _():
        flip_ref[:, :tokens] = own_ref[...].T
        flip_ref[:, tokens:] = other_ref[...].T
        for i in range(4 * quarter):
            at = pl.multiple_of(rows_from[i] * height, height)
            ordered_ref[i * height : (i + 1) * height, :] = flip_ref[pl.ds(at, height), :]

    def wide_copy(at, where, side):
        part = wide_ref.at[at, side * quarter : (side + 1) * quarter]
        lanes = pl.ds(pl.multiple_of(where * tile, tile), tile)
        return pltpu.make_async_copy(part, targets[side].at[:, :, lanes], sems.at[at, side])

    def tall_copy(at, j, r, target, i):
        rows = slice(j * width + r * height, j * width + (r + 1) * height)
        lanes = slice(units + r * D, units + (r + 1) * D)
        return pltpu.make_async_copy(
            tall_ref.at[at, rows], target.at[i, :, lanes], sems.at[at, 4 + 2 * j + r]
        )

    def wait(at):
        for side in range(4):
            wide_copy(at, 0, side).wait()
        for j in range(per_step):
            for r in range(2):
                tall_copy(at, j, r, targets[0], 0).wait()

    @pl.when((step >= 2) & (step < steps + 2))
    def _():
        wait(slot)

    @pl.when(step < steps)
    def _():
        up_w = jnp.concatenate([r[...] for r in ups], 1) if pieces > 1 else ups[0][...]
        down_w = jnp.concatenate([r[...] for r in downs], 0) if pieces > 1 else downs[0][...]
        sides = ((0, own_ref, own_g_ref), (tokens, other_ref, other_g_ref))
        cut = 256
        tasks = [(u, side) for u in range(0, tile, cut) for side in sides]
        found, active, grads = {}, {}, {}

        def products(u, side):
            _, x_ref, g_ref = side
            return nn(x_ref[...], up_w[:, u : u + cut]), nt(g_ref[...], down_w[u : u + cut])

        def units_of(n):
            u, (base, _, _) = tasks[n]
            up_value, down_grad = found.pop(n)
            value, slope = gelu_parts(up_value)
            value = value.astype(BF)
            grad = (down_grad * slope).astype(BF)
            active_ref[step, base : base + tokens, u : u + cut] = value
            grad_ref[step, base : base + tokens, u : u + cut] = grad
            active[n], grads[n] = value, grad

        def weights_of(n):
            u = tasks[n][0]
            grad = jnp.concatenate([grads.pop(n - 1), grads.pop(n)], 0)
            wide = nn(ordered_ref[...], grad).astype(BF)
            wide_ref[slot, :, :, u : u + cut] = wide.reshape(wide_ref.shape[1:3] + (cut,))
            tall = nn(active.pop(n - 1).T, own_g_ref[...]) + nn(active.pop(n).T, other_g_ref[...])
            tall_ref[slot, u : u + cut] = tall.astype(BF)

        for n in range(len(tasks) + 2):
            if n < len(tasks):
                found[n] = products(*tasks[n])
            if 0 <= n - 1 < len(tasks):
                units_of(n - 1)
            if n >= 3 and n % 2:
                weights_of(n - 2)
        for side in range(4):
            wide_copy(slot, step, side).start()
        for j in range(per_step):
            i = goes_to[step * per_step + j]
            for side, target in enumerate(targets):

                @pl.when(i // quarter == side)
                def _(j=j, i=i, side=side, target=target):
                    for r in range(2):
                        tall_copy(slot, j, r, target, i - side * quarter).start()

    @pl.when(step >= steps)
    def _():
        up = up_ref[...]
        if up.shape[1] > units:
            first = core_ref[0] == 0
            picked = []
            for at in range(0, 2 * units, 2 * width):
                picked.append(
                    jnp.where(first, up[:, at : at + width], up[:, at + width : at + 2 * width])
                )
            up = jnp.concatenate(picked, 1)
        active = jnp.concatenate([active_ref[i] for i in range(steps)], 1)
        out = nn(active, down_ref[...].reshape(units, -1))
        grad = jnp.concatenate([grad_ref[i] for i in range(steps)], 1)
        norm = nt(grad, up)
        out_ref[...] = out[:tokens]
        norm_ref[...] = norm[:tokens]
        sent_ref[0] = out[tokens:].astype(BF)
        sent_ref[1] = norm[tokens:].astype(BF)


def mlp(own, other, own_g, other_g, w_up, w_down, core, rows_from, goes_to):
    tokens = own.shape[0]
    chips = rows_from.shape[0]
    tile, out_tile = 512, 256
    units = w_up.shape[1] // 2
    steps = units // tile
    width = units // chips
    height = D // chips
    fine = width % 128 == 0
    tall = w_down.reshape(chips, 2, width, D)
    if fine:
        pieces, piece = tile // width, width
    else:
        pieces, piece = 1, tile
        w_up = w_up.reshape(D, chips, 2, width)[:, :, core].reshape(D, units)
        w_down = w_down.reshape(chips, 2, width, D)[:, core].reshape(units, D)

    def place(s, c, j):
        s = jnp.minimum(s, steps - 1)
        return 2 * (s * pieces + j) + c[0] if fine else s

    def column(s):
        return jnp.maximum(s - steps, 0)

    whole = pl.BlockSpec((tokens, D), lambda s, *_: (0, 0))
    up_specs = [
        pl.BlockSpec((D, piece), lambda s, c, *_, j=j: (0, place(s, c, j))) for j in range(pieces)
    ]
    down_specs = [
        pl.BlockSpec((piece, D), lambda s, c, *_, j=j: (place(s, c, j), 0)) for j in range(pieces)
    ]
    kept = pl.BlockSpec((tokens, out_tile), lambda s, *_: (0, column(s)))
    sums = jax.ShapeDtypeStruct((chips // 4, height, units + 2 * D), BF)
    return pl.pallas_call(
        partial(mlp_kernel, pieces, steps),
        grid_spec=pltpu.PrefetchScalarGridSpec(
            num_scalar_prefetch=3,
            grid=(steps + D // out_tile,),
            in_specs=[whole] * 4
            + up_specs
            + down_specs
            + [
                pl.BlockSpec((chips, None, width, out_tile), lambda s, c, *_: (0, c[0], 0, column(s))),
                pl.BlockSpec((out_tile, w_up.shape[1]), lambda s, *_: (column(s), 0)),
            ],
            out_specs=[
                kept,
                kept,
                pl.BlockSpec((2, tokens, out_tile), lambda s, *_: (0, 0, column(s))),
            ]
            + [pl.BlockSpec(memory_space=pl.ANY)] * 4,
            scratch_shapes=[
                pltpu.VMEM((D, 2 * tokens), BF),
                pltpu.VMEM((D, 2 * tokens), BF),
                pltpu.VMEM((2, chips, height, tile), BF),
                pltpu.VMEM((2, tile, D), BF),
                pltpu.VMEM((steps, 2 * tokens, tile), BF),
                pltpu.VMEM((steps, 2 * tokens, tile), BF),
                pltpu.SemaphoreType.DMA((2, 4 + 2 * (tile // width))),
            ],
        ),
        out_shape=[
            jax.ShapeDtypeStruct((tokens, D), F32),
            jax.ShapeDtypeStruct((tokens, D), F32),
            jax.ShapeDtypeStruct((2, tokens, D), BF),
            sums,
            sums,
            sums,
            sums,
        ],
        compiler_params=pltpu.CompilerParams(vmem_limit_bytes=60 * MIB),
        cost_estimate=SMALL,
        name="mlp_both_ways",
    )(
        core.reshape(1),
        rows_from,
        goes_to,
        own,
        other,
        own_g,
        other_g,
        *([w_up] * pieces),
        *([w_down] * pieces),
        tall,
        w_up,
    )


def cross_back_kernel(
    scalars,
    order_ref,
    got_ref,
    grad3_ref,
    hidden2_ref,
    g_ref,
    gain3_ref,
    gain2_ref,
    seen_ref,
    lse_ref,
    keys_ref,
    values_ref,
    states_ref,
    mixed_hbm,
    w_out_hbm,
    queries_hbm,
    w_query_hbm,
    hidden1_hbm,
    own_hbm,
    other_hbm,
    w_self_hbm,
    out_hbm,
    got_hbm,
    block_ref,
    hidden_grad_ref,
    own_grad_ref,
    other_grad_ref,
    text_ref,
    norms_ref,
    states_flip_ref,
    keep,
    send,
    mixed_ref,
    w_out_ref,
    queries_ref,
    w_query,
    hidden1,
    own_ref,
    other_ref,
    w_self,
    out_ref,
    out_got_ref,
    flip_ref,
    ordered_ref,
    keep_stage,
    send_stage,
    sems,
    out_sems,
):
    core = scalars[0]
    tokens = grad3_ref.shape[0]
    loads = [
        pltpu.make_async_copy(a, b, sems.at[i])
        for i, (a, b) in enumerate(
            (
                (mixed_hbm, mixed_ref),
                (w_out_hbm, w_out_ref),
                (queries_hbm, queries_ref),
                (w_query_hbm, w_query),
                (hidden1_hbm, hidden1),
                (own_hbm.at[:tokens], own_ref),
                (other_hbm, other_ref),
                (w_self_hbm, w_self),
                (out_hbm, out_ref),
                (got_hbm.at[0], out_got_ref),
            )
        )
    ]
    for load in loads:
        load.start()
    count = order_ref.shape[0]
    rows = D // count
    half = D // 2
    writes = []

    def order(depth):
        for i in range(count):
            at = pl.multiple_of(order_ref[i] * rows, rows)
            ordered_ref[i * rows : (i + 1) * rows, :depth] = flip_ref[pl.ds(at, rows), :depth]

    def write(slot, grads):
        keep_stage[slot] = ordered_ref[half:, :tokens].astype(BF)
        lane = slot * (tokens + D)
        lanes = slice(lane, lane + tokens + D)
        send_stage[:, lane : lane + tokens] = ordered_ref[:half, :tokens].astype(BF)
        send_stage[:, lane + tokens : lane + tokens + D] = grads
        writes.append(
            pltpu.make_async_copy(send_stage.at[:, lanes], send.at[:, lanes], out_sems.at[slot])
        )
        writes.append(
            pltpu.make_async_copy(keep_stage.at[slot], keep.at[slot], out_sems.at[4 + slot])
        )
        for copy in writes[-2:]:
            copy.start()

    kind = flip_ref.dtype
    loads[0].wait()
    flip_ref[:, :tokens] = mixed_ref[...].astype(kind).T
    hidden2 = hidden2_ref[...]
    grad3 = grad3_ref[...] + got_ref[...].astype(F32)
    unit, rstd = norm_parts(hidden2)
    norms_ref[4:5, :] = jnp.sum(grad3 * unit, axis=0, keepdims=True)
    norms_ref[5:6, :] = jnp.sum(grad3, axis=0, keepdims=True)
    norms_ref[6:8, :] = jnp.zeros((2, D), F32)
    grad_hidden = norm_back(unit, rstd, gain3_ref[...], grad3) + g_ref[...].astype(F32)
    hidden_grad_ref[...] = grad_hidden
    branch = grad_hidden.astype(BF)
    order(tokens)
    write(0, branch)
    loads[1].wait()
    grad_mixed = nt(branch, w_out_ref[...]).astype(BF)
    loads[2].wait()
    states = keys_ref.shape[0]
    half_lane = lax.broadcasted_iota(jnp.int32, (tokens, 2 * HEAD), 1) >= HEAD
    zero = jnp.zeros((tokens, 2 * HEAD), BF)
    k_flip = keys_ref[...].T

    def score(head):
        lanes = slice(head // 2 * 2 * HEAD, (head // 2 + 1) * 2 * HEAD)
        mine = half_lane == (head % 2 == 1)
        own_q = jnp.where(mine, queries_ref[:, lanes], zero)
        own_g = jnp.where(mine, grad_mixed[:, lanes], zero)
        return nt(keys_ref[:, lanes], own_q), nt(values_ref[:, lanes], own_g), own_q, own_g

    def soften(head, scores, score_grad, own_q, own_g):
        scores = scores * (SCALE * LOG2E) + seen_ref[...]
        weights = jnp.exp2(scores - lse_ref[head : head + 1, :])
        delta = jnp.sum(weights * score_grad, axis=0, keepdims=True)
        score_grad = (weights * (score_grad - delta)).astype(BF)
        return weights.astype(BF), score_grad, own_q, own_g

    scores, raised, flips, key_grads, value_grads = {}, {}, [], [], []
    for n in range(HEADS + 2):
        if n < HEADS:
            scores[n] = score(n)
        if 0 <= n - 1 < HEADS:
            raised[n - 1] = soften(n - 1, *scores.pop(n - 1))
        if n >= 2:
            head = n - 2
            weights, score_grad, own_q, own_g = raised.pop(head)
            key_part, value_part = nn(score_grad, own_q), nn(weights, own_g)
            if head % 2 == 0:
                key_grads.append(key_part)
                value_grads.append(value_part)
            else:
                key_grads[-1] += key_part
                value_grads[-1] += value_part
            part = nn(k_flip[head * HEAD : (head + 1) * HEAD], score_grad)
            flips.append((part * SCALE).astype(BF))
    query_grad = jnp.concatenate(flips, 0).T
    text_grad = jnp.concatenate([p * SCALE for p in key_grads] + value_grads, 1).astype(BF)
    text_ref[...] = text_grad
    flip_ref[:, :states] = states_ref[...].astype(kind).T
    order(states)
    states_flip_ref[...] = ordered_ref[half:, :states].astype(BF)
    part = states * 2 * D // half
    for i in range(half // states):
        send_stage[i * states : (i + 1) * states, 3 * (tokens + D) :] = text_grad[
            :, i * part : (i + 1) * part
        ]
    lanes = slice(3 * (tokens + D), 3 * (tokens + D) + part)
    writes.append(
        pltpu.make_async_copy(send_stage.at[:, lanes], send.at[:, lanes], out_sems.at[3])
    )
    writes[-1].start()
    for load in loads[3:5]:
        load.wait()
    grad2 = nt(query_grad, w_query[...])
    unit, rstd = norm_parts(hidden1[...])
    normed2 = unit * gain2_ref[0:1, :] + gain2_ref[1:2, :]
    flip_ref[:, :tokens] = normed2.astype(BF).astype(kind).T
    order(tokens)
    write(1, query_grad)
    norms_ref[2:3, :] = jnp.sum(grad2 * unit, axis=0, keepdims=True)
    norms_ref[3:4, :] = jnp.sum(grad2, axis=0, keepdims=True)
    norms_ref[0:2, :] = jnp.zeros((2, D), F32)
    grad_hidden = norm_back(unit, rstd, gain2_ref[0:1, :], grad2) + hidden_grad_ref[...]
    hidden_grad_ref[...] = grad_hidden
    branch = grad_hidden.astype(BF)
    for load in loads[5:8]:
        load.wait()
    own_rows = pl.ds(pl.multiple_of(core * half, half), half)
    other_rows = pl.ds(pl.multiple_of((1 - core) * half, half), half)
    own_grad_ref[...] = nt(branch, w_self[own_rows, :]).astype(BF)
    other_grad_ref[...] = nt(branch, w_self[other_rows, :]).astype(BF)
    flip_ref[own_rows, :tokens] = own_ref[...].astype(kind).T
    flip_ref[other_rows, :tokens] = other_ref[...].astype(kind).T
    order(tokens)
    write(2, branch)
    for load in loads[8:]:
        load.wait()
    block_ref[...] = (hidden2_ref[...] + out_ref[...] + out_got_ref[...].astype(F32)).astype(BF)
    for copy in writes:
        copy.wait()


def cross_back(
    out, got, grad3, hidden2, g, norms, seen, lse, mixed, w_out, text_kv, queries, states,
    w_query, hidden1, own, other, w_self, core, order,
):
    tokens, width = other.shape
    count = order.shape[0]
    texts = states.shape[0]
    kind = BF if (D // count) % 16 == 0 else F32

    def full(*shape):
        return pl.BlockSpec(shape, lambda b, *_: (0,) * len(shape))

    wide, late = full(tokens, D), pl.BlockSpec(memory_space=pl.ANY)
    return pl.pallas_call(
        cross_back_kernel,
        grid_spec=pltpu.PrefetchScalarGridSpec(
            num_scalar_prefetch=2,
            grid=(1,),
            in_specs=[
                pl.BlockSpec((None, tokens, D), lambda b, *_: (1, 0, 0)),
                wide,
                wide,
                wide,
                full(1, D),
                full(2, D),
                full(texts, 1),
                full(HEADS, tokens),
                full(texts, D),
                pl.BlockSpec((texts, D), lambda b, *_: (0, 1)),
                full(texts, D),
            ]
            + [late] * 10,
            out_specs=[
                wide,
                wide,
                full(tokens, width),
                full(tokens, width),
                full(texts, 2 * D),
                full(8, D),
                full(D // 2, texts),
                late,
                late,
            ],
            scratch_shapes=[
                pltpu.VMEM((tokens, D), BF),
                pltpu.VMEM((D, D), BF),
                pltpu.VMEM((tokens, D), BF),
                pltpu.VMEM((D, D), BF),
                pltpu.VMEM((tokens, D), F32),
                pltpu.VMEM((tokens, width), BF),
                pltpu.VMEM((tokens, width), BF),
                pltpu.VMEM((D, D), BF),
                pltpu.VMEM((tokens, D), F32),
                pltpu.VMEM((tokens, D), BF),
                pltpu.VMEM((D, tokens), kind),
                pltpu.VMEM((D, tokens), kind),
                pltpu.VMEM((3, D // 2, tokens), BF),
                pltpu.VMEM((D // 2, 3 * (tokens + D) + 4 * texts), BF),
                pltpu.SemaphoreType.DMA((10,)),
                pltpu.SemaphoreType.DMA((7,)),
            ],
        ),
        out_shape=[
            jax.ShapeDtypeStruct((tokens, D), BF),
            jax.ShapeDtypeStruct((tokens, D), F32),
            jax.ShapeDtypeStruct((tokens, width), BF),
            jax.ShapeDtypeStruct((tokens, width), BF),
            jax.ShapeDtypeStruct((texts, 2 * D), BF),
            jax.ShapeDtypeStruct((8, D), F32),
            jax.ShapeDtypeStruct((D // 2, texts), BF),
            jax.ShapeDtypeStruct((3, D // 2, tokens), BF),
            jax.ShapeDtypeStruct((D // 2, 3 * (tokens + D) + 4 * texts), BF),
        ],
        compiler_params=pltpu.CompilerParams(vmem_limit_bytes=60 * MIB),
        cost_estimate=SMALL,
        name="cross_attention_back",
    )(
        core.reshape(1), order, got, grad3, hidden2, g, norms[2].reshape(1, D),
        jnp.stack(norms[:2]), seen, lse, text_kv, text_kv, states, mixed, w_out, queries,
        w_query, hidden1, own, other, w_self, out, got,
    )


def pair_kernel(keep_ref, own_ref, got_ref, states_ref, grad_ref, grad_got_ref, *outs):
    first_ref, second_ref, text_ref = outs
    step = pl.program_id(0)
    half, tokens = keep_ref.shape
    texts = grad_ref.shape[0]

    def put(product):
        first_ref[...] = product[: half // 2].astype(BF)
        second_ref[...] = product[half // 2 :].astype(BF)

    @pl.when(step < 3)
    def _():
        product = nn(keep_ref[...], own_ref[:, tokens:])
        put(product + nn(got_ref[:, :tokens], got_ref[:, tokens:]))

    @pl.when(step >= 3)
    def _():
        got = grad_got_ref[...].astype(F32)
        got = jnp.concatenate([got[:texts], got[texts:]], 1)
        got = jnp.concatenate([got[texts // 2 :], got[: texts // 2]], 0)
        grad = (grad_ref[...].astype(F32) + got).astype(BF)
        text_ref[...] = grad[: texts // 2]
        put(nn(states_ref[...], grad))


def pair_gradients(keep, own, got, states, grad):
    _, half, tokens = keep.shape
    texts = grad.shape[0]

    def third(s):
        return jnp.minimum(s, 2)

    def later(s):
        return jnp.maximum(s - 3, 0)

    wide = pl.BlockSpec((half, tokens + D), lambda s: (0, third(s)))
    lane = 3 * (tokens + D) // (4 * texts)
    grads = pl.BlockSpec((texts, D), lambda s: (0, later(s)))
    out = pl.BlockSpec((half // 2, D), lambda s: (0, s))
    return pl.pallas_call(
        pair_kernel,
        grid=(5,),
        in_specs=[
            pl.BlockSpec((None, half, tokens), lambda s: (third(s), 0, 0)),
            wide,
            wide,
            pl.BlockSpec((half, texts), lambda s: (0, 0)),
            grads,
            pl.BlockSpec((2 * texts, 4 * texts), lambda s: (later(s), lane)),
        ],
        out_specs=[out, out, pl.BlockSpec((texts // 2, D), lambda s: (0, later(s)))],
        out_shape=[jax.ShapeDtypeStruct((half // 2, 5 * D), BF)] * 2
        + [jax.ShapeDtypeStruct((texts // 2, 2 * D), BF)],
        compiler_params=pltpu.CompilerParams(vmem_limit_bytes=60 * MIB),
        cost_estimate=SMALL,
        name="pair_gradients",
    )(keep, own, got, states, grad, got)


def last_kernel(
    blocks_ref,
    x_ref,
    part_ref,
    got_ref,
    hidden_ref,
    gain_ref,
    norms_ref,
    image_ref,
    keep,
    send,
    norm_flip,
):
    count = blocks_ref.shape[0]
    height, half = D // count, D // 2
    grad = part_ref[...] + got_ref[...].astype(F32)
    unit, rstd = norm_parts(x_ref[...].astype(F32))
    sums = [jnp.sum(grad * unit, axis=0, keepdims=True), jnp.sum(grad, axis=0, keepdims=True)]
    image = norm_back(unit, rstd, gain_ref[...], grad) + hidden_ref[...]
    image_ref[...] = image.astype(BF)
    fill = jnp.zeros((norm_flip.shape[1] - 8, D), F32)
    norm_flip[...] = jnp.concatenate(sums + [norms_ref[2:8, :], fill], 0).T
    for i in range(count):
        at = pl.ds(pl.multiple_of(blocks_ref[i] * height, height), height)
        to = i * height % half
        target = keep if i < count // 2 else send
        target[to : to + height, :] = norm_flip[at, :].astype(BF)


def last_part(x, part, got, hidden_grad, gain, norms, blocks):
    tokens = got.shape[0]

    def full(*shape):
        return pl.BlockSpec(shape, lambda b, *_: (0,) * len(shape))

    wide = full(tokens, D)
    return pl.pallas_call(
        last_kernel,
        grid_spec=pltpu.PrefetchScalarGridSpec(
            num_scalar_prefetch=1,
            grid=(1,),
            in_specs=[wide] * 4 + [full(1, D), full(8, D)],
            out_specs=[wide, full(D // 2, 128), full(D // 2, 128)],
            scratch_shapes=[pltpu.VMEM((D, 128), F32)],
        ),
        out_shape=[jax.ShapeDtypeStruct((tokens, D), BF)]
        + [jax.ShapeDtypeStruct((D // 2, 128), BF)] * 2,
        compiler_params=pltpu.CompilerParams(vmem_limit_bytes=60 * MIB),
        cost_estimate=SMALL,
        name="norm_back",
    )(blocks, x, part, got, hidden_grad, gain.reshape(1, D), norms)


def add_kernel(a_ref, b_ref, keep_ref, send_ref):
    block, half = pl.program_id(0), pl.num_programs(0) // 2
    total = a_ref[...] + b_ref[...]

    @pl.when(block < half)
    def _():
        send_ref[...] = total

    @pl.when(block >= half)
    def _():
        keep_ref[...] = total


def add_halves(a, b):
    count, height, width = a.shape
    blocks = 4
    half = blocks // 2
    shape = (count // blocks, height, width)
    turned = pl.BlockSpec(shape, lambda i: ((i + half) % blocks, 0, 0))
    return pl.pallas_call(
        add_kernel,
        grid=(blocks,),
        in_specs=[turned] * 2,
        out_specs=[
            pl.BlockSpec(shape, lambda i: (jnp.maximum(i - half, 0), 0, 0)),
            pl.BlockSpec(shape, lambda i: (jnp.minimum(i, half - 1), 0, 0)),
        ],
        out_shape=[jax.ShapeDtypeStruct((count // 2, height, width), BF)] * 2,
        compiler_params=pltpu.CompilerParams(vmem_limit_bytes=60 * MIB),
        cost_estimate=SMALL,
        name="add_halves",
    )(a, b)


def sum_kernel(a_ref, b_ref, sum_ref):
    sum_ref[...] = a_ref[...] + b_ref[...]


def add_rounded(a, b):
    spec = pl.BlockSpec((a.shape[0] // 4,) + a.shape[1:], lambda i: (i, 0, 0))
    return pl.pallas_call(
        sum_kernel,
        grid=(4,),
        in_specs=[spec] * 2,
        out_specs=spec,
        out_shape=jax.ShapeDtypeStruct(a.shape, BF),
        compiler_params=pltpu.CompilerParams(vmem_limit_bytes=60 * MIB),
        cost_estimate=SMALL,
        name="add_rounded",
    )(a, b)


def behind(value, *others):
    return lax.optimization_barrier((value,) + others)[0]


class Route:
    def __init__(self, plan, orders):
        self.orders = orders
        count = plan.chips
        maps = np.zeros((2, count), np.int32)
        for core in range(2):
            for i in range(count):
                for s, bit in enumerate(orders[core]):
                    maps[core, i] |= ((i >> (plan.levels - 1 - s)) & 1) << bit
        here, there = jnp.asarray(maps)[plan.core], jnp.asarray(maps)[1 - plan.core]
        self.blocks = jnp.bitwise_xor(plan.chip, here).astype(jnp.int32)
        sent = jnp.bitwise_xor(plan.chip, there).astype(jnp.int32)
        self.devices = jnp.concatenate([2 * sent + 1 - plan.core, 2 * self.blocks + plan.core])
        backs = np.argsort(maps, axis=1).astype(np.int32)
        away = jnp.bitwise_xor(plan.chip, jnp.arange(count, dtype=jnp.int32))
        self.goes_to = jnp.take(jnp.asarray(backs)[plan.core], away, mode="clip")


class Plan:
    def __init__(self, n_img, n_txt):
        self.n_txt = n_txt
        self.n = n_img * n_txt
        self.chips = self.n // 2
        self.ny = n_txt // 2
        self.levels = self.chips.bit_length() - 1
        self.me = lax.axis_index("img") * n_txt + lax.axis_index("txt")
        self.core = self.me % 2
        self.chip = self.me // 2
        self.y = lax.axis_index("txt") // 2
        sources = (self.y - jnp.arange(self.ny, dtype=jnp.int32)) % self.ny
        self.places = jnp.concatenate([2 * sources + self.core, 2 * sources + 1 - self.core])
        at = jnp.arange(n_txt, dtype=jnp.int32)
        self.rows = jnp.bitwise_xor(at % 2, self.core) * self.ny + (self.y - at // 2) % self.ny
        rest = list(range(2, self.levels))
        self.near = Route(self, ([1, 0] + rest, [0, 1] + rest))
        self.mixed = Route(self, ([1, 0] + rest, rest + [0, 1]))
        self.token = None

    def swap(self, value):
        return lax.ppermute(value, BOTH, [(d, d ^ 1) for d in range(self.n)])

    def shift_y(self, value, by):
        pairs = []
        for d in range(self.n):
            img, txt = divmod(d, self.n_txt)
            y, core = divmod(txt, 2)
            pairs.append((d, img * self.n_txt + ((y + by) % self.ny) * 2 + core))
        return lax.ppermute(value, BOTH, pairs)

    def halve(self, value, route, step):
        pairs = [(d, d ^ (2 << route.orders[d % 2][step])) for d in range(self.n)]
        return lax.ppermute(value, BOTH, pairs)

    def send_items(self, value, note=None):
        parts = []
        for k in range(self.ny):
            part = value[(self.y + k) % self.ny]
            if note is not None:
                part = jnp.concatenate([part, note], 0)
            parts.append(self.shift_y(part, k) if k else part)
        return parts

    def join_items(self, parts, length):
        notes = [p[length:] for p in parts] if parts[0].shape[0] > length else []
        return jnp.concatenate([p[:length] for p in parts] + notes, 0)

    def return_items(self, value):
        return [self.shift_y(value[k], -k) if k else value[0] for k in range(self.ny)]

    def order_items(self, parts):
        stacked = jnp.stack(parts)
        return jnp.stack([stacked[(i - self.y) % self.ny] for i in range(self.ny)])

    def start(self, keep, send, route, step=0):
        return keep, self.halve(send, route, step), route, step

    def quarter(self, value, route, k):
        pairs = []
        for d in range(self.n):
            first, second = route.orders[d % 2][:2]
            pairs.append((d, d ^ ((2 << first) * (k >> 1)) ^ ((2 << second) * (k & 1))))
        return lax.ppermute(value, BOTH, pairs)

    def advance(self, state, *joining):
        keep, got, route, step = state
        keep, got, _, *joining = lax.optimization_barrier((keep, got, self.token, *joining))
        if keep.shape[0] == 1:
            self.token = keep[0].astype(F32) + got[0].astype(F32)
            return self.token
        if keep.size > 1 << 20:
            keep, send = add_halves(keep, got)
        else:
            total = (keep.astype(F32) + got.astype(F32)).astype(BF)
            if joining:
                joined = sum((v.astype(F32) for v in joining[1:]), joining[0].astype(F32))
                total = jnp.concatenate([total, joined.astype(BF)], -1)
            keep, send = jnp.split(total, 2)
        keep, send = lax.optimization_barrier((keep, send))
        self.token = send
        return self.start(keep, send, route, step + 1)

    def then(self, *values):
        return lax.optimization_barrier(values + (self.token,))[:-1]


def per_device(
    n_img,
    n_txt,
    image_tokens,
    text_states,
    text_segments,
    item_segments,
    norm1_gain,
    norm1_bias,
    w_qkv,
    w_self_out,
    norm2_gain,
    norm2_bias,
    w_cross_q,
    w_cross_kv,
    w_cross_out,
    norm3_gain,
    norm3_bias,
    w_up,
    w_down,
    cotangent,
):
    plan = Plan(n_img, n_txt)
    core, n, chips, ny = plan.core, plan.n, plan.chips, plan.ny
    items, length, _ = image_tokens.shape
    tokens = items * length
    half_d = D // 2
    rows = D // n

    states = text_states.shape[1]
    ids = jnp.pad(text_segments.astype(BF), ((0, 15), (0, D - states)))
    note = jnp.concatenate([text_states[0], ids], 0)
    x_parts = plan.send_items(image_tokens, note)
    g_parts = plan.send_items(behind(cotangent, x_parts[-1]))
    x_own = plan.join_items(x_parts, length)
    x_other = plan.swap(x_own)

    notes = [v[tokens:].reshape(ny, states + 16, D) for v in (x_own, x_other)]
    notes = jnp.concatenate(notes, 0)
    ids = notes[:, states, :states].reshape(-1)
    states_all = notes[:, :states].reshape(-1, D)
    text_kv = nn(states_all, w_cross_kv).astype(BF)
    matches = ids == item_segments[0, plan.y].astype(BF)
    seen = jnp.where(matches, 0.0, MASKED).astype(F32)[:, None]

    joined, normed1 = project_all(
        x_own, x_other, norm1_gain, norm1_bias, w_qkv, core, plan.places, length
    )
    mixed, mixed_other, lse = attend(joined, plan.rows)
    mixed_got = plan.swap(mixed_other)
    g_own = plan.join_items([behind(p, mixed_got) for p in g_parts], length)
    g_other = plan.swap(g_own)

    norms = (norm2_gain, norm2_bias, norm3_gain, norm3_bias)
    hidden1, hidden2, normed3, cross_q, cross_mixed, cross_lse = cross_part(
        x_own,
        mixed,
        mixed_got,
        text_kv,
        seen,
        norms,
        w_self_out,
        w_cross_q,
        w_cross_out,
        core,
    )

    normed3_other = plan.swap(normed3)
    per_down = w_down.shape[0] // n
    out, grad3, sent, low_keep, high_keep, low_send, high_send = mlp(
        normed3,
        normed3_other,
        g_own,
        g_other,
        w_up,
        w_down,
        core,
        plan.mixed.blocks,
        plan.mixed.goes_to,
    )
    high_got = plan.halve(high_send, plan.mixed, 0)
    got = plan.swap(sent)


    block_out, grad_hidden1, grad_own, grad_other, grad_kv, norm_sums, states_flip, keep, send = (
        cross_back(
            out, got, grad3, hidden2, g_own, norms[:3], seen, cross_lse, cross_mixed, w_cross_out,
            text_kv, cross_q, states_all, w_cross_q, hidden1, mixed, mixed_got, w_self_out,
            core, plan.near.devices,
        )
    )
    grad_other, high_got = lax.optimization_barrier((grad_other, high_got))
    grad_got = plan.swap(grad_other)
    pair_got = plan.swap(behind(send, grad_got))
    plan.token = grad_other
    high_keep, high_got = plan.then(high_keep, high_got)
    low_got = plan.halve(behind(low_send, high_got), plan.mixed, 0)
    high_sum = add_rounded(high_keep, high_got)
    plan.token = high_sum
    next_got = plan.halve(high_sum, plan.mixed, 1)
    block_parts = plan.return_items(block_out.reshape(ny, length, D))
    (normed1,) = plan.then(normed1)
    plan.token = ordered1 = flip_ordered(normed1, plan.near.blocks)
    send, pair_got = plan.then(send, pair_got)
    middle_keep, middle_send, text_sum = pair_gradients(
        keep, send, pair_got, states_flip, grad_kv
    )
    plan.token = middle_send
    middle_sums = plan.start(
        middle_keep.reshape(chips // 2, rows, -1),
        middle_send.reshape(chips // 2, rows, -1),
        plan.near,
    )

    grad_got, grad_own = plan.then(grad_got, grad_own)
    last_keep, last_send, part_own, part_other = attend_back(
        joined, grad_own, grad_got, mixed, lse, ordered1, w_qkv, core, plan.rows
    )
    plan.token = part_other
    last_sums = plan.start(
        last_keep.reshape(chips // 2, 2 * rows, -1),
        last_send.reshape(chips // 2, 2 * rows, -1),
        plan.near,
    )
    part_got = plan.swap(part_other)
    low_keep, low_got, next_got, *block_parts = plan.then(
        low_keep, low_got, next_got, *block_parts
    )
    low_sum = low_keep.astype(F32) + low_got.astype(F32) + next_got.astype(F32)
    plan.token = low_sum = lax.optimization_barrier(low_sum.astype(BF))
    low_keep, low_send = jnp.split(low_sum, 2)
    mlp_sums = plan.start(low_keep, low_send, plan.mixed, 2)
    middle_sums = plan.advance(middle_sums)
    part_got, part_own = plan.then(part_got, part_own)
    image_grad, norm_keep, norm_send = last_part(
        x_own, part_own, part_got, grad_hidden1, norm1_gain, norm_sums, plan.near.blocks
    )
    plan.token = norm_send
    norm_quarters = jnp.concatenate([norm_keep, norm_send], 0).reshape(4, chips // 4, 2 * rows, -1)
    norm_got = [plan.quarter(norm_quarters[k], plan.near, k) for k in range(1, 4)]
    last_sums = plan.advance(last_sums)
    middle_sums = plan.advance(middle_sums)
    last_sums = plan.advance(last_sums, norm_quarters[0], *norm_got)
    mlp_sums = plan.advance(mlp_sums)
    text_sum, image_grad = plan.then(text_sum, image_grad)
    text_part = nt(text_sum, w_cross_kv)
    plan.token = text_part
    text_part = text_part.reshape(ny, states, D)
    text_parts = [plan.shift_y(text_part[r].astype(BF), -r) for r in range(1, ny)]
    image_parts = plan.return_items(image_grad.reshape(ny, length, D))
    for _ in range(plan.levels - 3):
        middle_sums = plan.advance(middle_sums)
        last_sums = plan.advance(last_sums)
        mlp_sums = plan.advance(mlp_sums)
    middle_sums = plan.advance(middle_sums)
    last_sums = plan.advance(last_sums)
    up_down = mlp_sums

    units = w_up.shape[1] // 2
    down_grad = jnp.concatenate([up_down[:, units : units + D], up_down[:, units + D :]], 0)
    parts = jnp.concatenate([up_down[:, :units], last_sums], 1).reshape(2, rows, -1)
    mine = parts[core]
    sent = parts[1 - core].astype(BF)
    theirs = plan.swap(sent).astype(F32)
    (theirs,) = plan.then(theirs)
    text_part, *text_parts = plan.then(text_part, *text_parts)
    text_grad = sum((p.astype(F32) for p in text_parts), text_part[0])
    image_grad = plan.order_items(plan.then(*image_parts)).astype(F32)
    plan.token = image_grad
    block_out = plan.order_items(plan.then(*block_parts))
    by_core = jnp.where(core == 0, jnp.stack([mine, theirs]), jnp.stack([theirs, mine]))
    up_grad = by_core[:, :, :units].reshape(2, rows, chips, per_down)
    up_grad = up_grad.transpose(1, 2, 0, 3).reshape(rows, 2 * units)
    wide = by_core[:, :, units : units + 3 * half_d].reshape(2, rows, -1, 3, 2 * HEAD)
    wide = wide.transpose(1, 3, 0, 2, 4).reshape(rows, 3 * D)
    norm_sums = mine[:, -128:-122] + theirs[:, -128:-122]
    return (
        block_out,
        image_grad,
        text_grad[None],
        norm_sums[:, 0],
        norm_sums[:, 1],
        wide,
        middle_sums[:, 2 * D : 3 * D],
        norm_sums[:, 2],
        norm_sums[:, 3],
        middle_sums[:, D : 2 * D],
        middle_sums[:, 3 * D :],
        middle_sums[:, :D],
        norm_sums[:, 4],
        norm_sums[:, 5],
        up_grad,
        down_grad,
    )


def solution(mesh):
    split = P("img", "txt", None)
    rows = P(BOTH)
    wide = P(BOTH, None)
    return jax.shard_map(
        partial(per_device, mesh.shape["img"], mesh.shape["txt"]),
        mesh=mesh,
        in_specs=(split, split, P("img", "txt"), P("img", None)) + (P(),) * 13 + (split,),
        out_specs=(
            (split,) * 3
            + (rows, rows, wide, wide)
            + (rows, rows, wide, wide, wide)
            + (rows, rows, wide, wide)
        ),
        check_vma=False,
    )
```

```python
from functools import partial

import jax
import jax.numpy as jnp
import numpy as np
from jax import lax
from jax.experimental import pallas as pl
from jax.experimental.pallas import tpu as pltpu
from jax.sharding import PartitionSpec as P

D = 1024
HEADS = 16
HEAD = 64
EPS = 1e-05
MASKED = -1e30
SCALE = HEAD**-0.5
LOG2E = 1.4426950408889634
BOTH = ("img", "txt")
BF = jnp.bfloat16
F32 = jnp.float32
QUERY_BLOCK = 256
MIB = 1 << 20
SMALL = pl.CostEstimate(flops=1 << 20, bytes_accessed=1 << 16, transcendentals=0)


def nn(a, b):
    return lax.dot_general(a, b, (((1,), (0,)), ((), ())), preferred_element_type=F32)


def nt(a, b):
    return lax.dot_general(a, b, (((1,), (1,)), ((), ())), preferred_element_type=F32)


def tn(a, b):
    return lax.dot_general(a, b, (((0,), (0,)), ((), ())), preferred_element_type=F32)


def norm_parts(values):
    center = values - jnp.mean(values, axis=-1, keepdims=True)
    rstd = lax.rsqrt(jnp.mean(center * center, axis=-1, keepdims=True) + EPS)
    return center * rstd, rstd


def norm_back(unit, rstd, gain, grad):
    scaled = grad * gain
    return rstd * (
        scaled
        - jnp.mean(scaled, axis=-1, keepdims=True)
        - unit * jnp.mean(scaled * unit, axis=-1, keepdims=True)
    )


TAIL = [
    0.5 * c
    for c in (
        -0.22753805372107494,
        0.8866680711331851,
        -0.6354061073102151,
        0.6495639241196378,
        0.09138668583849363,
        0.235325478247137,
    )
]


def gelu_parts(value):
    t = 1.0 / (1.0 + (0.39 * 0.5**0.5) * jnp.abs(value))
    bell = jnp.exp2(value * value * (-0.5 * LOG2E))
    tail = jnp.full_like(t, TAIL[0])
    for term in TAIL[1:]:
        tail = tail * t + term
    tail = tail * t * bell
    cdf = jnp.where(value > 0.0, 1.0 - tail, tail)
    return value * cdf, cdf + value * bell * (0.5 / np.pi) ** 0.5


def project_kernel(
    core_ref, place_ref, own_ref, other_ref, gain_ref, bias_ref, wq_ref, wk_ref, wv_ref, *refs
):
    joined_ref, normed_ref, held_ref = refs
    block, own_blocks = pl.program_id(0), (pl.num_programs(0) - 1) // 2
    slot = block % 2
    width = wq_ref.shape[1]
    before = held_ref[1 - slot]
    normed_ref[...] = before
    for s, w_ref in enumerate((wq_ref, wk_ref, wv_ref)):
        joined_ref[:, s * width : (s + 1) * width] = nn(before, w_ref[...]).astype(BF)
    tokens = jnp.where(block < own_blocks, own_ref[...], other_ref[...]).astype(F32)
    unit, _ = norm_parts(tokens)
    held_ref[slot] = (unit * gain_ref[...] + bias_ref[...]).astype(BF)


def project_all(own, other, gain, bias, w_qkv, core, places, length):
    blocks = places.shape[0]
    half = blocks // 2
    width = D // 2
    row = pl.BlockSpec((1, D), lambda b, *_: (0, 0))
    weights = [pl.BlockSpec((D, width), lambda b, c, p, s=s: (0, 2 * s + c[0])) for s in range(3)]
    return pl.pallas_call(
        project_kernel,
        grid_spec=pltpu.PrefetchScalarGridSpec(
            num_scalar_prefetch=2,
            grid=(blocks + 1,),
            in_specs=[
                pl.BlockSpec((length, D), lambda b, *_: (jnp.minimum(b, half - 1), 0)),
                pl.BlockSpec((length, D), lambda b, *_: (jnp.clip(b - half, 0, half - 1), 0)),
                row,
                row,
            ]
            + weights,
            out_specs=[
                pl.BlockSpec((length, 3 * width), lambda b, c, p: (p[jnp.maximum(b - 1, 0)], 0)),
                pl.BlockSpec((length, D), lambda b, c, p: (p[jnp.maximum(b - 1, 0)], 0)),
            ],
            scratch_shapes=[pltpu.VMEM((2, length, D), BF)],
        ),
        out_shape=[
            jax.ShapeDtypeStruct((blocks * length, 3 * width), BF),
            jax.ShapeDtypeStruct((blocks * length, D), BF),
        ],
        compiler_params=pltpu.CompilerParams(vmem_limit_bytes=60 * MIB),
        cost_estimate=SMALL,
        name="norm_and_project",
    )(
        core.reshape(1),
        places,
        own,
        other,
        gain.reshape(1, D),
        bias.reshape(1, D),
        w_qkv,
        w_qkv,
        w_qkv,
    )


def middle_kernel(
    core_ref,
    x_ref,
    own_ref,
    got_ref,
    keys_ref,
    values_ref,
    seen_ref,
    gain2_ref,
    bias2_ref,
    gain3_ref,
    bias3_ref,
    w_own_ref,
    w_got_ref,
    w_query_ref,
    w_out_ref,
    hidden1_ref,
    hidden2_ref,
    normed3_ref,
    queries_ref,
    mixed_ref,
    lse_ref,
):
    hidden = x_ref[...].astype(F32) + nn(own_ref[...], w_own_ref[...])
    hidden += nn(got_ref[...], w_got_ref[...])
    hidden1_ref[...] = hidden
    unit, _ = norm_parts(hidden)
    normed2 = (unit * gain2_ref[...] + bias2_ref[...]).astype(BF)
    queries = nn(normed2, w_query_ref[...]).astype(BF)
    queries_ref[...] = queries
    rows, states = queries.shape[0], keys_ref.shape[0]
    half = lax.broadcasted_iota(jnp.int32, (rows, 2 * HEAD), 1) >= HEAD
    v_flip = values_ref[...].T
    ones = jnp.ones((16, states), BF)
    zero = jnp.zeros((rows, 2 * HEAD), BF)

    def score(head):
        at, h = head // 2 * 2 * HEAD, head % 2
        own = jnp.where(half == (h == 1), queries[:, at : at + 2 * HEAD], zero)
        return nt(keys_ref[:, at : at + 2 * HEAD], own)

    def soften(scores):
        scores = scores * (SCALE * LOG2E) + seen_ref[...]
        top = jnp.max(scores, axis=0, keepdims=True)
        return jnp.exp2(scores - top).astype(BF), top

    outs, lses, scores, raised = [], [], {}, {}
    for n in range(HEADS + 2):
        if n < HEADS:
            scores[n] = score(n)
        if 0 <= n - 1 < HEADS:
            raised[n - 1] = soften(scores.pop(n - 1))
        if n >= 2:
            weights, top = raised.pop(n - 2)
            v_rows = jnp.concatenate([v_flip[(n - 2) * HEAD : (n - 1) * HEAD], ones], 0)
            mixed = nn(v_rows, weights)
            total = mixed[HEAD : HEAD + 1]
            lses.append(top + jnp.log2(total))
            outs.append((mixed[:HEAD] / total).astype(BF))
    lse_ref[...] = jnp.concatenate(lses, 0)
    mixed = jnp.concatenate(outs, 0).T
    mixed_ref[...] = mixed
    hidden += nn(mixed, w_out_ref[...])
    hidden2_ref[...] = hidden
    unit, _ = norm_parts(hidden)
    normed3_ref[...] = (unit * gain3_ref[...] + bias3_ref[...]).astype(BF)


def cross_part(x, own, got, text_kv, seen, norms, w_self_out, w_query, w_out, core):
    tokens, width = got.shape
    states = text_kv.shape[0]
    block = min(256, tokens)
    row = pl.BlockSpec((1, D), lambda b, c: (0, 0))
    wide = pl.BlockSpec((block, D), lambda b, c: (b, 0))
    narrow = pl.BlockSpec((block, width), lambda b, c: (b, 0))
    square = pl.BlockSpec((D, D), lambda b, c: (0, 0))
    return pl.pallas_call(
        middle_kernel,
        grid_spec=pltpu.PrefetchScalarGridSpec(
            num_scalar_prefetch=1,
            grid=(tokens // block,),
            in_specs=[
                wide,
                narrow,
                narrow,
                pl.BlockSpec((states, D), lambda b, c: (0, 0)),
                pl.BlockSpec((states, D), lambda b, c: (0, 1)),
                pl.BlockSpec((states, 1), lambda b, c: (0, 0)),
                row,
                row,
                row,
                row,
                pl.BlockSpec((width, D), lambda b, c: (c[0], 0)),
                pl.BlockSpec((width, D), lambda b, c: (1 - c[0], 0)),
                square,
                square,
            ],
            out_specs=[wide] * 5 + [pl.BlockSpec((HEADS, block), lambda b, c: (0, b))],
        ),
        out_shape=[
            jax.ShapeDtypeStruct((tokens, D), F32),
            jax.ShapeDtypeStruct((tokens, D), F32),
            jax.ShapeDtypeStruct((tokens, D), BF),
            jax.ShapeDtypeStruct((tokens, D), BF),
            jax.ShapeDtypeStruct((tokens, D), BF),
            jax.ShapeDtypeStruct((HEADS, tokens), F32),
        ],
        compiler_params=pltpu.CompilerParams(vmem_limit_bytes=60 * MIB),
        cost_estimate=SMALL,
        name="cross_attention_part",
    )(
        core.reshape(1),
        x,
        own,
        got,
        text_kv,
        text_kv,
        seen,
        *[v.reshape(1, D) for v in norms],
        w_self_out,
        w_self_out,
        w_query,
        w_out,
    )


def attend_kernel(row_ref, q_ref, k_ref, v_ref, all_ref, other_ref, lse_ref, out_ref):
    length = q_ref.shape[0]
    block = QUERY_BLOCK
    scale = SCALE * LOG2E
    half = lax.broadcasted_iota(jnp.int32, (block, 2 * HEAD), 1) >= HEAD
    key_row = lax.broadcasted_iota(jnp.int32, (block, block), 0)
    query_col = lax.broadcasted_iota(jnp.int32, (block, block), 1)
    seen = key_row <= query_col
    v_flip = v_ref[...].T
    ones = jnp.ones((16, length), BF)
    v_rows = [jnp.concatenate([v_flip[h * HEAD : (h + 1) * HEAD], ones], 0) for h in range(2)]

    def score(i, h):
        lo, hi = i * block, (i + 1) * block
        queries = q_ref[lo:hi, :]
        own = jnp.where(half == (h == 1), queries, jnp.zeros_like(queries))
        return nt(k_ref[lo:hi, :], own), nt(k_ref[:lo, :], own) if i else None

    def soften(i, h, diag, rest):
        diag = jnp.where(seen, diag, MASKED)
        top = jnp.max(diag, axis=0, keepdims=True)
        if i:
            top = jnp.maximum(top, jnp.max(rest, axis=0, keepdims=True))
            rest = jnp.exp2(rest * scale - top * scale).astype(BF)
        return jnp.exp2(diag * scale - top * scale).astype(BF), rest, top * scale

    def mix(i, h, diag, rest, base):
        lo, hi = i * block, (i + 1) * block
        mixed = nn(v_rows[h][:, lo:hi], diag)
        if i:
            mixed += nn(v_rows[h][:, :lo], rest)
        total = mixed[HEAD : HEAD + 1]
        lse_ref[0, h : h + 1, lo:hi] = base + jnp.log2(total)
        return mixed[:HEAD] / total

    tasks = [(i, h) for i in range(length // block) for h in range(2)]
    scores, raised, outs = {}, {}, []
    part = length // row_ref.shape[0]
    for n in range(len(tasks) + 2):
        if n < len(tasks):
            scores[n] = score(*tasks[n])
        if 0 <= n - 1 < len(tasks):
            raised[n - 1] = soften(*tasks[n - 1], *scores.pop(n - 1))
        if n >= 2:
            outs.append(mix(*tasks[n - 2], *raised.pop(n - 2)))
        if len(outs) == 2:
            lo = tasks[n - 2][0] * block
            result = jnp.concatenate(outs, 0).T.astype(BF)
            outs = []
            for at in range(0, block, part):
                row = pl.multiple_of(row_ref[(lo + at) // part] * part, part)
                out_ref[pl.ds(row, part), :] = result[at : at + part]
    all_ref[...] = out_ref[...]
    other_ref[...] = out_ref[length // 2 :, :]


def head_specs(length, pairs):
    return [
        pl.BlockSpec((length, 2 * HEAD), lambda p, *_, s=s: (0, s * pairs + p)) for s in range(3)
    ]


def attend(joined, rows):
    length, width = joined.shape[0], joined.shape[1] // 3
    pairs = width // (2 * HEAD)
    return pl.pallas_call(
        attend_kernel,
        grid_spec=pltpu.PrefetchScalarGridSpec(
            num_scalar_prefetch=1,
            grid=(pairs,),
            in_specs=head_specs(length, pairs),
            out_specs=[
                pl.BlockSpec((length, 2 * HEAD), lambda p, *_: (0, p)),
                pl.BlockSpec((length // 2, 2 * HEAD), lambda p, *_: (0, p)),
                pl.BlockSpec((1, 2, length), lambda p, *_: (p, 0, 0)),
            ],
            scratch_shapes=[pltpu.VMEM((length, 2 * HEAD), BF)],
        ),
        out_shape=[
            jax.ShapeDtypeStruct((length, width), BF),
            jax.ShapeDtypeStruct((length // 2, width), BF),
            jax.ShapeDtypeStruct((pairs, 2, length), F32),
        ],
        compiler_params=pltpu.CompilerParams(vmem_limit_bytes=60 * MIB),
        cost_estimate=SMALL,
        name="self_attention",
    )(rows, joined, joined, joined)


def attend_back_kernel(
    row_ref,
    block_ref,
    q_ref,
    k_ref,
    v_ref,
    own_g_ref,
    other_g_ref,
    mixed_ref,
    lse_ref,
    normed_hbm,
    wq_ref,
    wk_ref,
    wv_ref,
    keep_ref,
    send_ref,
    own_ref,
    other_ref,
    dq_sum,
    g_ref,
    o_ref,
    normed,
    flip_ref,
    ordered_ref,
    sum_ref,
    sem,
):
    pair, pairs = pl.program_id(0), pl.num_programs(0)
    load = pltpu.make_async_copy(normed_hbm, normed, sem)

    @pl.when(pair == 0)
    def _():
        load.start()

    length = q_ref.shape[0]
    places = row_ref.shape[0]
    part = length // places
    for place in range(places):
        row = row_ref[place]
        at = pl.ds(pl.multiple_of(row % (places // 2) * part, part), part)
        to = slice(place * part, (place + 1) * part)
        mine = row < places // 2
        g_ref[to, :] = jnp.where(mine, own_g_ref[at, :], other_g_ref[at, :])
        o_ref[to, :] = mixed_ref[pl.ds(pl.multiple_of(row * part, part), part), :]
    block = QUERY_BLOCK
    scale = SCALE * LOG2E
    half = lax.broadcasted_iota(jnp.int32, (length, 2 * HEAD), 1) >= HEAD
    key_row = lax.broadcasted_iota(jnp.int32, (block, block), 0)
    query_col = lax.broadcasted_iota(jnp.int32, (block, block), 1)
    seen = key_row <= query_col
    k_flip = k_ref[...].T
    zero = jnp.zeros((length, 2 * HEAD), BF)
    queries = [jnp.where(half == (h == 1), q_ref[...], zero) for h in range(2)]
    grads = [jnp.where(half == (h == 1), g_ref[...], zero) for h in range(2)]
    product = (g_ref[...].astype(F32) * o_ref[...].astype(F32)).T
    deltas = [jnp.sum(product[h * HEAD : (h + 1) * HEAD], axis=0, keepdims=True) for h in range(2)]

    def score(j, h):
        lo, hi = j * block, (j + 1) * block
        return nt(k_ref[lo:hi, :], queries[h][lo:]), nt(v_ref[lo:hi, :], grads[h][lo:])

    def soften(j, h, scores, score_grad):
        lo, hi = j * block, (j + 1) * block
        weights = jnp.exp2(scores * scale - lse_ref[0, h : h + 1, lo:])
        first = jnp.where(seen, weights[:, :block], 0.0)
        weights = jnp.concatenate([first, weights[:, block:]], 1) if hi < length else first
        score_grad = (weights * (score_grad - deltas[h][:, lo:])).astype(BF)
        return weights.astype(BF), score_grad

    def mix(j, h, weights, score_grad):
        lo, hi = j * block, (j + 1) * block
        rows = slice(h * HEAD, (h + 1) * HEAD)
        query_part = nn(k_flip[rows, lo:hi], score_grad)
        if j == 0:
            dq_sum[rows, :] = query_part
        else:
            dq_sum[rows, lo:] += query_part
        return nn(score_grad, queries[h][lo:]), nn(weights, grads[h][lo:])

    tasks = [(j, h) for j in range(length // block) for h in range(2)]
    scores, raised, outs, key_grads, value_grads = {}, {}, [], [], []
    for n in range(len(tasks) + 2):
        if n < len(tasks):
            scores[n] = score(*tasks[n])
        if 0 <= n - 1 < len(tasks):
            raised[n - 1] = soften(*tasks[n - 1], *scores.pop(n - 1))
        if n >= 2:
            outs.append(mix(*tasks[n - 2], *raised.pop(n - 2)))
        if len(outs) == 2:
            key_grads.append(((outs[0][0] + outs[1][0]) * SCALE).astype(BF))
            value_grads.append((outs[0][1] + outs[1][1]).astype(BF))
            outs = []
    query_grad = (dq_sum[...].T * SCALE).astype(BF)
    joined = jnp.concatenate(
        [query_grad, jnp.concatenate(key_grads, 0), jnp.concatenate(value_grads, 0)], 1
    )
    weights = jnp.concatenate([wq_ref[...], wk_ref[...], wv_ref[...]], 1)
    grad = nt(joined, weights)

    @pl.when(pair == 0)
    def _():
        sum_ref[...] = grad
        load.wait()
        flip_ref[...] = normed[...].T
        height = D // block_ref.shape[0]
        for i in range(block_ref.shape[0]):
            at = pl.ds(pl.multiple_of(block_ref[i] * height, height), height)
            ordered_ref[i * height : (i + 1) * height, :] = flip_ref[at, :]

    @pl.when(pair > 0)
    def _():
        sum_ref[...] += grad

    wide = nn(ordered_ref[...], joined).astype(BF)
    keep_ref[...] = wide[: D // 2]
    send_ref[...] = wide[D // 2 :]

    @pl.when(pair == pairs - 1)
    def _():
        for place in range(places):
            row = row_ref[place]
            at = pl.ds(pl.multiple_of(row % (places // 2) * part, part), part)
            rows = sum_ref[place * part : (place + 1) * part, :]

            @pl.when(row < places // 2)
            def _(at=at, rows=rows):
                own_ref[at, :] = rows

            @pl.when(row >= places // 2)
            def _(at=at, rows=rows):
                other_ref[at, :] = rows.astype(BF)


def attend_back(joined, own_g, other_g, mixed, lse, normed, w_qkv, core, rows, blocks):
    length, width = joined.shape[0], joined.shape[1] // 3
    pairs = width // (2 * HEAD)
    spec = pl.BlockSpec((length, 2 * HEAD), lambda p, *_: (0, p))
    half = pl.BlockSpec((length // 2, 2 * HEAD), lambda p, *_: (0, p))
    weights = [
        pl.BlockSpec((D, 2 * HEAD), lambda p, r, b, s=s: (0, (2 * s + r[r.shape[0] - 1]) * pairs + p))
        for s in range(3)
    ]
    sums = pl.BlockSpec((D // 2, 6 * HEAD), lambda p, *_: (0, p))
    out = pl.BlockSpec((length // 2, D), lambda p, *_: (0, 0))
    places = rows.shape[0]

    def body(row_ref, *refs):
        attend_back_kernel(Rows(row_ref, places), *refs)

    return pl.pallas_call(
        body,
        grid_spec=pltpu.PrefetchScalarGridSpec(
            num_scalar_prefetch=2,
            grid=(pairs,),
            in_specs=head_specs(length, pairs)
            + [half] * 2
            + [spec]
            + [pl.BlockSpec((1, 2, length), lambda p, *_: (p, 0, 0))]
            + [pl.BlockSpec(memory_space=pl.ANY)]
            + weights,
            out_specs=[sums, sums, out, out],
            scratch_shapes=[
                pltpu.VMEM((2 * HEAD, length), F32),
                pltpu.VMEM((length, 2 * HEAD), BF),
                pltpu.VMEM((length, 2 * HEAD), BF),
                pltpu.VMEM((length, D), BF),
                pltpu.VMEM((D, length), BF),
                pltpu.VMEM((D, length), BF),
                pltpu.VMEM((length, D), F32),
                pltpu.SemaphoreType.DMA,
            ],
        ),
        out_shape=[jax.ShapeDtypeStruct((D // 2, 3 * width), BF)] * 2
        + [
            jax.ShapeDtypeStruct((length // 2, D), F32),
            jax.ShapeDtypeStruct((length // 2, D), BF),
        ],
        compiler_params=pltpu.CompilerParams(vmem_limit_bytes=60 * MIB),
        cost_estimate=SMALL,
        name="self_attention_back",
    )(
        jnp.concatenate([rows, core.reshape(1)]), blocks, joined, joined, joined, own_g, other_g,
        mixed, lse, normed, w_qkv, w_qkv, w_qkv,
    )


class Rows:
    def __init__(self, ref, count):
        self.ref, self.shape = ref, (count,)

    def __getitem__(self, place):
        return self.ref[place]


def mlp_kernel(
    pieces,
    steps,
    core_ref,
    rows_from,
    goes_to,
    own_ref,
    other_ref,
    own_g_ref,
    other_g_ref,
    *refs,
):
    ups, downs = refs[:pieces], refs[pieces : 2 * pieces]
    down_ref, up_ref, out_ref, norm_ref, sent_ref, *targets = refs[2 * pieces : 2 * pieces + 9]
    flip_ref, ordered_ref, wide_ref, tall_ref, active_ref, grad_ref, sems = refs[2 * pieces + 9 :]
    step = pl.program_id(0)
    slot = step % 2
    tokens = own_ref.shape[0]
    quarter, height = targets[0].shape[0], targets[0].shape[1]
    tile = wide_ref.shape[3]
    width = 2 * height
    per_step = tile // width
    units = steps * tile

    @pl.when(step == 0)
    def _():
        flip_ref[:, :tokens] = own_ref[...].T
        flip_ref[:, tokens:] = other_ref[...].T
        for i in range(4 * quarter):
            at = pl.multiple_of(rows_from[i] * height, height)
            ordered_ref[i * height : (i + 1) * height, :] = flip_ref[pl.ds(at, height), :]

    def wide_copy(at, where, side):
        part = wide_ref.at[at, side * quarter : (side + 1) * quarter]
        lanes = pl.ds(pl.multiple_of(where * tile, tile), tile)
        return pltpu.make_async_copy(part, targets[side].at[:, :, lanes], sems.at[at, side])

    def tall_copy(at, j, r, target, i):
        rows = slice(j * width + r * height, j * width + (r + 1) * height)
        lanes = slice(units + r * D, units + (r + 1) * D)
        return pltpu.make_async_copy(
            tall_ref.at[at, rows], target.at[i, :, lanes], sems.at[at, 4 + 2 * j + r]
        )

    def wait(at):
        for side in range(4):
            wide_copy(at, 0, side).wait()
        for j in range(per_step):
            for r in range(2):
                tall_copy(at, j, r, targets[0], 0).wait()

    @pl.when((step >= 2) & (step < steps + 2))
    def _():
        wait(slot)

    @pl.when(step < steps)
    def _():
        up_w = jnp.concatenate([r[...] for r in ups], 1) if pieces > 1 else ups[0][...]
        down_w = jnp.concatenate([r[...] for r in downs], 0) if pieces > 1 else downs[0][...]
        sides = ((0, own_ref, own_g_ref), (tokens, other_ref, other_g_ref))
        cut = 256
        tasks = [(u, side) for u in range(0, tile, cut) for side in sides]
        found, active, grads = {}, {}, {}

        def products(u, side):
            _, x_ref, g_ref = side
            return nn(x_ref[...], up_w[:, u : u + cut]), nt(g_ref[...], down_w[u : u + cut])

        def units_of(n):
            u, (base, _, _) = tasks[n]
            up_value, down_grad = found.pop(n)
            value, slope = gelu_parts(up_value)
            value = value.astype(BF)
            grad = (down_grad * slope).astype(BF)
            active_ref[step, base : base + tokens, u : u + cut] = value
            grad_ref[step, base : base + tokens, u : u + cut] = grad
            active[n], grads[n] = value, grad

        def weights_of(n):
            u = tasks[n][0]
            grad = jnp.concatenate([grads.pop(n - 1), grads.pop(n)], 0)
            wide = nn(ordered_ref[...], grad).astype(BF)
            wide_ref[slot, :, :, u : u + cut] = wide.reshape(wide_ref.shape[1:3] + (cut,))
            tall = nn(active.pop(n - 1).T, own_g_ref[...]) + nn(active.pop(n).T, other_g_ref[...])
            tall_ref[slot, u : u + cut] = tall.astype(BF)

        for n in range(len(tasks) + 2):
            if n < len(tasks):
                found[n] = products(*tasks[n])
            if 0 <= n - 1 < len(tasks):
                units_of(n - 1)
            if n >= 3 and n % 2:
                weights_of(n - 2)
        for side in range(4):
            wide_copy(slot, step, side).start()
        for j in range(per_step):
            i = goes_to[step * per_step + j]
            for side, target in enumerate(targets):

                @pl.when(i // quarter == side)
                def _(j=j, i=i, side=side, target=target):
                    for r in range(2):
                        tall_copy(slot, j, r, target, i - side * quarter).start()

    @pl.when(step >= steps)
    def _():
        up = up_ref[...]
        if up.shape[1] > units:
            first = core_ref[0] == 0
            picked = []
            for at in range(0, 2 * units, 2 * width):
                picked.append(
                    jnp.where(first, up[:, at : at + width], up[:, at + width : at + 2 * width])
                )
            up = jnp.concatenate(picked, 1)
        active = jnp.concatenate([active_ref[i] for i in range(steps)], 1)
        out = nn(active, down_ref[...].reshape(units, -1))
        grad = jnp.concatenate([grad_ref[i] for i in range(steps)], 1)
        norm = nt(grad, up)
        out_ref[...] = out[:tokens]
        norm_ref[...] = norm[:tokens]
        sent_ref[0] = out[tokens:].astype(BF)
        sent_ref[1] = norm[tokens:].astype(BF)


def mlp(own, other, own_g, other_g, w_up, w_down, core, rows_from, goes_to):
    tokens = own.shape[0]
    chips = rows_from.shape[0]
    tile, out_tile = 512, 256
    units = w_up.shape[1] // 2
    steps = units // tile
    width = units // chips
    height = D // chips
    fine = width % 128 == 0
    tall = w_down.reshape(chips, 2, width, D)
    if fine:
        pieces, piece = tile // width, width
    else:
        pieces, piece = 1, tile
        w_up = w_up.reshape(D, chips, 2, width)[:, :, core].reshape(D, units)
        w_down = w_down.reshape(chips, 2, width, D)[:, core].reshape(units, D)

    def place(s, c, j):
        s = jnp.minimum(s, steps - 1)
        return 2 * (s * pieces + j) + c[0] if fine else s

    def column(s):
        return jnp.maximum(s - steps, 0)

    whole = pl.BlockSpec((tokens, D), lambda s, *_: (0, 0))
    up_specs = [
        pl.BlockSpec((D, piece), lambda s, c, *_, j=j: (0, place(s, c, j))) for j in range(pieces)
    ]
    down_specs = [
        pl.BlockSpec((piece, D), lambda s, c, *_, j=j: (place(s, c, j), 0)) for j in range(pieces)
    ]
    kept = pl.BlockSpec((tokens, out_tile), lambda s, *_: (0, column(s)))
    sums = jax.ShapeDtypeStruct((chips // 4, height, units + 2 * D), BF)
    return pl.pallas_call(
        partial(mlp_kernel, pieces, steps),
        grid_spec=pltpu.PrefetchScalarGridSpec(
            num_scalar_prefetch=3,
            grid=(steps + D // out_tile,),
            in_specs=[whole] * 4
            + up_specs
            + down_specs
            + [
                pl.BlockSpec((chips, None, width, out_tile), lambda s, c, *_: (0, c[0], 0, column(s))),
                pl.BlockSpec((out_tile, w_up.shape[1]), lambda s, *_: (column(s), 0)),
            ],
            out_specs=[
                kept,
                kept,
                pl.BlockSpec((2, tokens, out_tile), lambda s, *_: (0, 0, column(s))),
            ]
            + [pl.BlockSpec(memory_space=pl.ANY)] * 4,
            scratch_shapes=[
                pltpu.VMEM((D, 2 * tokens), BF),
                pltpu.VMEM((D, 2 * tokens), BF),
                pltpu.VMEM((2, chips, height, tile), BF),
                pltpu.VMEM((2, tile, D), BF),
                pltpu.VMEM((steps, 2 * tokens, tile), BF),
                pltpu.VMEM((steps, 2 * tokens, tile), BF),
                pltpu.SemaphoreType.DMA((2, 4 + 2 * (tile // width))),
            ],
        ),
        out_shape=[
            jax.ShapeDtypeStruct((tokens, D), F32),
            jax.ShapeDtypeStruct((tokens, D), F32),
            jax.ShapeDtypeStruct((2, tokens, D), BF),
            sums,
            sums,
            sums,
            sums,
        ],
        compiler_params=pltpu.CompilerParams(vmem_limit_bytes=60 * MIB),
        cost_estimate=SMALL,
        name="mlp_both_ways",
    )(
        core.reshape(1),
        rows_from,
        goes_to,
        own,
        other,
        own_g,
        other_g,
        *([w_up] * pieces),
        *([w_down] * pieces),
        tall,
        w_up,
    )


def cross_back_kernel(
    scalars,
    order_ref,
    got_ref,
    grad3_ref,
    hidden2_ref,
    g_ref,
    gain3_ref,
    gain2_ref,
    seen_ref,
    lse_ref,
    keys_ref,
    values_ref,
    states_ref,
    mixed_hbm,
    w_out_hbm,
    queries_hbm,
    w_query_hbm,
    hidden1_hbm,
    own_hbm,
    other_hbm,
    w_self_hbm,
    out_hbm,
    got_hbm,
    block_ref,
    hidden_grad_ref,
    own_grad_ref,
    other_grad_ref,
    text_ref,
    norms_ref,
    states_flip_ref,
    keep,
    send,
    mixed_ref,
    w_out_ref,
    queries_ref,
    w_query,
    hidden1,
    own_ref,
    other_ref,
    w_self,
    out_ref,
    out_got_ref,
    flip_ref,
    ordered_ref,
    keep_stage,
    send_stage,
    sems,
    out_sems,
):
    core = scalars[0]
    tokens = grad3_ref.shape[0]
    loads = [
        pltpu.make_async_copy(a, b, sems.at[i])
        for i, (a, b) in enumerate(
            (
                (mixed_hbm, mixed_ref),
                (w_out_hbm, w_out_ref),
                (queries_hbm, queries_ref),
                (w_query_hbm, w_query),
                (hidden1_hbm, hidden1),
                (own_hbm.at[:tokens], own_ref),
                (other_hbm, other_ref),
                (w_self_hbm, w_self),
                (out_hbm, out_ref),
                (got_hbm.at[0], out_got_ref),
            )
        )
    ]
    for load in loads:
        load.start()
    count = order_ref.shape[0]
    rows = D // count
    half = D // 2
    writes = []

    def order(depth):
        for i in range(count):
            at = pl.multiple_of(order_ref[i] * rows, rows)
            ordered_ref[i * rows : (i + 1) * rows, :depth] = flip_ref[pl.ds(at, rows), :depth]

    def write(slot, grads):
        keep_stage[slot] = ordered_ref[half:, :tokens].astype(BF)
        lane = slot * (tokens + D)
        lanes = slice(lane, lane + tokens + D)
        send_stage[:, lane : lane + tokens] = ordered_ref[:half, :tokens].astype(BF)
        send_stage[:, lane + tokens : lane + tokens + D] = grads
        writes.append(
            pltpu.make_async_copy(send_stage.at[:, lanes], send.at[:, lanes], out_sems.at[slot])
        )
        writes.append(
            pltpu.make_async_copy(keep_stage.at[slot], keep.at[slot], out_sems.at[4 + slot])
        )
        for copy in writes[-2:]:
            copy.start()

    kind = flip_ref.dtype
    loads[0].wait()
    flip_ref[:, :tokens] = mixed_ref[...].astype(kind).T
    hidden2 = hidden2_ref[...]
    grad3 = grad3_ref[...] + got_ref[...].astype(F32)
    unit, rstd = norm_parts(hidden2)
    norms_ref[4:5, :] = jnp.sum(grad3 * unit, axis=0, keepdims=True)
    norms_ref[5:6, :] = jnp.sum(grad3, axis=0, keepdims=True)
    norms_ref[6:8, :] = jnp.zeros((2, D), F32)
    grad_hidden = norm_back(unit, rstd, gain3_ref[...], grad3) + g_ref[...].astype(F32)
    hidden_grad_ref[...] = grad_hidden
    branch = grad_hidden.astype(BF)
    order(tokens)
    write(0, branch)
    loads[1].wait()
    grad_mixed = nt(branch, w_out_ref[...]).astype(BF)
    loads[2].wait()
    states = keys_ref.shape[0]
    half_lane = lax.broadcasted_iota(jnp.int32, (tokens, 2 * HEAD), 1) >= HEAD
    zero = jnp.zeros((tokens, 2 * HEAD), BF)
    k_flip = keys_ref[...].T

    def score(head):
        lanes = slice(head // 2 * 2 * HEAD, (head // 2 + 1) * 2 * HEAD)
        mine = half_lane == (head % 2 == 1)
        own_q = jnp.where(mine, queries_ref[:, lanes], zero)
        own_g = jnp.where(mine, grad_mixed[:, lanes], zero)
        return nt(keys_ref[:, lanes], own_q), nt(values_ref[:, lanes], own_g), own_q, own_g

    def soften(head, scores, score_grad, own_q, own_g):
        scores = scores * (SCALE * LOG2E) + seen_ref[...]
        weights = jnp.exp2(scores - lse_ref[head : head + 1, :])
        delta = jnp.sum(weights * score_grad, axis=0, keepdims=True)
        score_grad = (weights * (score_grad - delta)).astype(BF)
        return weights.astype(BF), score_grad, own_q, own_g

    scores, raised, flips, key_grads, value_grads = {}, {}, [], [], []
    for n in range(HEADS + 2):
        if n < HEADS:
            scores[n] = score(n)
        if 0 <= n - 1 < HEADS:
            raised[n - 1] = soften(n - 1, *scores.pop(n - 1))
        if n >= 2:
            head = n - 2
            weights, score_grad, own_q, own_g = raised.pop(head)
            key_part, value_part = nn(score_grad, own_q), nn(weights, own_g)
            if head % 2 == 0:
                key_grads.append(key_part)
                value_grads.append(value_part)
            else:
                key_grads[-1] += key_part
                value_grads[-1] += value_part
            part = nn(k_flip[head * HEAD : (head + 1) * HEAD], score_grad)
            flips.append((part * SCALE).astype(BF))
    query_grad = jnp.concatenate(flips, 0).T
    text_grad = jnp.concatenate([p * SCALE for p in key_grads] + value_grads, 1).astype(BF)
    text_ref[...] = text_grad
    flip_ref[:, :states] = states_ref[...].astype(kind).T
    order(states)
    states_flip_ref[...] = ordered_ref[half:, :states].astype(BF)
    part = states * 2 * D // half
    for i in range(half // states):
        send_stage[i * states : (i + 1) * states, 3 * (tokens + D) :] = text_grad[
            :, i * part : (i + 1) * part
        ]
    lanes = slice(3 * (tokens + D), 3 * (tokens + D) + part)
    writes.append(
        pltpu.make_async_copy(send_stage.at[:, lanes], send.at[:, lanes], out_sems.at[3])
    )
    writes[-1].start()
    for load in loads[3:5]:
        load.wait()
    grad2 = nt(query_grad, w_query[...])
    unit, rstd = norm_parts(hidden1[...])
    normed2 = unit * gain2_ref[0:1, :] + gain2_ref[1:2, :]
    flip_ref[:, :tokens] = normed2.astype(BF).astype(kind).T
    order(tokens)
    write(1, query_grad)
    norms_ref[2:3, :] = jnp.sum(grad2 * unit, axis=0, keepdims=True)
    norms_ref[3:4, :] = jnp.sum(grad2, axis=0, keepdims=True)
    norms_ref[0:2, :] = jnp.zeros((2, D), F32)
    grad_hidden = norm_back(unit, rstd, gain2_ref[0:1, :], grad2) + hidden_grad_ref[...]
    hidden_grad_ref[...] = grad_hidden
    branch = grad_hidden.astype(BF)
    for load in loads[5:8]:
        load.wait()
    own_rows = pl.ds(pl.multiple_of(core * half, half), half)
    other_rows = pl.ds(pl.multiple_of((1 - core) * half, half), half)
    own_grad_ref[...] = nt(branch, w_self[own_rows, :]).astype(BF)
    other_grad_ref[...] = nt(branch, w_self[other_rows, :]).astype(BF)
    flip_ref[own_rows, :tokens] = own_ref[...].astype(kind).T
    flip_ref[other_rows, :tokens] = other_ref[...].astype(kind).T
    order(tokens)
    write(2, branch)
    for load in loads[8:]:
        load.wait()
    block_ref[...] = (hidden2_ref[...] + out_ref[...] + out_got_ref[...].astype(F32)).astype(BF)
    for copy in writes:
        copy.wait()


def cross_back(
    out, got, grad3, hidden2, g, norms, seen, lse, mixed, w_out, text_kv, queries, states,
    w_query, hidden1, own, other, w_self, core, order,
):
    tokens, width = other.shape
    count = order.shape[0]
    texts = states.shape[0]
    kind = BF if (D // count) % 16 == 0 else F32

    def full(*shape):
        return pl.BlockSpec(shape, lambda b, *_: (0,) * len(shape))

    wide, late = full(tokens, D), pl.BlockSpec(memory_space=pl.ANY)
    return pl.pallas_call(
        cross_back_kernel,
        grid_spec=pltpu.PrefetchScalarGridSpec(
            num_scalar_prefetch=2,
            grid=(1,),
            in_specs=[
                pl.BlockSpec((None, tokens, D), lambda b, *_: (1, 0, 0)),
                wide,
                wide,
                wide,
                full(1, D),
                full(2, D),
                full(texts, 1),
                full(HEADS, tokens),
                full(texts, D),
                pl.BlockSpec((texts, D), lambda b, *_: (0, 1)),
                full(texts, D),
            ]
            + [late] * 10,
            out_specs=[
                wide,
                wide,
                full(tokens, width),
                full(tokens, width),
                full(texts, 2 * D),
                full(8, D),
                full(D // 2, texts),
                late,
                late,
            ],
            scratch_shapes=[
                pltpu.VMEM((tokens, D), BF),
                pltpu.VMEM((D, D), BF),
                pltpu.VMEM((tokens, D), BF),
                pltpu.VMEM((D, D), BF),
                pltpu.VMEM((tokens, D), F32),
                pltpu.VMEM((tokens, width), BF),
                pltpu.VMEM((tokens, width), BF),
                pltpu.VMEM((D, D), BF),
                pltpu.VMEM((tokens, D), F32),
                pltpu.VMEM((tokens, D), BF),
                pltpu.VMEM((D, tokens), kind),
                pltpu.VMEM((D, tokens), kind),
                pltpu.VMEM((3, D // 2, tokens), BF),
                pltpu.VMEM((D // 2, 3 * (tokens + D) + 4 * texts), BF),
                pltpu.SemaphoreType.DMA((10,)),
                pltpu.SemaphoreType.DMA((7,)),
            ],
        ),
        out_shape=[
            jax.ShapeDtypeStruct((tokens, D), BF),
            jax.ShapeDtypeStruct((tokens, D), F32),
            jax.ShapeDtypeStruct((tokens, width), BF),
            jax.ShapeDtypeStruct((tokens, width), BF),
            jax.ShapeDtypeStruct((texts, 2 * D), BF),
            jax.ShapeDtypeStruct((8, D), F32),
            jax.ShapeDtypeStruct((D // 2, texts), BF),
            jax.ShapeDtypeStruct((3, D // 2, tokens), BF),
            jax.ShapeDtypeStruct((D // 2, 3 * (tokens + D) + 4 * texts), BF),
        ],
        compiler_params=pltpu.CompilerParams(vmem_limit_bytes=60 * MIB),
        cost_estimate=SMALL,
        name="cross_attention_back",
    )(
        core.reshape(1), order, got, grad3, hidden2, g, norms[2].reshape(1, D),
        jnp.stack(norms[:2]), seen, lse, text_kv, text_kv, states, mixed, w_out, queries,
        w_query, hidden1, own, other, w_self, out, got,
    )


def pair_kernel(keep_ref, own_ref, got_ref, states_ref, grad_ref, grad_got_ref, *outs):
    first_ref, second_ref, text_ref = outs
    step = pl.program_id(0)
    half, tokens = keep_ref.shape
    texts = grad_ref.shape[0]

    def put(product):
        first_ref[...] = product[: half // 2].astype(BF)
        second_ref[...] = product[half // 2 :].astype(BF)

    @pl.when(step < 3)
    def _():
        product = nn(keep_ref[...], own_ref[:, tokens:])
        put(product + nn(got_ref[:, :tokens], got_ref[:, tokens:]))

    @pl.when(step >= 3)
    def _():
        got = grad_got_ref[...].astype(F32)
        got = jnp.concatenate([got[:texts], got[texts:]], 1)
        got = jnp.concatenate([got[texts // 2 :], got[: texts // 2]], 0)
        grad = (grad_ref[...].astype(F32) + got).astype(BF)
        text_ref[...] = grad[: texts // 2]
        put(nn(states_ref[...], grad))


def pair_gradients(keep, own, got, states, grad):
    _, half, tokens = keep.shape
    texts = grad.shape[0]

    def third(s):
        return jnp.minimum(s, 2)

    def later(s):
        return jnp.maximum(s - 3, 0)

    wide = pl.BlockSpec((half, tokens + D), lambda s: (0, third(s)))
    lane = 3 * (tokens + D) // (4 * texts)
    grads = pl.BlockSpec((texts, D), lambda s: (0, later(s)))
    out = pl.BlockSpec((half // 2, D), lambda s: (0, s))
    return pl.pallas_call(
        pair_kernel,
        grid=(5,),
        in_specs=[
            pl.BlockSpec((None, half, tokens), lambda s: (third(s), 0, 0)),
            wide,
            wide,
            pl.BlockSpec((half, texts), lambda s: (0, 0)),
            grads,
            pl.BlockSpec((2 * texts, 4 * texts), lambda s: (later(s), lane)),
        ],
        out_specs=[out, out, pl.BlockSpec((texts // 2, D), lambda s: (0, later(s)))],
        out_shape=[jax.ShapeDtypeStruct((half // 2, 5 * D), BF)] * 2
        + [jax.ShapeDtypeStruct((texts // 2, 2 * D), BF)],
        compiler_params=pltpu.CompilerParams(vmem_limit_bytes=60 * MIB),
        cost_estimate=SMALL,
        name="pair_gradients",
    )(keep, own, got, states, grad, got)


def last_kernel(
    blocks_ref,
    x_ref,
    part_ref,
    got_ref,
    hidden_ref,
    gain_ref,
    norms_ref,
    image_ref,
    keep,
    send,
    norm_flip,
):
    count = blocks_ref.shape[0]
    height, half = D // count, D // 2
    grad = part_ref[...] + got_ref[...].astype(F32)
    unit, rstd = norm_parts(x_ref[...].astype(F32))
    sums = [jnp.sum(grad * unit, axis=0, keepdims=True), jnp.sum(grad, axis=0, keepdims=True)]
    image = norm_back(unit, rstd, gain_ref[...], grad) + hidden_ref[...]
    image_ref[...] = image.astype(BF)
    fill = jnp.zeros((norm_flip.shape[1] - 8, D), F32)
    norm_flip[...] = jnp.concatenate(sums + [norms_ref[2:8, :], fill], 0).T
    for i in range(count):
        at = pl.ds(pl.multiple_of(blocks_ref[i] * height, height), height)
        to = i * height % half
        target = keep if i < count // 2 else send
        target[to : to + height, :] = norm_flip[at, :].astype(BF)


def last_part(x, part, got, hidden_grad, gain, norms, blocks):
    tokens = got.shape[0]

    def full(*shape):
        return pl.BlockSpec(shape, lambda b, *_: (0,) * len(shape))

    wide = full(tokens, D)
    return pl.pallas_call(
        last_kernel,
        grid_spec=pltpu.PrefetchScalarGridSpec(
            num_scalar_prefetch=1,
            grid=(1,),
            in_specs=[wide] * 4 + [full(1, D), full(8, D)],
            out_specs=[wide, full(D // 2, 128), full(D // 2, 128)],
            scratch_shapes=[pltpu.VMEM((D, 128), F32)],
        ),
        out_shape=[jax.ShapeDtypeStruct((tokens, D), BF)]
        + [jax.ShapeDtypeStruct((D // 2, 128), BF)] * 2,
        compiler_params=pltpu.CompilerParams(vmem_limit_bytes=60 * MIB),
        cost_estimate=SMALL,
        name="norm_back",
    )(blocks, x, part, got, hidden_grad, gain.reshape(1, D), norms)


def add_kernel(a_ref, b_ref, keep_ref, send_ref):
    block, half = pl.program_id(0), pl.num_programs(0) // 2
    total = a_ref[...] + b_ref[...]

    @pl.when(block < half)
    def _():
        send_ref[...] = total

    @pl.when(block >= half)
    def _():
        keep_ref[...] = total


def add_halves(a, b):
    count, height, width = a.shape
    blocks = 4
    half = blocks // 2
    shape = (count // blocks, height, width)
    turned = pl.BlockSpec(shape, lambda i: ((i + half) % blocks, 0, 0))
    return pl.pallas_call(
        add_kernel,
        grid=(blocks,),
        in_specs=[turned] * 2,
        out_specs=[
            pl.BlockSpec(shape, lambda i: (jnp.maximum(i - half, 0), 0, 0)),
            pl.BlockSpec(shape, lambda i: (jnp.minimum(i, half - 1), 0, 0)),
        ],
        out_shape=[jax.ShapeDtypeStruct((count // 2, height, width), BF)] * 2,
        compiler_params=pltpu.CompilerParams(vmem_limit_bytes=60 * MIB),
        cost_estimate=SMALL,
        name="add_halves",
    )(a, b)


def behind(value, *others):
    return lax.optimization_barrier((value,) + others)[0]


class Route:
    def __init__(self, plan, orders):
        self.orders = orders
        count = plan.chips
        maps = np.zeros((2, count), np.int32)
        for core in range(2):
            for i in range(count):
                for s, bit in enumerate(orders[core]):
                    maps[core, i] |= ((i >> (plan.levels - 1 - s)) & 1) << bit
        here, there = jnp.asarray(maps)[plan.core], jnp.asarray(maps)[1 - plan.core]
        self.blocks = jnp.bitwise_xor(plan.chip, here).astype(jnp.int32)
        sent = jnp.bitwise_xor(plan.chip, there).astype(jnp.int32)
        self.devices = jnp.concatenate([2 * sent + 1 - plan.core, 2 * self.blocks + plan.core])
        backs = np.argsort(maps, axis=1).astype(np.int32)
        away = jnp.bitwise_xor(plan.chip, jnp.arange(count, dtype=jnp.int32))
        self.goes_to = jnp.take(jnp.asarray(backs)[plan.core], away, mode="clip")


class Plan:
    def __init__(self, n_img, n_txt):
        self.n_txt = n_txt
        self.n = n_img * n_txt
        self.chips = self.n // 2
        self.ny = n_txt // 2
        self.levels = self.chips.bit_length() - 1
        self.me = lax.axis_index("img") * n_txt + lax.axis_index("txt")
        self.core = self.me % 2
        self.chip = self.me // 2
        self.y = lax.axis_index("txt") // 2
        sources = (self.y - jnp.arange(self.ny, dtype=jnp.int32)) % self.ny
        self.places = jnp.concatenate([2 * sources + self.core, 2 * sources + 1 - self.core])
        at = jnp.arange(n_txt, dtype=jnp.int32)
        self.rows = jnp.bitwise_xor(at % 2, self.core) * self.ny + (self.y - at // 2) % self.ny
        rest = list(range(2, self.levels))
        self.near = Route(self, ([1, 0] + rest, [0, 1] + rest))
        self.other = Route(self, ([1, 0] + rest, rest + [1, 0]))
        self.small = Route(self, ([0] + rest + [1], [0] + rest + [1]))
        self.mixed = Route(self, ([1, 0] + rest, rest + [0, 1]))
        self.token = None

    def swap(self, value):
        return lax.ppermute(value, BOTH, [(d, d ^ 1) for d in range(self.n)])

    def shift_y(self, value, by):
        pairs = []
        for d in range(self.n):
            img, txt = divmod(d, self.n_txt)
            y, core = divmod(txt, 2)
            pairs.append((d, img * self.n_txt + ((y + by) % self.ny) * 2 + core))
        return lax.ppermute(value, BOTH, pairs)

    def halve(self, value, route, step):
        pairs = [(d, d ^ (2 << route.orders[d % 2][step])) for d in range(self.n)]
        return lax.ppermute(value, BOTH, pairs)

    def send_items(self, value, note=None):
        parts = []
        for k in range(self.ny):
            part = value[(self.y + k) % self.ny]
            if note is not None:
                part = jnp.concatenate([part, note], 0)
            parts.append(self.shift_y(part, k) if k else part)
        return parts

    def join_items(self, parts, length):
        notes = [p[length:] for p in parts] if parts[0].shape[0] > length else []
        return jnp.concatenate([p[:length] for p in parts] + notes, 0)

    def return_items(self, value):
        return [self.shift_y(value[k], -k) if k else value[0] for k in range(self.ny)]

    def order_items(self, parts):
        stacked = jnp.stack(parts)
        return jnp.stack([stacked[(i - self.y) % self.ny] for i in range(self.ny)])

    def start(self, keep, send, route, step=0):
        return keep, self.halve(send, route, step), route, step

    def advance(self, state):
        keep, got, route, step = state
        keep, got, _ = lax.optimization_barrier((keep, got, self.token))
        if keep.shape[0] == 1:
            self.token = keep[0].astype(F32) + got[0].astype(F32)
            return self.token
        if keep.size > 1 << 20:
            keep, send = add_halves(keep, got)
        else:
            total = (keep.astype(F32) + got.astype(F32)).astype(BF)
            keep, send = jnp.split(total, 2)
        keep, send = lax.optimization_barrier((keep, send))
        self.token = send
        return self.start(keep, send, route, step + 1)

    def then(self, *values):
        return lax.optimization_barrier(values + (self.token,))[:-1]


def per_device(
    n_img,
    n_txt,
    image_tokens,
    text_states,
    text_segments,
    item_segments,
    norm1_gain,
    norm1_bias,
    w_qkv,
    w_self_out,
    norm2_gain,
    norm2_bias,
    w_cross_q,
    w_cross_kv,
    w_cross_out,
    norm3_gain,
    norm3_bias,
    w_up,
    w_down,
    cotangent,
):
    plan = Plan(n_img, n_txt)
    core, n, chips, ny = plan.core, plan.n, plan.chips, plan.ny
    items, length, _ = image_tokens.shape
    tokens = items * length
    half_d = D // 2
    rows = D // n

    states = text_states.shape[1]
    ids = jnp.pad(text_segments.astype(BF), ((0, 15), (0, D - states)))
    note = jnp.concatenate([text_states[0], ids], 0)
    x_parts = plan.send_items(image_tokens, note)
    g_parts = plan.send_items(behind(cotangent, x_parts[-1]))
    x_own = plan.join_items(x_parts, length)
    x_other = plan.swap(x_own)

    notes = [v[tokens:].reshape(ny, states + 16, D) for v in (x_own, x_other)]
    notes = jnp.concatenate(notes, 0)
    ids = notes[:, states, :states].reshape(-1)
    states_all = notes[:, :states].reshape(-1, D)
    text_kv = nn(states_all, w_cross_kv).astype(BF)
    matches = ids == item_segments[0, plan.y].astype(BF)
    seen = jnp.where(matches, 0.0, MASKED).astype(F32)[:, None]

    joined, normed1 = project_all(
        x_own, x_other, norm1_gain, norm1_bias, w_qkv, core, plan.places, length
    )
    mixed, mixed_other, lse = attend(joined, plan.rows)
    mixed_got = plan.swap(mixed_other)
    g_own = plan.join_items([behind(p, mixed_got) for p in g_parts], length)
    g_other = plan.swap(g_own)

    norms = (norm2_gain, norm2_bias, norm3_gain, norm3_bias)
    hidden1, hidden2, normed3, cross_q, cross_mixed, cross_lse = cross_part(
        x_own,
        mixed,
        mixed_got,
        text_kv,
        seen,
        norms,
        w_self_out,
        w_cross_q,
        w_cross_out,
        core,
    )

    normed3_other = plan.swap(normed3)
    per_down = w_down.shape[0] // n
    out, grad3, sent, low_keep, high_keep, low_send, high_send = mlp(
        normed3,
        normed3_other,
        g_own,
        g_other,
        w_up,
        w_down,
        core,
        plan.mixed.blocks,
        plan.mixed.goes_to,
    )
    high_got = plan.halve(high_send, plan.mixed, 0)
    got = plan.swap(sent)


    block_out, grad_hidden1, grad_own, grad_other, grad_kv, norm_sums, states_flip, keep, send = (
        cross_back(
            out, got, grad3, hidden2, g_own, norms[:3], seen, cross_lse, cross_mixed, w_cross_out,
            text_kv, cross_q, states_all, w_cross_q, hidden1, mixed, mixed_got, w_self_out,
            core, plan.other.devices,
        )
    )
    grad_other, high_got = lax.optimization_barrier((grad_other, high_got))
    grad_got = plan.swap(grad_other)
    pair_got = plan.swap(behind(send, grad_got))
    plan.token = grad_other
    high_keep, high_got = plan.then(high_keep, high_got)
    low_got = plan.halve(behind(low_send, high_got), plan.mixed, 0)
    high_sum = (high_keep.astype(F32) + high_got.astype(F32)).astype(BF)
    plan.token = high_sum
    next_got = plan.halve(high_sum, plan.mixed, 1)
    block_parts = plan.return_items(block_out.reshape(ny, length, D))

    grad_got, grad_own = plan.then(grad_got, grad_own)
    last_keep, last_send, part_own, part_other = attend_back(
        joined, grad_own, grad_got, mixed, lse, normed1, w_qkv, core, plan.rows, plan.near.blocks
    )
    plan.token = part_other
    last_sums = plan.start(
        last_keep.reshape(chips // 2, 2 * rows, -1),
        last_send.reshape(chips // 2, 2 * rows, -1),
        plan.near,
    )
    send, pair_got, *block_parts = plan.then(send, pair_got, *block_parts)
    middle_keep, middle_send, text_sum = pair_gradients(
        keep, send, pair_got, states_flip, grad_kv
    )
    plan.token = middle_send
    middle_sums = plan.start(
        middle_keep.reshape(chips // 2, rows, -1),
        middle_send.reshape(chips // 2, rows, -1),
        plan.other,
    )
    part_got = plan.swap(behind(part_other, middle_send))
    low_keep, low_got, next_got = plan.then(low_keep, low_got, next_got)
    low_sum = low_keep.astype(F32) + low_got.astype(F32) + next_got.astype(F32)
    plan.token = low_sum = lax.optimization_barrier(low_sum.astype(BF))
    low_keep, low_send = jnp.split(low_sum, 2)
    mlp_sums = plan.start(low_keep, low_send, plan.mixed, 2)
    part_got, part_own = plan.then(part_got, part_own)
    image_grad, norm_keep, norm_send = last_part(
        x_own, part_own, part_got, grad_hidden1, norm1_gain, norm_sums, plan.small.blocks
    )
    plan.token = norm_send
    norm_group = plan.start(
        norm_keep.reshape(chips // 2, 2 * rows, -1),
        norm_send.reshape(chips // 2, 2 * rows, -1),
        plan.small,
    )
    last_sums = plan.advance(last_sums)
    mlp_sums = plan.advance(mlp_sums)
    middle_sums = plan.advance(middle_sums)
    last_sums = plan.advance(last_sums)
    norm_group = plan.advance(norm_group)
    text_sum, image_grad = plan.then(text_sum, image_grad)
    text_part = nt(text_sum, w_cross_kv)
    plan.token = text_part
    text_part = text_part.reshape(ny, states, D)
    text_parts = [plan.shift_y(text_part[r].astype(BF), -r) for r in range(1, ny)]
    image_parts = plan.return_items(image_grad.reshape(ny, length, D))
    for _ in range(plan.levels - 3):
        last_sums = plan.advance(last_sums)
    norm_group = plan.advance(norm_group)
    for _ in range(plan.levels - 3):
        mlp_sums = plan.advance(mlp_sums)
    for _ in range(plan.levels - 3):
        middle_sums = plan.advance(middle_sums)
        norm_group = plan.advance(norm_group)
    middle_sums = plan.advance(middle_sums)
    last_sums = plan.advance(last_sums)
    norm_group = plan.advance(norm_group)
    last_sums = jnp.concatenate([last_sums, norm_group], 1)
    up_down = mlp_sums

    units = w_up.shape[1] // 2
    down_grad = jnp.concatenate([up_down[:, units : units + D], up_down[:, units + D :]], 0)
    parts = jnp.concatenate([up_down[:, :units], last_sums], 1).reshape(2, rows, -1)
    mine = parts[core]
    sent = parts[1 - core].astype(BF)
    theirs = plan.swap(sent).astype(F32)
    middle_sums = plan.advance(middle_sums)
    (theirs,) = plan.then(theirs)
    text_part, *text_parts = plan.then(text_part, *text_parts)
    text_grad = sum((p.astype(F32) for p in text_parts), text_part[0])
    image_grad = plan.order_items(plan.then(*image_parts)).astype(F32)
    plan.token = image_grad
    block_out = plan.order_items(plan.then(*block_parts))
    by_core = jnp.where(core == 0, jnp.stack([mine, theirs]), jnp.stack([theirs, mine]))
    up_grad = by_core[:, :, :units].reshape(2, rows, chips, per_down)
    up_grad = up_grad.transpose(1, 2, 0, 3).reshape(rows, 2 * units)
    wide = by_core[:, :, units : units + 3 * half_d].reshape(2, rows, -1, 3, 2 * HEAD)
    wide = wide.transpose(1, 3, 0, 2, 4).reshape(rows, 3 * D)
    norm_sums = mine[:, -128:-122] + theirs[:, -128:-122]
    return (
        block_out,
        image_grad,
        text_grad[None],
        norm_sums[:, 0],
        norm_sums[:, 1],
        wide,
        middle_sums[:, 2 * D : 3 * D],
        norm_sums[:, 2],
        norm_sums[:, 3],
        middle_sums[:, D : 2 * D],
        middle_sums[:, 3 * D :],
        middle_sums[:, :D],
        norm_sums[:, 4],
        norm_sums[:, 5],
        up_grad,
        down_grad,
    )


def solution(mesh):
    split = P("img", "txt", None)
    rows = P(BOTH)
    wide = P(BOTH, None)
    return jax.shard_map(
        partial(per_device, mesh.shape["img"], mesh.shape["txt"]),
        mesh=mesh,
        in_specs=(split, split, P("img", "txt"), P("img", None)) + (P(),) * 13 + (split,),
        out_specs=(
            (split,) * 3
            + (rows, rows, wide, wide)
            + (rows, rows, wide, wide, wide)
            + (rows, rows, wide, wide)
        ),
        check_vma=False,
    )
```

```python
from functools import partial

import jax
import jax.numpy as jnp
import numpy as np
from jax import lax
from jax.experimental import pallas as pl
from jax.experimental.pallas import tpu as pltpu
from jax.sharding import PartitionSpec as P

D = 1024
HEADS = 16
HEAD = 64
EPS = 1e-05
MASKED = -1e30
SCALE = HEAD**-0.5
LOG2E = 1.4426950408889634
BOTH = ("img", "txt")
BF = jnp.bfloat16
F32 = jnp.float32
QUERY_BLOCK = 256
MIB = 1 << 20
SMALL = pl.CostEstimate(flops=1 << 20, bytes_accessed=1 << 16, transcendentals=0)


def nn(a, b):
    return lax.dot_general(a, b, (((1,), (0,)), ((), ())), preferred_element_type=F32)


def nt(a, b):
    return lax.dot_general(a, b, (((1,), (1,)), ((), ())), preferred_element_type=F32)


def tn(a, b):
    return lax.dot_general(a, b, (((0,), (0,)), ((), ())), preferred_element_type=F32)


def norm_parts(values):
    center = values - jnp.mean(values, axis=-1, keepdims=True)
    rstd = lax.rsqrt(jnp.mean(center * center, axis=-1, keepdims=True) + EPS)
    return center * rstd, rstd


def norm_back(unit, rstd, gain, grad):
    scaled = grad * gain
    return rstd * (
        scaled
        - jnp.mean(scaled, axis=-1, keepdims=True)
        - unit * jnp.mean(scaled * unit, axis=-1, keepdims=True)
    )


TAIL = [
    0.5 * c
    for c in (
        -0.22753805372107494,
        0.8866680711331851,
        -0.6354061073102151,
        0.6495639241196378,
        0.09138668583849363,
        0.235325478247137,
    )
]


def gelu_parts(value):
    t = 1.0 / (1.0 + (0.39 * 0.5**0.5) * jnp.abs(value))
    bell = jnp.exp2(value * value * (-0.5 * LOG2E))
    tail = jnp.full_like(t, TAIL[0])
    for term in TAIL[1:]:
        tail = tail * t + term
    tail = tail * t * bell
    cdf = jnp.where(value > 0.0, 1.0 - tail, tail)
    return value * cdf, cdf + value * bell * (0.5 / np.pi) ** 0.5


def project_kernel(
    core_ref, place_ref, own_ref, other_ref, gain_ref, bias_ref, wq_ref, wk_ref, wv_ref, *refs
):
    joined_ref, normed_ref, held_ref = refs
    block, own_blocks = pl.program_id(0), (pl.num_programs(0) - 1) // 2
    slot = block % 2
    width = wq_ref.shape[1]
    before = held_ref[1 - slot]
    normed_ref[...] = before
    for s, w_ref in enumerate((wq_ref, wk_ref, wv_ref)):
        joined_ref[:, s * width : (s + 1) * width] = nn(before, w_ref[...]).astype(BF)
    tokens = jnp.where(block < own_blocks, own_ref[...], other_ref[...]).astype(F32)
    unit, _ = norm_parts(tokens)
    held_ref[slot] = (unit * gain_ref[...] + bias_ref[...]).astype(BF)


def project_all(own, other, gain, bias, w_qkv, core, places, length):
    blocks = places.shape[0]
    half = blocks // 2
    width = D // 2
    row = pl.BlockSpec((1, D), lambda b, *_: (0, 0))
    weights = [pl.BlockSpec((D, width), lambda b, c, p, s=s: (0, 2 * s + c[0])) for s in range(3)]
    return pl.pallas_call(
        project_kernel,
        grid_spec=pltpu.PrefetchScalarGridSpec(
            num_scalar_prefetch=2,
            grid=(blocks + 1,),
            in_specs=[
                pl.BlockSpec((length, D), lambda b, *_: (jnp.minimum(b, half - 1), 0)),
                pl.BlockSpec((length, D), lambda b, *_: (jnp.clip(b - half, 0, half - 1), 0)),
                row,
                row,
            ]
            + weights,
            out_specs=[
                pl.BlockSpec((length, 3 * width), lambda b, c, p: (p[jnp.maximum(b - 1, 0)], 0)),
                pl.BlockSpec((length, D), lambda b, c, p: (p[jnp.maximum(b - 1, 0)], 0)),
            ],
            scratch_shapes=[pltpu.VMEM((2, length, D), BF)],
        ),
        out_shape=[
            jax.ShapeDtypeStruct((blocks * length, 3 * width), BF),
            jax.ShapeDtypeStruct((blocks * length, D), BF),
        ],
        compiler_params=pltpu.CompilerParams(vmem_limit_bytes=60 * MIB),
        cost_estimate=SMALL,
        name="norm_and_project",
    )(
        core.reshape(1),
        places,
        own,
        other,
        gain.reshape(1, D),
        bias.reshape(1, D),
        w_qkv,
        w_qkv,
        w_qkv,
    )


def middle_kernel(
    core_ref,
    x_ref,
    own_ref,
    got_ref,
    keys_ref,
    values_ref,
    seen_ref,
    gain2_ref,
    bias2_ref,
    gain3_ref,
    bias3_ref,
    w_own_ref,
    w_got_ref,
    w_query_ref,
    w_out_ref,
    hidden1_ref,
    hidden2_ref,
    normed3_ref,
    queries_ref,
    mixed_ref,
    lse_ref,
):
    hidden = x_ref[...].astype(F32) + nn(own_ref[...], w_own_ref[...])
    hidden += nn(got_ref[...], w_got_ref[...])
    hidden1_ref[...] = hidden
    unit, _ = norm_parts(hidden)
    normed2 = (unit * gain2_ref[...] + bias2_ref[...]).astype(BF)
    queries = nn(normed2, w_query_ref[...]).astype(BF)
    queries_ref[...] = queries
    rows, states = queries.shape[0], keys_ref.shape[0]
    half = lax.broadcasted_iota(jnp.int32, (rows, 2 * HEAD), 1) >= HEAD
    v_flip = values_ref[...].T
    ones = jnp.ones((16, states), BF)
    zero = jnp.zeros((rows, 2 * HEAD), BF)

    def score(head):
        at, h = head // 2 * 2 * HEAD, head % 2
        own = jnp.where(half == (h == 1), queries[:, at : at + 2 * HEAD], zero)
        return nt(keys_ref[:, at : at + 2 * HEAD], own)

    def soften(scores):
        scores = scores * (SCALE * LOG2E) + seen_ref[...]
        top = jnp.max(scores, axis=0, keepdims=True)
        return jnp.exp2(scores - top).astype(BF), top

    outs, lses, scores, raised = [], [], {}, {}
    for n in range(HEADS + 2):
        if n < HEADS:
            scores[n] = score(n)
        if 0 <= n - 1 < HEADS:
            raised[n - 1] = soften(scores.pop(n - 1))
        if n >= 2:
            weights, top = raised.pop(n - 2)
            v_rows = jnp.concatenate([v_flip[(n - 2) * HEAD : (n - 1) * HEAD], ones], 0)
            mixed = nn(v_rows, weights)
            total = mixed[HEAD : HEAD + 1]
            lses.append(top + jnp.log2(total))
            outs.append((mixed[:HEAD] / total).astype(BF))
    lse_ref[...] = jnp.concatenate(lses, 0)
    mixed = jnp.concatenate(outs, 0).T
    mixed_ref[...] = mixed
    hidden += nn(mixed, w_out_ref[...])
    hidden2_ref[...] = hidden
    unit, _ = norm_parts(hidden)
    normed3_ref[...] = (unit * gain3_ref[...] + bias3_ref[...]).astype(BF)


def cross_part(x, own, got, text_kv, seen, norms, w_self_out, w_query, w_out, core):
    tokens, width = got.shape
    states = text_kv.shape[0]
    block = min(256, tokens)
    row = pl.BlockSpec((1, D), lambda b, c: (0, 0))
    wide = pl.BlockSpec((block, D), lambda b, c: (b, 0))
    narrow = pl.BlockSpec((block, width), lambda b, c: (b, 0))
    square = pl.BlockSpec((D, D), lambda b, c: (0, 0))
    return pl.pallas_call(
        middle_kernel,
        grid_spec=pltpu.PrefetchScalarGridSpec(
            num_scalar_prefetch=1,
            grid=(tokens // block,),
            in_specs=[
                wide,
                narrow,
                narrow,
                pl.BlockSpec((states, D), lambda b, c: (0, 0)),
                pl.BlockSpec((states, D), lambda b, c: (0, 1)),
                pl.BlockSpec((states, 1), lambda b, c: (0, 0)),
                row,
                row,
                row,
                row,
                pl.BlockSpec((width, D), lambda b, c: (c[0], 0)),
                pl.BlockSpec((width, D), lambda b, c: (1 - c[0], 0)),
                square,
                square,
            ],
            out_specs=[wide] * 5 + [pl.BlockSpec((HEADS, block), lambda b, c: (0, b))],
        ),
        out_shape=[
            jax.ShapeDtypeStruct((tokens, D), F32),
            jax.ShapeDtypeStruct((tokens, D), F32),
            jax.ShapeDtypeStruct((tokens, D), BF),
            jax.ShapeDtypeStruct((tokens, D), BF),
            jax.ShapeDtypeStruct((tokens, D), BF),
            jax.ShapeDtypeStruct((HEADS, tokens), F32),
        ],
        compiler_params=pltpu.CompilerParams(vmem_limit_bytes=60 * MIB),
        cost_estimate=SMALL,
        name="cross_attention_part",
    )(
        core.reshape(1),
        x,
        own,
        got,
        text_kv,
        text_kv,
        seen,
        *[v.reshape(1, D) for v in norms],
        w_self_out,
        w_self_out,
        w_query,
        w_out,
    )


def attend_kernel(row_ref, q_ref, k_ref, v_ref, all_ref, other_ref, lse_ref, out_ref):
    length = q_ref.shape[0]
    block = QUERY_BLOCK
    scale = SCALE * LOG2E
    half = lax.broadcasted_iota(jnp.int32, (block, 2 * HEAD), 1) >= HEAD
    key_row = lax.broadcasted_iota(jnp.int32, (block, block), 0)
    query_col = lax.broadcasted_iota(jnp.int32, (block, block), 1)
    seen = key_row <= query_col
    v_flip = v_ref[...].T
    ones = jnp.ones((16, length), BF)
    v_rows = [jnp.concatenate([v_flip[h * HEAD : (h + 1) * HEAD], ones], 0) for h in range(2)]

    def score(i, h):
        lo, hi = i * block, (i + 1) * block
        queries = q_ref[lo:hi, :]
        own = jnp.where(half == (h == 1), queries, jnp.zeros_like(queries))
        return nt(k_ref[lo:hi, :], own), nt(k_ref[:lo, :], own) if i else None

    def soften(i, h, diag, rest):
        diag = jnp.where(seen, diag, MASKED)
        top = jnp.max(diag, axis=0, keepdims=True)
        if i:
            top = jnp.maximum(top, jnp.max(rest, axis=0, keepdims=True))
            rest = jnp.exp2(rest * scale - top * scale).astype(BF)
        return jnp.exp2(diag * scale - top * scale).astype(BF), rest, top * scale

    def mix(i, h, diag, rest, base):
        lo, hi = i * block, (i + 1) * block
        mixed = nn(v_rows[h][:, lo:hi], diag)
        if i:
            mixed += nn(v_rows[h][:, :lo], rest)
        total = mixed[HEAD : HEAD + 1]
        lse_ref[0, h : h + 1, lo:hi] = base + jnp.log2(total)
        return mixed[:HEAD] / total

    tasks = [(i, h) for i in range(length // block) for h in range(2)]
    scores, raised, outs = {}, {}, []
    part = length // row_ref.shape[0]
    for n in range(len(tasks) + 2):
        if n < len(tasks):
            scores[n] = score(*tasks[n])
        if 0 <= n - 1 < len(tasks):
            raised[n - 1] = soften(*tasks[n - 1], *scores.pop(n - 1))
        if n >= 2:
            outs.append(mix(*tasks[n - 2], *raised.pop(n - 2)))
        if len(outs) == 2:
            lo = tasks[n - 2][0] * block
            result = jnp.concatenate(outs, 0).T.astype(BF)
            outs = []
            for at in range(0, block, part):
                row = pl.multiple_of(row_ref[(lo + at) // part] * part, part)
                out_ref[pl.ds(row, part), :] = result[at : at + part]
    all_ref[...] = out_ref[...]
    other_ref[...] = out_ref[length // 2 :, :]


def head_specs(length, pairs):
    return [
        pl.BlockSpec((length, 2 * HEAD), lambda p, *_, s=s: (0, s * pairs + p)) for s in range(3)
    ]


def attend(joined, rows):
    length, width = joined.shape[0], joined.shape[1] // 3
    pairs = width // (2 * HEAD)
    return pl.pallas_call(
        attend_kernel,
        grid_spec=pltpu.PrefetchScalarGridSpec(
            num_scalar_prefetch=1,
            grid=(pairs,),
            in_specs=head_specs(length, pairs),
            out_specs=[
                pl.BlockSpec((length, 2 * HEAD), lambda p, *_: (0, p)),
                pl.BlockSpec((length // 2, 2 * HEAD), lambda p, *_: (0, p)),
                pl.BlockSpec((1, 2, length), lambda p, *_: (p, 0, 0)),
            ],
            scratch_shapes=[pltpu.VMEM((length, 2 * HEAD), BF)],
        ),
        out_shape=[
            jax.ShapeDtypeStruct((length, width), BF),
            jax.ShapeDtypeStruct((length // 2, width), BF),
            jax.ShapeDtypeStruct((pairs, 2, length), F32),
        ],
        compiler_params=pltpu.CompilerParams(vmem_limit_bytes=60 * MIB),
        cost_estimate=SMALL,
        name="self_attention",
    )(rows, joined, joined, joined)


def attend_back_kernel(
    row_ref,
    block_ref,
    q_ref,
    k_ref,
    v_ref,
    own_g_ref,
    other_g_ref,
    mixed_ref,
    lse_ref,
    normed_hbm,
    wq_ref,
    wk_ref,
    wv_ref,
    keep_ref,
    send_ref,
    own_ref,
    other_ref,
    dq_sum,
    g_ref,
    o_ref,
    normed,
    flip_ref,
    ordered_ref,
    sum_ref,
    sem,
):
    pair, pairs = pl.program_id(0), pl.num_programs(0)
    load = pltpu.make_async_copy(normed_hbm, normed, sem)

    @pl.when(pair == 0)
    def _():
        load.start()

    length = q_ref.shape[0]
    places = row_ref.shape[0]
    part = length // places
    for place in range(places):
        row = row_ref[place]
        at = pl.ds(pl.multiple_of(row % (places // 2) * part, part), part)
        to = slice(place * part, (place + 1) * part)
        mine = row < places // 2
        g_ref[to, :] = jnp.where(mine, own_g_ref[at, :], other_g_ref[at, :])
        o_ref[to, :] = mixed_ref[pl.ds(pl.multiple_of(row * part, part), part), :]
    block = QUERY_BLOCK
    scale = SCALE * LOG2E
    half = lax.broadcasted_iota(jnp.int32, (length, 2 * HEAD), 1) >= HEAD
    key_row = lax.broadcasted_iota(jnp.int32, (block, block), 0)
    query_col = lax.broadcasted_iota(jnp.int32, (block, block), 1)
    seen = key_row <= query_col
    k_flip = k_ref[...].T
    zero = jnp.zeros((length, 2 * HEAD), BF)
    queries = [jnp.where(half == (h == 1), q_ref[...], zero) for h in range(2)]
    grads = [jnp.where(half == (h == 1), g_ref[...], zero) for h in range(2)]
    product = (g_ref[...].astype(F32) * o_ref[...].astype(F32)).T
    deltas = [jnp.sum(product[h * HEAD : (h + 1) * HEAD], axis=0, keepdims=True) for h in range(2)]

    def score(j, h):
        lo, hi = j * block, (j + 1) * block
        return nt(k_ref[lo:hi, :], queries[h][lo:]), nt(v_ref[lo:hi, :], grads[h][lo:])

    def soften(j, h, scores, score_grad):
        lo, hi = j * block, (j + 1) * block
        weights = jnp.exp2(scores * scale - lse_ref[0, h : h + 1, lo:])
        first = jnp.where(seen, weights[:, :block], 0.0)
        weights = jnp.concatenate([first, weights[:, block:]], 1) if hi < length else first
        score_grad = (weights * (score_grad - deltas[h][:, lo:])).astype(BF)
        return weights.astype(BF), score_grad

    def mix(j, h, weights, score_grad):
        lo, hi = j * block, (j + 1) * block
        rows = slice(h * HEAD, (h + 1) * HEAD)
        query_part = nn(k_flip[rows, lo:hi], score_grad)
        if j == 0:
            dq_sum[rows, :] = query_part
        else:
            dq_sum[rows, lo:] += query_part
        return nn(score_grad, queries[h][lo:]), nn(weights, grads[h][lo:])

    tasks = [(j, h) for j in range(length // block) for h in range(2)]
    scores, raised, outs, key_grads, value_grads = {}, {}, [], [], []
    for n in range(len(tasks) + 2):
        if n < len(tasks):
            scores[n] = score(*tasks[n])
        if 0 <= n - 1 < len(tasks):
            raised[n - 1] = soften(*tasks[n - 1], *scores.pop(n - 1))
        if n >= 2:
            outs.append(mix(*tasks[n - 2], *raised.pop(n - 2)))
        if len(outs) == 2:
            key_grads.append(((outs[0][0] + outs[1][0]) * SCALE).astype(BF))
            value_grads.append((outs[0][1] + outs[1][1]).astype(BF))
            outs = []
    query_grad = (dq_sum[...].T * SCALE).astype(BF)
    joined = jnp.concatenate(
        [query_grad, jnp.concatenate(key_grads, 0), jnp.concatenate(value_grads, 0)], 1
    )
    weights = jnp.concatenate([wq_ref[...], wk_ref[...], wv_ref[...]], 1)
    grad = nt(joined, weights)

    @pl.when(pair == 0)
    def _():
        sum_ref[...] = grad
        load.wait()
        flip_ref[...] = normed[...].T
        height = D // block_ref.shape[0]
        for i in range(block_ref.shape[0]):
            at = pl.ds(pl.multiple_of(block_ref[i] * height, height), height)
            ordered_ref[i * height : (i + 1) * height, :] = flip_ref[at, :]

    @pl.when(pair > 0)
    def _():
        sum_ref[...] += grad

    wide = nn(ordered_ref[...], joined).astype(BF)
    keep_ref[...] = wide[: D // 2]
    send_ref[...] = wide[D // 2 :]

    @pl.when(pair == pairs - 1)
    def _():
        for place in range(places):
            row = row_ref[place]
            at = pl.ds(pl.multiple_of(row % (places // 2) * part, part), part)
            rows = sum_ref[place * part : (place + 1) * part, :]

            @pl.when(row < places // 2)
            def _(at=at, rows=rows):
                own_ref[at, :] = rows

            @pl.when(row >= places // 2)
            def _(at=at, rows=rows):
                other_ref[at, :] = rows.astype(BF)


def attend_back(joined, own_g, other_g, mixed, lse, normed, w_qkv, core, rows, blocks):
    length, width = joined.shape[0], joined.shape[1] // 3
    pairs = width // (2 * HEAD)
    spec = pl.BlockSpec((length, 2 * HEAD), lambda p, *_: (0, p))
    half = pl.BlockSpec((length // 2, 2 * HEAD), lambda p, *_: (0, p))
    weights = [
        pl.BlockSpec((D, 2 * HEAD), lambda p, r, b, s=s: (0, (2 * s + r[r.shape[0] - 1]) * pairs + p))
        for s in range(3)
    ]
    sums = pl.BlockSpec((D // 2, 6 * HEAD), lambda p, *_: (0, p))
    out = pl.BlockSpec((length // 2, D), lambda p, *_: (0, 0))
    places = rows.shape[0]

    def body(row_ref, *refs):
        attend_back_kernel(Rows(row_ref, places), *refs)

    return pl.pallas_call(
        body,
        grid_spec=pltpu.PrefetchScalarGridSpec(
            num_scalar_prefetch=2,
            grid=(pairs,),
            in_specs=head_specs(length, pairs)
            + [half] * 2
            + [spec]
            + [pl.BlockSpec((1, 2, length), lambda p, *_: (p, 0, 0))]
            + [pl.BlockSpec(memory_space=pl.ANY)]
            + weights,
            out_specs=[sums, sums, out, out],
            scratch_shapes=[
                pltpu.VMEM((2 * HEAD, length), F32),
                pltpu.VMEM((length, 2 * HEAD), BF),
                pltpu.VMEM((length, 2 * HEAD), BF),
                pltpu.VMEM((length, D), BF),
                pltpu.VMEM((D, length), BF),
                pltpu.VMEM((D, length), BF),
                pltpu.VMEM((length, D), F32),
                pltpu.SemaphoreType.DMA,
            ],
        ),
        out_shape=[jax.ShapeDtypeStruct((D // 2, 3 * width), BF)] * 2
        + [
            jax.ShapeDtypeStruct((length // 2, D), F32),
            jax.ShapeDtypeStruct((length // 2, D), BF),
        ],
        compiler_params=pltpu.CompilerParams(vmem_limit_bytes=60 * MIB),
        cost_estimate=SMALL,
        name="self_attention_back",
    )(
        jnp.concatenate([rows, core.reshape(1)]), blocks, joined, joined, joined, own_g, other_g,
        mixed, lse, normed, w_qkv, w_qkv, w_qkv,
    )


class Rows:
    def __init__(self, ref, count):
        self.ref, self.shape = ref, (count,)

    def __getitem__(self, place):
        return self.ref[place]


def mlp_kernel(
    pieces,
    steps,
    core_ref,
    rows_from,
    goes_to,
    own_ref,
    other_ref,
    own_g_ref,
    other_g_ref,
    *refs,
):
    ups, downs = refs[:pieces], refs[pieces : 2 * pieces]
    down_ref, up_ref, out_ref, norm_ref, sent_ref, *targets = refs[2 * pieces : 2 * pieces + 9]
    flip_ref, ordered_ref, wide_ref, tall_ref, active_ref, grad_ref, sems = refs[2 * pieces + 9 :]
    step = pl.program_id(0)
    slot = step % 2
    tokens = own_ref.shape[0]
    quarter, height = targets[0].shape[0], targets[0].shape[1]
    tile = wide_ref.shape[3]
    width = 2 * height
    per_step = tile // width
    units = steps * tile

    @pl.when(step == 0)
    def _():
        flip_ref[:, :tokens] = own_ref[...].T
        flip_ref[:, tokens:] = other_ref[...].T
        for i in range(4 * quarter):
            at = pl.multiple_of(rows_from[i] * height, height)
            ordered_ref[i * height : (i + 1) * height, :] = flip_ref[pl.ds(at, height), :]

    def wide_copy(at, where, side):
        part = wide_ref.at[at, side * quarter : (side + 1) * quarter]
        lanes = pl.ds(pl.multiple_of(where * tile, tile), tile)
        return pltpu.make_async_copy(part, targets[side].at[:, :, lanes], sems.at[at, side])

    def tall_copy(at, j, r, target, i):
        rows = slice(j * width + r * height, j * width + (r + 1) * height)
        lanes = slice(units + r * D, units + (r + 1) * D)
        return pltpu.make_async_copy(
            tall_ref.at[at, rows], target.at[i, :, lanes], sems.at[at, 4 + 2 * j + r]
        )

    def wait(at):
        for side in range(4):
            wide_copy(at, 0, side).wait()
        for j in range(per_step):
            for r in range(2):
                tall_copy(at, j, r, targets[0], 0).wait()

    @pl.when((step >= 2) & (step < steps + 2))
    def _():
        wait(slot)

    @pl.when(step < steps)
    def _():
        up_w = jnp.concatenate([r[...] for r in ups], 1) if pieces > 1 else ups[0][...]
        down_w = jnp.concatenate([r[...] for r in downs], 0) if pieces > 1 else downs[0][...]
        sides = ((0, own_ref, own_g_ref), (tokens, other_ref, other_g_ref))
        cut = 256
        tasks = [(u, side) for u in range(0, tile, cut) for side in sides]
        found, active, grads = {}, {}, {}

        def products(u, side):
            _, x_ref, g_ref = side
            return nn(x_ref[...], up_w[:, u : u + cut]), nt(g_ref[...], down_w[u : u + cut])

        def units_of(n):
            u, (base, _, _) = tasks[n]
            up_value, down_grad = found.pop(n)
            value, slope = gelu_parts(up_value)
            value = value.astype(BF)
            grad = (down_grad * slope).astype(BF)
            active_ref[step, base : base + tokens, u : u + cut] = value
            grad_ref[step, base : base + tokens, u : u + cut] = grad
            active[n], grads[n] = value, grad

        def weights_of(n):
            u = tasks[n][0]
            grad = jnp.concatenate([grads.pop(n - 1), grads.pop(n)], 0)
            wide = nn(ordered_ref[...], grad).astype(BF)
            wide_ref[slot, :, :, u : u + cut] = wide.reshape(wide_ref.shape[1:3] + (cut,))
            tall = nn(active.pop(n - 1).T, own_g_ref[...]) + nn(active.pop(n).T, other_g_ref[...])
            tall_ref[slot, u : u + cut] = tall.astype(BF)

        for n in range(len(tasks) + 2):
            if n < len(tasks):
                found[n] = products(*tasks[n])
            if 0 <= n - 1 < len(tasks):
                units_of(n - 1)
            if n >= 3 and n % 2:
                weights_of(n - 2)
        for side in range(4):
            wide_copy(slot, step, side).start()
        for j in range(per_step):
            i = goes_to[step * per_step + j]
            for side, target in enumerate(targets):

                @pl.when(i // quarter == side)
                def _(j=j, i=i, side=side, target=target):
                    for r in range(2):
                        tall_copy(slot, j, r, target, i - side * quarter).start()

    @pl.when(step >= steps)
    def _():
        up = up_ref[...]
        if up.shape[1] > units:
            first = core_ref[0] == 0
            picked = []
            for at in range(0, 2 * units, 2 * width):
                picked.append(
                    jnp.where(first, up[:, at : at + width], up[:, at + width : at + 2 * width])
                )
            up = jnp.concatenate(picked, 1)
        active = jnp.concatenate([active_ref[i] for i in range(steps)], 1)
        out = nn(active, down_ref[...].reshape(units, -1))
        grad = jnp.concatenate([grad_ref[i] for i in range(steps)], 1)
        norm = nt(grad, up)
        out_ref[...] = out[:tokens]
        norm_ref[...] = norm[:tokens]
        sent_ref[0] = out[tokens:].astype(BF)
        sent_ref[1] = norm[tokens:].astype(BF)


def mlp(own, other, own_g, other_g, w_up, w_down, core, rows_from, goes_to):
    tokens = own.shape[0]
    chips = rows_from.shape[0]
    tile, out_tile = 512, 256
    units = w_up.shape[1] // 2
    steps = units // tile
    width = units // chips
    height = D // chips
    fine = width % 128 == 0
    tall = w_down.reshape(chips, 2, width, D)
    if fine:
        pieces, piece = tile // width, width
    else:
        pieces, piece = 1, tile
        w_up = w_up.reshape(D, chips, 2, width)[:, :, core].reshape(D, units)
        w_down = w_down.reshape(chips, 2, width, D)[:, core].reshape(units, D)

    def place(s, c, j):
        s = jnp.minimum(s, steps - 1)
        return 2 * (s * pieces + j) + c[0] if fine else s

    def column(s):
        return jnp.maximum(s - steps, 0)

    whole = pl.BlockSpec((tokens, D), lambda s, *_: (0, 0))
    up_specs = [
        pl.BlockSpec((D, piece), lambda s, c, *_, j=j: (0, place(s, c, j))) for j in range(pieces)
    ]
    down_specs = [
        pl.BlockSpec((piece, D), lambda s, c, *_, j=j: (place(s, c, j), 0)) for j in range(pieces)
    ]
    kept = pl.BlockSpec((tokens, out_tile), lambda s, *_: (0, column(s)))
    sums = jax.ShapeDtypeStruct((chips // 4, height, units + 2 * D), BF)
    return pl.pallas_call(
        partial(mlp_kernel, pieces, steps),
        grid_spec=pltpu.PrefetchScalarGridSpec(
            num_scalar_prefetch=3,
            grid=(steps + D // out_tile,),
            in_specs=[whole] * 4
            + up_specs
            + down_specs
            + [
                pl.BlockSpec((chips, None, width, out_tile), lambda s, c, *_: (0, c[0], 0, column(s))),
                pl.BlockSpec((out_tile, w_up.shape[1]), lambda s, *_: (column(s), 0)),
            ],
            out_specs=[
                kept,
                kept,
                pl.BlockSpec((2, tokens, out_tile), lambda s, *_: (0, 0, column(s))),
            ]
            + [pl.BlockSpec(memory_space=pl.ANY)] * 4,
            scratch_shapes=[
                pltpu.VMEM((D, 2 * tokens), BF),
                pltpu.VMEM((D, 2 * tokens), BF),
                pltpu.VMEM((2, chips, height, tile), BF),
                pltpu.VMEM((2, tile, D), BF),
                pltpu.VMEM((steps, 2 * tokens, tile), BF),
                pltpu.VMEM((steps, 2 * tokens, tile), BF),
                pltpu.SemaphoreType.DMA((2, 4 + 2 * (tile // width))),
            ],
        ),
        out_shape=[
            jax.ShapeDtypeStruct((tokens, D), F32),
            jax.ShapeDtypeStruct((tokens, D), F32),
            jax.ShapeDtypeStruct((2, tokens, D), BF),
            sums,
            sums,
            sums,
            sums,
        ],
        compiler_params=pltpu.CompilerParams(vmem_limit_bytes=60 * MIB),
        cost_estimate=SMALL,
        name="mlp_both_ways",
    )(
        core.reshape(1),
        rows_from,
        goes_to,
        own,
        other,
        own_g,
        other_g,
        *([w_up] * pieces),
        *([w_down] * pieces),
        tall,
        w_up,
    )


def cross_back_kernel(
    scalars,
    order_ref,
    got_ref,
    grad3_ref,
    hidden2_ref,
    g_ref,
    gain3_ref,
    gain2_ref,
    seen_ref,
    lse_ref,
    keys_ref,
    values_ref,
    states_ref,
    mixed_hbm,
    w_out_hbm,
    queries_hbm,
    w_query_hbm,
    hidden1_hbm,
    own_hbm,
    other_hbm,
    w_self_hbm,
    out_hbm,
    got_hbm,
    block_ref,
    hidden_grad_ref,
    own_grad_ref,
    other_grad_ref,
    text_ref,
    norms_ref,
    states_flip_ref,
    keep,
    send,
    mixed_ref,
    w_out_ref,
    queries_ref,
    w_query,
    hidden1,
    own_ref,
    other_ref,
    w_self,
    out_ref,
    out_got_ref,
    flip_ref,
    ordered_ref,
    keep_stage,
    send_stage,
    sems,
    out_sems,
):
    core = scalars[0]
    tokens = grad3_ref.shape[0]
    loads = [
        pltpu.make_async_copy(a, b, sems.at[i])
        for i, (a, b) in enumerate(
            (
                (mixed_hbm, mixed_ref),
                (w_out_hbm, w_out_ref),
                (queries_hbm, queries_ref),
                (w_query_hbm, w_query),
                (hidden1_hbm, hidden1),
                (own_hbm.at[:tokens], own_ref),
                (other_hbm, other_ref),
                (w_self_hbm, w_self),
                (out_hbm, out_ref),
                (got_hbm.at[0], out_got_ref),
            )
        )
    ]
    for load in loads:
        load.start()
    count = order_ref.shape[0]
    rows = D // count
    half = D // 2
    writes = []

    def order(depth):
        for i in range(count):
            at = pl.multiple_of(order_ref[i] * rows, rows)
            ordered_ref[i * rows : (i + 1) * rows, :depth] = flip_ref[pl.ds(at, rows), :depth]

    def write(slot, grads):
        keep_stage[slot] = ordered_ref[half:, :tokens].astype(BF)
        lane = slot * (tokens + D)
        lanes = slice(lane, lane + tokens + D)
        send_stage[:, lane : lane + tokens] = ordered_ref[:half, :tokens].astype(BF)
        send_stage[:, lane + tokens : lane + tokens + D] = grads
        writes.append(
            pltpu.make_async_copy(send_stage.at[:, lanes], send.at[:, lanes], out_sems.at[slot])
        )
        writes.append(
            pltpu.make_async_copy(keep_stage.at[slot], keep.at[slot], out_sems.at[4 + slot])
        )
        for copy in writes[-2:]:
            copy.start()

    kind = flip_ref.dtype
    loads[0].wait()
    flip_ref[:, :tokens] = mixed_ref[...].astype(kind).T
    hidden2 = hidden2_ref[...]
    grad3 = grad3_ref[...] + got_ref[...].astype(F32)
    unit, rstd = norm_parts(hidden2)
    norms_ref[4:5, :] = jnp.sum(grad3 * unit, axis=0, keepdims=True)
    norms_ref[5:6, :] = jnp.sum(grad3, axis=0, keepdims=True)
    norms_ref[6:8, :] = jnp.zeros((2, D), F32)
    grad_hidden = norm_back(unit, rstd, gain3_ref[...], grad3) + g_ref[...].astype(F32)
    hidden_grad_ref[...] = grad_hidden
    branch = grad_hidden.astype(BF)
    order(tokens)
    write(0, branch)
    loads[1].wait()
    grad_mixed = nt(branch, w_out_ref[...]).astype(BF)
    loads[2].wait()
    states = keys_ref.shape[0]
    half_lane = lax.broadcasted_iota(jnp.int32, (tokens, 2 * HEAD), 1) >= HEAD
    zero = jnp.zeros((tokens, 2 * HEAD), BF)
    k_flip = keys_ref[...].T

    def score(head):
        lanes = slice(head // 2 * 2 * HEAD, (head // 2 + 1) * 2 * HEAD)
        mine = half_lane == (head % 2 == 1)
        own_q = jnp.where(mine, queries_ref[:, lanes], zero)
        own_g = jnp.where(mine, grad_mixed[:, lanes], zero)
        return nt(keys_ref[:, lanes], own_q), nt(values_ref[:, lanes], own_g), own_q, own_g

    def soften(head, scores, score_grad, own_q, own_g):
        scores = scores * (SCALE * LOG2E) + seen_ref[...]
        weights = jnp.exp2(scores - lse_ref[head : head + 1, :])
        delta = jnp.sum(weights * score_grad, axis=0, keepdims=True)
        score_grad = (weights * (score_grad - delta)).astype(BF)
        return weights.astype(BF), score_grad, own_q, own_g

    scores, raised, flips, key_grads, value_grads = {}, {}, [], [], []
    for n in range(HEADS + 2):
        if n < HEADS:
            scores[n] = score(n)
        if 0 <= n - 1 < HEADS:
            raised[n - 1] = soften(n - 1, *scores.pop(n - 1))
        if n >= 2:
            head = n - 2
            weights, score_grad, own_q, own_g = raised.pop(head)
            key_part, value_part = nn(score_grad, own_q), nn(weights, own_g)
            if head % 2 == 0:
                key_grads.append(key_part)
                value_grads.append(value_part)
            else:
                key_grads[-1] += key_part
                value_grads[-1] += value_part
            part = nn(k_flip[head * HEAD : (head + 1) * HEAD], score_grad)
            flips.append((part * SCALE).astype(BF))
    query_grad = jnp.concatenate(flips, 0).T
    text_grad = jnp.concatenate([p * SCALE for p in key_grads] + value_grads, 1).astype(BF)
    text_ref[...] = text_grad
    flip_ref[:, :states] = states_ref[...].astype(kind).T
    order(states)
    states_flip_ref[...] = ordered_ref[half:, :states].astype(BF)
    part = states * 2 * D // half
    for i in range(half // states):
        send_stage[i * states : (i + 1) * states, 3 * (tokens + D) :] = text_grad[
            :, i * part : (i + 1) * part
        ]
    lanes = slice(3 * (tokens + D), 3 * (tokens + D) + part)
    writes.append(
        pltpu.make_async_copy(send_stage.at[:, lanes], send.at[:, lanes], out_sems.at[3])
    )
    writes[-1].start()
    for load in loads[3:5]:
        load.wait()
    grad2 = nt(query_grad, w_query[...])
    unit, rstd = norm_parts(hidden1[...])
    normed2 = unit * gain2_ref[0:1, :] + gain2_ref[1:2, :]
    flip_ref[:, :tokens] = normed2.astype(BF).astype(kind).T
    order(tokens)
    write(1, query_grad)
    norms_ref[2:3, :] = jnp.sum(grad2 * unit, axis=0, keepdims=True)
    norms_ref[3:4, :] = jnp.sum(grad2, axis=0, keepdims=True)
    norms_ref[0:2, :] = jnp.zeros((2, D), F32)
    grad_hidden = norm_back(unit, rstd, gain2_ref[0:1, :], grad2) + hidden_grad_ref[...]
    hidden_grad_ref[...] = grad_hidden
    branch = grad_hidden.astype(BF)
    for load in loads[5:8]:
        load.wait()
    own_rows = pl.ds(pl.multiple_of(core * half, half), half)
    other_rows = pl.ds(pl.multiple_of((1 - core) * half, half), half)
    own_grad_ref[...] = nt(branch, w_self[own_rows, :]).astype(BF)
    other_grad_ref[...] = nt(branch, w_self[other_rows, :]).astype(BF)
    flip_ref[own_rows, :tokens] = own_ref[...].astype(kind).T
    flip_ref[other_rows, :tokens] = other_ref[...].astype(kind).T
    order(tokens)
    write(2, branch)
    for load in loads[8:]:
        load.wait()
    block_ref[...] = (hidden2_ref[...] + out_ref[...] + out_got_ref[...].astype(F32)).astype(BF)
    for copy in writes:
        copy.wait()


def cross_back(
    out, got, grad3, hidden2, g, norms, seen, lse, mixed, w_out, text_kv, queries, states,
    w_query, hidden1, own, other, w_self, core, order,
):
    tokens, width = other.shape
    count = order.shape[0]
    texts = states.shape[0]
    kind = BF if (D // count) % 16 == 0 else F32

    def full(*shape):
        return pl.BlockSpec(shape, lambda b, *_: (0,) * len(shape))

    wide, late = full(tokens, D), pl.BlockSpec(memory_space=pl.ANY)
    return pl.pallas_call(
        cross_back_kernel,
        grid_spec=pltpu.PrefetchScalarGridSpec(
            num_scalar_prefetch=2,
            grid=(1,),
            in_specs=[
                pl.BlockSpec((None, tokens, D), lambda b, *_: (1, 0, 0)),
                wide,
                wide,
                wide,
                full(1, D),
                full(2, D),
                full(texts, 1),
                full(HEADS, tokens),
                full(texts, D),
                pl.BlockSpec((texts, D), lambda b, *_: (0, 1)),
                full(texts, D),
            ]
            + [late] * 10,
            out_specs=[
                wide,
                wide,
                full(tokens, width),
                full(tokens, width),
                full(texts, 2 * D),
                full(8, D),
                full(D // 2, texts),
                late,
                late,
            ],
            scratch_shapes=[
                pltpu.VMEM((tokens, D), BF),
                pltpu.VMEM((D, D), BF),
                pltpu.VMEM((tokens, D), BF),
                pltpu.VMEM((D, D), BF),
                pltpu.VMEM((tokens, D), F32),
                pltpu.VMEM((tokens, width), BF),
                pltpu.VMEM((tokens, width), BF),
                pltpu.VMEM((D, D), BF),
                pltpu.VMEM((tokens, D), F32),
                pltpu.VMEM((tokens, D), BF),
                pltpu.VMEM((D, tokens), kind),
                pltpu.VMEM((D, tokens), kind),
                pltpu.VMEM((3, D // 2, tokens), BF),
                pltpu.VMEM((D // 2, 3 * (tokens + D) + 4 * texts), BF),
                pltpu.SemaphoreType.DMA((10,)),
                pltpu.SemaphoreType.DMA((7,)),
            ],
        ),
        out_shape=[
            jax.ShapeDtypeStruct((tokens, D), BF),
            jax.ShapeDtypeStruct((tokens, D), F32),
            jax.ShapeDtypeStruct((tokens, width), BF),
            jax.ShapeDtypeStruct((tokens, width), BF),
            jax.ShapeDtypeStruct((texts, 2 * D), BF),
            jax.ShapeDtypeStruct((8, D), F32),
            jax.ShapeDtypeStruct((D // 2, texts), BF),
            jax.ShapeDtypeStruct((3, D // 2, tokens), BF),
            jax.ShapeDtypeStruct((D // 2, 3 * (tokens + D) + 4 * texts), BF),
        ],
        compiler_params=pltpu.CompilerParams(vmem_limit_bytes=60 * MIB),
        cost_estimate=SMALL,
        name="cross_attention_back",
    )(
        core.reshape(1), order, got, grad3, hidden2, g, norms[2].reshape(1, D),
        jnp.stack(norms[:2]), seen, lse, text_kv, text_kv, states, mixed, w_out, queries,
        w_query, hidden1, own, other, w_self, out, got,
    )


def pair_kernel(keep_ref, own_ref, got_ref, states_ref, grad_ref, grad_got_ref, *outs):
    first_ref, second_ref, text_ref = outs
    step = pl.program_id(0)
    half, tokens = keep_ref.shape
    texts = grad_ref.shape[0]

    def put(product):
        first_ref[...] = product[: half // 2].astype(BF)
        second_ref[...] = product[half // 2 :].astype(BF)

    @pl.when(step < 3)
    def _():
        product = nn(keep_ref[...], own_ref[:, tokens:])
        put(product + nn(got_ref[:, :tokens], got_ref[:, tokens:]))

    @pl.when(step >= 3)
    def _():
        got = grad_got_ref[...].astype(F32)
        got = jnp.concatenate([got[:texts], got[texts:]], 1)
        got = jnp.concatenate([got[texts // 2 :], got[: texts // 2]], 0)
        grad = (grad_ref[...].astype(F32) + got).astype(BF)
        text_ref[...] = grad[: texts // 2]
        put(nn(states_ref[...], grad))


def pair_gradients(keep, own, got, states, grad):
    _, half, tokens = keep.shape
    texts = grad.shape[0]

    def third(s):
        return jnp.minimum(s, 2)

    def later(s):
        return jnp.maximum(s - 3, 0)

    wide = pl.BlockSpec((half, tokens + D), lambda s: (0, third(s)))
    lane = 3 * (tokens + D) // (4 * texts)
    grads = pl.BlockSpec((texts, D), lambda s: (0, later(s)))
    out = pl.BlockSpec((half // 2, D), lambda s: (0, s))
    return pl.pallas_call(
        pair_kernel,
        grid=(5,),
        in_specs=[
            pl.BlockSpec((None, half, tokens), lambda s: (third(s), 0, 0)),
            wide,
            wide,
            pl.BlockSpec((half, texts), lambda s: (0, 0)),
            grads,
            pl.BlockSpec((2 * texts, 4 * texts), lambda s: (later(s), lane)),
        ],
        out_specs=[out, out, pl.BlockSpec((texts // 2, D), lambda s: (0, later(s)))],
        out_shape=[jax.ShapeDtypeStruct((half // 2, 5 * D), BF)] * 2
        + [jax.ShapeDtypeStruct((texts // 2, 2 * D), BF)],
        compiler_params=pltpu.CompilerParams(vmem_limit_bytes=60 * MIB),
        cost_estimate=SMALL,
        name="pair_gradients",
    )(keep, own, got, states, grad, got)


def last_kernel(
    blocks_ref,
    x_ref,
    part_ref,
    got_ref,
    hidden_ref,
    gain_ref,
    norms_ref,
    image_ref,
    keep,
    send,
    norm_flip,
):
    count = blocks_ref.shape[0]
    height, half = D // count, D // 2
    grad = part_ref[...] + got_ref[...].astype(F32)
    unit, rstd = norm_parts(x_ref[...].astype(F32))
    sums = [jnp.sum(grad * unit, axis=0, keepdims=True), jnp.sum(grad, axis=0, keepdims=True)]
    image = norm_back(unit, rstd, gain_ref[...], grad) + hidden_ref[...]
    image_ref[...] = image.astype(BF)
    fill = jnp.zeros((norm_flip.shape[1] - 8, D), F32)
    norm_flip[...] = jnp.concatenate(sums + [norms_ref[2:8, :], fill], 0).T
    for i in range(count):
        at = pl.ds(pl.multiple_of(blocks_ref[i] * height, height), height)
        to = i * height % half
        target = keep if i < count // 2 else send
        target[to : to + height, :] = norm_flip[at, :].astype(BF)


def last_part(x, part, got, hidden_grad, gain, norms, blocks):
    tokens = got.shape[0]

    def full(*shape):
        return pl.BlockSpec(shape, lambda b, *_: (0,) * len(shape))

    wide = full(tokens, D)
    return pl.pallas_call(
        last_kernel,
        grid_spec=pltpu.PrefetchScalarGridSpec(
            num_scalar_prefetch=1,
            grid=(1,),
            in_specs=[wide] * 4 + [full(1, D), full(8, D)],
            out_specs=[wide, full(D // 2, 128), full(D // 2, 128)],
            scratch_shapes=[pltpu.VMEM((D, 128), F32)],
        ),
        out_shape=[jax.ShapeDtypeStruct((tokens, D), BF)]
        + [jax.ShapeDtypeStruct((D // 2, 128), BF)] * 2,
        compiler_params=pltpu.CompilerParams(vmem_limit_bytes=60 * MIB),
        cost_estimate=SMALL,
        name="norm_back",
    )(blocks, x, part, got, hidden_grad, gain.reshape(1, D), norms)


def add_kernel(a_ref, b_ref, keep_ref, send_ref):
    block, half = pl.program_id(0), pl.num_programs(0) // 2
    total = a_ref[...] + b_ref[...]

    @pl.when(block < half)
    def _():
        send_ref[...] = total

    @pl.when(block >= half)
    def _():
        keep_ref[...] = total


def add_halves(a, b):
    count, height, width = a.shape
    blocks = 4
    half = blocks // 2
    shape = (count // blocks, height, width)
    turned = pl.BlockSpec(shape, lambda i: ((i + half) % blocks, 0, 0))
    return pl.pallas_call(
        add_kernel,
        grid=(blocks,),
        in_specs=[turned] * 2,
        out_specs=[
            pl.BlockSpec(shape, lambda i: (jnp.maximum(i - half, 0), 0, 0)),
            pl.BlockSpec(shape, lambda i: (jnp.minimum(i, half - 1), 0, 0)),
        ],
        out_shape=[jax.ShapeDtypeStruct((count // 2, height, width), BF)] * 2,
        compiler_params=pltpu.CompilerParams(vmem_limit_bytes=60 * MIB),
        cost_estimate=SMALL,
        name="add_halves",
    )(a, b)


def behind(value, *others):
    return lax.optimization_barrier((value,) + others)[0]


class Route:
    def __init__(self, plan, orders):
        self.orders = orders
        count = plan.chips
        maps = np.zeros((2, count), np.int32)
        for core in range(2):
            for i in range(count):
                for s, bit in enumerate(orders[core]):
                    maps[core, i] |= ((i >> (plan.levels - 1 - s)) & 1) << bit
        here, there = jnp.asarray(maps)[plan.core], jnp.asarray(maps)[1 - plan.core]
        self.blocks = jnp.bitwise_xor(plan.chip, here).astype(jnp.int32)
        sent = jnp.bitwise_xor(plan.chip, there).astype(jnp.int32)
        self.devices = jnp.concatenate([2 * sent + 1 - plan.core, 2 * self.blocks + plan.core])
        backs = np.argsort(maps, axis=1).astype(np.int32)
        away = jnp.bitwise_xor(plan.chip, jnp.arange(count, dtype=jnp.int32))
        self.goes_to = jnp.take(jnp.asarray(backs)[plan.core], away, mode="clip")


class Plan:
    def __init__(self, n_img, n_txt):
        self.n_txt = n_txt
        self.n = n_img * n_txt
        self.chips = self.n // 2
        self.ny = n_txt // 2
        self.levels = self.chips.bit_length() - 1
        self.me = lax.axis_index("img") * n_txt + lax.axis_index("txt")
        self.core = self.me % 2
        self.chip = self.me // 2
        self.y = lax.axis_index("txt") // 2
        sources = (self.y - jnp.arange(self.ny, dtype=jnp.int32)) % self.ny
        self.places = jnp.concatenate([2 * sources + self.core, 2 * sources + 1 - self.core])
        at = jnp.arange(n_txt, dtype=jnp.int32)
        self.rows = jnp.bitwise_xor(at % 2, self.core) * self.ny + (self.y - at // 2) % self.ny
        rest = list(range(2, self.levels))
        self.near = Route(self, ([1, 0] + rest, [0, 1] + rest))
        self.small = Route(self, ([0] + rest + [1], [0] + rest + [1]))
        self.mixed = Route(self, ([1, 0] + rest, rest + [0, 1]))
        self.token = None

    def swap(self, value):
        return lax.ppermute(value, BOTH, [(d, d ^ 1) for d in range(self.n)])

    def shift_y(self, value, by):
        pairs = []
        for d in range(self.n):
            img, txt = divmod(d, self.n_txt)
            y, core = divmod(txt, 2)
            pairs.append((d, img * self.n_txt + ((y + by) % self.ny) * 2 + core))
        return lax.ppermute(value, BOTH, pairs)

    def halve(self, value, route, step):
        pairs = [(d, d ^ (2 << route.orders[d % 2][step])) for d in range(self.n)]
        return lax.ppermute(value, BOTH, pairs)

    def send_items(self, value, note=None):
        parts = []
        for k in range(self.ny):
            part = value[(self.y + k) % self.ny]
            if note is not None:
                part = jnp.concatenate([part, note], 0)
            parts.append(self.shift_y(part, k) if k else part)
        return parts

    def join_items(self, parts, length):
        notes = [p[length:] for p in parts] if parts[0].shape[0] > length else []
        return jnp.concatenate([p[:length] for p in parts] + notes, 0)

    def return_items(self, value):
        return [self.shift_y(value[k], -k) if k else value[0] for k in range(self.ny)]

    def order_items(self, parts):
        stacked = jnp.stack(parts)
        return jnp.stack([stacked[(i - self.y) % self.ny] for i in range(self.ny)])

    def start(self, keep, send, route, step=0):
        return keep, self.halve(send, route, step), route, step

    def advance(self, state):
        keep, got, route, step = state
        keep, got, _ = lax.optimization_barrier((keep, got, self.token))
        if keep.shape[0] == 1:
            self.token = keep[0].astype(F32) + got[0].astype(F32)
            return self.token
        if keep.size > 1 << 20:
            keep, send = add_halves(keep, got)
        else:
            total = (keep.astype(F32) + got.astype(F32)).astype(BF)
            keep, send = jnp.split(total, 2)
        keep, send = lax.optimization_barrier((keep, send))
        self.token = send
        return self.start(keep, send, route, step + 1)

    def then(self, *values):
        return lax.optimization_barrier(values + (self.token,))[:-1]


def per_device(
    n_img,
    n_txt,
    image_tokens,
    text_states,
    text_segments,
    item_segments,
    norm1_gain,
    norm1_bias,
    w_qkv,
    w_self_out,
    norm2_gain,
    norm2_bias,
    w_cross_q,
    w_cross_kv,
    w_cross_out,
    norm3_gain,
    norm3_bias,
    w_up,
    w_down,
    cotangent,
):
    plan = Plan(n_img, n_txt)
    core, n, chips, ny = plan.core, plan.n, plan.chips, plan.ny
    items, length, _ = image_tokens.shape
    tokens = items * length
    half_d = D // 2
    rows = D // n

    states = text_states.shape[1]
    ids = jnp.pad(text_segments.astype(BF), ((0, 15), (0, D - states)))
    note = jnp.concatenate([text_states[0], ids], 0)
    x_parts = plan.send_items(image_tokens, note)
    g_parts = plan.send_items(behind(cotangent, x_parts[-1]))
    x_own = plan.join_items(x_parts, length)
    x_other = plan.swap(x_own)

    notes = [v[tokens:].reshape(ny, states + 16, D) for v in (x_own, x_other)]
    notes = jnp.concatenate(notes, 0)
    ids = notes[:, states, :states].reshape(-1)
    states_all = notes[:, :states].reshape(-1, D)
    text_kv = nn(states_all, w_cross_kv).astype(BF)
    matches = ids == item_segments[0, plan.y].astype(BF)
    seen = jnp.where(matches, 0.0, MASKED).astype(F32)[:, None]

    joined, normed1 = project_all(
        x_own, x_other, norm1_gain, norm1_bias, w_qkv, core, plan.places, length
    )
    mixed, mixed_other, lse = attend(joined, plan.rows)
    mixed_got = plan.swap(mixed_other)
    g_own = plan.join_items([behind(p, mixed_got) for p in g_parts], length)
    g_other = plan.swap(g_own)

    norms = (norm2_gain, norm2_bias, norm3_gain, norm3_bias)
    hidden1, hidden2, normed3, cross_q, cross_mixed, cross_lse = cross_part(
        x_own,
        mixed,
        mixed_got,
        text_kv,
        seen,
        norms,
        w_self_out,
        w_cross_q,
        w_cross_out,
        core,
    )

    normed3_other = plan.swap(normed3)
    per_down = w_down.shape[0] // n
    out, grad3, sent, low_keep, high_keep, low_send, high_send = mlp(
        normed3,
        normed3_other,
        g_own,
        g_other,
        w_up,
        w_down,
        core,
        plan.mixed.blocks,
        plan.mixed.goes_to,
    )
    high_got = plan.halve(high_send, plan.mixed, 0)
    got = plan.swap(sent)


    block_out, grad_hidden1, grad_own, grad_other, grad_kv, norm_sums, states_flip, keep, send = (
        cross_back(
            out, got, grad3, hidden2, g_own, norms[:3], seen, cross_lse, cross_mixed, w_cross_out,
            text_kv, cross_q, states_all, w_cross_q, hidden1, mixed, mixed_got, w_self_out,
            core, plan.near.devices,
        )
    )
    grad_other, high_got = lax.optimization_barrier((grad_other, high_got))
    grad_got = plan.swap(grad_other)
    pair_got = plan.swap(behind(send, grad_got))
    plan.token = grad_other
    high_keep, high_got = plan.then(high_keep, high_got)
    low_got = plan.halve(behind(low_send, high_got), plan.mixed, 0)
    high_sum = (high_keep.astype(F32) + high_got.astype(F32)).astype(BF)
    plan.token = high_sum
    next_got = plan.halve(high_sum, plan.mixed, 1)
    block_parts = plan.return_items(block_out.reshape(ny, length, D))

    grad_got, grad_own = plan.then(grad_got, grad_own)
    last_keep, last_send, part_own, part_other = attend_back(
        joined, grad_own, grad_got, mixed, lse, normed1, w_qkv, core, plan.rows, plan.near.blocks
    )
    plan.token = part_other
    last_sums = plan.start(
        last_keep.reshape(chips // 2, 2 * rows, -1),
        last_send.reshape(chips // 2, 2 * rows, -1),
        plan.near,
    )
    send, pair_got, *block_parts = plan.then(send, pair_got, *block_parts)
    middle_keep, middle_send, text_sum = pair_gradients(
        keep, send, pair_got, states_flip, grad_kv
    )
    plan.token = middle_send
    middle_sums = plan.start(
        middle_keep.reshape(chips // 2, rows, -1),
        middle_send.reshape(chips // 2, rows, -1),
        plan.near,
    )
    part_got = plan.swap(behind(part_other, middle_send))
    low_keep, low_got, next_got = plan.then(low_keep, low_got, next_got)
    low_sum = low_keep.astype(F32) + low_got.astype(F32) + next_got.astype(F32)
    plan.token = low_sum = lax.optimization_barrier(low_sum.astype(BF))
    low_keep, low_send = jnp.split(low_sum, 2)
    mlp_sums = plan.start(low_keep, low_send, plan.mixed, 2)
    part_got, part_own = plan.then(part_got, part_own)
    image_grad, norm_keep, norm_send = last_part(
        x_own, part_own, part_got, grad_hidden1, norm1_gain, norm_sums, plan.small.blocks
    )
    plan.token = norm_send
    norm_group = plan.start(
        norm_keep.reshape(chips // 2, 2 * rows, -1),
        norm_send.reshape(chips // 2, 2 * rows, -1),
        plan.small,
    )
    last_sums = plan.advance(last_sums)
    mlp_sums = plan.advance(mlp_sums)
    middle_sums = plan.advance(middle_sums)
    last_sums = plan.advance(last_sums)
    norm_group = plan.advance(norm_group)
    text_sum, image_grad = plan.then(text_sum, image_grad)
    text_part = nt(text_sum, w_cross_kv)
    plan.token = text_part
    text_part = text_part.reshape(ny, states, D)
    text_parts = [plan.shift_y(text_part[r].astype(BF), -r) for r in range(1, ny)]
    image_parts = plan.return_items(image_grad.reshape(ny, length, D))
    block_out = plan.order_items(plan.then(*block_parts))
    for _ in range(plan.levels - 3):
        last_sums = plan.advance(last_sums)
    norm_group = plan.advance(norm_group)
    for _ in range(plan.levels - 3):
        mlp_sums = plan.advance(mlp_sums)
    for _ in range(plan.levels - 3):
        middle_sums = plan.advance(middle_sums)
        norm_group = plan.advance(norm_group)
    middle_sums = plan.advance(middle_sums)
    last_sums = plan.advance(last_sums)
    norm_group = plan.advance(norm_group)
    last_sums = jnp.concatenate([last_sums, norm_group], 1)
    up_down = mlp_sums

    units = w_up.shape[1] // 2
    down_grad = jnp.concatenate([up_down[:, units : units + D], up_down[:, units + D :]], 0)
    parts = jnp.concatenate([up_down[:, :units], last_sums], 1).reshape(2, rows, -1)
    mine = parts[core]
    sent = parts[1 - core].astype(BF)
    theirs = plan.swap(sent)
    plan.token = sent
    text_part, *text_parts = plan.then(text_part, *text_parts)
    text_grad = sum((p.astype(F32) for p in text_parts), text_part[0])
    image_grad = plan.order_items(plan.then(*image_parts)).astype(F32)
    plan.token = image_grad
    (theirs,) = plan.then(theirs)
    theirs = theirs.astype(F32)
    by_core = jnp.where(core == 0, jnp.stack([mine, theirs]), jnp.stack([theirs, mine]))
    up_grad = by_core[:, :, :units].reshape(2, rows, chips, per_down)
    up_grad = up_grad.transpose(1, 2, 0, 3).reshape(rows, 2 * units)
    wide = by_core[:, :, units : units + 3 * half_d].reshape(2, rows, -1, 3, 2 * HEAD)
    wide = wide.transpose(1, 3, 0, 2, 4).reshape(rows, 3 * D)
    up_grad, wide = lax.optimization_barrier((up_grad, wide))
    plan.token = wide
    middle_sums = plan.advance(middle_sums)
    norm_sums = mine[:, -128:-122] + theirs[:, -128:-122]
    return (
        block_out,
        image_grad,
        text_grad[None],
        norm_sums[:, 0],
        norm_sums[:, 1],
        wide,
        middle_sums[:, 2 * D : 3 * D],
        norm_sums[:, 2],
        norm_sums[:, 3],
        middle_sums[:, D : 2 * D],
        middle_sums[:, 3 * D :],
        middle_sums[:, :D],
        norm_sums[:, 4],
        norm_sums[:, 5],
        up_grad,
        down_grad,
    )


def solution(mesh):
    split = P("img", "txt", None)
    rows = P(BOTH)
    wide = P(BOTH, None)
    return jax.shard_map(
        partial(per_device, mesh.shape["img"], mesh.shape["txt"]),
        mesh=mesh,
        in_specs=(split, split, P("img", "txt"), P("img", None)) + (P(),) * 13 + (split,),
        out_specs=(
            (split,) * 3
            + (rows, rows, wide, wide)
            + (rows, rows, wide, wide, wide)
            + (rows, rows, wide, wide)
        ),
        check_vma=False,
    )
```

```python
from functools import partial

import jax
import jax.numpy as jnp
import numpy as np
from jax import lax
from jax.experimental import pallas as pl
from jax.experimental.pallas import tpu as pltpu
from jax.sharding import PartitionSpec as P

D = 1024
HEADS = 16
HEAD = 64
EPS = 1e-05
MASKED = -1e30
SCALE = HEAD**-0.5
LOG2E = 1.4426950408889634
BOTH = ("img", "txt")
BF = jnp.bfloat16
F32 = jnp.float32
QUERY_BLOCK = 256
MIB = 1 << 20
SMALL = pl.CostEstimate(flops=1 << 20, bytes_accessed=1 << 16, transcendentals=0)


def nn(a, b):
    return lax.dot_general(a, b, (((1,), (0,)), ((), ())), preferred_element_type=F32)


def nt(a, b):
    return lax.dot_general(a, b, (((1,), (1,)), ((), ())), preferred_element_type=F32)


def tn(a, b):
    return lax.dot_general(a, b, (((0,), (0,)), ((), ())), preferred_element_type=F32)


def norm_parts(values):
    center = values - jnp.mean(values, axis=-1, keepdims=True)
    rstd = lax.rsqrt(jnp.mean(center * center, axis=-1, keepdims=True) + EPS)
    return center * rstd, rstd


def norm_back(unit, rstd, gain, grad):
    scaled = grad * gain
    return rstd * (
        scaled
        - jnp.mean(scaled, axis=-1, keepdims=True)
        - unit * jnp.mean(scaled * unit, axis=-1, keepdims=True)
    )


TAIL = [
    0.5 * c
    for c in (
        -0.22753805372107494,
        0.8866680711331851,
        -0.6354061073102151,
        0.6495639241196378,
        0.09138668583849363,
        0.235325478247137,
    )
]


def gelu_parts(value):
    t = 1.0 / (1.0 + (0.39 * 0.5**0.5) * jnp.abs(value))
    bell = jnp.exp2(value * value * (-0.5 * LOG2E))
    tail = jnp.full_like(t, TAIL[0])
    for term in TAIL[1:]:
        tail = tail * t + term
    tail = tail * t * bell
    cdf = jnp.where(value > 0.0, 1.0 - tail, tail)
    return value * cdf, cdf + value * bell * (0.5 / np.pi) ** 0.5


def project_kernel(
    core_ref, place_ref, own_ref, other_ref, gain_ref, bias_ref, wq_ref, wk_ref, wv_ref, *refs
):
    joined_ref, normed_ref, held_ref = refs
    block, own_blocks = pl.program_id(0), (pl.num_programs(0) - 1) // 2
    slot = block % 2
    width = wq_ref.shape[1]
    before = held_ref[1 - slot]
    normed_ref[...] = before
    for s, w_ref in enumerate((wq_ref, wk_ref, wv_ref)):
        joined_ref[:, s * width : (s + 1) * width] = nn(before, w_ref[...]).astype(BF)
    tokens = jnp.where(block < own_blocks, own_ref[...], other_ref[...]).astype(F32)
    unit, _ = norm_parts(tokens)
    held_ref[slot] = (unit * gain_ref[...] + bias_ref[...]).astype(BF)


def project_all(own, other, gain, bias, w_qkv, core, places, length):
    blocks = places.shape[0]
    half = blocks // 2
    width = D // 2
    row = pl.BlockSpec((1, D), lambda b, *_: (0, 0))
    weights = [pl.BlockSpec((D, width), lambda b, c, p, s=s: (0, 2 * s + c[0])) for s in range(3)]
    return pl.pallas_call(
        project_kernel,
        grid_spec=pltpu.PrefetchScalarGridSpec(
            num_scalar_prefetch=2,
            grid=(blocks + 1,),
            in_specs=[
                pl.BlockSpec((length, D), lambda b, *_: (jnp.minimum(b, half - 1), 0)),
                pl.BlockSpec((length, D), lambda b, *_: (jnp.clip(b - half, 0, half - 1), 0)),
                row,
                row,
            ]
            + weights,
            out_specs=[
                pl.BlockSpec((length, 3 * width), lambda b, c, p: (p[jnp.maximum(b - 1, 0)], 0)),
                pl.BlockSpec((length, D), lambda b, c, p: (p[jnp.maximum(b - 1, 0)], 0)),
            ],
            scratch_shapes=[pltpu.VMEM((2, length, D), BF)],
        ),
        out_shape=[
            jax.ShapeDtypeStruct((blocks * length, 3 * width), BF),
            jax.ShapeDtypeStruct((blocks * length, D), BF),
        ],
        compiler_params=pltpu.CompilerParams(vmem_limit_bytes=60 * MIB),
        cost_estimate=SMALL,
        name="norm_and_project",
    )(
        core.reshape(1),
        places,
        own,
        other,
        gain.reshape(1, D),
        bias.reshape(1, D),
        w_qkv,
        w_qkv,
        w_qkv,
    )


def middle_kernel(
    core_ref,
    x_ref,
    own_ref,
    got_ref,
    keys_ref,
    values_ref,
    seen_ref,
    gain2_ref,
    bias2_ref,
    gain3_ref,
    bias3_ref,
    w_own_ref,
    w_got_ref,
    w_query_ref,
    w_out_ref,
    hidden1_ref,
    hidden2_ref,
    normed3_ref,
    queries_ref,
    mixed_ref,
    lse_ref,
):
    hidden = x_ref[...].astype(F32) + nn(own_ref[...], w_own_ref[...])
    hidden += nn(got_ref[...], w_got_ref[...])
    hidden1_ref[...] = hidden
    unit, _ = norm_parts(hidden)
    normed2 = (unit * gain2_ref[...] + bias2_ref[...]).astype(BF)
    queries = nn(normed2, w_query_ref[...]).astype(BF)
    queries_ref[...] = queries
    rows, states = queries.shape[0], keys_ref.shape[0]
    half = lax.broadcasted_iota(jnp.int32, (rows, 2 * HEAD), 1) >= HEAD
    v_flip = values_ref[...].T
    ones = jnp.ones((16, states), BF)
    zero = jnp.zeros((rows, 2 * HEAD), BF)

    def score(head):
        at, h = head // 2 * 2 * HEAD, head % 2
        own = jnp.where(half == (h == 1), queries[:, at : at + 2 * HEAD], zero)
        return nt(keys_ref[:, at : at + 2 * HEAD], own)

    def soften(scores):
        scores = scores * (SCALE * LOG2E) + seen_ref[...]
        top = jnp.max(scores, axis=0, keepdims=True)
        return jnp.exp2(scores - top).astype(BF), top

    outs, lses, scores, raised = [], [], {}, {}
    for n in range(HEADS + 2):
        if n < HEADS:
            scores[n] = score(n)
        if 0 <= n - 1 < HEADS:
            raised[n - 1] = soften(scores.pop(n - 1))
        if n >= 2:
            weights, top = raised.pop(n - 2)
            v_rows = jnp.concatenate([v_flip[(n - 2) * HEAD : (n - 1) * HEAD], ones], 0)
            mixed = nn(v_rows, weights)
            total = mixed[HEAD : HEAD + 1]
            lses.append(top + jnp.log2(total))
            outs.append((mixed[:HEAD] / total).astype(BF))
    lse_ref[...] = jnp.concatenate(lses, 0)
    mixed = jnp.concatenate(outs, 0).T
    mixed_ref[...] = mixed
    hidden += nn(mixed, w_out_ref[...])
    hidden2_ref[...] = hidden
    unit, _ = norm_parts(hidden)
    normed3_ref[...] = (unit * gain3_ref[...] + bias3_ref[...]).astype(BF)


def cross_part(x, own, got, text_kv, seen, norms, w_self_out, w_query, w_out, core):
    tokens, width = got.shape
    states = text_kv.shape[0]
    block = min(256, tokens)
    row = pl.BlockSpec((1, D), lambda b, c: (0, 0))
    wide = pl.BlockSpec((block, D), lambda b, c: (b, 0))
    narrow = pl.BlockSpec((block, width), lambda b, c: (b, 0))
    square = pl.BlockSpec((D, D), lambda b, c: (0, 0))
    return pl.pallas_call(
        middle_kernel,
        grid_spec=pltpu.PrefetchScalarGridSpec(
            num_scalar_prefetch=1,
            grid=(tokens // block,),
            in_specs=[
                wide,
                narrow,
                narrow,
                pl.BlockSpec((states, D), lambda b, c: (0, 0)),
                pl.BlockSpec((states, D), lambda b, c: (0, 1)),
                pl.BlockSpec((states, 1), lambda b, c: (0, 0)),
                row,
                row,
                row,
                row,
                pl.BlockSpec((width, D), lambda b, c: (c[0], 0)),
                pl.BlockSpec((width, D), lambda b, c: (1 - c[0], 0)),
                square,
                square,
            ],
            out_specs=[wide] * 5 + [pl.BlockSpec((HEADS, block), lambda b, c: (0, b))],
        ),
        out_shape=[
            jax.ShapeDtypeStruct((tokens, D), F32),
            jax.ShapeDtypeStruct((tokens, D), F32),
            jax.ShapeDtypeStruct((tokens, D), BF),
            jax.ShapeDtypeStruct((tokens, D), BF),
            jax.ShapeDtypeStruct((tokens, D), BF),
            jax.ShapeDtypeStruct((HEADS, tokens), F32),
        ],
        compiler_params=pltpu.CompilerParams(vmem_limit_bytes=60 * MIB),
        cost_estimate=SMALL,
        name="cross_attention_part",
    )(
        core.reshape(1),
        x,
        own,
        got,
        text_kv,
        text_kv,
        seen,
        *[v.reshape(1, D) for v in norms],
        w_self_out,
        w_self_out,
        w_query,
        w_out,
    )


def attend_kernel(row_ref, q_ref, k_ref, v_ref, all_ref, other_ref, lse_ref, out_ref):
    length = q_ref.shape[0]
    block = QUERY_BLOCK
    scale = SCALE * LOG2E
    half = lax.broadcasted_iota(jnp.int32, (block, 2 * HEAD), 1) >= HEAD
    key_row = lax.broadcasted_iota(jnp.int32, (block, block), 0)
    query_col = lax.broadcasted_iota(jnp.int32, (block, block), 1)
    seen = key_row <= query_col
    v_flip = v_ref[...].T
    ones = jnp.ones((16, length), BF)
    v_rows = [jnp.concatenate([v_flip[h * HEAD : (h + 1) * HEAD], ones], 0) for h in range(2)]

    def score(i, h):
        lo, hi = i * block, (i + 1) * block
        queries = q_ref[lo:hi, :]
        own = jnp.where(half == (h == 1), queries, jnp.zeros_like(queries))
        return nt(k_ref[lo:hi, :], own), nt(k_ref[:lo, :], own) if i else None

    def soften(i, h, diag, rest):
        diag = jnp.where(seen, diag, MASKED)
        top = jnp.max(diag, axis=0, keepdims=True)
        if i:
            top = jnp.maximum(top, jnp.max(rest, axis=0, keepdims=True))
            rest = jnp.exp2(rest * scale - top * scale).astype(BF)
        return jnp.exp2(diag * scale - top * scale).astype(BF), rest, top * scale

    def mix(i, h, diag, rest, base):
        lo, hi = i * block, (i + 1) * block
        mixed = nn(v_rows[h][:, lo:hi], diag)
        if i:
            mixed += nn(v_rows[h][:, :lo], rest)
        total = mixed[HEAD : HEAD + 1]
        lse_ref[0, h : h + 1, lo:hi] = base + jnp.log2(total)
        return mixed[:HEAD] / total

    tasks = [(i, h) for i in range(length // block) for h in range(2)]
    scores, raised, outs = {}, {}, []
    part = length // row_ref.shape[0]
    for n in range(len(tasks) + 2):
        if n < len(tasks):
            scores[n] = score(*tasks[n])
        if 0 <= n - 1 < len(tasks):
            raised[n - 1] = soften(*tasks[n - 1], *scores.pop(n - 1))
        if n >= 2:
            outs.append(mix(*tasks[n - 2], *raised.pop(n - 2)))
        if len(outs) == 2:
            lo = tasks[n - 2][0] * block
            result = jnp.concatenate(outs, 0).T.astype(BF)
            outs = []
            for at in range(0, block, part):
                row = pl.multiple_of(row_ref[(lo + at) // part] * part, part)
                out_ref[pl.ds(row, part), :] = result[at : at + part]
    all_ref[...] = out_ref[...]
    other_ref[...] = out_ref[length // 2 :, :]


def head_specs(length, pairs):
    return [
        pl.BlockSpec((length, 2 * HEAD), lambda p, *_, s=s: (0, s * pairs + p)) for s in range(3)
    ]


def attend(joined, rows):
    length, width = joined.shape[0], joined.shape[1] // 3
    pairs = width // (2 * HEAD)
    return pl.pallas_call(
        attend_kernel,
        grid_spec=pltpu.PrefetchScalarGridSpec(
            num_scalar_prefetch=1,
            grid=(pairs,),
            in_specs=head_specs(length, pairs),
            out_specs=[
                pl.BlockSpec((length, 2 * HEAD), lambda p, *_: (0, p)),
                pl.BlockSpec((length // 2, 2 * HEAD), lambda p, *_: (0, p)),
                pl.BlockSpec((1, 2, length), lambda p, *_: (p, 0, 0)),
            ],
            scratch_shapes=[pltpu.VMEM((length, 2 * HEAD), BF)],
        ),
        out_shape=[
            jax.ShapeDtypeStruct((length, width), BF),
            jax.ShapeDtypeStruct((length // 2, width), BF),
            jax.ShapeDtypeStruct((pairs, 2, length), F32),
        ],
        compiler_params=pltpu.CompilerParams(vmem_limit_bytes=60 * MIB),
        cost_estimate=SMALL,
        name="self_attention",
    )(rows, joined, joined, joined)


def attend_back_kernel(
    row_ref,
    block_ref,
    q_ref,
    k_ref,
    v_ref,
    own_g_ref,
    other_g_ref,
    mixed_ref,
    lse_ref,
    normed_hbm,
    wq_ref,
    wk_ref,
    wv_ref,
    keep_ref,
    send_ref,
    own_ref,
    other_ref,
    dq_sum,
    g_ref,
    o_ref,
    normed,
    flip_ref,
    ordered_ref,
    sum_ref,
    sem,
):
    pair, pairs = pl.program_id(0), pl.num_programs(0)
    load = pltpu.make_async_copy(normed_hbm, normed, sem)

    @pl.when(pair == 0)
    def _():
        load.start()

    length = q_ref.shape[0]
    places = row_ref.shape[0]
    part = length // places
    for place in range(places):
        row = row_ref[place]
        at = pl.ds(pl.multiple_of(row % (places // 2) * part, part), part)
        to = slice(place * part, (place + 1) * part)
        mine = row < places // 2
        g_ref[to, :] = jnp.where(mine, own_g_ref[at, :], other_g_ref[at, :])
        o_ref[to, :] = mixed_ref[pl.ds(pl.multiple_of(row * part, part), part), :]
    block = QUERY_BLOCK
    scale = SCALE * LOG2E
    half = lax.broadcasted_iota(jnp.int32, (length, 2 * HEAD), 1) >= HEAD
    key_row = lax.broadcasted_iota(jnp.int32, (block, block), 0)
    query_col = lax.broadcasted_iota(jnp.int32, (block, block), 1)
    seen = key_row <= query_col
    k_flip = k_ref[...].T
    zero = jnp.zeros((length, 2 * HEAD), BF)
    queries = [jnp.where(half == (h == 1), q_ref[...], zero) for h in range(2)]
    grads = [jnp.where(half == (h == 1), g_ref[...], zero) for h in range(2)]
    product = (g_ref[...].astype(F32) * o_ref[...].astype(F32)).T
    deltas = [jnp.sum(product[h * HEAD : (h + 1) * HEAD], axis=0, keepdims=True) for h in range(2)]

    def score(j, h):
        lo, hi = j * block, (j + 1) * block
        return nt(k_ref[lo:hi, :], queries[h][lo:]), nt(v_ref[lo:hi, :], grads[h][lo:])

    def soften(j, h, scores, score_grad):
        lo, hi = j * block, (j + 1) * block
        weights = jnp.exp2(scores * scale - lse_ref[0, h : h + 1, lo:])
        first = jnp.where(seen, weights[:, :block], 0.0)
        weights = jnp.concatenate([first, weights[:, block:]], 1) if hi < length else first
        score_grad = (weights * (score_grad - deltas[h][:, lo:])).astype(BF)
        return weights.astype(BF), score_grad

    def mix(j, h, weights, score_grad):
        lo, hi = j * block, (j + 1) * block
        rows = slice(h * HEAD, (h + 1) * HEAD)
        query_part = nn(k_flip[rows, lo:hi], score_grad)
        if j == 0:
            dq_sum[rows, :] = query_part
        else:
            dq_sum[rows, lo:] += query_part
        return nn(score_grad, queries[h][lo:]), nn(weights, grads[h][lo:])

    tasks = [(j, h) for j in range(length // block) for h in range(2)]
    scores, raised, outs, key_grads, value_grads = {}, {}, [], [], []
    for n in range(len(tasks) + 2):
        if n < len(tasks):
            scores[n] = score(*tasks[n])
        if 0 <= n - 1 < len(tasks):
            raised[n - 1] = soften(*tasks[n - 1], *scores.pop(n - 1))
        if n >= 2:
            outs.append(mix(*tasks[n - 2], *raised.pop(n - 2)))
        if len(outs) == 2:
            key_grads.append(((outs[0][0] + outs[1][0]) * SCALE).astype(BF))
            value_grads.append((outs[0][1] + outs[1][1]).astype(BF))
            outs = []
    query_grad = (dq_sum[...].T * SCALE).astype(BF)
    joined = jnp.concatenate(
        [query_grad, jnp.concatenate(key_grads, 0), jnp.concatenate(value_grads, 0)], 1
    )
    weights = jnp.concatenate([wq_ref[...], wk_ref[...], wv_ref[...]], 1)
    grad = nt(joined, weights)

    @pl.when(pair == 0)
    def _():
        sum_ref[...] = grad
        load.wait()
        flip_ref[...] = normed[...].T
        height = D // block_ref.shape[0]
        for i in range(block_ref.shape[0]):
            at = pl.ds(pl.multiple_of(block_ref[i] * height, height), height)
            ordered_ref[i * height : (i + 1) * height, :] = flip_ref[at, :]

    @pl.when(pair > 0)
    def _():
        sum_ref[...] += grad

    wide = nn(ordered_ref[...], joined).astype(BF)
    keep_ref[...] = wide[: D // 2]
    send_ref[...] = wide[D // 2 :]

    @pl.when(pair == pairs - 1)
    def _():
        for place in range(places):
            row = row_ref[place]
            at = pl.ds(pl.multiple_of(row % (places // 2) * part, part), part)
            rows = sum_ref[place * part : (place + 1) * part, :]

            @pl.when(row < places // 2)
            def _(at=at, rows=rows):
                own_ref[at, :] = rows

            @pl.when(row >= places // 2)
            def _(at=at, rows=rows):
                other_ref[at, :] = rows.astype(BF)


def attend_back(joined, own_g, other_g, mixed, lse, normed, w_qkv, core, rows, blocks):
    length, width = joined.shape[0], joined.shape[1] // 3
    pairs = width // (2 * HEAD)
    spec = pl.BlockSpec((length, 2 * HEAD), lambda p, *_: (0, p))
    half = pl.BlockSpec((length // 2, 2 * HEAD), lambda p, *_: (0, p))
    weights = [
        pl.BlockSpec((D, 2 * HEAD), lambda p, r, b, s=s: (0, (2 * s + r[r.shape[0] - 1]) * pairs + p))
        for s in range(3)
    ]
    sums = pl.BlockSpec((D // 2, 6 * HEAD), lambda p, *_: (0, p))
    out = pl.BlockSpec((length // 2, D), lambda p, *_: (0, 0))
    places = rows.shape[0]

    def body(row_ref, *refs):
        attend_back_kernel(Rows(row_ref, places), *refs)

    return pl.pallas_call(
        body,
        grid_spec=pltpu.PrefetchScalarGridSpec(
            num_scalar_prefetch=2,
            grid=(pairs,),
            in_specs=head_specs(length, pairs)
            + [half] * 2
            + [spec]
            + [pl.BlockSpec((1, 2, length), lambda p, *_: (p, 0, 0))]
            + [pl.BlockSpec(memory_space=pl.ANY)]
            + weights,
            out_specs=[sums, sums, out, out],
            scratch_shapes=[
                pltpu.VMEM((2 * HEAD, length), F32),
                pltpu.VMEM((length, 2 * HEAD), BF),
                pltpu.VMEM((length, 2 * HEAD), BF),
                pltpu.VMEM((length, D), BF),
                pltpu.VMEM((D, length), BF),
                pltpu.VMEM((D, length), BF),
                pltpu.VMEM((length, D), F32),
                pltpu.SemaphoreType.DMA,
            ],
        ),
        out_shape=[jax.ShapeDtypeStruct((D // 2, 3 * width), BF)] * 2
        + [
            jax.ShapeDtypeStruct((length // 2, D), F32),
            jax.ShapeDtypeStruct((length // 2, D), BF),
        ],
        compiler_params=pltpu.CompilerParams(vmem_limit_bytes=60 * MIB),
        cost_estimate=SMALL,
        name="self_attention_back",
    )(
        jnp.concatenate([rows, core.reshape(1)]), blocks, joined, joined, joined, own_g, other_g,
        mixed, lse, normed, w_qkv, w_qkv, w_qkv,
    )


class Rows:
    def __init__(self, ref, count):
        self.ref, self.shape = ref, (count,)

    def __getitem__(self, place):
        return self.ref[place]


def mlp_kernel(
    pieces,
    steps,
    core_ref,
    rows_from,
    goes_to,
    own_ref,
    other_ref,
    own_g_ref,
    other_g_ref,
    *refs,
):
    ups, downs = refs[:pieces], refs[pieces : 2 * pieces]
    down_ref, up_ref, out_ref, norm_ref, sent_ref, *targets = refs[2 * pieces : 2 * pieces + 9]
    flip_ref, ordered_ref, wide_ref, tall_ref, active_ref, grad_ref, sems = refs[2 * pieces + 9 :]
    step = pl.program_id(0)
    slot = step % 2
    tokens = own_ref.shape[0]
    quarter, height = targets[0].shape[0], targets[0].shape[1]
    tile = wide_ref.shape[3]
    width = 2 * height
    per_step = tile // width
    units = steps * tile

    @pl.when(step == 0)
    def _():
        flip_ref[:, :tokens] = own_ref[...].T
        flip_ref[:, tokens:] = other_ref[...].T
        for i in range(4 * quarter):
            at = pl.multiple_of(rows_from[i] * height, height)
            ordered_ref[i * height : (i + 1) * height, :] = flip_ref[pl.ds(at, height), :]

    def wide_copy(at, where, side):
        part = wide_ref.at[at, side * quarter : (side + 1) * quarter]
        lanes = pl.ds(pl.multiple_of(where * tile, tile), tile)
        return pltpu.make_async_copy(part, targets[side].at[:, :, lanes], sems.at[at, side])

    def tall_copy(at, j, r, target, i):
        rows = slice(j * width + r * height, j * width + (r + 1) * height)
        lanes = slice(units + r * D, units + (r + 1) * D)
        return pltpu.make_async_copy(
            tall_ref.at[at, rows], target.at[i, :, lanes], sems.at[at, 4 + 2 * j + r]
        )

    def wait(at):
        for side in range(4):
            wide_copy(at, 0, side).wait()
        for j in range(per_step):
            for r in range(2):
                tall_copy(at, j, r, targets[0], 0).wait()

    @pl.when((step >= 2) & (step < steps + 2))
    def _():
        wait(slot)

    @pl.when(step < steps)
    def _():
        up_w = jnp.concatenate([r[...] for r in ups], 1) if pieces > 1 else ups[0][...]
        down_w = jnp.concatenate([r[...] for r in downs], 0) if pieces > 1 else downs[0][...]
        sides = ((0, own_ref, own_g_ref), (tokens, other_ref, other_g_ref))
        cut = 256
        tasks = [(u, side) for u in range(0, tile, cut) for side in sides]
        found, active, grads = {}, {}, {}

        def products(u, side):
            _, x_ref, g_ref = side
            return nn(x_ref[...], up_w[:, u : u + cut]), nt(g_ref[...], down_w[u : u + cut])

        def units_of(n):
            u, (base, _, _) = tasks[n]
            up_value, down_grad = found.pop(n)
            value, slope = gelu_parts(up_value)
            value = value.astype(BF)
            grad = (down_grad * slope).astype(BF)
            active_ref[step, base : base + tokens, u : u + cut] = value
            grad_ref[step, base : base + tokens, u : u + cut] = grad
            active[n], grads[n] = value, grad

        def weights_of(n):
            u = tasks[n][0]
            grad = jnp.concatenate([grads.pop(n - 1), grads.pop(n)], 0)
            wide = nn(ordered_ref[...], grad).astype(BF)
            wide_ref[slot, :, :, u : u + cut] = wide.reshape(wide_ref.shape[1:3] + (cut,))
            tall = nn(active.pop(n - 1).T, own_g_ref[...]) + nn(active.pop(n).T, other_g_ref[...])
            tall_ref[slot, u : u + cut] = tall.astype(BF)

        for n in range(len(tasks) + 2):
            if n < len(tasks):
                found[n] = products(*tasks[n])
            if 0 <= n - 1 < len(tasks):
                units_of(n - 1)
            if n >= 3 and n % 2:
                weights_of(n - 2)
        for side in range(4):
            wide_copy(slot, step, side).start()
        for j in range(per_step):
            i = goes_to[step * per_step + j]
            for side, target in enumerate(targets):

                @pl.when(i // quarter == side)
                def _(j=j, i=i, side=side, target=target):
                    for r in range(2):
                        tall_copy(slot, j, r, target, i - side * quarter).start()

    @pl.when(step >= steps)
    def _():
        up = up_ref[...]
        if up.shape[1] > units:
            first = core_ref[0] == 0
            picked = []
            for at in range(0, 2 * units, 2 * width):
                picked.append(
                    jnp.where(first, up[:, at : at + width], up[:, at + width : at + 2 * width])
                )
            up = jnp.concatenate(picked, 1)
        active = jnp.concatenate([active_ref[i] for i in range(steps)], 1)
        out = nn(active, down_ref[...].reshape(units, -1))
        grad = jnp.concatenate([grad_ref[i] for i in range(steps)], 1)
        norm = nt(grad, up)
        out_ref[...] = out[:tokens]
        norm_ref[...] = norm[:tokens]
        sent_ref[0] = out[tokens:].astype(BF)
        sent_ref[1] = norm[tokens:].astype(BF)


def mlp(own, other, own_g, other_g, w_up, w_down, core, rows_from, goes_to):
    tokens = own.shape[0]
    chips = rows_from.shape[0]
    tile, out_tile = 512, 256
    units = w_up.shape[1] // 2
    steps = units // tile
    width = units // chips
    height = D // chips
    fine = width % 128 == 0
    tall = w_down.reshape(chips, 2, width, D)
    if fine:
        pieces, piece = tile // width, width
    else:
        pieces, piece = 1, tile
        w_up = w_up.reshape(D, chips, 2, width)[:, :, core].reshape(D, units)
        w_down = w_down.reshape(chips, 2, width, D)[:, core].reshape(units, D)

    def place(s, c, j):
        s = jnp.minimum(s, steps - 1)
        return 2 * (s * pieces + j) + c[0] if fine else s

    def column(s):
        return jnp.maximum(s - steps, 0)

    whole = pl.BlockSpec((tokens, D), lambda s, *_: (0, 0))
    up_specs = [
        pl.BlockSpec((D, piece), lambda s, c, *_, j=j: (0, place(s, c, j))) for j in range(pieces)
    ]
    down_specs = [
        pl.BlockSpec((piece, D), lambda s, c, *_, j=j: (place(s, c, j), 0)) for j in range(pieces)
    ]
    kept = pl.BlockSpec((tokens, out_tile), lambda s, *_: (0, column(s)))
    sums = jax.ShapeDtypeStruct((chips // 4, height, units + 2 * D), BF)
    return pl.pallas_call(
        partial(mlp_kernel, pieces, steps),
        grid_spec=pltpu.PrefetchScalarGridSpec(
            num_scalar_prefetch=3,
            grid=(steps + D // out_tile,),
            in_specs=[whole] * 4
            + up_specs
            + down_specs
            + [
                pl.BlockSpec((chips, None, width, out_tile), lambda s, c, *_: (0, c[0], 0, column(s))),
                pl.BlockSpec((out_tile, w_up.shape[1]), lambda s, *_: (column(s), 0)),
            ],
            out_specs=[
                kept,
                kept,
                pl.BlockSpec((2, tokens, out_tile), lambda s, *_: (0, 0, column(s))),
            ]
            + [pl.BlockSpec(memory_space=pl.ANY)] * 4,
            scratch_shapes=[
                pltpu.VMEM((D, 2 * tokens), BF),
                pltpu.VMEM((D, 2 * tokens), BF),
                pltpu.VMEM((2, chips, height, tile), BF),
                pltpu.VMEM((2, tile, D), BF),
                pltpu.VMEM((steps, 2 * tokens, tile), BF),
                pltpu.VMEM((steps, 2 * tokens, tile), BF),
                pltpu.SemaphoreType.DMA((2, 4 + 2 * (tile // width))),
            ],
        ),
        out_shape=[
            jax.ShapeDtypeStruct((tokens, D), F32),
            jax.ShapeDtypeStruct((tokens, D), F32),
            jax.ShapeDtypeStruct((2, tokens, D), BF),
            sums,
            sums,
            sums,
            sums,
        ],
        compiler_params=pltpu.CompilerParams(vmem_limit_bytes=60 * MIB),
        cost_estimate=SMALL,
        name="mlp_both_ways",
    )(
        core.reshape(1),
        rows_from,
        goes_to,
        own,
        other,
        own_g,
        other_g,
        *([w_up] * pieces),
        *([w_down] * pieces),
        tall,
        w_up,
    )


def cross_back_kernel(
    scalars,
    order_ref,
    got_ref,
    grad3_ref,
    hidden2_ref,
    g_ref,
    gain3_ref,
    gain2_ref,
    seen_ref,
    lse_ref,
    keys_ref,
    values_ref,
    states_ref,
    mixed_hbm,
    w_out_hbm,
    queries_hbm,
    w_query_hbm,
    hidden1_hbm,
    own_hbm,
    other_hbm,
    w_self_hbm,
    out_hbm,
    got_hbm,
    block_ref,
    hidden_grad_ref,
    own_grad_ref,
    other_grad_ref,
    text_ref,
    norms_ref,
    states_flip_ref,
    keep,
    send,
    mixed_ref,
    w_out_ref,
    queries_ref,
    w_query,
    hidden1,
    own_ref,
    other_ref,
    w_self,
    out_ref,
    out_got_ref,
    flip_ref,
    ordered_ref,
    keep_stage,
    send_stage,
    sems,
    out_sems,
):
    core = scalars[0]
    tokens = grad3_ref.shape[0]
    loads = [
        pltpu.make_async_copy(a, b, sems.at[i])
        for i, (a, b) in enumerate(
            (
                (mixed_hbm, mixed_ref),
                (w_out_hbm, w_out_ref),
                (queries_hbm, queries_ref),
                (w_query_hbm, w_query),
                (hidden1_hbm, hidden1),
                (own_hbm.at[:tokens], own_ref),
                (other_hbm, other_ref),
                (w_self_hbm, w_self),
                (out_hbm, out_ref),
                (got_hbm.at[0], out_got_ref),
            )
        )
    ]
    for load in loads:
        load.start()
    count = order_ref.shape[0]
    rows = D // count
    half = D // 2
    writes = []

    def order(depth):
        for i in range(count):
            at = pl.multiple_of(order_ref[i] * rows, rows)
            ordered_ref[i * rows : (i + 1) * rows, :depth] = flip_ref[pl.ds(at, rows), :depth]

    def write(slot, grads):
        keep_stage[slot] = ordered_ref[half:, :tokens].astype(BF)
        lane = slot * (tokens + D)
        lanes = slice(lane, lane + tokens + D)
        send_stage[:, lane : lane + tokens] = ordered_ref[:half, :tokens].astype(BF)
        send_stage[:, lane + tokens : lane + tokens + D] = grads
        writes.append(
            pltpu.make_async_copy(send_stage.at[:, lanes], send.at[:, lanes], out_sems.at[slot])
        )
        writes.append(
            pltpu.make_async_copy(keep_stage.at[slot], keep.at[slot], out_sems.at[4 + slot])
        )
        for copy in writes[-2:]:
            copy.start()

    kind = flip_ref.dtype
    loads[0].wait()
    flip_ref[:, :tokens] = mixed_ref[...].astype(kind).T
    hidden2 = hidden2_ref[...]
    grad3 = grad3_ref[...] + got_ref[...].astype(F32)
    unit, rstd = norm_parts(hidden2)
    norms_ref[4:5, :] = jnp.sum(grad3 * unit, axis=0, keepdims=True)
    norms_ref[5:6, :] = jnp.sum(grad3, axis=0, keepdims=True)
    norms_ref[6:8, :] = jnp.zeros((2, D), F32)
    grad_hidden = norm_back(unit, rstd, gain3_ref[...], grad3) + g_ref[...].astype(F32)
    hidden_grad_ref[...] = grad_hidden
    branch = grad_hidden.astype(BF)
    order(tokens)
    write(0, branch)
    loads[1].wait()
    grad_mixed = nt(branch, w_out_ref[...]).astype(BF)
    loads[2].wait()
    states = keys_ref.shape[0]
    half_lane = lax.broadcasted_iota(jnp.int32, (tokens, 2 * HEAD), 1) >= HEAD
    zero = jnp.zeros((tokens, 2 * HEAD), BF)
    k_flip = keys_ref[...].T

    def score(head):
        lanes = slice(head // 2 * 2 * HEAD, (head // 2 + 1) * 2 * HEAD)
        mine = half_lane == (head % 2 == 1)
        own_q = jnp.where(mine, queries_ref[:, lanes], zero)
        own_g = jnp.where(mine, grad_mixed[:, lanes], zero)
        return nt(keys_ref[:, lanes], own_q), nt(values_ref[:, lanes], own_g), own_q, own_g

    def soften(head, scores, score_grad, own_q, own_g):
        scores = scores * (SCALE * LOG2E) + seen_ref[...]
        weights = jnp.exp2(scores - lse_ref[head : head + 1, :])
        delta = jnp.sum(weights * score_grad, axis=0, keepdims=True)
        score_grad = (weights * (score_grad - delta)).astype(BF)
        return weights.astype(BF), score_grad, own_q, own_g

    scores, raised, flips, key_grads, value_grads = {}, {}, [], [], []
    for n in range(HEADS + 2):
        if n < HEADS:
            scores[n] = score(n)
        if 0 <= n - 1 < HEADS:
            raised[n - 1] = soften(n - 1, *scores.pop(n - 1))
        if n >= 2:
            head = n - 2
            weights, score_grad, own_q, own_g = raised.pop(head)
            key_part, value_part = nn(score_grad, own_q), nn(weights, own_g)
            if head % 2 == 0:
                key_grads.append(key_part)
                value_grads.append(value_part)
            else:
                key_grads[-1] += key_part
                value_grads[-1] += value_part
            part = nn(k_flip[head * HEAD : (head + 1) * HEAD], score_grad)
            flips.append((part * SCALE).astype(BF))
    query_grad = jnp.concatenate(flips, 0).T
    text_grad = jnp.concatenate([p * SCALE for p in key_grads] + value_grads, 1).astype(BF)
    text_ref[...] = text_grad
    flip_ref[:, :states] = states_ref[...].astype(kind).T
    order(states)
    states_flip_ref[...] = ordered_ref[half:, :states].astype(BF)
    part = states * 2 * D // half
    for i in range(half // states):
        send_stage[i * states : (i + 1) * states, 3 * (tokens + D) :] = text_grad[
            :, i * part : (i + 1) * part
        ]
    lanes = slice(3 * (tokens + D), 3 * (tokens + D) + part)
    writes.append(
        pltpu.make_async_copy(send_stage.at[:, lanes], send.at[:, lanes], out_sems.at[3])
    )
    writes[-1].start()
    for load in loads[3:5]:
        load.wait()
    grad2 = nt(query_grad, w_query[...])
    unit, rstd = norm_parts(hidden1[...])
    normed2 = unit * gain2_ref[0:1, :] + gain2_ref[1:2, :]
    flip_ref[:, :tokens] = normed2.astype(BF).astype(kind).T
    order(tokens)
    write(1, query_grad)
    norms_ref[2:3, :] = jnp.sum(grad2 * unit, axis=0, keepdims=True)
    norms_ref[3:4, :] = jnp.sum(grad2, axis=0, keepdims=True)
    norms_ref[0:2, :] = jnp.zeros((2, D), F32)
    grad_hidden = norm_back(unit, rstd, gain2_ref[0:1, :], grad2) + hidden_grad_ref[...]
    hidden_grad_ref[...] = grad_hidden
    branch = grad_hidden.astype(BF)
    for load in loads[5:8]:
        load.wait()
    own_rows = pl.ds(pl.multiple_of(core * half, half), half)
    other_rows = pl.ds(pl.multiple_of((1 - core) * half, half), half)
    own_grad_ref[...] = nt(branch, w_self[own_rows, :]).astype(BF)
    other_grad_ref[...] = nt(branch, w_self[other_rows, :]).astype(BF)
    flip_ref[own_rows, :tokens] = own_ref[...].astype(kind).T
    flip_ref[other_rows, :tokens] = other_ref[...].astype(kind).T
    order(tokens)
    write(2, branch)
    for load in loads[8:]:
        load.wait()
    block_ref[...] = (hidden2_ref[...] + out_ref[...] + out_got_ref[...].astype(F32)).astype(BF)
    for copy in writes:
        copy.wait()


def cross_back(
    out, got, grad3, hidden2, g, norms, seen, lse, mixed, w_out, text_kv, queries, states,
    w_query, hidden1, own, other, w_self, core, order,
):
    tokens, width = other.shape
    count = order.shape[0]
    texts = states.shape[0]
    kind = BF if (D // count) % 16 == 0 else F32

    def full(*shape):
        return pl.BlockSpec(shape, lambda b, *_: (0,) * len(shape))

    wide, late = full(tokens, D), pl.BlockSpec(memory_space=pl.ANY)
    return pl.pallas_call(
        cross_back_kernel,
        grid_spec=pltpu.PrefetchScalarGridSpec(
            num_scalar_prefetch=2,
            grid=(1,),
            in_specs=[
                pl.BlockSpec((None, tokens, D), lambda b, *_: (1, 0, 0)),
                wide,
                wide,
                wide,
                full(1, D),
                full(2, D),
                full(texts, 1),
                full(HEADS, tokens),
                full(texts, D),
                pl.BlockSpec((texts, D), lambda b, *_: (0, 1)),
                full(texts, D),
            ]
            + [late] * 10,
            out_specs=[
                wide,
                wide,
                full(tokens, width),
                full(tokens, width),
                full(texts, 2 * D),
                full(8, D),
                full(D // 2, texts),
                late,
                late,
            ],
            scratch_shapes=[
                pltpu.VMEM((tokens, D), BF),
                pltpu.VMEM((D, D), BF),
                pltpu.VMEM((tokens, D), BF),
                pltpu.VMEM((D, D), BF),
                pltpu.VMEM((tokens, D), F32),
                pltpu.VMEM((tokens, width), BF),
                pltpu.VMEM((tokens, width), BF),
                pltpu.VMEM((D, D), BF),
                pltpu.VMEM((tokens, D), F32),
                pltpu.VMEM((tokens, D), BF),
                pltpu.VMEM((D, tokens), kind),
                pltpu.VMEM((D, tokens), kind),
                pltpu.VMEM((3, D // 2, tokens), BF),
                pltpu.VMEM((D // 2, 3 * (tokens + D) + 4 * texts), BF),
                pltpu.SemaphoreType.DMA((10,)),
                pltpu.SemaphoreType.DMA((7,)),
            ],
        ),
        out_shape=[
            jax.ShapeDtypeStruct((tokens, D), BF),
            jax.ShapeDtypeStruct((tokens, D), F32),
            jax.ShapeDtypeStruct((tokens, width), BF),
            jax.ShapeDtypeStruct((tokens, width), BF),
            jax.ShapeDtypeStruct((texts, 2 * D), BF),
            jax.ShapeDtypeStruct((8, D), F32),
            jax.ShapeDtypeStruct((D // 2, texts), BF),
            jax.ShapeDtypeStruct((3, D // 2, tokens), BF),
            jax.ShapeDtypeStruct((D // 2, 3 * (tokens + D) + 4 * texts), BF),
        ],
        compiler_params=pltpu.CompilerParams(vmem_limit_bytes=60 * MIB),
        cost_estimate=SMALL,
        name="cross_attention_back",
    )(
        core.reshape(1), order, got, grad3, hidden2, g, norms[2].reshape(1, D),
        jnp.stack(norms[:2]), seen, lse, text_kv, text_kv, states, mixed, w_out, queries,
        w_query, hidden1, own, other, w_self, out, got,
    )


def pair_kernel(keep_ref, own_ref, got_ref, states_ref, grad_ref, grad_got_ref, *outs):
    first_ref, second_ref, text_ref = outs
    step = pl.program_id(0)
    half, tokens = keep_ref.shape
    texts = grad_ref.shape[0]

    def put(product):
        first_ref[...] = product[: half // 2].astype(BF)
        second_ref[...] = product[half // 2 :].astype(BF)

    @pl.when(step < 3)
    def _():
        product = nn(keep_ref[...], own_ref[:, tokens:])
        put(product + nn(got_ref[:, :tokens], got_ref[:, tokens:]))

    @pl.when(step >= 3)
    def _():
        got = grad_got_ref[...].astype(F32)
        got = jnp.concatenate([got[:texts], got[texts:]], 1)
        got = jnp.concatenate([got[texts // 2 :], got[: texts // 2]], 0)
        grad = (grad_ref[...].astype(F32) + got).astype(BF)
        text_ref[...] = grad[: texts // 2]
        put(nn(states_ref[...], grad))


def pair_gradients(keep, own, got, states, grad):
    _, half, tokens = keep.shape
    texts = grad.shape[0]

    def third(s):
        return jnp.minimum(s, 2)

    def later(s):
        return jnp.maximum(s - 3, 0)

    wide = pl.BlockSpec((half, tokens + D), lambda s: (0, third(s)))
    lane = 3 * (tokens + D) // (4 * texts)
    grads = pl.BlockSpec((texts, D), lambda s: (0, later(s)))
    out = pl.BlockSpec((half // 2, D), lambda s: (0, s))
    return pl.pallas_call(
        pair_kernel,
        grid=(5,),
        in_specs=[
            pl.BlockSpec((None, half, tokens), lambda s: (third(s), 0, 0)),
            wide,
            wide,
            pl.BlockSpec((half, texts), lambda s: (0, 0)),
            grads,
            pl.BlockSpec((2 * texts, 4 * texts), lambda s: (later(s), lane)),
        ],
        out_specs=[out, out, pl.BlockSpec((texts // 2, D), lambda s: (0, later(s)))],
        out_shape=[jax.ShapeDtypeStruct((half // 2, 5 * D), BF)] * 2
        + [jax.ShapeDtypeStruct((texts // 2, 2 * D), BF)],
        compiler_params=pltpu.CompilerParams(vmem_limit_bytes=60 * MIB),
        cost_estimate=SMALL,
        name="pair_gradients",
    )(keep, own, got, states, grad, got)


def last_kernel(
    blocks_ref,
    x_ref,
    part_ref,
    got_ref,
    hidden_ref,
    gain_ref,
    norms_ref,
    image_ref,
    keep,
    send,
    norm_flip,
):
    count = blocks_ref.shape[0]
    height, half = D // count, D // 2
    grad = part_ref[...] + got_ref[...].astype(F32)
    unit, rstd = norm_parts(x_ref[...].astype(F32))
    sums = [jnp.sum(grad * unit, axis=0, keepdims=True), jnp.sum(grad, axis=0, keepdims=True)]
    image = norm_back(unit, rstd, gain_ref[...], grad) + hidden_ref[...]
    image_ref[...] = image.astype(BF)
    fill = jnp.zeros((norm_flip.shape[1] - 8, D), F32)
    norm_flip[...] = jnp.concatenate(sums + [norms_ref[2:8, :], fill], 0).T
    for i in range(count):
        at = pl.ds(pl.multiple_of(blocks_ref[i] * height, height), height)
        to = i * height % half
        target = keep if i < count // 2 else send
        target[to : to + height, :] = norm_flip[at, :].astype(BF)


def last_part(x, part, got, hidden_grad, gain, norms, blocks):
    tokens = got.shape[0]

    def full(*shape):
        return pl.BlockSpec(shape, lambda b, *_: (0,) * len(shape))

    wide = full(tokens, D)
    return pl.pallas_call(
        last_kernel,
        grid_spec=pltpu.PrefetchScalarGridSpec(
            num_scalar_prefetch=1,
            grid=(1,),
            in_specs=[wide] * 4 + [full(1, D), full(8, D)],
            out_specs=[wide, full(D // 2, 128), full(D // 2, 128)],
            scratch_shapes=[pltpu.VMEM((D, 128), F32)],
        ),
        out_shape=[jax.ShapeDtypeStruct((tokens, D), BF)]
        + [jax.ShapeDtypeStruct((D // 2, 128), BF)] * 2,
        compiler_params=pltpu.CompilerParams(vmem_limit_bytes=60 * MIB),
        cost_estimate=SMALL,
        name="norm_back",
    )(blocks, x, part, got, hidden_grad, gain.reshape(1, D), norms)


def add_kernel(a_ref, b_ref, keep_ref, send_ref):
    block, half = pl.program_id(0), pl.num_programs(0) // 2
    total = a_ref[...] + b_ref[...]

    @pl.when(block < half)
    def _():
        send_ref[...] = total

    @pl.when(block >= half)
    def _():
        keep_ref[...] = total


def add_halves(a, b):
    count, height, width = a.shape
    blocks = 4
    half = blocks // 2
    shape = (count // blocks, height, width)
    turned = pl.BlockSpec(shape, lambda i: ((i + half) % blocks, 0, 0))
    return pl.pallas_call(
        add_kernel,
        grid=(blocks,),
        in_specs=[turned] * 2,
        out_specs=[
            pl.BlockSpec(shape, lambda i: (jnp.maximum(i - half, 0), 0, 0)),
            pl.BlockSpec(shape, lambda i: (jnp.minimum(i, half - 1), 0, 0)),
        ],
        out_shape=[jax.ShapeDtypeStruct((count // 2, height, width), BF)] * 2,
        compiler_params=pltpu.CompilerParams(vmem_limit_bytes=60 * MIB),
        cost_estimate=SMALL,
        name="add_halves",
    )(a, b)


def behind(value, *others):
    return lax.optimization_barrier((value,) + others)[0]


class Route:
    def __init__(self, plan, orders):
        self.orders = orders
        count = plan.chips
        maps = np.zeros((2, count), np.int32)
        for core in range(2):
            for i in range(count):
                for s, bit in enumerate(orders[core]):
                    maps[core, i] |= ((i >> (plan.levels - 1 - s)) & 1) << bit
        here, there = jnp.asarray(maps)[plan.core], jnp.asarray(maps)[1 - plan.core]
        self.blocks = jnp.bitwise_xor(plan.chip, here).astype(jnp.int32)
        sent = jnp.bitwise_xor(plan.chip, there).astype(jnp.int32)
        self.devices = jnp.concatenate([2 * sent + 1 - plan.core, 2 * self.blocks + plan.core])
        backs = np.argsort(maps, axis=1).astype(np.int32)
        away = jnp.bitwise_xor(plan.chip, jnp.arange(count, dtype=jnp.int32))
        self.goes_to = jnp.take(jnp.asarray(backs)[plan.core], away, mode="clip")


class Plan:
    def __init__(self, n_img, n_txt):
        self.n_txt = n_txt
        self.n = n_img * n_txt
        self.chips = self.n // 2
        self.ny = n_txt // 2
        self.levels = self.chips.bit_length() - 1
        self.me = lax.axis_index("img") * n_txt + lax.axis_index("txt")
        self.core = self.me % 2
        self.chip = self.me // 2
        self.y = lax.axis_index("txt") // 2
        sources = (self.y - jnp.arange(self.ny, dtype=jnp.int32)) % self.ny
        self.places = jnp.concatenate([2 * sources + self.core, 2 * sources + 1 - self.core])
        at = jnp.arange(n_txt, dtype=jnp.int32)
        self.rows = jnp.bitwise_xor(at % 2, self.core) * self.ny + (self.y - at // 2) % self.ny
        rest = list(range(2, self.levels))
        self.near = Route(self, ([1, 0] + rest, [0, 1] + rest))
        self.small = Route(self, ([0] + rest + [1], [0] + rest + [1]))
        self.mixed = Route(self, ([1, 0] + rest, rest + [0, 1]))
        self.token = None

    def swap(self, value):
        return lax.ppermute(value, BOTH, [(d, d ^ 1) for d in range(self.n)])

    def shift_y(self, value, by):
        pairs = []
        for d in range(self.n):
            img, txt = divmod(d, self.n_txt)
            y, core = divmod(txt, 2)
            pairs.append((d, img * self.n_txt + ((y + by) % self.ny) * 2 + core))
        return lax.ppermute(value, BOTH, pairs)

    def halve(self, value, route, step):
        pairs = [(d, d ^ (2 << route.orders[d % 2][step])) for d in range(self.n)]
        return lax.ppermute(value, BOTH, pairs)

    def send_items(self, value, note=None):
        parts = []
        for k in range(self.ny):
            part = value[(self.y + k) % self.ny]
            if note is not None:
                part = jnp.concatenate([part, note], 0)
            parts.append(self.shift_y(part, k) if k else part)
        return parts

    def join_items(self, parts, length):
        notes = [p[length:] for p in parts] if parts[0].shape[0] > length else []
        return jnp.concatenate([p[:length] for p in parts] + notes, 0)

    def return_items(self, value):
        return [self.shift_y(value[k], -k) if k else value[0] for k in range(self.ny)]

    def order_items(self, parts):
        stacked = jnp.stack(parts)
        return jnp.stack([stacked[(i - self.y) % self.ny] for i in range(self.ny)])

    def start(self, keep, send, route, step=0):
        return keep, self.halve(send, route, step), route, step

    def advance(self, state):
        keep, got, route, step = state
        keep, got, _ = lax.optimization_barrier((keep, got, self.token))
        if keep.shape[0] == 1:
            self.token = keep[0].astype(F32) + got[0].astype(F32)
            return self.token
        if keep.size > 1 << 20:
            keep, send = add_halves(keep, got)
        else:
            total = (keep.astype(F32) + got.astype(F32)).astype(BF)
            keep, send = jnp.split(total, 2)
        keep, send = lax.optimization_barrier((keep, send))
        self.token = send
        return self.start(keep, send, route, step + 1)

    def then(self, *values):
        return lax.optimization_barrier(values + (self.token,))[:-1]


def per_device(
    n_img,
    n_txt,
    image_tokens,
    text_states,
    text_segments,
    item_segments,
    norm1_gain,
    norm1_bias,
    w_qkv,
    w_self_out,
    norm2_gain,
    norm2_bias,
    w_cross_q,
    w_cross_kv,
    w_cross_out,
    norm3_gain,
    norm3_bias,
    w_up,
    w_down,
    cotangent,
):
    plan = Plan(n_img, n_txt)
    core, n, chips, ny = plan.core, plan.n, plan.chips, plan.ny
    items, length, _ = image_tokens.shape
    tokens = items * length
    half_d = D // 2
    rows = D // n

    states = text_states.shape[1]
    ids = jnp.pad(text_segments.astype(BF), ((0, 15), (0, D - states)))
    note = jnp.concatenate([text_states[0], ids], 0)
    x_parts = plan.send_items(image_tokens, note)
    g_parts = plan.send_items(behind(cotangent, x_parts[-1]))
    x_own = plan.join_items(x_parts, length)
    x_other = plan.swap(x_own)

    notes = [v[tokens:].reshape(ny, states + 16, D) for v in (x_own, x_other)]
    notes = jnp.concatenate(notes, 0)
    ids = notes[:, states, :states].reshape(-1)
    states_all = notes[:, :states].reshape(-1, D)
    text_kv = nn(states_all, w_cross_kv).astype(BF)
    matches = ids == item_segments[0, plan.y].astype(BF)
    seen = jnp.where(matches, 0.0, MASKED).astype(F32)[:, None]

    joined, normed1 = project_all(
        x_own, x_other, norm1_gain, norm1_bias, w_qkv, core, plan.places, length
    )
    mixed, mixed_other, lse = attend(joined, plan.rows)
    mixed_got = plan.swap(mixed_other)
    g_own = plan.join_items([behind(p, mixed_got) for p in g_parts], length)
    g_other = plan.swap(g_own)

    norms = (norm2_gain, norm2_bias, norm3_gain, norm3_bias)
    hidden1, hidden2, normed3, cross_q, cross_mixed, cross_lse = cross_part(
        x_own,
        mixed,
        mixed_got,
        text_kv,
        seen,
        norms,
        w_self_out,
        w_cross_q,
        w_cross_out,
        core,
    )

    normed3_other = plan.swap(normed3)
    per_down = w_down.shape[0] // n
    out, grad3, sent, low_keep, high_keep, low_send, high_send = mlp(
        normed3,
        normed3_other,
        g_own,
        g_other,
        w_up,
        w_down,
        core,
        plan.mixed.blocks,
        plan.mixed.goes_to,
    )
    high_got = plan.halve(high_send, plan.mixed, 0)
    got = plan.swap(sent)


    block_out, grad_hidden1, grad_own, grad_other, grad_kv, norm_sums, states_flip, keep, send = (
        cross_back(
            out, got, grad3, hidden2, g_own, norms[:3], seen, cross_lse, cross_mixed, w_cross_out,
            text_kv, cross_q, states_all, w_cross_q, hidden1, mixed, mixed_got, w_self_out,
            core, plan.near.devices,
        )
    )
    grad_other, high_got = lax.optimization_barrier((grad_other, high_got))
    grad_got = plan.swap(grad_other)
    pair_got = plan.swap(behind(send, grad_got))
    plan.token = grad_other
    high_keep, high_got = plan.then(high_keep, high_got)
    low_got = plan.halve(behind(low_send, high_got), plan.mixed, 0)
    high_sum = (high_keep.astype(F32) + high_got.astype(F32)).astype(BF)
    plan.token = high_sum
    next_got = plan.halve(high_sum, plan.mixed, 1)
    block_parts = plan.return_items(block_out.reshape(ny, length, D))

    grad_got, grad_own = plan.then(grad_got, grad_own)
    last_keep, last_send, part_own, part_other = attend_back(
        joined, grad_own, grad_got, mixed, lse, normed1, w_qkv, core, plan.rows, plan.near.blocks
    )
    plan.token = part_other
    last_sums = plan.start(
        last_keep.reshape(chips // 2, 2 * rows, -1),
        last_send.reshape(chips // 2, 2 * rows, -1),
        plan.near,
    )
    send, pair_got, *block_parts = plan.then(send, pair_got, *block_parts)
    middle_keep, middle_send, text_sum = pair_gradients(
        keep, send, pair_got, states_flip, grad_kv
    )
    plan.token = middle_send
    middle_sums = plan.start(
        middle_keep.reshape(chips // 2, rows, -1),
        middle_send.reshape(chips // 2, rows, -1),
        plan.near,
    )
    part_got = plan.swap(behind(part_other, middle_send))
    low_keep, low_got, next_got = plan.then(low_keep, low_got, next_got)
    low_sum = low_keep.astype(F32) + low_got.astype(F32) + next_got.astype(F32)
    plan.token = low_sum = lax.optimization_barrier(low_sum.astype(BF))
    low_keep, low_send = jnp.split(low_sum, 2)
    mlp_sums = plan.start(low_keep, low_send, plan.mixed, 2)
    part_got, part_own = plan.then(part_got, part_own)
    image_grad, norm_keep, norm_send = last_part(
        x_own, part_own, part_got, grad_hidden1, norm1_gain, norm_sums, plan.small.blocks
    )
    plan.token = norm_send
    norm_group = plan.start(
        norm_keep.reshape(chips // 2, 2 * rows, -1),
        norm_send.reshape(chips // 2, 2 * rows, -1),
        plan.small,
    )
    last_sums = plan.advance(last_sums)
    mlp_sums = plan.advance(mlp_sums)
    last_sums = plan.advance(last_sums)
    middle_sums = plan.advance(middle_sums)
    norm_group = plan.advance(norm_group)
    text_sum, image_grad = plan.then(text_sum, image_grad)
    text_part = nt(text_sum, w_cross_kv)
    plan.token = text_part
    text_part = text_part.reshape(ny, states, D)
    text_parts = [plan.shift_y(text_part[r].astype(BF), -r) for r in range(1, ny)]
    image_parts = plan.return_items(image_grad.reshape(ny, length, D))
    block_out = plan.order_items(plan.then(*block_parts))
    for _ in range(plan.levels - 3):
        last_sums = plan.advance(last_sums)
    norm_group = plan.advance(norm_group)
    for _ in range(plan.levels - 3):
        mlp_sums = plan.advance(mlp_sums)
    for _ in range(plan.levels - 3):
        middle_sums = plan.advance(middle_sums)
        norm_group = plan.advance(norm_group)
    middle_sums = plan.advance(middle_sums)
    last_sums = plan.advance(last_sums)
    norm_group = plan.advance(norm_group)
    last_sums = jnp.concatenate([last_sums, norm_group], 1)
    up_down = mlp_sums

    units = w_up.shape[1] // 2
    down_grad = jnp.concatenate([up_down[:, units : units + D], up_down[:, units + D :]], 0)
    parts = jnp.concatenate([up_down[:, :units], last_sums], 1).reshape(2, rows, -1)
    mine = parts[core]
    sent = parts[1 - core].astype(BF)
    theirs = plan.swap(sent)
    plan.token = sent
    text_part, *text_parts = plan.then(text_part, *text_parts)
    text_grad = sum((p.astype(F32) for p in text_parts), text_part[0])
    image_grad = plan.order_items(plan.then(*image_parts)).astype(F32)
    plan.token = image_grad
    (theirs,) = plan.then(theirs)
    theirs = theirs.astype(F32)
    by_core = jnp.where(core == 0, jnp.stack([mine, theirs]), jnp.stack([theirs, mine]))
    up_grad = by_core[:, :, :units].reshape(2, rows, chips, per_down)
    up_grad = up_grad.transpose(1, 2, 0, 3).reshape(rows, 2 * units)
    wide = by_core[:, :, units : units + 3 * half_d].reshape(2, rows, -1, 3, 2 * HEAD)
    wide = wide.transpose(1, 3, 0, 2, 4).reshape(rows, 3 * D)
    up_grad, wide = lax.optimization_barrier((up_grad, wide))
    plan.token = wide
    middle_sums = plan.advance(middle_sums)
    norm_sums = mine[:, -128:-122] + theirs[:, -128:-122]
    return (
        block_out,
        image_grad,
        text_grad[None],
        norm_sums[:, 0],
        norm_sums[:, 1],
        wide,
        middle_sums[:, 2 * D : 3 * D],
        norm_sums[:, 2],
        norm_sums[:, 3],
        middle_sums[:, D : 2 * D],
        middle_sums[:, 3 * D :],
        middle_sums[:, :D],
        norm_sums[:, 4],
        norm_sums[:, 5],
        up_grad,
        down_grad,
    )


def solution(mesh):
    split = P("img", "txt", None)
    rows = P(BOTH)
    wide = P(BOTH, None)
    return jax.shard_map(
        partial(per_device, mesh.shape["img"], mesh.shape["txt"]),
        mesh=mesh,
        in_specs=(split, split, P("img", "txt"), P("img", None)) + (P(),) * 13 + (split,),
        out_specs=(
            (split,) * 3
            + (rows, rows, wide, wide)
            + (rows, rows, wide, wide, wide)
            + (rows, rows, wide, wide)
        ),
        check_vma=False,
    )
```

```python
from functools import partial

import jax
import jax.numpy as jnp
import numpy as np
from jax import lax
from jax.experimental import pallas as pl
from jax.experimental.pallas import tpu as pltpu
from jax.sharding import PartitionSpec as P

D = 1024
HEADS = 16
HEAD = 64
EPS = 1e-05
MASKED = -1e30
SCALE = HEAD**-0.5
LOG2E = 1.4426950408889634
BOTH = ("img", "txt")
BF = jnp.bfloat16
F32 = jnp.float32
QUERY_BLOCK = 256
MIB = 1 << 20
SMALL = pl.CostEstimate(flops=1 << 20, bytes_accessed=1 << 16, transcendentals=0)


def nn(a, b):
    return lax.dot_general(a, b, (((1,), (0,)), ((), ())), preferred_element_type=F32)


def nt(a, b):
    return lax.dot_general(a, b, (((1,), (1,)), ((), ())), preferred_element_type=F32)


def tn(a, b):
    return lax.dot_general(a, b, (((0,), (0,)), ((), ())), preferred_element_type=F32)


def norm_parts(values):
    center = values - jnp.mean(values, axis=-1, keepdims=True)
    rstd = lax.rsqrt(jnp.mean(center * center, axis=-1, keepdims=True) + EPS)
    return center * rstd, rstd


def norm_back(unit, rstd, gain, grad):
    scaled = grad * gain
    return rstd * (
        scaled
        - jnp.mean(scaled, axis=-1, keepdims=True)
        - unit * jnp.mean(scaled * unit, axis=-1, keepdims=True)
    )


TAIL = [
    0.5 * c
    for c in (
        -0.22753805372107494,
        0.8866680711331851,
        -0.6354061073102151,
        0.6495639241196378,
        0.09138668583849363,
        0.235325478247137,
    )
]


def gelu_parts(value):
    t = 1.0 / (1.0 + (0.39 * 0.5**0.5) * jnp.abs(value))
    bell = jnp.exp2(value * value * (-0.5 * LOG2E))
    tail = jnp.full_like(t, TAIL[0])
    for term in TAIL[1:]:
        tail = tail * t + term
    tail = tail * t * bell
    cdf = jnp.where(value > 0.0, 1.0 - tail, tail)
    return value * cdf, cdf + value * bell * (0.5 / np.pi) ** 0.5


def project_kernel(
    core_ref, place_ref, own_ref, other_ref, gain_ref, bias_ref, wq_ref, wk_ref, wv_ref, *refs
):
    joined_ref, normed_ref, held_ref = refs
    block, own_blocks = pl.program_id(0), (pl.num_programs(0) - 1) // 2
    slot = block % 2
    width = wq_ref.shape[1]
    before = held_ref[1 - slot]
    normed_ref[...] = before
    for s, w_ref in enumerate((wq_ref, wk_ref, wv_ref)):
        joined_ref[:, s * width : (s + 1) * width] = nn(before, w_ref[...]).astype(BF)
    tokens = jnp.where(block < own_blocks, own_ref[...], other_ref[...]).astype(F32)
    unit, _ = norm_parts(tokens)
    held_ref[slot] = (unit * gain_ref[...] + bias_ref[...]).astype(BF)


def project_all(own, other, gain, bias, w_qkv, core, places, length):
    blocks = places.shape[0]
    half = blocks // 2
    width = D // 2
    row = pl.BlockSpec((1, D), lambda b, *_: (0, 0))
    weights = [pl.BlockSpec((D, width), lambda b, c, p, s=s: (0, 2 * s + c[0])) for s in range(3)]
    return pl.pallas_call(
        project_kernel,
        grid_spec=pltpu.PrefetchScalarGridSpec(
            num_scalar_prefetch=2,
            grid=(blocks + 1,),
            in_specs=[
                pl.BlockSpec((length, D), lambda b, *_: (jnp.minimum(b, half - 1), 0)),
                pl.BlockSpec((length, D), lambda b, *_: (jnp.clip(b - half, 0, half - 1), 0)),
                row,
                row,
            ]
            + weights,
            out_specs=[
                pl.BlockSpec((length, 3 * width), lambda b, c, p: (p[jnp.maximum(b - 1, 0)], 0)),
                pl.BlockSpec((length, D), lambda b, c, p: (p[jnp.maximum(b - 1, 0)], 0)),
            ],
            scratch_shapes=[pltpu.VMEM((2, length, D), BF)],
        ),
        out_shape=[
            jax.ShapeDtypeStruct((blocks * length, 3 * width), BF),
            jax.ShapeDtypeStruct((blocks * length, D), BF),
        ],
        compiler_params=pltpu.CompilerParams(vmem_limit_bytes=60 * MIB),
        cost_estimate=SMALL,
        name="norm_and_project",
    )(
        core.reshape(1),
        places,
        own,
        other,
        gain.reshape(1, D),
        bias.reshape(1, D),
        w_qkv,
        w_qkv,
        w_qkv,
    )


def middle_kernel(
    core_ref,
    x_ref,
    own_ref,
    got_ref,
    keys_ref,
    values_ref,
    seen_ref,
    gain2_ref,
    bias2_ref,
    gain3_ref,
    bias3_ref,
    w_own_ref,
    w_got_ref,
    w_query_ref,
    w_out_ref,
    hidden1_ref,
    hidden2_ref,
    normed3_ref,
    queries_ref,
    mixed_ref,
    lse_ref,
):
    hidden = x_ref[...].astype(F32) + nn(own_ref[...], w_own_ref[...])
    hidden += nn(got_ref[...], w_got_ref[...])
    hidden1_ref[...] = hidden
    unit, _ = norm_parts(hidden)
    normed2 = (unit * gain2_ref[...] + bias2_ref[...]).astype(BF)
    queries = nn(normed2, w_query_ref[...]).astype(BF)
    queries_ref[...] = queries
    rows, states = queries.shape[0], keys_ref.shape[0]
    half = lax.broadcasted_iota(jnp.int32, (rows, 2 * HEAD), 1) >= HEAD
    v_flip = values_ref[...].T
    ones = jnp.ones((16, states), BF)
    zero = jnp.zeros((rows, 2 * HEAD), BF)

    def score(head):
        at, h = head // 2 * 2 * HEAD, head % 2
        own = jnp.where(half == (h == 1), queries[:, at : at + 2 * HEAD], zero)
        return nt(keys_ref[:, at : at + 2 * HEAD], own)

    def soften(scores):
        scores = scores * (SCALE * LOG2E) + seen_ref[...]
        top = jnp.max(scores, axis=0, keepdims=True)
        return jnp.exp2(scores - top).astype(BF), top

    outs, lses, scores, raised = [], [], {}, {}
    for n in range(HEADS + 2):
        if n < HEADS:
            scores[n] = score(n)
        if 0 <= n - 1 < HEADS:
            raised[n - 1] = soften(scores.pop(n - 1))
        if n >= 2:
            weights, top = raised.pop(n - 2)
            v_rows = jnp.concatenate([v_flip[(n - 2) * HEAD : (n - 1) * HEAD], ones], 0)
            mixed = nn(v_rows, weights)
            total = mixed[HEAD : HEAD + 1]
            lses.append(top + jnp.log2(total))
            outs.append((mixed[:HEAD] / total).astype(BF))
    lse_ref[...] = jnp.concatenate(lses, 0)
    mixed = jnp.concatenate(outs, 0).T
    mixed_ref[...] = mixed
    hidden += nn(mixed, w_out_ref[...])
    hidden2_ref[...] = hidden
    unit, _ = norm_parts(hidden)
    normed3_ref[...] = (unit * gain3_ref[...] + bias3_ref[...]).astype(BF)


def cross_part(x, own, got, text_kv, seen, norms, w_self_out, w_query, w_out, core):
    tokens, width = got.shape
    states = text_kv.shape[0]
    block = min(256, tokens)
    row = pl.BlockSpec((1, D), lambda b, c: (0, 0))
    wide = pl.BlockSpec((block, D), lambda b, c: (b, 0))
    narrow = pl.BlockSpec((block, width), lambda b, c: (b, 0))
    square = pl.BlockSpec((D, D), lambda b, c: (0, 0))
    return pl.pallas_call(
        middle_kernel,
        grid_spec=pltpu.PrefetchScalarGridSpec(
            num_scalar_prefetch=1,
            grid=(tokens // block,),
            in_specs=[
                wide,
                narrow,
                narrow,
                pl.BlockSpec((states, D), lambda b, c: (0, 0)),
                pl.BlockSpec((states, D), lambda b, c: (0, 1)),
                pl.BlockSpec((states, 1), lambda b, c: (0, 0)),
                row,
                row,
                row,
                row,
                pl.BlockSpec((width, D), lambda b, c: (c[0], 0)),
                pl.BlockSpec((width, D), lambda b, c: (1 - c[0], 0)),
                square,
                square,
            ],
            out_specs=[wide] * 5 + [pl.BlockSpec((HEADS, block), lambda b, c: (0, b))],
        ),
        out_shape=[
            jax.ShapeDtypeStruct((tokens, D), F32),
            jax.ShapeDtypeStruct((tokens, D), F32),
            jax.ShapeDtypeStruct((tokens, D), BF),
            jax.ShapeDtypeStruct((tokens, D), BF),
            jax.ShapeDtypeStruct((tokens, D), BF),
            jax.ShapeDtypeStruct((HEADS, tokens), F32),
        ],
        compiler_params=pltpu.CompilerParams(vmem_limit_bytes=60 * MIB),
        cost_estimate=SMALL,
        name="cross_attention_part",
    )(
        core.reshape(1),
        x,
        own,
        got,
        text_kv,
        text_kv,
        seen,
        *[v.reshape(1, D) for v in norms],
        w_self_out,
        w_self_out,
        w_query,
        w_out,
    )


def attend_kernel(row_ref, q_ref, k_ref, v_ref, all_ref, other_ref, lse_ref, out_ref):
    length = q_ref.shape[0]
    block = QUERY_BLOCK
    scale = SCALE * LOG2E
    half = lax.broadcasted_iota(jnp.int32, (block, 2 * HEAD), 1) >= HEAD
    key_row = lax.broadcasted_iota(jnp.int32, (block, block), 0)
    query_col = lax.broadcasted_iota(jnp.int32, (block, block), 1)
    seen = key_row <= query_col
    v_flip = v_ref[...].T
    ones = jnp.ones((16, length), BF)
    v_rows = [jnp.concatenate([v_flip[h * HEAD : (h + 1) * HEAD], ones], 0) for h in range(2)]

    def score(i, h):
        lo, hi = i * block, (i + 1) * block
        queries = q_ref[lo:hi, :]
        own = jnp.where(half == (h == 1), queries, jnp.zeros_like(queries))
        return nt(k_ref[lo:hi, :], own), nt(k_ref[:lo, :], own) if i else None

    def soften(i, h, diag, rest):
        diag = jnp.where(seen, diag, MASKED)
        top = jnp.max(diag, axis=0, keepdims=True)
        if i:
            top = jnp.maximum(top, jnp.max(rest, axis=0, keepdims=True))
            rest = jnp.exp2(rest * scale - top * scale).astype(BF)
        return jnp.exp2(diag * scale - top * scale).astype(BF), rest, top * scale

    def mix(i, h, diag, rest, base):
        lo, hi = i * block, (i + 1) * block
        mixed = nn(v_rows[h][:, lo:hi], diag)
        if i:
            mixed += nn(v_rows[h][:, :lo], rest)
        total = mixed[HEAD : HEAD + 1]
        lse_ref[0, h : h + 1, lo:hi] = base + jnp.log2(total)
        return mixed[:HEAD] / total

    tasks = [(i, h) for i in range(length // block) for h in range(2)]
    scores, raised, outs = {}, {}, []
    part = length // row_ref.shape[0]
    for n in range(len(tasks) + 2):
        if n < len(tasks):
            scores[n] = score(*tasks[n])
        if 0 <= n - 1 < len(tasks):
            raised[n - 1] = soften(*tasks[n - 1], *scores.pop(n - 1))
        if n >= 2:
            outs.append(mix(*tasks[n - 2], *raised.pop(n - 2)))
        if len(outs) == 2:
            lo = tasks[n - 2][0] * block
            result = jnp.concatenate(outs, 0).T.astype(BF)
            outs = []
            for at in range(0, block, part):
                row = pl.multiple_of(row_ref[(lo + at) // part] * part, part)
                out_ref[pl.ds(row, part), :] = result[at : at + part]
    all_ref[...] = out_ref[...]
    other_ref[...] = out_ref[length // 2 :, :]


def head_specs(length, pairs):
    return [
        pl.BlockSpec((length, 2 * HEAD), lambda p, *_, s=s: (0, s * pairs + p)) for s in range(3)
    ]


def attend(joined, rows):
    length, width = joined.shape[0], joined.shape[1] // 3
    pairs = width // (2 * HEAD)
    return pl.pallas_call(
        attend_kernel,
        grid_spec=pltpu.PrefetchScalarGridSpec(
            num_scalar_prefetch=1,
            grid=(pairs,),
            in_specs=head_specs(length, pairs),
            out_specs=[
                pl.BlockSpec((length, 2 * HEAD), lambda p, *_: (0, p)),
                pl.BlockSpec((length // 2, 2 * HEAD), lambda p, *_: (0, p)),
                pl.BlockSpec((1, 2, length), lambda p, *_: (p, 0, 0)),
            ],
            scratch_shapes=[pltpu.VMEM((length, 2 * HEAD), BF)],
        ),
        out_shape=[
            jax.ShapeDtypeStruct((length, width), BF),
            jax.ShapeDtypeStruct((length // 2, width), BF),
            jax.ShapeDtypeStruct((pairs, 2, length), F32),
        ],
        compiler_params=pltpu.CompilerParams(vmem_limit_bytes=60 * MIB),
        cost_estimate=SMALL,
        name="self_attention",
    )(rows, joined, joined, joined)


def attend_back_kernel(
    row_ref,
    block_ref,
    q_ref,
    k_ref,
    v_ref,
    own_g_ref,
    other_g_ref,
    mixed_ref,
    lse_ref,
    normed_hbm,
    wq_ref,
    wk_ref,
    wv_ref,
    keep_ref,
    send_ref,
    own_ref,
    other_ref,
    dq_sum,
    g_ref,
    o_ref,
    normed,
    flip_ref,
    ordered_ref,
    sum_ref,
    sem,
):
    pair, pairs = pl.program_id(0), pl.num_programs(0)
    load = pltpu.make_async_copy(normed_hbm, normed, sem)

    @pl.when(pair == 0)
    def _():
        load.start()

    length = q_ref.shape[0]
    places = row_ref.shape[0]
    part = length // places
    for place in range(places):
        row = row_ref[place]
        at = pl.ds(pl.multiple_of(row % (places // 2) * part, part), part)
        to = slice(place * part, (place + 1) * part)
        mine = row < places // 2
        g_ref[to, :] = jnp.where(mine, own_g_ref[at, :], other_g_ref[at, :])
        o_ref[to, :] = mixed_ref[pl.ds(pl.multiple_of(row * part, part), part), :]
    block = QUERY_BLOCK
    scale = SCALE * LOG2E
    half = lax.broadcasted_iota(jnp.int32, (length, 2 * HEAD), 1) >= HEAD
    key_row = lax.broadcasted_iota(jnp.int32, (block, block), 0)
    query_col = lax.broadcasted_iota(jnp.int32, (block, block), 1)
    seen = key_row <= query_col
    k_flip = k_ref[...].T
    zero = jnp.zeros((length, 2 * HEAD), BF)
    queries = [jnp.where(half == (h == 1), q_ref[...], zero) for h in range(2)]
    grads = [jnp.where(half == (h == 1), g_ref[...], zero) for h in range(2)]
    product = (g_ref[...].astype(F32) * o_ref[...].astype(F32)).T
    deltas = [jnp.sum(product[h * HEAD : (h + 1) * HEAD], axis=0, keepdims=True) for h in range(2)]

    def score(j, h):
        lo, hi = j * block, (j + 1) * block
        return nt(k_ref[lo:hi, :], queries[h][lo:]), nt(v_ref[lo:hi, :], grads[h][lo:])

    def soften(j, h, scores, score_grad):
        lo, hi = j * block, (j + 1) * block
        weights = jnp.exp2(scores * scale - lse_ref[0, h : h + 1, lo:])
        first = jnp.where(seen, weights[:, :block], 0.0)
        weights = jnp.concatenate([first, weights[:, block:]], 1) if hi < length else first
        score_grad = (weights * (score_grad - deltas[h][:, lo:])).astype(BF)
        return weights.astype(BF), score_grad

    def mix(j, h, weights, score_grad):
        lo, hi = j * block, (j + 1) * block
        rows = slice(h * HEAD, (h + 1) * HEAD)
        query_part = nn(k_flip[rows, lo:hi], score_grad)
        if j == 0:
            dq_sum[rows, :] = query_part
        else:
            dq_sum[rows, lo:] += query_part
        return nn(score_grad, queries[h][lo:]), nn(weights, grads[h][lo:])

    tasks = [(j, h) for j in range(length // block) for h in range(2)]
    scores, raised, outs, key_grads, value_grads = {}, {}, [], [], []
    for n in range(len(tasks) + 2):
        if n < len(tasks):
            scores[n] = score(*tasks[n])
        if 0 <= n - 1 < len(tasks):
            raised[n - 1] = soften(*tasks[n - 1], *scores.pop(n - 1))
        if n >= 2:
            outs.append(mix(*tasks[n - 2], *raised.pop(n - 2)))
        if len(outs) == 2:
            key_grads.append(((outs[0][0] + outs[1][0]) * SCALE).astype(BF))
            value_grads.append((outs[0][1] + outs[1][1]).astype(BF))
            outs = []
    query_grad = (dq_sum[...].T * SCALE).astype(BF)
    joined = jnp.concatenate(
        [query_grad, jnp.concatenate(key_grads, 0), jnp.concatenate(value_grads, 0)], 1
    )
    weights = jnp.concatenate([wq_ref[...], wk_ref[...], wv_ref[...]], 1)
    grad = nt(joined, weights)

    @pl.when(pair == 0)
    def _():
        sum_ref[...] = grad
        load.wait()
        flip_ref[...] = normed[...].T
        height = D // block_ref.shape[0]
        for i in range(block_ref.shape[0]):
            at = pl.ds(pl.multiple_of(block_ref[i] * height, height), height)
            ordered_ref[i * height : (i + 1) * height, :] = flip_ref[at, :]

    @pl.when(pair > 0)
    def _():
        sum_ref[...] += grad

    wide = nn(ordered_ref[...], joined).astype(BF)
    keep_ref[...] = wide[: D // 2]
    send_ref[...] = wide[D // 2 :]

    @pl.when(pair == pairs - 1)
    def _():
        for place in range(places):
            row = row_ref[place]
            at = pl.ds(pl.multiple_of(row % (places // 2) * part, part), part)
            rows = sum_ref[place * part : (place + 1) * part, :]

            @pl.when(row < places // 2)
            def _(at=at, rows=rows):
                own_ref[at, :] = rows

            @pl.when(row >= places // 2)
            def _(at=at, rows=rows):
                other_ref[at, :] = rows.astype(BF)


def attend_back(joined, own_g, other_g, mixed, lse, normed, w_qkv, core, rows, blocks):
    length, width = joined.shape[0], joined.shape[1] // 3
    pairs = width // (2 * HEAD)
    spec = pl.BlockSpec((length, 2 * HEAD), lambda p, *_: (0, p))
    half = pl.BlockSpec((length // 2, 2 * HEAD), lambda p, *_: (0, p))
    weights = [
        pl.BlockSpec((D, 2 * HEAD), lambda p, r, b, s=s: (0, (2 * s + r[r.shape[0] - 1]) * pairs + p))
        for s in range(3)
    ]
    sums = pl.BlockSpec((D // 2, 6 * HEAD), lambda p, *_: (0, p))
    out = pl.BlockSpec((length // 2, D), lambda p, *_: (0, 0))
    places = rows.shape[0]

    def body(row_ref, *refs):
        attend_back_kernel(Rows(row_ref, places), *refs)

    return pl.pallas_call(
        body,
        grid_spec=pltpu.PrefetchScalarGridSpec(
            num_scalar_prefetch=2,
            grid=(pairs,),
            in_specs=head_specs(length, pairs)
            + [half] * 2
            + [spec]
            + [pl.BlockSpec((1, 2, length), lambda p, *_: (p, 0, 0))]
            + [pl.BlockSpec(memory_space=pl.ANY)]
            + weights,
            out_specs=[sums, sums, out, out],
            scratch_shapes=[
                pltpu.VMEM((2 * HEAD, length), F32),
                pltpu.VMEM((length, 2 * HEAD), BF),
                pltpu.VMEM((length, 2 * HEAD), BF),
                pltpu.VMEM((length, D), BF),
                pltpu.VMEM((D, length), BF),
                pltpu.VMEM((D, length), BF),
                pltpu.VMEM((length, D), F32),
                pltpu.SemaphoreType.DMA,
            ],
        ),
        out_shape=[jax.ShapeDtypeStruct((D // 2, 3 * width), BF)] * 2
        + [
            jax.ShapeDtypeStruct((length // 2, D), F32),
            jax.ShapeDtypeStruct((length // 2, D), BF),
        ],
        compiler_params=pltpu.CompilerParams(vmem_limit_bytes=60 * MIB),
        cost_estimate=SMALL,
        name="self_attention_back",
    )(
        jnp.concatenate([rows, core.reshape(1)]), blocks, joined, joined, joined, own_g, other_g,
        mixed, lse, normed, w_qkv, w_qkv, w_qkv,
    )


class Rows:
    def __init__(self, ref, count):
        self.ref, self.shape = ref, (count,)

    def __getitem__(self, place):
        return self.ref[place]


def mlp_kernel(
    pieces,
    steps,
    core_ref,
    rows_from,
    goes_to,
    own_ref,
    other_ref,
    own_g_ref,
    other_g_ref,
    *refs,
):
    ups, downs = refs[:pieces], refs[pieces : 2 * pieces]
    down_ref, up_ref, out_ref, norm_ref, sent_ref, *targets = refs[2 * pieces : 2 * pieces + 9]
    flip_ref, ordered_ref, wide_ref, tall_ref, active_ref, grad_ref, sems = refs[2 * pieces + 9 :]
    step = pl.program_id(0)
    slot = step % 2
    tokens = own_ref.shape[0]
    quarter, height = targets[0].shape[0], targets[0].shape[1]
    tile = wide_ref.shape[3]
    width = 2 * height
    per_step = tile // width
    units = steps * tile

    @pl.when(step == 0)
    def _():
        flip_ref[:, :tokens] = own_ref[...].T
        flip_ref[:, tokens:] = other_ref[...].T
        for i in range(4 * quarter):
            at = pl.multiple_of(rows_from[i] * height, height)
            ordered_ref[i * height : (i + 1) * height, :] = flip_ref[pl.ds(at, height), :]

    def wide_copy(at, where, side):
        part = wide_ref.at[at, side * quarter : (side + 1) * quarter]
        lanes = pl.ds(pl.multiple_of(where * tile, tile), tile)
        return pltpu.make_async_copy(part, targets[side].at[:, :, lanes], sems.at[at, side])

    def tall_copy(at, j, r, target, i):
        rows = slice(j * width + r * height, j * width + (r + 1) * height)
        lanes = slice(units + r * D, units + (r + 1) * D)
        return pltpu.make_async_copy(
            tall_ref.at[at, rows], target.at[i, :, lanes], sems.at[at, 4 + 2 * j + r]
        )

    def wait(at):
        for side in range(4):
            wide_copy(at, 0, side).wait()
        for j in range(per_step):
            for r in range(2):
                tall_copy(at, j, r, targets[0], 0).wait()

    @pl.when((step >= 2) & (step < steps + 2))
    def _():
        wait(slot)

    @pl.when(step < steps)
    def _():
        up_w = jnp.concatenate([r[...] for r in ups], 1) if pieces > 1 else ups[0][...]
        down_w = jnp.concatenate([r[...] for r in downs], 0) if pieces > 1 else downs[0][...]
        sides = ((0, own_ref, own_g_ref), (tokens, other_ref, other_g_ref))
        cut = 256
        tasks = [(u, side) for u in range(0, tile, cut) for side in sides]
        found, active, grads = {}, {}, {}

        def products(u, side):
            _, x_ref, g_ref = side
            return nn(x_ref[...], up_w[:, u : u + cut]), nt(g_ref[...], down_w[u : u + cut])

        def units_of(n):
            u, (base, _, _) = tasks[n]
            up_value, down_grad = found.pop(n)
            value, slope = gelu_parts(up_value)
            value = value.astype(BF)
            grad = (down_grad * slope).astype(BF)
            active_ref[step, base : base + tokens, u : u + cut] = value
            grad_ref[step, base : base + tokens, u : u + cut] = grad
            active[n], grads[n] = value, grad

        def weights_of(n):
            u = tasks[n][0]
            grad = jnp.concatenate([grads.pop(n - 1), grads.pop(n)], 0)
            wide = nn(ordered_ref[...], grad).astype(BF)
            wide_ref[slot, :, :, u : u + cut] = wide.reshape(wide_ref.shape[1:3] + (cut,))
            tall = nn(active.pop(n - 1).T, own_g_ref[...]) + nn(active.pop(n).T, other_g_ref[...])
            tall_ref[slot, u : u + cut] = tall.astype(BF)

        for n in range(len(tasks) + 2):
            if n < len(tasks):
                found[n] = products(*tasks[n])
            if 0 <= n - 1 < len(tasks):
                units_of(n - 1)
            if n >= 3 and n % 2:
                weights_of(n - 2)
        for side in range(4):
            wide_copy(slot, step, side).start()
        for j in range(per_step):
            i = goes_to[step * per_step + j]
            for side, target in enumerate(targets):

                @pl.when(i // quarter == side)
                def _(j=j, i=i, side=side, target=target):
                    for r in range(2):
                        tall_copy(slot, j, r, target, i - side * quarter).start()

    @pl.when(step >= steps)
    def _():
        up = up_ref[...]
        if up.shape[1] > units:
            first = core_ref[0] == 0
            picked = []
            for at in range(0, 2 * units, 2 * width):
                picked.append(
                    jnp.where(first, up[:, at : at + width], up[:, at + width : at + 2 * width])
                )
            up = jnp.concatenate(picked, 1)
        active = jnp.concatenate([active_ref[i] for i in range(steps)], 1)
        out = nn(active, down_ref[...].reshape(units, -1))
        grad = jnp.concatenate([grad_ref[i] for i in range(steps)], 1)
        norm = nt(grad, up)
        out_ref[...] = out[:tokens]
        norm_ref[...] = norm[:tokens]
        sent_ref[0] = out[tokens:].astype(BF)
        sent_ref[1] = norm[tokens:].astype(BF)


def mlp(own, other, own_g, other_g, w_up, w_down, core, rows_from, goes_to):
    tokens = own.shape[0]
    chips = rows_from.shape[0]
    tile, out_tile = 512, 256
    units = w_up.shape[1] // 2
    steps = units // tile
    width = units // chips
    height = D // chips
    fine = width % 128 == 0
    tall = w_down.reshape(chips, 2, width, D)
    if fine:
        pieces, piece = tile // width, width
    else:
        pieces, piece = 1, tile
        w_up = w_up.reshape(D, chips, 2, width)[:, :, core].reshape(D, units)
        w_down = w_down.reshape(chips, 2, width, D)[:, core].reshape(units, D)

    def place(s, c, j):
        s = jnp.minimum(s, steps - 1)
        return 2 * (s * pieces + j) + c[0] if fine else s

    def column(s):
        return jnp.maximum(s - steps, 0)

    whole = pl.BlockSpec((tokens, D), lambda s, *_: (0, 0))
    up_specs = [
        pl.BlockSpec((D, piece), lambda s, c, *_, j=j: (0, place(s, c, j))) for j in range(pieces)
    ]
    down_specs = [
        pl.BlockSpec((piece, D), lambda s, c, *_, j=j: (place(s, c, j), 0)) for j in range(pieces)
    ]
    kept = pl.BlockSpec((tokens, out_tile), lambda s, *_: (0, column(s)))
    sums = jax.ShapeDtypeStruct((chips // 4, height, units + 2 * D), BF)
    return pl.pallas_call(
        partial(mlp_kernel, pieces, steps),
        grid_spec=pltpu.PrefetchScalarGridSpec(
            num_scalar_prefetch=3,
            grid=(steps + D // out_tile,),
            in_specs=[whole] * 4
            + up_specs
            + down_specs
            + [
                pl.BlockSpec((chips, None, width, out_tile), lambda s, c, *_: (0, c[0], 0, column(s))),
                pl.BlockSpec((out_tile, w_up.shape[1]), lambda s, *_: (column(s), 0)),
            ],
            out_specs=[
                kept,
                kept,
                pl.BlockSpec((2, tokens, out_tile), lambda s, *_: (0, 0, column(s))),
            ]
            + [pl.BlockSpec(memory_space=pl.ANY)] * 4,
            scratch_shapes=[
                pltpu.VMEM((D, 2 * tokens), BF),
                pltpu.VMEM((D, 2 * tokens), BF),
                pltpu.VMEM((2, chips, height, tile), BF),
                pltpu.VMEM((2, tile, D), BF),
                pltpu.VMEM((steps, 2 * tokens, tile), BF),
                pltpu.VMEM((steps, 2 * tokens, tile), BF),
                pltpu.SemaphoreType.DMA((2, 4 + 2 * (tile // width))),
            ],
        ),
        out_shape=[
            jax.ShapeDtypeStruct((tokens, D), F32),
            jax.ShapeDtypeStruct((tokens, D), F32),
            jax.ShapeDtypeStruct((2, tokens, D), BF),
            sums,
            sums,
            sums,
            sums,
        ],
        compiler_params=pltpu.CompilerParams(vmem_limit_bytes=60 * MIB),
        cost_estimate=SMALL,
        name="mlp_both_ways",
    )(
        core.reshape(1),
        rows_from,
        goes_to,
        own,
        other,
        own_g,
        other_g,
        *([w_up] * pieces),
        *([w_down] * pieces),
        tall,
        w_up,
    )


def cross_back_kernel(
    scalars,
    order_ref,
    got_ref,
    grad3_ref,
    hidden2_ref,
    g_ref,
    gain3_ref,
    gain2_ref,
    seen_ref,
    lse_ref,
    keys_ref,
    values_ref,
    states_ref,
    mixed_hbm,
    w_out_hbm,
    queries_hbm,
    w_query_hbm,
    hidden1_hbm,
    own_hbm,
    other_hbm,
    w_self_hbm,
    out_hbm,
    got_hbm,
    block_ref,
    hidden_grad_ref,
    own_grad_ref,
    other_grad_ref,
    text_ref,
    norms_ref,
    states_flip_ref,
    keep,
    send,
    mixed_ref,
    w_out_ref,
    queries_ref,
    w_query,
    hidden1,
    own_ref,
    other_ref,
    w_self,
    out_ref,
    out_got_ref,
    flip_ref,
    ordered_ref,
    keep_stage,
    send_stage,
    sems,
    out_sems,
):
    core = scalars[0]
    tokens = grad3_ref.shape[0]
    loads = [
        pltpu.make_async_copy(a, b, sems.at[i])
        for i, (a, b) in enumerate(
            (
                (mixed_hbm, mixed_ref),
                (w_out_hbm, w_out_ref),
                (queries_hbm, queries_ref),
                (w_query_hbm, w_query),
                (hidden1_hbm, hidden1),
                (own_hbm.at[:tokens], own_ref),
                (other_hbm, other_ref),
                (w_self_hbm, w_self),
                (out_hbm, out_ref),
                (got_hbm.at[0], out_got_ref),
            )
        )
    ]
    for load in loads:
        load.start()
    count = order_ref.shape[0]
    rows = D // count
    half = D // 2
    writes = []

    def order(depth):
        for i in range(count):
            at = pl.multiple_of(order_ref[i] * rows, rows)
            ordered_ref[i * rows : (i + 1) * rows, :depth] = flip_ref[pl.ds(at, rows), :depth]

    def write(slot, grads):
        keep_stage[slot] = ordered_ref[half:, :tokens].astype(BF)
        lane = slot * (tokens + D)
        lanes = slice(lane, lane + tokens + D)
        send_stage[:, lane : lane + tokens] = ordered_ref[:half, :tokens].astype(BF)
        send_stage[:, lane + tokens : lane + tokens + D] = grads
        writes.append(
            pltpu.make_async_copy(send_stage.at[:, lanes], send.at[:, lanes], out_sems.at[slot])
        )
        writes.append(
            pltpu.make_async_copy(keep_stage.at[slot], keep.at[slot], out_sems.at[4 + slot])
        )
        for copy in writes[-2:]:
            copy.start()

    kind = flip_ref.dtype
    loads[0].wait()
    flip_ref[:, :tokens] = mixed_ref[...].astype(kind).T
    hidden2 = hidden2_ref[...]
    grad3 = grad3_ref[...] + got_ref[...].astype(F32)
    unit, rstd = norm_parts(hidden2)
    norms_ref[4:5, :] = jnp.sum(grad3 * unit, axis=0, keepdims=True)
    norms_ref[5:6, :] = jnp.sum(grad3, axis=0, keepdims=True)
    norms_ref[6:8, :] = jnp.zeros((2, D), F32)
    grad_hidden = norm_back(unit, rstd, gain3_ref[...], grad3) + g_ref[...].astype(F32)
    hidden_grad_ref[...] = grad_hidden
    branch = grad_hidden.astype(BF)
    order(tokens)
    write(0, branch)
    loads[1].wait()
    grad_mixed = nt(branch, w_out_ref[...]).astype(BF)
    loads[2].wait()
    states = keys_ref.shape[0]
    half_lane = lax.broadcasted_iota(jnp.int32, (tokens, 2 * HEAD), 1) >= HEAD
    zero = jnp.zeros((tokens, 2 * HEAD), BF)
    k_flip = keys_ref[...].T

    def score(head):
        lanes = slice(head // 2 * 2 * HEAD, (head // 2 + 1) * 2 * HEAD)
        mine = half_lane == (head % 2 == 1)
        own_q = jnp.where(mine, queries_ref[:, lanes], zero)
        own_g = jnp.where(mine, grad_mixed[:, lanes], zero)
        return nt(keys_ref[:, lanes], own_q), nt(values_ref[:, lanes], own_g), own_q, own_g

    def soften(head, scores, score_grad, own_q, own_g):
        scores = scores * (SCALE * LOG2E) + seen_ref[...]
        weights = jnp.exp2(scores - lse_ref[head : head + 1, :])
        delta = jnp.sum(weights * score_grad, axis=0, keepdims=True)
        score_grad = (weights * (score_grad - delta)).astype(BF)
        return weights.astype(BF), score_grad, own_q, own_g

    scores, raised, flips, key_grads, value_grads = {}, {}, [], [], []
    for n in range(HEADS + 2):
        if n < HEADS:
            scores[n] = score(n)
        if 0 <= n - 1 < HEADS:
            raised[n - 1] = soften(n - 1, *scores.pop(n - 1))
        if n >= 2:
            head = n - 2
            weights, score_grad, own_q, own_g = raised.pop(head)
            key_part, value_part = nn(score_grad, own_q), nn(weights, own_g)
            if head % 2 == 0:
                key_grads.append(key_part)
                value_grads.append(value_part)
            else:
                key_grads[-1] += key_part
                value_grads[-1] += value_part
            part = nn(k_flip[head * HEAD : (head + 1) * HEAD], score_grad)
            flips.append((part * SCALE).astype(BF))
    query_grad = jnp.concatenate(flips, 0).T
    text_grad = jnp.concatenate([p * SCALE for p in key_grads] + value_grads, 1).astype(BF)
    text_ref[...] = text_grad
    flip_ref[:, :states] = states_ref[...].astype(kind).T
    order(states)
    states_flip_ref[...] = ordered_ref[half:, :states].astype(BF)
    part = states * 2 * D // half
    for i in range(half // states):
        send_stage[i * states : (i + 1) * states, 3 * (tokens + D) :] = text_grad[
            :, i * part : (i + 1) * part
        ]
    lanes = slice(3 * (tokens + D), 3 * (tokens + D) + part)
    writes.append(
        pltpu.make_async_copy(send_stage.at[:, lanes], send.at[:, lanes], out_sems.at[3])
    )
    writes[-1].start()
    for load in loads[3:5]:
        load.wait()
    grad2 = nt(query_grad, w_query[...])
    unit, rstd = norm_parts(hidden1[...])
    normed2 = unit * gain2_ref[0:1, :] + gain2_ref[1:2, :]
    flip_ref[:, :tokens] = normed2.astype(BF).astype(kind).T
    order(tokens)
    write(1, query_grad)
    norms_ref[2:3, :] = jnp.sum(grad2 * unit, axis=0, keepdims=True)
    norms_ref[3:4, :] = jnp.sum(grad2, axis=0, keepdims=True)
    norms_ref[0:2, :] = jnp.zeros((2, D), F32)
    grad_hidden = norm_back(unit, rstd, gain2_ref[0:1, :], grad2) + hidden_grad_ref[...]
    hidden_grad_ref[...] = grad_hidden
    branch = grad_hidden.astype(BF)
    for load in loads[5:8]:
        load.wait()
    own_rows = pl.ds(pl.multiple_of(core * half, half), half)
    other_rows = pl.ds(pl.multiple_of((1 - core) * half, half), half)
    own_grad_ref[...] = nt(branch, w_self[own_rows, :]).astype(BF)
    other_grad_ref[...] = nt(branch, w_self[other_rows, :]).astype(BF)
    flip_ref[own_rows, :tokens] = own_ref[...].astype(kind).T
    flip_ref[other_rows, :tokens] = other_ref[...].astype(kind).T
    order(tokens)
    write(2, branch)
    for load in loads[8:]:
        load.wait()
    block_ref[...] = (hidden2_ref[...] + out_ref[...] + out_got_ref[...].astype(F32)).astype(BF)
    for copy in writes:
        copy.wait()


def cross_back(
    out, got, grad3, hidden2, g, norms, seen, lse, mixed, w_out, text_kv, queries, states,
    w_query, hidden1, own, other, w_self, core, order,
):
    tokens, width = other.shape
    count = order.shape[0]
    texts = states.shape[0]
    kind = BF if (D // count) % 16 == 0 else F32

    def full(*shape):
        return pl.BlockSpec(shape, lambda b, *_: (0,) * len(shape))

    wide, late = full(tokens, D), pl.BlockSpec(memory_space=pl.ANY)
    return pl.pallas_call(
        cross_back_kernel,
        grid_spec=pltpu.PrefetchScalarGridSpec(
            num_scalar_prefetch=2,
            grid=(1,),
            in_specs=[
                pl.BlockSpec((None, tokens, D), lambda b, *_: (1, 0, 0)),
                wide,
                wide,
                wide,
                full(1, D),
                full(2, D),
                full(texts, 1),
                full(HEADS, tokens),
                full(texts, D),
                pl.BlockSpec((texts, D), lambda b, *_: (0, 1)),
                full(texts, D),
            ]
            + [late] * 10,
            out_specs=[
                wide,
                wide,
                full(tokens, width),
                full(tokens, width),
                full(texts, 2 * D),
                full(8, D),
                full(D // 2, texts),
                late,
                late,
            ],
            scratch_shapes=[
                pltpu.VMEM((tokens, D), BF),
                pltpu.VMEM((D, D), BF),
                pltpu.VMEM((tokens, D), BF),
                pltpu.VMEM((D, D), BF),
                pltpu.VMEM((tokens, D), F32),
                pltpu.VMEM((tokens, width), BF),
                pltpu.VMEM((tokens, width), BF),
                pltpu.VMEM((D, D), BF),
                pltpu.VMEM((tokens, D), F32),
                pltpu.VMEM((tokens, D), BF),
                pltpu.VMEM((D, tokens), kind),
                pltpu.VMEM((D, tokens), kind),
                pltpu.VMEM((3, D // 2, tokens), BF),
                pltpu.VMEM((D // 2, 3 * (tokens + D) + 4 * texts), BF),
                pltpu.SemaphoreType.DMA((10,)),
                pltpu.SemaphoreType.DMA((7,)),
            ],
        ),
        out_shape=[
            jax.ShapeDtypeStruct((tokens, D), BF),
            jax.ShapeDtypeStruct((tokens, D), F32),
            jax.ShapeDtypeStruct((tokens, width), BF),
            jax.ShapeDtypeStruct((tokens, width), BF),
            jax.ShapeDtypeStruct((texts, 2 * D), BF),
            jax.ShapeDtypeStruct((8, D), F32),
            jax.ShapeDtypeStruct((D // 2, texts), BF),
            jax.ShapeDtypeStruct((3, D // 2, tokens), BF),
            jax.ShapeDtypeStruct((D // 2, 3 * (tokens + D) + 4 * texts), BF),
        ],
        compiler_params=pltpu.CompilerParams(vmem_limit_bytes=60 * MIB),
        cost_estimate=SMALL,
        name="cross_attention_back",
    )(
        core.reshape(1), order, got, grad3, hidden2, g, norms[2].reshape(1, D),
        jnp.stack(norms[:2]), seen, lse, text_kv, text_kv, states, mixed, w_out, queries,
        w_query, hidden1, own, other, w_self, out, got,
    )


def pair_kernel(keep_ref, own_ref, got_ref, states_ref, grad_ref, grad_got_ref, *outs):
    first_ref, second_ref, text_ref = outs
    step = pl.program_id(0)
    half, tokens = keep_ref.shape
    texts = grad_ref.shape[0]

    def put(product):
        first_ref[...] = product[: half // 2].astype(BF)
        second_ref[...] = product[half // 2 :].astype(BF)

    @pl.when(step < 3)
    def _():
        product = nn(keep_ref[...], own_ref[:, tokens:])
        put(product + nn(got_ref[:, :tokens], got_ref[:, tokens:]))

    @pl.when(step >= 3)
    def _():
        got = grad_got_ref[...].astype(F32)
        got = jnp.concatenate([got[:texts], got[texts:]], 1)
        got = jnp.concatenate([got[texts // 2 :], got[: texts // 2]], 0)
        grad = (grad_ref[...].astype(F32) + got).astype(BF)
        text_ref[...] = grad[: texts // 2]
        put(nn(states_ref[...], grad))


def pair_gradients(keep, own, got, states, grad):
    _, half, tokens = keep.shape
    texts = grad.shape[0]

    def third(s):
        return jnp.minimum(s, 2)

    def later(s):
        return jnp.maximum(s - 3, 0)

    wide = pl.BlockSpec((half, tokens + D), lambda s: (0, third(s)))
    lane = 3 * (tokens + D) // (4 * texts)
    grads = pl.BlockSpec((texts, D), lambda s: (0, later(s)))
    out = pl.BlockSpec((half // 2, D), lambda s: (0, s))
    return pl.pallas_call(
        pair_kernel,
        grid=(5,),
        in_specs=[
            pl.BlockSpec((None, half, tokens), lambda s: (third(s), 0, 0)),
            wide,
            wide,
            pl.BlockSpec((half, texts), lambda s: (0, 0)),
            grads,
            pl.BlockSpec((2 * texts, 4 * texts), lambda s: (later(s), lane)),
        ],
        out_specs=[out, out, pl.BlockSpec((texts // 2, D), lambda s: (0, later(s)))],
        out_shape=[jax.ShapeDtypeStruct((half // 2, 5 * D), BF)] * 2
        + [jax.ShapeDtypeStruct((texts // 2, 2 * D), BF)],
        compiler_params=pltpu.CompilerParams(vmem_limit_bytes=60 * MIB),
        cost_estimate=SMALL,
        name="pair_gradients",
    )(keep, own, got, states, grad, got)


def last_kernel(
    blocks_ref,
    x_ref,
    part_ref,
    got_ref,
    hidden_ref,
    gain_ref,
    norms_ref,
    image_ref,
    keep,
    send,
    norm_flip,
):
    count = blocks_ref.shape[0]
    height, half = D // count, D // 2
    grad = part_ref[...] + got_ref[...].astype(F32)
    unit, rstd = norm_parts(x_ref[...].astype(F32))
    sums = [jnp.sum(grad * unit, axis=0, keepdims=True), jnp.sum(grad, axis=0, keepdims=True)]
    image = norm_back(unit, rstd, gain_ref[...], grad) + hidden_ref[...]
    image_ref[...] = image.astype(BF)
    fill = jnp.zeros((norm_flip.shape[1] - 8, D), F32)
    norm_flip[...] = jnp.concatenate(sums + [norms_ref[2:8, :], fill], 0).T
    for i in range(count):
        at = pl.ds(pl.multiple_of(blocks_ref[i] * height, height), height)
        to = i * height % half
        target = keep if i < count // 2 else send
        target[to : to + height, :] = norm_flip[at, :].astype(BF)


def last_part(x, part, got, hidden_grad, gain, norms, blocks):
    tokens = got.shape[0]

    def full(*shape):
        return pl.BlockSpec(shape, lambda b, *_: (0,) * len(shape))

    wide = full(tokens, D)
    return pl.pallas_call(
        last_kernel,
        grid_spec=pltpu.PrefetchScalarGridSpec(
            num_scalar_prefetch=1,
            grid=(1,),
            in_specs=[wide] * 4 + [full(1, D), full(8, D)],
            out_specs=[wide, full(D // 2, 128), full(D // 2, 128)],
            scratch_shapes=[pltpu.VMEM((D, 128), F32)],
        ),
        out_shape=[jax.ShapeDtypeStruct((tokens, D), BF)]
        + [jax.ShapeDtypeStruct((D // 2, 128), BF)] * 2,
        compiler_params=pltpu.CompilerParams(vmem_limit_bytes=60 * MIB),
        cost_estimate=SMALL,
        name="norm_back",
    )(blocks, x, part, got, hidden_grad, gain.reshape(1, D), norms)


def add_kernel(a_ref, b_ref, keep_ref, send_ref):
    block, half = pl.program_id(0), pl.num_programs(0) // 2
    total = a_ref[...] + b_ref[...]

    @pl.when(block < half)
    def _():
        send_ref[...] = total

    @pl.when(block >= half)
    def _():
        keep_ref[...] = total


def add_halves(a, b):
    count, height, width = a.shape
    blocks = 4
    half = blocks // 2
    shape = (count // blocks, height, width)
    turned = pl.BlockSpec(shape, lambda i: ((i + half) % blocks, 0, 0))
    return pl.pallas_call(
        add_kernel,
        grid=(blocks,),
        in_specs=[turned] * 2,
        out_specs=[
            pl.BlockSpec(shape, lambda i: (jnp.maximum(i - half, 0), 0, 0)),
            pl.BlockSpec(shape, lambda i: (jnp.minimum(i, half - 1), 0, 0)),
        ],
        out_shape=[jax.ShapeDtypeStruct((count // 2, height, width), BF)] * 2,
        compiler_params=pltpu.CompilerParams(vmem_limit_bytes=60 * MIB),
        cost_estimate=SMALL,
        name="add_halves",
    )(a, b)


def behind(value, *others):
    return lax.optimization_barrier((value,) + others)[0]


class Route:
    def __init__(self, plan, orders):
        self.orders = orders
        count = plan.chips
        maps = np.zeros((2, count), np.int32)
        for core in range(2):
            for i in range(count):
                for s, bit in enumerate(orders[core]):
                    maps[core, i] |= ((i >> (plan.levels - 1 - s)) & 1) << bit
        here, there = jnp.asarray(maps)[plan.core], jnp.asarray(maps)[1 - plan.core]
        self.blocks = jnp.bitwise_xor(plan.chip, here).astype(jnp.int32)
        sent = jnp.bitwise_xor(plan.chip, there).astype(jnp.int32)
        self.devices = jnp.concatenate([2 * sent + 1 - plan.core, 2 * self.blocks + plan.core])
        backs = np.argsort(maps, axis=1).astype(np.int32)
        away = jnp.bitwise_xor(plan.chip, jnp.arange(count, dtype=jnp.int32))
        self.goes_to = jnp.take(jnp.asarray(backs)[plan.core], away, mode="clip")


class Plan:
    def __init__(self, n_img, n_txt):
        self.n_txt = n_txt
        self.n = n_img * n_txt
        self.chips = self.n // 2
        self.ny = n_txt // 2
        self.levels = self.chips.bit_length() - 1
        self.me = lax.axis_index("img") * n_txt + lax.axis_index("txt")
        self.core = self.me % 2
        self.chip = self.me // 2
        self.y = lax.axis_index("txt") // 2
        sources = (self.y - jnp.arange(self.ny, dtype=jnp.int32)) % self.ny
        self.places = jnp.concatenate([2 * sources + self.core, 2 * sources + 1 - self.core])
        at = jnp.arange(n_txt, dtype=jnp.int32)
        self.rows = jnp.bitwise_xor(at % 2, self.core) * self.ny + (self.y - at // 2) % self.ny
        rest = list(range(2, self.levels))
        self.near = Route(self, ([1, 0] + rest, [0, 1] + rest))
        self.small = Route(self, ([0] + rest + [1], [0] + rest + [1]))
        self.mixed = Route(self, ([1, 0] + rest, rest + [0, 1]))
        self.token = None

    def swap(self, value):
        return lax.ppermute(value, BOTH, [(d, d ^ 1) for d in range(self.n)])

    def shift_y(self, value, by):
        pairs = []
        for d in range(self.n):
            img, txt = divmod(d, self.n_txt)
            y, core = divmod(txt, 2)
            pairs.append((d, img * self.n_txt + ((y + by) % self.ny) * 2 + core))
        return lax.ppermute(value, BOTH, pairs)

    def halve(self, value, route, step):
        pairs = [(d, d ^ (2 << route.orders[d % 2][step])) for d in range(self.n)]
        return lax.ppermute(value, BOTH, pairs)

    def send_items(self, value, note=None):
        parts = []
        for k in range(self.ny):
            part = value[(self.y + k) % self.ny]
            if note is not None:
                part = jnp.concatenate([part, note], 0)
            parts.append(self.shift_y(part, k) if k else part)
        return parts

    def join_items(self, parts, length):
        notes = [p[length:] for p in parts] if parts[0].shape[0] > length else []
        return jnp.concatenate([p[:length] for p in parts] + notes, 0)

    def return_items(self, value):
        return [self.shift_y(value[k], -k) if k else value[0] for k in range(self.ny)]

    def order_items(self, parts):
        stacked = jnp.stack(parts)
        return jnp.stack([stacked[(i - self.y) % self.ny] for i in range(self.ny)])

    def start(self, keep, send, route, step=0):
        return keep, self.halve(send, route, step), route, step

    def advance(self, state):
        keep, got, route, step = state
        keep, got, _ = lax.optimization_barrier((keep, got, self.token))
        if keep.shape[0] == 1:
            self.token = keep[0].astype(F32) + got[0].astype(F32)
            return self.token
        if keep.size > 1 << 20:
            keep, send = add_halves(keep, got)
        else:
            total = (keep.astype(F32) + got.astype(F32)).astype(BF)
            keep, send = jnp.split(total, 2)
        keep, send = lax.optimization_barrier((keep, send))
        self.token = send
        return self.start(keep, send, route, step + 1)

    def then(self, *values):
        return lax.optimization_barrier(values + (self.token,))[:-1]


def per_device(
    n_img,
    n_txt,
    image_tokens,
    text_states,
    text_segments,
    item_segments,
    norm1_gain,
    norm1_bias,
    w_qkv,
    w_self_out,
    norm2_gain,
    norm2_bias,
    w_cross_q,
    w_cross_kv,
    w_cross_out,
    norm3_gain,
    norm3_bias,
    w_up,
    w_down,
    cotangent,
):
    plan = Plan(n_img, n_txt)
    core, n, chips, ny = plan.core, plan.n, plan.chips, plan.ny
    items, length, _ = image_tokens.shape
    tokens = items * length
    half_d = D // 2
    rows = D // n

    states = text_states.shape[1]
    ids = jnp.pad(text_segments.astype(BF), ((0, 15), (0, D - states)))
    note = jnp.concatenate([text_states[0], ids], 0)
    x_parts = plan.send_items(image_tokens, note)
    g_parts = plan.send_items(behind(cotangent, x_parts[-1]))
    x_own = plan.join_items(x_parts, length)
    x_other = plan.swap(x_own)

    notes = [v[tokens:].reshape(ny, states + 16, D) for v in (x_own, x_other)]
    notes = jnp.concatenate(notes, 0)
    ids = notes[:, states, :states].reshape(-1)
    states_all = notes[:, :states].reshape(-1, D)
    text_kv = nn(states_all, w_cross_kv).astype(BF)
    matches = ids == item_segments[0, plan.y].astype(BF)
    seen = jnp.where(matches, 0.0, MASKED).astype(F32)[:, None]

    joined, normed1 = project_all(
        x_own, x_other, norm1_gain, norm1_bias, w_qkv, core, plan.places, length
    )
    mixed, mixed_other, lse = attend(joined, plan.rows)
    mixed_got = plan.swap(mixed_other)
    g_own = plan.join_items([behind(p, mixed_got) for p in g_parts], length)
    g_other = plan.swap(g_own)

    norms = (norm2_gain, norm2_bias, norm3_gain, norm3_bias)
    hidden1, hidden2, normed3, cross_q, cross_mixed, cross_lse = cross_part(
        x_own,
        mixed,
        mixed_got,
        text_kv,
        seen,
        norms,
        w_self_out,
        w_cross_q,
        w_cross_out,
        core,
    )

    normed3_other = plan.swap(normed3)
    per_down = w_down.shape[0] // n
    out, grad3, sent, low_keep, high_keep, low_send, high_send = mlp(
        normed3,
        normed3_other,
        g_own,
        g_other,
        w_up,
        w_down,
        core,
        plan.mixed.blocks,
        plan.mixed.goes_to,
    )
    high_got = plan.halve(high_send, plan.mixed, 0)
    got = plan.swap(sent)


    block_out, grad_hidden1, grad_own, grad_other, grad_kv, norm_sums, states_flip, keep, send = (
        cross_back(
            out, got, grad3, hidden2, g_own, norms[:3], seen, cross_lse, cross_mixed, w_cross_out,
            text_kv, cross_q, states_all, w_cross_q, hidden1, mixed, mixed_got, w_self_out,
            core, plan.near.devices,
        )
    )
    grad_other, high_got = lax.optimization_barrier((grad_other, high_got))
    grad_got = plan.swap(grad_other)
    pair_got = plan.swap(behind(send, grad_got))
    plan.token = grad_other
    high_keep, high_got = plan.then(high_keep, high_got)
    low_got = plan.halve(behind(low_send, high_got), plan.mixed, 0)
    high_sum = (high_keep.astype(F32) + high_got.astype(F32)).astype(BF)
    plan.token = high_sum
    next_got = plan.halve(high_sum, plan.mixed, 1)
    block_parts = plan.return_items(block_out.reshape(ny, length, D))

    grad_got, grad_own = plan.then(grad_got, grad_own)
    last_keep, last_send, part_own, part_other = attend_back(
        joined, grad_own, grad_got, mixed, lse, normed1, w_qkv, core, plan.rows, plan.near.blocks
    )
    plan.token = part_other
    last_sums = plan.start(
        last_keep.reshape(chips // 2, 2 * rows, -1),
        last_send.reshape(chips // 2, 2 * rows, -1),
        plan.near,
    )
    send, pair_got, *block_parts = plan.then(send, pair_got, *block_parts)
    middle_keep, middle_send, text_sum = pair_gradients(
        keep, send, pair_got, states_flip, grad_kv
    )
    plan.token = middle_send
    middle_sums = plan.start(
        middle_keep.reshape(chips // 2, rows, -1),
        middle_send.reshape(chips // 2, rows, -1),
        plan.near,
    )
    part_got = plan.swap(behind(part_other, middle_send))
    low_keep, low_got, next_got = plan.then(low_keep, low_got, next_got)
    low_sum = low_keep.astype(F32) + low_got.astype(F32) + next_got.astype(F32)
    plan.token = low_sum = lax.optimization_barrier(low_sum.astype(BF))
    low_keep, low_send = jnp.split(low_sum, 2)
    mlp_sums = plan.start(low_keep, low_send, plan.mixed, 2)
    part_got, part_own = plan.then(part_got, part_own)
    image_grad, norm_keep, norm_send = last_part(
        x_own, part_own, part_got, grad_hidden1, norm1_gain, norm_sums, plan.small.blocks
    )
    plan.token = norm_send
    norm_group = plan.start(
        norm_keep.reshape(chips // 2, 2 * rows, -1),
        norm_send.reshape(chips // 2, 2 * rows, -1),
        plan.small,
    )
    last_sums = plan.advance(last_sums)
    mlp_sums = plan.advance(mlp_sums)
    last_sums = plan.advance(last_sums)
    middle_sums = plan.advance(middle_sums)
    norm_group = plan.advance(norm_group)
    text_sum, image_grad = plan.then(text_sum, image_grad)
    text_part = nt(text_sum, w_cross_kv)
    plan.token = text_part
    text_part = text_part.reshape(ny, states, D)
    text_parts = [plan.shift_y(text_part[r].astype(BF), -r) for r in range(1, ny)]
    block_out = plan.order_items(plan.then(*block_parts))
    for _ in range(plan.levels - 3):
        last_sums = plan.advance(last_sums)
    norm_group = plan.advance(norm_group)
    for _ in range(plan.levels - 3):
        mlp_sums = plan.advance(mlp_sums)
    for _ in range(plan.levels - 3):
        middle_sums = plan.advance(middle_sums)
        (image_grad,) = plan.then(image_grad)
        norm_group = plan.advance(norm_group)
    image_parts = plan.return_items(image_grad.reshape(ny, length, D))
    middle_sums = plan.advance(middle_sums)
    last_sums = plan.advance(last_sums)
    norm_group = plan.advance(norm_group)
    last_sums = jnp.concatenate([last_sums, norm_group], 1)
    up_down = mlp_sums

    units = w_up.shape[1] // 2
    down_grad = jnp.concatenate([up_down[:, units : units + D], up_down[:, units + D :]], 0)
    parts = jnp.concatenate([up_down[:, :units], last_sums], 1).reshape(2, rows, -1)
    mine = parts[core]
    sent = parts[1 - core].astype(BF)
    theirs = plan.swap(sent)
    plan.token = sent
    text_part, *text_parts = plan.then(text_part, *text_parts)
    text_grad = sum((p.astype(F32) for p in text_parts), text_part[0])
    image_grad = plan.order_items(plan.then(*image_parts)).astype(F32)
    plan.token = image_grad
    (theirs,) = plan.then(theirs)
    theirs = theirs.astype(F32)
    by_core = jnp.where(core == 0, jnp.stack([mine, theirs]), jnp.stack([theirs, mine]))
    up_grad = by_core[:, :, :units].reshape(2, rows, chips, per_down)
    up_grad = up_grad.transpose(1, 2, 0, 3).reshape(rows, 2 * units)
    wide = by_core[:, :, units : units + 3 * half_d].reshape(2, rows, -1, 3, 2 * HEAD)
    wide = wide.transpose(1, 3, 0, 2, 4).reshape(rows, 3 * D)
    up_grad, wide = lax.optimization_barrier((up_grad, wide))
    plan.token = wide
    middle_sums = plan.advance(middle_sums)
    norm_sums = mine[:, -128:-122] + theirs[:, -128:-122]
    return (
        block_out,
        image_grad,
        text_grad[None],
        norm_sums[:, 0],
        norm_sums[:, 1],
        wide,
        middle_sums[:, 2 * D : 3 * D],
        norm_sums[:, 2],
        norm_sums[:, 3],
        middle_sums[:, D : 2 * D],
        middle_sums[:, 3 * D :],
        middle_sums[:, :D],
        norm_sums[:, 4],
        norm_sums[:, 5],
        up_grad,
        down_grad,
    )


def solution(mesh):
    split = P("img", "txt", None)
    rows = P(BOTH)
    wide = P(BOTH, None)
    return jax.shard_map(
        partial(per_device, mesh.shape["img"], mesh.shape["txt"]),
        mesh=mesh,
        in_specs=(split, split, P("img", "txt"), P("img", None)) + (P(),) * 13 + (split,),
        out_specs=(
            (split,) * 3
            + (rows, rows, wide, wide)
            + (rows, rows, wide, wide, wide)
            + (rows, rows, wide, wide)
        ),
        check_vma=False,
    )
```

```python
from functools import partial

import jax
import jax.numpy as jnp
import numpy as np
from jax import lax
from jax.experimental import pallas as pl
from jax.experimental.pallas import tpu as pltpu
from jax.sharding import PartitionSpec as P

D = 1024
HEADS = 16
HEAD = 64
EPS = 1e-05
MASKED = -1e30
SCALE = HEAD**-0.5
LOG2E = 1.4426950408889634
BOTH = ("img", "txt")
BF = jnp.bfloat16
F32 = jnp.float32
QUERY_BLOCK = 256
MIB = 1 << 20
SMALL = pl.CostEstimate(flops=1 << 20, bytes_accessed=1 << 16, transcendentals=0)


def nn(a, b):
    return lax.dot_general(a, b, (((1,), (0,)), ((), ())), preferred_element_type=F32)


def nt(a, b):
    return lax.dot_general(a, b, (((1,), (1,)), ((), ())), preferred_element_type=F32)


def tn(a, b):
    return lax.dot_general(a, b, (((0,), (0,)), ((), ())), preferred_element_type=F32)


def norm_parts(values):
    center = values - jnp.mean(values, axis=-1, keepdims=True)
    rstd = lax.rsqrt(jnp.mean(center * center, axis=-1, keepdims=True) + EPS)
    return center * rstd, rstd


def norm_back(unit, rstd, gain, grad):
    scaled = grad * gain
    return rstd * (
        scaled
        - jnp.mean(scaled, axis=-1, keepdims=True)
        - unit * jnp.mean(scaled * unit, axis=-1, keepdims=True)
    )


TAIL = [
    0.5 * c
    for c in (
        -0.22753805372107494,
        0.8866680711331851,
        -0.6354061073102151,
        0.6495639241196378,
        0.09138668583849363,
        0.235325478247137,
    )
]


def gelu_parts(value):
    t = 1.0 / (1.0 + (0.39 * 0.5**0.5) * jnp.abs(value))
    bell = jnp.exp2(value * value * (-0.5 * LOG2E))
    tail = jnp.full_like(t, TAIL[0])
    for term in TAIL[1:]:
        tail = tail * t + term
    tail = tail * t * bell
    cdf = jnp.where(value > 0.0, 1.0 - tail, tail)
    return value * cdf, cdf + value * bell * (0.5 / np.pi) ** 0.5


def project_kernel(
    core_ref, place_ref, own_ref, other_ref, gain_ref, bias_ref, wq_ref, wk_ref, wv_ref, *refs
):
    joined_ref, normed_ref, held_ref = refs
    block, own_blocks = pl.program_id(0), (pl.num_programs(0) - 1) // 2
    slot = block % 2
    width = wq_ref.shape[1]
    before = held_ref[1 - slot]
    normed_ref[...] = before
    for s, w_ref in enumerate((wq_ref, wk_ref, wv_ref)):
        joined_ref[:, s * width : (s + 1) * width] = nn(before, w_ref[...]).astype(BF)
    tokens = jnp.where(block < own_blocks, own_ref[...], other_ref[...]).astype(F32)
    unit, _ = norm_parts(tokens)
    held_ref[slot] = (unit * gain_ref[...] + bias_ref[...]).astype(BF)


def project_all(own, other, gain, bias, w_qkv, core, places, length):
    blocks = places.shape[0]
    half = blocks // 2
    width = D // 2
    row = pl.BlockSpec((1, D), lambda b, *_: (0, 0))
    weights = [pl.BlockSpec((D, width), lambda b, c, p, s=s: (0, 2 * s + c[0])) for s in range(3)]
    return pl.pallas_call(
        project_kernel,
        grid_spec=pltpu.PrefetchScalarGridSpec(
            num_scalar_prefetch=2,
            grid=(blocks + 1,),
            in_specs=[
                pl.BlockSpec((length, D), lambda b, *_: (jnp.minimum(b, half - 1), 0)),
                pl.BlockSpec((length, D), lambda b, *_: (jnp.clip(b - half, 0, half - 1), 0)),
                row,
                row,
            ]
            + weights,
            out_specs=[
                pl.BlockSpec((length, 3 * width), lambda b, c, p: (p[jnp.maximum(b - 1, 0)], 0)),
                pl.BlockSpec((length, D), lambda b, c, p: (p[jnp.maximum(b - 1, 0)], 0)),
            ],
            scratch_shapes=[pltpu.VMEM((2, length, D), BF)],
        ),
        out_shape=[
            jax.ShapeDtypeStruct((blocks * length, 3 * width), BF),
            jax.ShapeDtypeStruct((blocks * length, D), BF),
        ],
        compiler_params=pltpu.CompilerParams(vmem_limit_bytes=60 * MIB),
        cost_estimate=SMALL,
        name="norm_and_project",
    )(
        core.reshape(1),
        places,
        own,
        other,
        gain.reshape(1, D),
        bias.reshape(1, D),
        w_qkv,
        w_qkv,
        w_qkv,
    )


def middle_kernel(
    core_ref,
    x_ref,
    own_ref,
    got_ref,
    keys_ref,
    values_ref,
    seen_ref,
    gain2_ref,
    bias2_ref,
    gain3_ref,
    bias3_ref,
    w_own_ref,
    w_got_ref,
    w_query_ref,
    w_out_ref,
    hidden1_ref,
    hidden2_ref,
    normed3_ref,
    queries_ref,
    mixed_ref,
    lse_ref,
):
    hidden = x_ref[...].astype(F32) + nn(own_ref[...], w_own_ref[...])
    hidden += nn(got_ref[...], w_got_ref[...])
    hidden1_ref[...] = hidden
    unit, _ = norm_parts(hidden)
    normed2 = (unit * gain2_ref[...] + bias2_ref[...]).astype(BF)
    queries = nn(normed2, w_query_ref[...]).astype(BF)
    queries_ref[...] = queries
    rows, states = queries.shape[0], keys_ref.shape[0]
    half = lax.broadcasted_iota(jnp.int32, (rows, 2 * HEAD), 1) >= HEAD
    v_flip = values_ref[...].T
    ones = jnp.ones((16, states), BF)
    zero = jnp.zeros((rows, 2 * HEAD), BF)

    def score(head):
        at, h = head // 2 * 2 * HEAD, head % 2
        own = jnp.where(half == (h == 1), queries[:, at : at + 2 * HEAD], zero)
        return nt(keys_ref[:, at : at + 2 * HEAD], own)

    def soften(scores):
        scores = scores * (SCALE * LOG2E) + seen_ref[...]
        top = jnp.max(scores, axis=0, keepdims=True)
        return jnp.exp2(scores - top).astype(BF), top

    outs, lses, scores, raised = [], [], {}, {}
    for n in range(HEADS + 2):
        if n < HEADS:
            scores[n] = score(n)
        if 0 <= n - 1 < HEADS:
            raised[n - 1] = soften(scores.pop(n - 1))
        if n >= 2:
            weights, top = raised.pop(n - 2)
            v_rows = jnp.concatenate([v_flip[(n - 2) * HEAD : (n - 1) * HEAD], ones], 0)
            mixed = nn(v_rows, weights)
            total = mixed[HEAD : HEAD + 1]
            lses.append(top + jnp.log2(total))
            outs.append((mixed[:HEAD] / total).astype(BF))
    lse_ref[...] = jnp.concatenate(lses, 0)
    mixed = jnp.concatenate(outs, 0).T
    mixed_ref[...] = mixed
    hidden += nn(mixed, w_out_ref[...])
    hidden2_ref[...] = hidden
    unit, _ = norm_parts(hidden)
    normed3_ref[...] = (unit * gain3_ref[...] + bias3_ref[...]).astype(BF)


def cross_part(x, own, got, text_kv, seen, norms, w_self_out, w_query, w_out, core):
    tokens, width = got.shape
    states = text_kv.shape[0]
    block = min(256, tokens)
    row = pl.BlockSpec((1, D), lambda b, c: (0, 0))
    wide = pl.BlockSpec((block, D), lambda b, c: (b, 0))
    narrow = pl.BlockSpec((block, width), lambda b, c: (b, 0))
    square = pl.BlockSpec((D, D), lambda b, c: (0, 0))
    return pl.pallas_call(
        middle_kernel,
        grid_spec=pltpu.PrefetchScalarGridSpec(
            num_scalar_prefetch=1,
            grid=(tokens // block,),
            in_specs=[
                wide,
                narrow,
                narrow,
                pl.BlockSpec((states, D), lambda b, c: (0, 0)),
                pl.BlockSpec((states, D), lambda b, c: (0, 1)),
                pl.BlockSpec((states, 1), lambda b, c: (0, 0)),
                row,
                row,
                row,
                row,
                pl.BlockSpec((width, D), lambda b, c: (c[0], 0)),
                pl.BlockSpec((width, D), lambda b, c: (1 - c[0], 0)),
                square,
                square,
            ],
            out_specs=[wide] * 5 + [pl.BlockSpec((HEADS, block), lambda b, c: (0, b))],
        ),
        out_shape=[
            jax.ShapeDtypeStruct((tokens, D), F32),
            jax.ShapeDtypeStruct((tokens, D), F32),
            jax.ShapeDtypeStruct((tokens, D), BF),
            jax.ShapeDtypeStruct((tokens, D), BF),
            jax.ShapeDtypeStruct((tokens, D), BF),
            jax.ShapeDtypeStruct((HEADS, tokens), F32),
        ],
        compiler_params=pltpu.CompilerParams(vmem_limit_bytes=60 * MIB),
        cost_estimate=SMALL,
        name="cross_attention_part",
    )(
        core.reshape(1),
        x,
        own,
        got,
        text_kv,
        text_kv,
        seen,
        *[v.reshape(1, D) for v in norms],
        w_self_out,
        w_self_out,
        w_query,
        w_out,
    )


def attend_kernel(row_ref, q_ref, k_ref, v_ref, all_ref, other_ref, lse_ref, out_ref):
    length = q_ref.shape[0]
    block = QUERY_BLOCK
    scale = SCALE * LOG2E
    half = lax.broadcasted_iota(jnp.int32, (block, 2 * HEAD), 1) >= HEAD
    key_row = lax.broadcasted_iota(jnp.int32, (block, block), 0)
    query_col = lax.broadcasted_iota(jnp.int32, (block, block), 1)
    seen = key_row <= query_col
    v_flip = v_ref[...].T
    ones = jnp.ones((16, length), BF)
    v_rows = [jnp.concatenate([v_flip[h * HEAD : (h + 1) * HEAD], ones], 0) for h in range(2)]

    def score(i, h):
        lo, hi = i * block, (i + 1) * block
        queries = q_ref[lo:hi, :]
        own = jnp.where(half == (h == 1), queries, jnp.zeros_like(queries))
        return nt(k_ref[lo:hi, :], own), nt(k_ref[:lo, :], own) if i else None

    def soften(i, h, diag, rest):
        diag = jnp.where(seen, diag, MASKED)
        top = jnp.max(diag, axis=0, keepdims=True)
        if i:
            top = jnp.maximum(top, jnp.max(rest, axis=0, keepdims=True))
            rest = jnp.exp2(rest * scale - top * scale).astype(BF)
        return jnp.exp2(diag * scale - top * scale).astype(BF), rest, top * scale

    def mix(i, h, diag, rest, base):
        lo, hi = i * block, (i + 1) * block
        mixed = nn(v_rows[h][:, lo:hi], diag)
        if i:
            mixed += nn(v_rows[h][:, :lo], rest)
        total = mixed[HEAD : HEAD + 1]
        lse_ref[0, h : h + 1, lo:hi] = base + jnp.log2(total)
        return mixed[:HEAD] / total

    tasks = [(i, h) for i in range(length // block) for h in range(2)]
    scores, raised, outs = {}, {}, []
    part = length // row_ref.shape[0]
    for n in range(len(tasks) + 2):
        if n < len(tasks):
            scores[n] = score(*tasks[n])
        if 0 <= n - 1 < len(tasks):
            raised[n - 1] = soften(*tasks[n - 1], *scores.pop(n - 1))
        if n >= 2:
            outs.append(mix(*tasks[n - 2], *raised.pop(n - 2)))
        if len(outs) == 2:
            lo = tasks[n - 2][0] * block
            result = jnp.concatenate(outs, 0).T.astype(BF)
            outs = []
            for at in range(0, block, part):
                row = pl.multiple_of(row_ref[(lo + at) // part] * part, part)
                out_ref[pl.ds(row, part), :] = result[at : at + part]
    all_ref[...] = out_ref[...]
    other_ref[...] = out_ref[length // 2 :, :]


def head_specs(length, pairs):
    return [
        pl.BlockSpec((length, 2 * HEAD), lambda p, *_, s=s: (0, s * pairs + p)) for s in range(3)
    ]


def attend(joined, rows):
    length, width = joined.shape[0], joined.shape[1] // 3
    pairs = width // (2 * HEAD)
    return pl.pallas_call(
        attend_kernel,
        grid_spec=pltpu.PrefetchScalarGridSpec(
            num_scalar_prefetch=1,
            grid=(pairs,),
            in_specs=head_specs(length, pairs),
            out_specs=[
                pl.BlockSpec((length, 2 * HEAD), lambda p, *_: (0, p)),
                pl.BlockSpec((length // 2, 2 * HEAD), lambda p, *_: (0, p)),
                pl.BlockSpec((1, 2, length), lambda p, *_: (p, 0, 0)),
            ],
            scratch_shapes=[pltpu.VMEM((length, 2 * HEAD), BF)],
        ),
        out_shape=[
            jax.ShapeDtypeStruct((length, width), BF),
            jax.ShapeDtypeStruct((length // 2, width), BF),
            jax.ShapeDtypeStruct((pairs, 2, length), F32),
        ],
        compiler_params=pltpu.CompilerParams(vmem_limit_bytes=60 * MIB),
        cost_estimate=SMALL,
        name="self_attention",
    )(rows, joined, joined, joined)


def attend_back_kernel(
    row_ref,
    block_ref,
    q_ref,
    k_ref,
    v_ref,
    own_g_ref,
    other_g_ref,
    mixed_ref,
    lse_ref,
    normed_hbm,
    wq_ref,
    wk_ref,
    wv_ref,
    keep_ref,
    send_ref,
    own_ref,
    other_ref,
    dq_sum,
    g_ref,
    o_ref,
    normed,
    flip_ref,
    ordered_ref,
    sum_ref,
    sem,
):
    pair, pairs = pl.program_id(0), pl.num_programs(0)
    load = pltpu.make_async_copy(normed_hbm, normed, sem)

    @pl.when(pair == 0)
    def _():
        load.start()

    length = q_ref.shape[0]
    places = row_ref.shape[0]
    part = length // places
    for place in range(places):
        row = row_ref[place]
        at = pl.ds(pl.multiple_of(row % (places // 2) * part, part), part)
        to = slice(place * part, (place + 1) * part)
        mine = row < places // 2
        g_ref[to, :] = jnp.where(mine, own_g_ref[at, :], other_g_ref[at, :])
        o_ref[to, :] = mixed_ref[pl.ds(pl.multiple_of(row * part, part), part), :]
    block = QUERY_BLOCK
    scale = SCALE * LOG2E
    half = lax.broadcasted_iota(jnp.int32, (length, 2 * HEAD), 1) >= HEAD
    key_row = lax.broadcasted_iota(jnp.int32, (block, block), 0)
    query_col = lax.broadcasted_iota(jnp.int32, (block, block), 1)
    seen = key_row <= query_col
    k_flip = k_ref[...].T
    zero = jnp.zeros((length, 2 * HEAD), BF)
    queries = [jnp.where(half == (h == 1), q_ref[...], zero) for h in range(2)]
    grads = [jnp.where(half == (h == 1), g_ref[...], zero) for h in range(2)]
    product = (g_ref[...].astype(F32) * o_ref[...].astype(F32)).T
    deltas = [jnp.sum(product[h * HEAD : (h + 1) * HEAD], axis=0, keepdims=True) for h in range(2)]

    def score(j, h):
        lo, hi = j * block, (j + 1) * block
        return nt(k_ref[lo:hi, :], queries[h][lo:]), nt(v_ref[lo:hi, :], grads[h][lo:])

    def soften(j, h, scores, score_grad):
        lo, hi = j * block, (j + 1) * block
        weights = jnp.exp2(scores * scale - lse_ref[0, h : h + 1, lo:])
        first = jnp.where(seen, weights[:, :block], 0.0)
        weights = jnp.concatenate([first, weights[:, block:]], 1) if hi < length else first
        score_grad = (weights * (score_grad - deltas[h][:, lo:])).astype(BF)
        return weights.astype(BF), score_grad

    def mix(j, h, weights, score_grad):
        lo, hi = j * block, (j + 1) * block
        rows = slice(h * HEAD, (h + 1) * HEAD)
        query_part = nn(k_flip[rows, lo:hi], score_grad)
        if j == 0:
            dq_sum[rows, :] = query_part
        else:
            dq_sum[rows, lo:] += query_part
        return nn(score_grad, queries[h][lo:]), nn(weights, grads[h][lo:])

    tasks = [(j, h) for j in range(length // block) for h in range(2)]
    scores, raised, outs, key_grads, value_grads = {}, {}, [], [], []
    for n in range(len(tasks) + 2):
        if n < len(tasks):
            scores[n] = score(*tasks[n])
        if 0 <= n - 1 < len(tasks):
            raised[n - 1] = soften(*tasks[n - 1], *scores.pop(n - 1))
        if n >= 2:
            outs.append(mix(*tasks[n - 2], *raised.pop(n - 2)))
        if len(outs) == 2:
            key_grads.append(((outs[0][0] + outs[1][0]) * SCALE).astype(BF))
            value_grads.append((outs[0][1] + outs[1][1]).astype(BF))
            outs = []
    query_grad = (dq_sum[...].T * SCALE).astype(BF)
    joined = jnp.concatenate(
        [query_grad, jnp.concatenate(key_grads, 0), jnp.concatenate(value_grads, 0)], 1
    )
    weights = jnp.concatenate([wq_ref[...], wk_ref[...], wv_ref[...]], 1)
    grad = nt(joined, weights)

    @pl.when(pair == 0)
    def _():
        sum_ref[...] = grad
        load.wait()
        flip_ref[...] = normed[...].T
        height = D // block_ref.shape[0]
        for i in range(block_ref.shape[0]):
            at = pl.ds(pl.multiple_of(block_ref[i] * height, height), height)
            ordered_ref[i * height : (i + 1) * height, :] = flip_ref[at, :]

    @pl.when(pair > 0)
    def _():
        sum_ref[...] += grad

    wide = nn(ordered_ref[...], joined).astype(BF)
    keep_ref[...] = wide[: D // 2]
    send_ref[...] = wide[D // 2 :]

    @pl.when(pair == pairs - 1)
    def _():
        for place in range(places):
            row = row_ref[place]
            at = pl.ds(pl.multiple_of(row % (places // 2) * part, part), part)
            rows = sum_ref[place * part : (place + 1) * part, :]

            @pl.when(row < places // 2)
            def _(at=at, rows=rows):
                own_ref[at, :] = rows

            @pl.when(row >= places // 2)
            def _(at=at, rows=rows):
                other_ref[at, :] = rows.astype(BF)


def attend_back(joined, own_g, other_g, mixed, lse, normed, w_qkv, core, rows, blocks):
    length, width = joined.shape[0], joined.shape[1] // 3
    pairs = width // (2 * HEAD)
    spec = pl.BlockSpec((length, 2 * HEAD), lambda p, *_: (0, p))
    half = pl.BlockSpec((length // 2, 2 * HEAD), lambda p, *_: (0, p))
    weights = [
        pl.BlockSpec((D, 2 * HEAD), lambda p, r, b, s=s: (0, (2 * s + r[r.shape[0] - 1]) * pairs + p))
        for s in range(3)
    ]
    sums = pl.BlockSpec((D // 2, 6 * HEAD), lambda p, *_: (0, p))
    out = pl.BlockSpec((length // 2, D), lambda p, *_: (0, 0))
    places = rows.shape[0]

    def body(row_ref, *refs):
        attend_back_kernel(Rows(row_ref, places), *refs)

    return pl.pallas_call(
        body,
        grid_spec=pltpu.PrefetchScalarGridSpec(
            num_scalar_prefetch=2,
            grid=(pairs,),
            in_specs=head_specs(length, pairs)
            + [half] * 2
            + [spec]
            + [pl.BlockSpec((1, 2, length), lambda p, *_: (p, 0, 0))]
            + [pl.BlockSpec(memory_space=pl.ANY)]
            + weights,
            out_specs=[sums, sums, out, out],
            scratch_shapes=[
                pltpu.VMEM((2 * HEAD, length), F32),
                pltpu.VMEM((length, 2 * HEAD), BF),
                pltpu.VMEM((length, 2 * HEAD), BF),
                pltpu.VMEM((length, D), BF),
                pltpu.VMEM((D, length), BF),
                pltpu.VMEM((D, length), BF),
                pltpu.VMEM((length, D), F32),
                pltpu.SemaphoreType.DMA,
            ],
        ),
        out_shape=[jax.ShapeDtypeStruct((D // 2, 3 * width), BF)] * 2
        + [
            jax.ShapeDtypeStruct((length // 2, D), F32),
            jax.ShapeDtypeStruct((length // 2, D), BF),
        ],
        compiler_params=pltpu.CompilerParams(vmem_limit_bytes=60 * MIB),
        cost_estimate=SMALL,
        name="self_attention_back",
    )(
        jnp.concatenate([rows, core.reshape(1)]), blocks, joined, joined, joined, own_g, other_g,
        mixed, lse, normed, w_qkv, w_qkv, w_qkv,
    )


class Rows:
    def __init__(self, ref, count):
        self.ref, self.shape = ref, (count,)

    def __getitem__(self, place):
        return self.ref[place]


def mlp_kernel(
    pieces,
    steps,
    core_ref,
    rows_from,
    goes_to,
    own_ref,
    other_ref,
    own_g_ref,
    other_g_ref,
    *refs,
):
    ups, downs = refs[:pieces], refs[pieces : 2 * pieces]
    down_ref, up_ref, out_ref, norm_ref, sent_ref, *targets = refs[2 * pieces : 2 * pieces + 9]
    flip_ref, ordered_ref, wide_ref, tall_ref, active_ref, grad_ref, sems = refs[2 * pieces + 9 :]
    step = pl.program_id(0)
    slot = step % 2
    tokens = own_ref.shape[0]
    quarter, height = targets[0].shape[0], targets[0].shape[1]
    tile = wide_ref.shape[3]
    width = 2 * height
    per_step = tile // width
    units = steps * tile

    @pl.when(step == 0)
    def _():
        flip_ref[:, :tokens] = own_ref[...].T
        flip_ref[:, tokens:] = other_ref[...].T
        for i in range(4 * quarter):
            at = pl.multiple_of(rows_from[i] * height, height)
            ordered_ref[i * height : (i + 1) * height, :] = flip_ref[pl.ds(at, height), :]

    def wide_copy(at, where, side):
        part = wide_ref.at[at, side * quarter : (side + 1) * quarter]
        lanes = pl.ds(pl.multiple_of(where * tile, tile), tile)
        return pltpu.make_async_copy(part, targets[side].at[:, :, lanes], sems.at[at, side])

    def tall_copy(at, j, r, target, i):
        rows = slice(j * width + r * height, j * width + (r + 1) * height)
        lanes = slice(units + r * D, units + (r + 1) * D)
        return pltpu.make_async_copy(
            tall_ref.at[at, rows], target.at[i, :, lanes], sems.at[at, 4 + 2 * j + r]
        )

    def wait(at):
        for side in range(4):
            wide_copy(at, 0, side).wait()
        for j in range(per_step):
            for r in range(2):
                tall_copy(at, j, r, targets[0], 0).wait()

    @pl.when((step >= 2) & (step < steps + 2))
    def _():
        wait(slot)

    @pl.when(step < steps)
    def _():
        up_w = jnp.concatenate([r[...] for r in ups], 1) if pieces > 1 else ups[0][...]
        down_w = jnp.concatenate([r[...] for r in downs], 0) if pieces > 1 else downs[0][...]
        sides = ((0, own_ref, own_g_ref), (tokens, other_ref, other_g_ref))
        cut = 256
        tasks = [(u, side) for u in range(0, tile, cut) for side in sides]
        found, active, grads = {}, {}, {}

        def products(u, side):
            _, x_ref, g_ref = side
            return nn(x_ref[...], up_w[:, u : u + cut]), nt(g_ref[...], down_w[u : u + cut])

        def units_of(n):
            u, (base, _, _) = tasks[n]
            up_value, down_grad = found.pop(n)
            value, slope = gelu_parts(up_value)
            value = value.astype(BF)
            grad = (down_grad * slope).astype(BF)
            active_ref[step, base : base + tokens, u : u + cut] = value
            grad_ref[step, base : base + tokens, u : u + cut] = grad
            active[n], grads[n] = value, grad

        def weights_of(n):
            u = tasks[n][0]
            grad = jnp.concatenate([grads.pop(n - 1), grads.pop(n)], 0)
            wide = nn(ordered_ref[...], grad).astype(BF)
            wide_ref[slot, :, :, u : u + cut] = wide.reshape(wide_ref.shape[1:3] + (cut,))
            tall = nn(active.pop(n - 1).T, own_g_ref[...]) + nn(active.pop(n).T, other_g_ref[...])
            tall_ref[slot, u : u + cut] = tall.astype(BF)

        for n in range(len(tasks) + 2):
            if n < len(tasks):
                found[n] = products(*tasks[n])
            if 0 <= n - 1 < len(tasks):
                units_of(n - 1)
            if n >= 3 and n % 2:
                weights_of(n - 2)
        for side in range(4):
            wide_copy(slot, step, side).start()
        for j in range(per_step):
            i = goes_to[step * per_step + j]
            for side, target in enumerate(targets):

                @pl.when(i // quarter == side)
                def _(j=j, i=i, side=side, target=target):
                    for r in range(2):
                        tall_copy(slot, j, r, target, i - side * quarter).start()

    @pl.when(step >= steps)
    def _():
        up = up_ref[...]
        if up.shape[1] > units:
            first = core_ref[0] == 0
            picked = []
            for at in range(0, 2 * units, 2 * width):
                picked.append(
                    jnp.where(first, up[:, at : at + width], up[:, at + width : at + 2 * width])
                )
            up = jnp.concatenate(picked, 1)
        active = jnp.concatenate([active_ref[i] for i in range(steps)], 1)
        out = nn(active, down_ref[...].reshape(units, -1))
        grad = jnp.concatenate([grad_ref[i] for i in range(steps)], 1)
        norm = nt(grad, up)
        out_ref[...] = out[:tokens]
        norm_ref[...] = norm[:tokens]
        sent_ref[0] = out[tokens:].astype(BF)
        sent_ref[1] = norm[tokens:].astype(BF)


def mlp(own, other, own_g, other_g, w_up, w_down, core, rows_from, goes_to):
    tokens = own.shape[0]
    chips = rows_from.shape[0]
    tile, out_tile = 512, 256
    units = w_up.shape[1] // 2
    steps = units // tile
    width = units // chips
    height = D // chips
    fine = width % 128 == 0
    tall = w_down.reshape(chips, 2, width, D)
    if fine:
        pieces, piece = tile // width, width
    else:
        pieces, piece = 1, tile
        w_up = w_up.reshape(D, chips, 2, width)[:, :, core].reshape(D, units)
        w_down = w_down.reshape(chips, 2, width, D)[:, core].reshape(units, D)

    def place(s, c, j):
        s = jnp.minimum(s, steps - 1)
        return 2 * (s * pieces + j) + c[0] if fine else s

    def column(s):
        return jnp.maximum(s - steps, 0)

    whole = pl.BlockSpec((tokens, D), lambda s, *_: (0, 0))
    up_specs = [
        pl.BlockSpec((D, piece), lambda s, c, *_, j=j: (0, place(s, c, j))) for j in range(pieces)
    ]
    down_specs = [
        pl.BlockSpec((piece, D), lambda s, c, *_, j=j: (place(s, c, j), 0)) for j in range(pieces)
    ]
    kept = pl.BlockSpec((tokens, out_tile), lambda s, *_: (0, column(s)))
    sums = jax.ShapeDtypeStruct((chips // 4, height, units + 2 * D), BF)
    return pl.pallas_call(
        partial(mlp_kernel, pieces, steps),
        grid_spec=pltpu.PrefetchScalarGridSpec(
            num_scalar_prefetch=3,
            grid=(steps + D // out_tile,),
            in_specs=[whole] * 4
            + up_specs
            + down_specs
            + [
                pl.BlockSpec((chips, None, width, out_tile), lambda s, c, *_: (0, c[0], 0, column(s))),
                pl.BlockSpec((out_tile, w_up.shape[1]), lambda s, *_: (column(s), 0)),
            ],
            out_specs=[
                kept,
                kept,
                pl.BlockSpec((2, tokens, out_tile), lambda s, *_: (0, 0, column(s))),
            ]
            + [pl.BlockSpec(memory_space=pl.ANY)] * 4,
            scratch_shapes=[
                pltpu.VMEM((D, 2 * tokens), BF),
                pltpu.VMEM((D, 2 * tokens), BF),
                pltpu.VMEM((2, chips, height, tile), BF),
                pltpu.VMEM((2, tile, D), BF),
                pltpu.VMEM((steps, 2 * tokens, tile), BF),
                pltpu.VMEM((steps, 2 * tokens, tile), BF),
                pltpu.SemaphoreType.DMA((2, 4 + 2 * (tile // width))),
            ],
        ),
        out_shape=[
            jax.ShapeDtypeStruct((tokens, D), F32),
            jax.ShapeDtypeStruct((tokens, D), F32),
            jax.ShapeDtypeStruct((2, tokens, D), BF),
            sums,
            sums,
            sums,
            sums,
        ],
        compiler_params=pltpu.CompilerParams(vmem_limit_bytes=60 * MIB),
        cost_estimate=SMALL,
        name="mlp_both_ways",
    )(
        core.reshape(1),
        rows_from,
        goes_to,
        own,
        other,
        own_g,
        other_g,
        *([w_up] * pieces),
        *([w_down] * pieces),
        tall,
        w_up,
    )


def cross_back_kernel(
    scalars,
    order_ref,
    got_ref,
    grad3_ref,
    hidden2_ref,
    g_ref,
    gain3_ref,
    gain2_ref,
    seen_ref,
    lse_ref,
    keys_ref,
    values_ref,
    states_ref,
    mixed_hbm,
    w_out_hbm,
    queries_hbm,
    w_query_hbm,
    hidden1_hbm,
    own_hbm,
    other_hbm,
    w_self_hbm,
    out_hbm,
    got_hbm,
    block_ref,
    hidden_grad_ref,
    own_grad_ref,
    other_grad_ref,
    text_ref,
    norms_ref,
    states_flip_ref,
    keep,
    send,
    mixed_ref,
    w_out_ref,
    queries_ref,
    w_query,
    hidden1,
    own_ref,
    other_ref,
    w_self,
    out_ref,
    out_got_ref,
    flip_ref,
    ordered_ref,
    keep_stage,
    send_stage,
    sems,
    out_sems,
):
    core = scalars[0]
    tokens = grad3_ref.shape[0]
    loads = [
        pltpu.make_async_copy(a, b, sems.at[i])
        for i, (a, b) in enumerate(
            (
                (mixed_hbm, mixed_ref),
                (w_out_hbm, w_out_ref),
                (queries_hbm, queries_ref),
                (w_query_hbm, w_query),
                (hidden1_hbm, hidden1),
                (own_hbm.at[:tokens], own_ref),
                (other_hbm, other_ref),
                (w_self_hbm, w_self),
                (out_hbm, out_ref),
                (got_hbm.at[0], out_got_ref),
            )
        )
    ]
    for load in loads:
        load.start()
    count = order_ref.shape[0]
    rows = D // count
    half = D // 2
    writes = []

    def order(depth):
        for i in range(count):
            at = pl.multiple_of(order_ref[i] * rows, rows)
            ordered_ref[i * rows : (i + 1) * rows, :depth] = flip_ref[pl.ds(at, rows), :depth]

    def write(slot, grads):
        keep_stage[slot] = ordered_ref[half:, :tokens].astype(BF)
        lane = slot * (tokens + D)
        lanes = slice(lane, lane + tokens + D)
        send_stage[:, lane : lane + tokens] = ordered_ref[:half, :tokens].astype(BF)
        send_stage[:, lane + tokens : lane + tokens + D] = grads
        writes.append(
            pltpu.make_async_copy(send_stage.at[:, lanes], send.at[:, lanes], out_sems.at[slot])
        )
        writes.append(
            pltpu.make_async_copy(keep_stage.at[slot], keep.at[slot], out_sems.at[4 + slot])
        )
        for copy in writes[-2:]:
            copy.start()

    kind = flip_ref.dtype
    loads[0].wait()
    flip_ref[:, :tokens] = mixed_ref[...].astype(kind).T
    hidden2 = hidden2_ref[...]
    grad3 = grad3_ref[...] + got_ref[...].astype(F32)
    unit, rstd = norm_parts(hidden2)
    norms_ref[4:5, :] = jnp.sum(grad3 * unit, axis=0, keepdims=True)
    norms_ref[5:6, :] = jnp.sum(grad3, axis=0, keepdims=True)
    norms_ref[6:8, :] = jnp.zeros((2, D), F32)
    grad_hidden = norm_back(unit, rstd, gain3_ref[...], grad3) + g_ref[...].astype(F32)
    hidden_grad_ref[...] = grad_hidden
    branch = grad_hidden.astype(BF)
    order(tokens)
    write(0, branch)
    loads[1].wait()
    grad_mixed = nt(branch, w_out_ref[...]).astype(BF)
    loads[2].wait()
    states = keys_ref.shape[0]
    half_lane = lax.broadcasted_iota(jnp.int32, (tokens, 2 * HEAD), 1) >= HEAD
    zero = jnp.zeros((tokens, 2 * HEAD), BF)
    k_flip = keys_ref[...].T

    def score(head):
        lanes = slice(head // 2 * 2 * HEAD, (head // 2 + 1) * 2 * HEAD)
        mine = half_lane == (head % 2 == 1)
        own_q = jnp.where(mine, queries_ref[:, lanes], zero)
        own_g = jnp.where(mine, grad_mixed[:, lanes], zero)
        return nt(keys_ref[:, lanes], own_q), nt(values_ref[:, lanes], own_g), own_q, own_g

    def soften(head, scores, score_grad, own_q, own_g):
        scores = scores * (SCALE * LOG2E) + seen_ref[...]
        weights = jnp.exp2(scores - lse_ref[head : head + 1, :])
        delta = jnp.sum(weights * score_grad, axis=0, keepdims=True)
        score_grad = (weights * (score_grad - delta)).astype(BF)
        return weights.astype(BF), score_grad, own_q, own_g

    scores, raised, flips, key_grads, value_grads = {}, {}, [], [], []
    for n in range(HEADS + 2):
        if n < HEADS:
            scores[n] = score(n)
        if 0 <= n - 1 < HEADS:
            raised[n - 1] = soften(n - 1, *scores.pop(n - 1))
        if n >= 2:
            head = n - 2
            weights, score_grad, own_q, own_g = raised.pop(head)
            key_part, value_part = nn(score_grad, own_q), nn(weights, own_g)
            if head % 2 == 0:
                key_grads.append(key_part)
                value_grads.append(value_part)
            else:
                key_grads[-1] += key_part
                value_grads[-1] += value_part
            part = nn(k_flip[head * HEAD : (head + 1) * HEAD], score_grad)
            flips.append((part * SCALE).astype(BF))
    query_grad = jnp.concatenate(flips, 0).T
    text_grad = jnp.concatenate([p * SCALE for p in key_grads] + value_grads, 1).astype(BF)
    text_ref[...] = text_grad
    flip_ref[:, :states] = states_ref[...].astype(kind).T
    order(states)
    states_flip_ref[...] = ordered_ref[half:, :states].astype(BF)
    part = states * 2 * D // half
    for i in range(half // states):
        send_stage[i * states : (i + 1) * states, 3 * (tokens + D) :] = text_grad[
            :, i * part : (i + 1) * part
        ]
    lanes = slice(3 * (tokens + D), 3 * (tokens + D) + part)
    writes.append(
        pltpu.make_async_copy(send_stage.at[:, lanes], send.at[:, lanes], out_sems.at[3])
    )
    writes[-1].start()
    for load in loads[3:5]:
        load.wait()
    grad2 = nt(query_grad, w_query[...])
    unit, rstd = norm_parts(hidden1[...])
    normed2 = unit * gain2_ref[0:1, :] + gain2_ref[1:2, :]
    flip_ref[:, :tokens] = normed2.astype(BF).astype(kind).T
    order(tokens)
    write(1, query_grad)
    norms_ref[2:3, :] = jnp.sum(grad2 * unit, axis=0, keepdims=True)
    norms_ref[3:4, :] = jnp.sum(grad2, axis=0, keepdims=True)
    norms_ref[0:2, :] = jnp.zeros((2, D), F32)
    grad_hidden = norm_back(unit, rstd, gain2_ref[0:1, :], grad2) + hidden_grad_ref[...]
    hidden_grad_ref[...] = grad_hidden
    branch = grad_hidden.astype(BF)
    for load in loads[5:8]:
        load.wait()
    own_rows = pl.ds(pl.multiple_of(core * half, half), half)
    other_rows = pl.ds(pl.multiple_of((1 - core) * half, half), half)
    own_grad_ref[...] = nt(branch, w_self[own_rows, :]).astype(BF)
    other_grad_ref[...] = nt(branch, w_self[other_rows, :]).astype(BF)
    flip_ref[own_rows, :tokens] = own_ref[...].astype(kind).T
    flip_ref[other_rows, :tokens] = other_ref[...].astype(kind).T
    order(tokens)
    write(2, branch)
    for load in loads[8:]:
        load.wait()
    block_ref[...] = (hidden2_ref[...] + out_ref[...] + out_got_ref[...].astype(F32)).astype(BF)
    for copy in writes:
        copy.wait()


def cross_back(
    out, got, grad3, hidden2, g, norms, seen, lse, mixed, w_out, text_kv, queries, states,
    w_query, hidden1, own, other, w_self, core, order,
):
    tokens, width = other.shape
    count = order.shape[0]
    texts = states.shape[0]
    kind = BF if (D // count) % 16 == 0 else F32

    def full(*shape):
        return pl.BlockSpec(shape, lambda b, *_: (0,) * len(shape))

    wide, late = full(tokens, D), pl.BlockSpec(memory_space=pl.ANY)
    return pl.pallas_call(
        cross_back_kernel,
        grid_spec=pltpu.PrefetchScalarGridSpec(
            num_scalar_prefetch=2,
            grid=(1,),
            in_specs=[
                pl.BlockSpec((None, tokens, D), lambda b, *_: (1, 0, 0)),
                wide,
                wide,
                wide,
                full(1, D),
                full(2, D),
                full(texts, 1),
                full(HEADS, tokens),
                full(texts, D),
                pl.BlockSpec((texts, D), lambda b, *_: (0, 1)),
                full(texts, D),
            ]
            + [late] * 10,
            out_specs=[
                wide,
                wide,
                full(tokens, width),
                full(tokens, width),
                full(texts, 2 * D),
                full(8, D),
                full(D // 2, texts),
                late,
                late,
            ],
            scratch_shapes=[
                pltpu.VMEM((tokens, D), BF),
                pltpu.VMEM((D, D), BF),
                pltpu.VMEM((tokens, D), BF),
                pltpu.VMEM((D, D), BF),
                pltpu.VMEM((tokens, D), F32),
                pltpu.VMEM((tokens, width), BF),
                pltpu.VMEM((tokens, width), BF),
                pltpu.VMEM((D, D), BF),
                pltpu.VMEM((tokens, D), F32),
                pltpu.VMEM((tokens, D), BF),
                pltpu.VMEM((D, tokens), kind),
                pltpu.VMEM((D, tokens), kind),
                pltpu.VMEM((3, D // 2, tokens), BF),
                pltpu.VMEM((D // 2, 3 * (tokens + D) + 4 * texts), BF),
                pltpu.SemaphoreType.DMA((10,)),
                pltpu.SemaphoreType.DMA((7,)),
            ],
        ),
        out_shape=[
            jax.ShapeDtypeStruct((tokens, D), BF),
            jax.ShapeDtypeStruct((tokens, D), F32),
            jax.ShapeDtypeStruct((tokens, width), BF),
            jax.ShapeDtypeStruct((tokens, width), BF),
            jax.ShapeDtypeStruct((texts, 2 * D), BF),
            jax.ShapeDtypeStruct((8, D), F32),
            jax.ShapeDtypeStruct((D // 2, texts), BF),
            jax.ShapeDtypeStruct((3, D // 2, tokens), BF),
            jax.ShapeDtypeStruct((D // 2, 3 * (tokens + D) + 4 * texts), BF),
        ],
        compiler_params=pltpu.CompilerParams(vmem_limit_bytes=60 * MIB),
        cost_estimate=SMALL,
        name="cross_attention_back",
    )(
        core.reshape(1), order, got, grad3, hidden2, g, norms[2].reshape(1, D),
        jnp.stack(norms[:2]), seen, lse, text_kv, text_kv, states, mixed, w_out, queries,
        w_query, hidden1, own, other, w_self, out, got,
    )


def pair_kernel(keep_ref, own_ref, got_ref, states_ref, grad_ref, grad_got_ref, *outs):
    first_ref, second_ref, text_ref = outs
    step = pl.program_id(0)
    half, tokens = keep_ref.shape
    texts = grad_ref.shape[0]

    def put(product):
        first_ref[...] = product[: half // 2].astype(BF)
        second_ref[...] = product[half // 2 :].astype(BF)

    @pl.when(step < 3)
    def _():
        product = nn(keep_ref[...], own_ref[:, tokens:])
        put(product + nn(got_ref[:, :tokens], got_ref[:, tokens:]))

    @pl.when(step >= 3)
    def _():
        got = grad_got_ref[...].astype(F32)
        got = jnp.concatenate([got[:texts], got[texts:]], 1)
        got = jnp.concatenate([got[texts // 2 :], got[: texts // 2]], 0)
        grad = (grad_ref[...].astype(F32) + got).astype(BF)
        text_ref[...] = grad[: texts // 2]
        put(nn(states_ref[...], grad))


def pair_gradients(keep, own, got, states, grad):
    _, half, tokens = keep.shape
    texts = grad.shape[0]

    def third(s):
        return jnp.minimum(s, 2)

    def later(s):
        return jnp.maximum(s - 3, 0)

    wide = pl.BlockSpec((half, tokens + D), lambda s: (0, third(s)))
    lane = 3 * (tokens + D) // (4 * texts)
    grads = pl.BlockSpec((texts, D), lambda s: (0, later(s)))
    out = pl.BlockSpec((half // 2, D), lambda s: (0, s))
    return pl.pallas_call(
        pair_kernel,
        grid=(5,),
        in_specs=[
            pl.BlockSpec((None, half, tokens), lambda s: (third(s), 0, 0)),
            wide,
            wide,
            pl.BlockSpec((half, texts), lambda s: (0, 0)),
            grads,
            pl.BlockSpec((2 * texts, 4 * texts), lambda s: (later(s), lane)),
        ],
        out_specs=[out, out, pl.BlockSpec((texts // 2, D), lambda s: (0, later(s)))],
        out_shape=[jax.ShapeDtypeStruct((half // 2, 5 * D), BF)] * 2
        + [jax.ShapeDtypeStruct((texts // 2, 2 * D), BF)],
        compiler_params=pltpu.CompilerParams(vmem_limit_bytes=60 * MIB),
        cost_estimate=SMALL,
        name="pair_gradients",
    )(keep, own, got, states, grad, got)


def last_kernel(
    blocks_ref,
    x_ref,
    part_ref,
    got_ref,
    hidden_ref,
    gain_ref,
    norms_ref,
    image_ref,
    keep,
    send,
    norm_flip,
):
    count = blocks_ref.shape[0]
    height, half = D // count, D // 2
    grad = part_ref[...] + got_ref[...].astype(F32)
    unit, rstd = norm_parts(x_ref[...].astype(F32))
    sums = [jnp.sum(grad * unit, axis=0, keepdims=True), jnp.sum(grad, axis=0, keepdims=True)]
    image = norm_back(unit, rstd, gain_ref[...], grad) + hidden_ref[...]
    image_ref[...] = image.astype(BF)
    fill = jnp.zeros((norm_flip.shape[1] - 8, D), F32)
    norm_flip[...] = jnp.concatenate(sums + [norms_ref[2:8, :], fill], 0).T
    for i in range(count):
        at = pl.ds(pl.multiple_of(blocks_ref[i] * height, height), height)
        to = i * height % half
        target = keep if i < count // 2 else send
        target[to : to + height, :] = norm_flip[at, :].astype(BF)


def last_part(x, part, got, hidden_grad, gain, norms, blocks):
    tokens = got.shape[0]

    def full(*shape):
        return pl.BlockSpec(shape, lambda b, *_: (0,) * len(shape))

    wide = full(tokens, D)
    return pl.pallas_call(
        last_kernel,
        grid_spec=pltpu.PrefetchScalarGridSpec(
            num_scalar_prefetch=1,
            grid=(1,),
            in_specs=[wide] * 4 + [full(1, D), full(8, D)],
            out_specs=[wide, full(D // 2, 128), full(D // 2, 128)],
            scratch_shapes=[pltpu.VMEM((D, 128), F32)],
        ),
        out_shape=[jax.ShapeDtypeStruct((tokens, D), BF)]
        + [jax.ShapeDtypeStruct((D // 2, 128), BF)] * 2,
        compiler_params=pltpu.CompilerParams(vmem_limit_bytes=60 * MIB),
        cost_estimate=SMALL,
        name="norm_back",
    )(blocks, x, part, got, hidden_grad, gain.reshape(1, D), norms)


def add_kernel(a_ref, b_ref, keep_ref, send_ref):
    block, half = pl.program_id(0), pl.num_programs(0) // 2
    total = a_ref[...] + b_ref[...]

    @pl.when(block < half)
    def _():
        send_ref[...] = total

    @pl.when(block >= half)
    def _():
        keep_ref[...] = total


def add_halves(a, b):
    count, height, width = a.shape
    blocks = 4
    half = blocks // 2
    shape = (count // blocks, height, width)
    turned = pl.BlockSpec(shape, lambda i: ((i + half) % blocks, 0, 0))
    return pl.pallas_call(
        add_kernel,
        grid=(blocks,),
        in_specs=[turned] * 2,
        out_specs=[
            pl.BlockSpec(shape, lambda i: (jnp.maximum(i - half, 0), 0, 0)),
            pl.BlockSpec(shape, lambda i: (jnp.minimum(i, half - 1), 0, 0)),
        ],
        out_shape=[jax.ShapeDtypeStruct((count // 2, height, width), BF)] * 2,
        compiler_params=pltpu.CompilerParams(vmem_limit_bytes=60 * MIB),
        cost_estimate=SMALL,
        name="add_halves",
    )(a, b)


def behind(value, *others):
    return lax.optimization_barrier((value,) + others)[0]


class Route:
    def __init__(self, plan, orders):
        self.orders = orders
        count = plan.chips
        maps = np.zeros((2, count), np.int32)
        for core in range(2):
            for i in range(count):
                for s, bit in enumerate(orders[core]):
                    maps[core, i] |= ((i >> (plan.levels - 1 - s)) & 1) << bit
        here, there = jnp.asarray(maps)[plan.core], jnp.asarray(maps)[1 - plan.core]
        self.blocks = jnp.bitwise_xor(plan.chip, here).astype(jnp.int32)
        sent = jnp.bitwise_xor(plan.chip, there).astype(jnp.int32)
        self.devices = jnp.concatenate([2 * sent + 1 - plan.core, 2 * self.blocks + plan.core])
        backs = np.argsort(maps, axis=1).astype(np.int32)
        away = jnp.bitwise_xor(plan.chip, jnp.arange(count, dtype=jnp.int32))
        self.goes_to = jnp.take(jnp.asarray(backs)[plan.core], away, mode="clip")


class Plan:
    def __init__(self, n_img, n_txt):
        self.n_txt = n_txt
        self.n = n_img * n_txt
        self.chips = self.n // 2
        self.ny = n_txt // 2
        self.levels = self.chips.bit_length() - 1
        self.me = lax.axis_index("img") * n_txt + lax.axis_index("txt")
        self.core = self.me % 2
        self.chip = self.me // 2
        self.y = lax.axis_index("txt") // 2
        sources = (self.y - jnp.arange(self.ny, dtype=jnp.int32)) % self.ny
        self.places = jnp.concatenate([2 * sources + self.core, 2 * sources + 1 - self.core])
        at = jnp.arange(n_txt, dtype=jnp.int32)
        self.rows = jnp.bitwise_xor(at % 2, self.core) * self.ny + (self.y - at // 2) % self.ny
        rest = list(range(2, self.levels))
        self.near = Route(self, ([1, 0] + rest, [0, 1] + rest))
        self.small = Route(self, ([0] + rest + [1], [0] + rest + [1]))
        self.mixed = Route(self, ([1, 0] + rest, rest + [0, 1]))
        self.token = None

    def swap(self, value):
        return lax.ppermute(value, BOTH, [(d, d ^ 1) for d in range(self.n)])

    def shift_y(self, value, by):
        pairs = []
        for d in range(self.n):
            img, txt = divmod(d, self.n_txt)
            y, core = divmod(txt, 2)
            pairs.append((d, img * self.n_txt + ((y + by) % self.ny) * 2 + core))
        return lax.ppermute(value, BOTH, pairs)

    def halve(self, value, route, step):
        pairs = [(d, d ^ (2 << route.orders[d % 2][step])) for d in range(self.n)]
        return lax.ppermute(value, BOTH, pairs)

    def send_items(self, value, note=None):
        parts = []
        for k in range(self.ny):
            part = value[(self.y + k) % self.ny]
            if note is not None:
                part = jnp.concatenate([part, note], 0)
            parts.append(self.shift_y(part, k) if k else part)
        return parts

    def join_items(self, parts, length):
        notes = [p[length:] for p in parts] if parts[0].shape[0] > length else []
        return jnp.concatenate([p[:length] for p in parts] + notes, 0)

    def return_items(self, value):
        return [self.shift_y(value[k], -k) if k else value[0] for k in range(self.ny)]

    def order_items(self, parts):
        stacked = jnp.stack(parts)
        return jnp.stack([stacked[(i - self.y) % self.ny] for i in range(self.ny)])

    def start(self, keep, send, route, step=0):
        return keep, self.halve(send, route, step), route, step

    def advance(self, state):
        keep, got, route, step = state
        keep, got, _ = lax.optimization_barrier((keep, got, self.token))
        if keep.shape[0] == 1:
            self.token = keep[0].astype(F32) + got[0].astype(F32)
            return self.token
        if keep.size > 1 << 20:
            keep, send = add_halves(keep, got)
        else:
            total = (keep.astype(F32) + got.astype(F32)).astype(BF)
            keep, send = jnp.split(total, 2)
        keep, send = lax.optimization_barrier((keep, send))
        self.token = send
        return self.start(keep, send, route, step + 1)

    def then(self, *values):
        return lax.optimization_barrier(values + (self.token,))[:-1]


def per_device(
    n_img,
    n_txt,
    image_tokens,
    text_states,
    text_segments,
    item_segments,
    norm1_gain,
    norm1_bias,
    w_qkv,
    w_self_out,
    norm2_gain,
    norm2_bias,
    w_cross_q,
    w_cross_kv,
    w_cross_out,
    norm3_gain,
    norm3_bias,
    w_up,
    w_down,
    cotangent,
):
    plan = Plan(n_img, n_txt)
    core, n, chips, ny = plan.core, plan.n, plan.chips, plan.ny
    items, length, _ = image_tokens.shape
    tokens = items * length
    half_d = D // 2
    rows = D // n

    states = text_states.shape[1]
    ids = jnp.pad(text_segments.astype(BF), ((0, 15), (0, D - states)))
    note = jnp.concatenate([text_states[0], ids], 0)
    x_parts = plan.send_items(image_tokens, note)
    g_parts = plan.send_items(behind(cotangent, x_parts[-1]))
    x_own = plan.join_items(x_parts, length)
    x_other = plan.swap(x_own)

    notes = [v[tokens:].reshape(ny, states + 16, D) for v in (x_own, x_other)]
    notes = jnp.concatenate(notes, 0)
    ids = notes[:, states, :states].reshape(-1)
    states_all = notes[:, :states].reshape(-1, D)
    text_kv = nn(states_all, w_cross_kv).astype(BF)
    matches = ids == item_segments[0, plan.y].astype(BF)
    seen = jnp.where(matches, 0.0, MASKED).astype(F32)[:, None]

    joined, normed1 = project_all(
        x_own, x_other, norm1_gain, norm1_bias, w_qkv, core, plan.places, length
    )
    mixed, mixed_other, lse = attend(joined, plan.rows)
    mixed_got = plan.swap(mixed_other)
    g_own = plan.join_items([behind(p, mixed_got) for p in g_parts], length)
    g_other = plan.swap(g_own)

    norms = (norm2_gain, norm2_bias, norm3_gain, norm3_bias)
    hidden1, hidden2, normed3, cross_q, cross_mixed, cross_lse = cross_part(
        x_own,
        mixed,
        mixed_got,
        text_kv,
        seen,
        norms,
        w_self_out,
        w_cross_q,
        w_cross_out,
        core,
    )

    normed3_other = plan.swap(normed3)
    per_down = w_down.shape[0] // n
    out, grad3, sent, low_keep, high_keep, low_send, high_send = mlp(
        normed3,
        normed3_other,
        g_own,
        g_other,
        w_up,
        w_down,
        core,
        plan.mixed.blocks,
        plan.mixed.goes_to,
    )
    high_got = plan.halve(high_send, plan.mixed, 0)
    got = plan.swap(sent)


    block_out, grad_hidden1, grad_own, grad_other, grad_kv, norm_sums, states_flip, keep, send = (
        cross_back(
            out, got, grad3, hidden2, g_own, norms[:3], seen, cross_lse, cross_mixed, w_cross_out,
            text_kv, cross_q, states_all, w_cross_q, hidden1, mixed, mixed_got, w_self_out,
            core, plan.near.devices,
        )
    )
    grad_other, high_got = lax.optimization_barrier((grad_other, high_got))
    grad_got = plan.swap(grad_other)
    pair_got = plan.swap(behind(send, grad_got))
    plan.token = grad_other
    high_keep, high_got = plan.then(high_keep, high_got)
    low_got = plan.halve(behind(low_send, high_got), plan.mixed, 0)
    high_sum = (high_keep.astype(F32) + high_got.astype(F32)).astype(BF)
    plan.token = high_sum
    next_got = plan.halve(high_sum, plan.mixed, 1)
    block_parts = plan.return_items(block_out.reshape(ny, length, D))

    grad_got, grad_own = plan.then(grad_got, grad_own)
    last_keep, last_send, part_own, part_other = attend_back(
        joined, grad_own, grad_got, mixed, lse, normed1, w_qkv, core, plan.rows, plan.near.blocks
    )
    plan.token = part_other
    last_sums = plan.start(
        last_keep.reshape(chips // 2, 2 * rows, -1),
        last_send.reshape(chips // 2, 2 * rows, -1),
        plan.near,
    )
    send, pair_got, *block_parts = plan.then(send, pair_got, *block_parts)
    middle_keep, middle_send, text_sum = pair_gradients(
        keep, send, pair_got, states_flip, grad_kv
    )
    plan.token = middle_send
    middle_sums = plan.start(
        middle_keep.reshape(chips // 2, rows, -1),
        middle_send.reshape(chips // 2, rows, -1),
        plan.near,
    )
    part_got = plan.swap(behind(part_other, middle_send))
    part_got, part_own = plan.then(part_got, part_own)
    image_grad, norm_keep, norm_send = last_part(
        x_own, part_own, part_got, grad_hidden1, norm1_gain, norm_sums, plan.small.blocks
    )
    plan.token = norm_send
    norm_group = plan.start(
        norm_keep.reshape(chips // 2, 2 * rows, -1),
        norm_send.reshape(chips // 2, 2 * rows, -1),
        plan.small,
    )
    low_keep, low_got, next_got = plan.then(low_keep, low_got, next_got)
    low_sum = low_keep.astype(F32) + low_got.astype(F32) + next_got.astype(F32)
    plan.token = low_sum = lax.optimization_barrier(low_sum.astype(BF))
    low_keep, low_send = jnp.split(low_sum, 2)
    mlp_sums = plan.start(low_keep, low_send, plan.mixed, 2)
    last_sums = plan.advance(last_sums)
    last_sums = plan.advance(last_sums)
    middle_sums = plan.advance(middle_sums)
    mlp_sums = plan.advance(mlp_sums)
    norm_group = plan.advance(norm_group)
    text_sum, image_grad = plan.then(text_sum, image_grad)
    text_part = nt(text_sum, w_cross_kv)
    plan.token = text_part
    text_part = text_part.reshape(ny, states, D)
    text_parts = [plan.shift_y(text_part[r].astype(BF), -r) for r in range(1, ny)]
    block_out = plan.order_items(plan.then(*block_parts))
    for _ in range(plan.levels - 3):
        last_sums = plan.advance(last_sums)
    norm_group = plan.advance(norm_group)
    for _ in range(plan.levels - 3):
        mlp_sums = plan.advance(mlp_sums)
    for _ in range(plan.levels - 3):
        middle_sums = plan.advance(middle_sums)
        (image_grad,) = plan.then(image_grad)
        norm_group = plan.advance(norm_group)
    image_parts = plan.return_items(image_grad.reshape(ny, length, D))
    middle_sums = plan.advance(middle_sums)
    last_sums = plan.advance(last_sums)
    norm_group = plan.advance(norm_group)
    last_sums = jnp.concatenate([last_sums, norm_group], 1)
    up_down = mlp_sums

    units = w_up.shape[1] // 2
    down_grad = jnp.concatenate([up_down[:, units : units + D], up_down[:, units + D :]], 0)
    parts = jnp.concatenate([up_down[:, :units], last_sums], 1).reshape(2, rows, -1)
    mine = parts[core]
    sent = parts[1 - core].astype(BF)
    theirs = plan.swap(sent)
    plan.token = sent
    text_part, *text_parts = plan.then(text_part, *text_parts)
    text_grad = sum((p.astype(F32) for p in text_parts), text_part[0])
    image_grad = plan.order_items(plan.then(*image_parts)).astype(F32)
    plan.token = image_grad
    (theirs,) = plan.then(theirs)
    theirs = theirs.astype(F32)
    by_core = jnp.where(core == 0, jnp.stack([mine, theirs]), jnp.stack([theirs, mine]))
    up_grad = by_core[:, :, :units].reshape(2, rows, chips, per_down)
    up_grad = up_grad.transpose(1, 2, 0, 3).reshape(rows, 2 * units)
    wide = by_core[:, :, units : units + 3 * half_d].reshape(2, rows, -1, 3, 2 * HEAD)
    wide = wide.transpose(1, 3, 0, 2, 4).reshape(rows, 3 * D)
    up_grad, wide = lax.optimization_barrier((up_grad, wide))
    plan.token = wide
    middle_sums = plan.advance(middle_sums)
    norm_sums = mine[:, -128:-122] + theirs[:, -128:-122]
    return (
        block_out,
        image_grad,
        text_grad[None],
        norm_sums[:, 0],
        norm_sums[:, 1],
        wide,
        middle_sums[:, 2 * D : 3 * D],
        norm_sums[:, 2],
        norm_sums[:, 3],
        middle_sums[:, D : 2 * D],
        middle_sums[:, 3 * D :],
        middle_sums[:, :D],
        norm_sums[:, 4],
        norm_sums[:, 5],
        up_grad,
        down_grad,
    )


def solution(mesh):
    split = P("img", "txt", None)
    rows = P(BOTH)
    wide = P(BOTH, None)
    return jax.shard_map(
        partial(per_device, mesh.shape["img"], mesh.shape["txt"]),
        mesh=mesh,
        in_specs=(split, split, P("img", "txt"), P("img", None)) + (P(),) * 13 + (split,),
        out_specs=(
            (split,) * 3
            + (rows, rows, wide, wide)
            + (rows, rows, wide, wide, wide)
            + (rows, rows, wide, wide)
        ),
        check_vma=False,
    )
```
